32 devices in a mesh: dp: 8 (over z, x), tensor: 4 (over y, core).
Axes of the slice: x: 2, y: 2, z: 4, core: 2. Of those that a mesh axis runs over, the one named last changes fastest.
Arguments:
- tokens: bfloat16 [8192, 1152], P(('dp', 'tensor')), may hold values from -6 to 6
- cotangent: bfloat16 [8192, 1152], P(('dp', 'tensor')), may hold values from -6 to 6
- prefix: int32 [8], P('dp'), may hold values from 102 to 512, as said below
- query_weight: float32 [1152, 1024], P('dp', 'tensor'), may hold values from -0.1875 to 0.1875
- keyval_weight: float32 [1152, 512], P('dp'), may hold values from -0.1875 to 0.1875
- output_weight: float32 [1152, 1024], P('dp', 'tensor'), may hold values from -0.1875 to 0.1875
- gateup_weight: float32 [1152, 2, 6912], P('dp', None, 'tensor'), may hold values from -0.1875 to 0.1875
- down_weight: float32 [1152, 6912], P('dp', 'tensor'), may hold values from -0.078125 to 0.078125
- norm_gains: float32 [5120], P('dp'), may hold values from -0.5 to 0.5
- query_first: float32 [1152, 1024], P('dp', 'tensor'), may hold values from -512 to 512
- keyval_first: float32 [1152, 512], P('dp'), may hold values from -256 to 256
- output_first: float32 [1152, 1024], P('dp', 'tensor'), may hold values from -64 to 64
- gateup_first: float32 [1152, 2, 6912], P('dp', None, 'tensor'), may hold values from -24 to 24
- down_first: float32 [1152, 6912], P('dp', 'tensor'), may hold values from -64 to 64
- gains_first: float32 [5120], P('dp'), may hold values from -128 to 128
- query_second: float32 [1152, 1024], P('dp', 'tensor'), may hold values from 27787.264 to 110100.48
- keyval_second: float32 [1152, 512], P('dp'), may hold values from 6946.816 to 27525.12
- output_second: float32 [1152, 1024], P('dp', 'tensor'), may hold values from 434.176 to 1720.32
- gateup_second: float32 [1152, 2, 6912], P('dp', None, 'tensor'), may hold values from 69.46816 to 275.2512
- down_second: float32 [1152, 6912], P('dp', 'tensor'), may hold values from 434.176 to 1720.32
- gains_second: float32 [5120], P('dp'), may hold values from 1736.704 to 6881.28
Outputs:
- block_out: bfloat16 [8192, 1152], P(('dp', 'tensor'))
- tokens_grad: bfloat16 [8192, 1152], P(('dp', 'tensor'))
- query_moment: float32 [1152, 1024], P('dp', 'tensor')
- query_square: float32 [1152, 1024], P('dp', 'tensor')
- query_master: float32 [1152, 1024], P('dp', 'tensor')
- keyval_moment: float32 [1152, 512], P('dp')
- keyval_square: float32 [1152, 512], P('dp')
- keyval_master: float32 [1152, 512], P('dp')
- output_moment: float32 [1152, 1024], P('dp', 'tensor')
- output_square: float32 [1152, 1024], P('dp', 'tensor')
- output_master: float32 [1152, 1024], P('dp', 'tensor')
- gateup_moment: float32 [1152, 2, 6912], P('dp', None, 'tensor')
- gateup_square: float32 [1152, 2, 6912], P('dp', None, 'tensor')
- gateup_master: float32 [1152, 2, 6912], P('dp', None, 'tensor')
- down_moment: float32 [1152, 6912], P('dp', 'tensor')
- down_square: float32 [1152, 6912], P('dp', 'tensor')
- down_master: float32 [1152, 6912], P('dp', 'tensor')
- gains_moment: float32 [5120], P('dp')
- gains_square: float32 [5120], P('dp')
- gains_master: float32 [5120], P('dp')
The draws below stay inside these ranges and needn't reach their ends.
Inputs may be any that keep to these rules, and one draw needn't show every extreme that they name: prefix[s] is how many leading tokens of sequence s see one another in both directions; in every draw some sequence has exactly 512 and another exactly 102.
All inputs are finite; a program needn't handle non-finite values.
Results may differ from the reference program's by a relative error of at most 0.023.
Values may be sent and summed in bfloat16 or wider, within the bound.
A program may use at most 192 MiB of HBM per device.

```python
import math
import jax
import jax.numpy as jnp
from jax import lax

D = 1152
FF = 6912
HEADS = 4
HEAD_DIM = 256
STEP = 10
LEN = 1024
SEQS = 8
TOKENS = 8192
GAINS = 5120


def draw_prefix(key, part):
    key = jax.random.fold_in(key, 7)
    low_end = LEN // 10
    high_end = LEN // 2
    key_draw, key_pick = jax.random.split(key)
    values = jax.random.randint(key_draw, (SEQS,), low_end, high_end + 1, dtype=jnp.int32)
    shuffled = jax.random.permutation(key_pick, SEQS)
    values = values.at[shuffled[0]].set(high_end)
    values = values.at[shuffled[1]].set(low_end)
    return values


def steps_of(stream_key, dims, cuts, least, top_value):
    def one(position, shards_of):
        steps = jax.random.uniform(jax.random.fold_in(jax.random.fold_in(stream_key, 6), position), (shards_of,), jnp.float32, least / len(cuts), top_value / len(cuts))
        return jnp.repeat(jnp.exp(steps), dims[position] // shards_of).reshape((-1,) + (1,) * (len(dims) - position - 1))

    gain = one(*cuts[0])
    for cut in cuts[1:]:
        gain = gain * one(*cut)
    return gain


def centred(own_key, extent, spread, bound, cuts=(), kind=jnp.bfloat16):
    array = jax.random.normal(own_key, extent, jnp.float32) * spread
    if len(cuts) > 0:
        array = steps_of(own_key, extent, cuts, -0.22, 0.18) * array
    return jnp.clip(array, min=-bound, max=bound).astype(kind)


def setup_inputs(seed: int = 0) -> dict:
    seeds = jax.random.split(jax.random.key(seed), 22)
    return {
        "tokens": centred(seeds[0], (TOKENS, D), 1.0, 6.0, ((0, 32),)),
        "cotangent": centred(seeds[1], (TOKENS, D), 1.0, 6.0, ((0, 32),)),
        "prefix": draw_prefix(jax.random.fold_in(seeds[21], 71), 0),
        "query_weight": centred(seeds[3], (D, HEADS * HEAD_DIM), D ** -0.5, 0.1875, ((0, 8), (1, 4)), jnp.float32),
        "keyval_weight": centred(seeds[4], (D, 2 * HEAD_DIM), D ** -0.5, 0.1875, ((0, 8),), jnp.float32),
        "output_weight": centred(seeds[5], (D, HEADS * HEAD_DIM), (HEADS * HEAD_DIM) ** -0.5, 0.1875, ((0, 8), (1, 4)), jnp.float32),
        "gateup_weight": centred(seeds[6], (D, 2, FF), D ** -0.5, 0.1875, ((0, 8), (2, 4)), jnp.float32),
        "down_weight": centred(seeds[7], (D, FF), FF ** -0.5, 0.078125, ((0, 8), (1, 4)), jnp.float32),
        "norm_gains": jnp.clip(jax.random.uniform(seeds[8], (GAINS,), jnp.float32, -0.5, 0.5) * steps_of(seeds[8], (GAINS,), ((0, 8),), -0.4, 0.0), -0.5, 0.5),
        "query_first": centred(seeds[9], (D, HEADS * HEAD_DIM), (0.11 * 8 * TOKENS ** 0.5), 512.0, ((0, 8), (1, 4)), jnp.float32),
        "keyval_first": centred(seeds[10], (D, 2 * HEAD_DIM), (0.11 * 4 * TOKENS ** 0.5), 256.0, ((0, 8),), jnp.float32),
        "output_first": centred(seeds[11], (D, HEADS * HEAD_DIM), (0.11 * TOKENS ** 0.5), 64.0, ((0, 8), (1, 4)), jnp.float32),
        "gateup_first": centred(seeds[12], (D, 2, FF), (0.11 * 0.4 * TOKENS ** 0.5), 24.0, ((0, 8), (2, 4)), jnp.float32),
        "down_first": centred(seeds[13], (D, FF), (0.11 * TOKENS ** 0.5), 64.0, ((0, 8), (1, 4)), jnp.float32),
        "gains_first": centred(seeds[14], (GAINS,), (0.11 * 2 * TOKENS ** 0.5), 128.0, ((0, 8),), jnp.float32),
        "query_second": jnp.clip(jnp.exp(math.log(110100.48) - 1.3768156 * jax.random.uniform(seeds[15], (D, HEADS * HEAD_DIM), jnp.float32) ** steps_of(seeds[15], (D, HEADS * HEAD_DIM), ((0, 8), (1, 4)), -0.2, 0.2)), 27787.264, 110100.48),
        "keyval_second": jnp.clip(jnp.exp(math.log(27525.12) - 1.3768156 * jax.random.uniform(seeds[16], (D, 2 * HEAD_DIM), jnp.float32) ** steps_of(seeds[16], (D, 2 * HEAD_DIM), ((0, 8),), -0.2, 0.2)), 6946.816, 27525.12),
        "output_second": jnp.clip(jnp.exp(math.log(1720.32) - 1.3768156 * jax.random.uniform(seeds[17], (D, HEADS * HEAD_DIM), jnp.float32) ** steps_of(seeds[17], (D, HEADS * HEAD_DIM), ((0, 8), (1, 4)), -0.2, 0.2)), 434.176, 1720.32),
        "gateup_second": jnp.clip(jnp.exp(math.log(275.2512) - 1.3768155 * jax.random.uniform(seeds[18], (D, 2, FF), jnp.float32) ** steps_of(seeds[18], (D, 2, FF), ((0, 8), (2, 4)), -0.2, 0.2)), 69.46816, 275.2512),
        "down_second": jnp.clip(jnp.exp(math.log(1720.32) - 1.3768156 * jax.random.uniform(seeds[19], (D, FF), jnp.float32) ** steps_of(seeds[19], (D, FF), ((0, 8), (1, 4)), -0.2, 0.2)), 434.176, 1720.32),
        "gains_second": jnp.clip(jnp.exp(math.log(6881.28) - 1.3768156 * jax.random.uniform(seeds[20], (GAINS,), jnp.float32) ** steps_of(seeds[20], (GAINS,), ((0, 8),), -0.2, 0.2)), 1736.704, 6881.28),
    }


@jax.custom_vjp
def low(v):
    return lax.optimization_barrier(v.astype(jnp.bfloat16)).astype(jnp.float32)

@jax.custom_vjp
def low_back(v):
    return v

def low_keep(v):
    return (low(v), None)

def low_pass(kept, grad):
    return (grad,)

def back_keep(v):
    return (v, None)

def back_low(kept, grad):
    return (low(grad),)
low.defvjp(low_keep, low_pass)
low_back.defvjp(back_keep, back_low)
eps_norm = 1e-06
query_scale = 0.0625
rope_base = 1000000.0
beta_first = 0.9
beta_second = 0.95
adam_eps = 1e-08
decay_rate = 0.01
masked_fill = -1e+30
highest = lax.Precision.HIGHEST

def matmul(left, right):
    return jnp.dot(left, right, precision=highest, preferred_element_type=jnp.float32)

def rms_scale(vector, gain_vec):
    return vector * lax.rsqrt(lax.optimization_barrier(jnp.mean(vector * vector, axis=-1, keepdims=True)) + eps_norm) * (1.0 + gain_vec)

def rotate(vector, positions):
    half_dim = vector.shape[-1] // 2
    inv_freq = rope_base ** (-2.0 * jnp.arange(half_dim).astype(jnp.float32) / vector.shape[-1])
    angles = positions[:, None] * inv_freq[None, :]
    cosine = jnp.cos(angles)[:, None, :]
    sine_v = jnp.sin(angles)[:, None, :]
    front_half = vector[..., :half_dim]
    back_half = vector[..., half_dim:]
    return jnp.concatenate([front_half * cosine - back_half * sine_v, back_half * cosine + front_half * sine_v], axis=-1)

def attend(query_rot, key_rot, value_low, prefix_len):
    length = query_rot.shape[0]
    span_rows = min(512, length)
    columns = jnp.arange(length, dtype=jnp.int32)

    def one_block(row_start):
        row_ids = row_start + jnp.arange(span_rows, dtype=jnp.int32)
        q_blk = lax.dynamic_slice_in_dim(query_rot, row_start, span_rows, 0)
        raw_scores = low_back(jnp.einsum('rhd,kd->hrk', q_blk, key_rot, precision=highest) * query_scale)
        allowed = (columns[None, :] <= row_ids[:, None]) | (columns[None, :] < prefix_len)
        masked = jnp.where(allowed[None], raw_scores, masked_fill)
        row_peak = lax.optimization_barrier(jnp.max(masked, axis=-1, keepdims=True))
        shifted = jnp.exp(masked - row_peak)
        soft_probs = low(shifted / lax.optimization_barrier(jnp.sum(shifted, axis=-1, keepdims=True)))
        return jnp.einsum('hrk,kd->rhd', soft_probs, value_low, precision=highest)
    starts = jnp.arange(0, length, span_rows, dtype=jnp.int32)
    pieces = lax.map(jax.checkpoint(one_block), starts)
    return pieces.reshape(length, query_rot.shape[1], query_rot.shape[2])

def layer(inputs, query_weight, keyval_weight, output_weight, gateup_weight, down_weight, norm_gains, prefix_len):
    d_model = inputs.shape[1]
    length = inputs.shape[0]
    head_dim = keyval_weight.shape[1] // 2
    query_w = low(query_weight)
    keyval_w = low(keyval_weight)
    output_w = low(output_weight)
    gateup_w = low(gateup_weight)
    down_w = low(down_weight)
    gains_low = low(norm_gains)
    gain_input = gains_low[0:d_model]
    gain_attn = gains_low[d_model:2 * d_model]
    gain_pre = gains_low[2 * d_model:3 * d_model]
    gain_ffn = gains_low[3 * d_model:4 * d_model]
    gain_query = gains_low[4 * d_model:4 * d_model + head_dim]
    gain_key = gains_low[4 * d_model + head_dim:4 * d_model + 2 * head_dim]
    positions = jnp.arange(length).astype(jnp.float32)
    normed = low(rms_scale(inputs, gain_input))
    query_raw = low_back(matmul(normed, query_w)).reshape(length, -1, head_dim)
    keyval_raw = low_back(matmul(normed, keyval_w))
    query_rot = low(rotate(rms_scale(query_raw, gain_query), positions))
    key_rot = low(rotate(rms_scale(keyval_raw[:, None, :head_dim], gain_key), positions)[:, 0])
    value_low = low(keyval_raw[:, head_dim:])
    attended = low(low_back(attend(query_rot, key_rot, value_low, prefix_len))).reshape(length, -1)
    projected = low_back(matmul(attended, output_w.T))
    hidden_state = inputs + rms_scale(projected, gain_attn)
    normed_two = low(rms_scale(hidden_state, gain_pre))
    gateup = low_back(matmul(normed_two, gateup_w.reshape(d_model, -1)))
    units = gateup.shape[1] // 2
    activation = low(jax.nn.gelu(gateup[:, :units], approximate=True) * gateup[:, units:])
    down_rows = low_back(matmul(activation, down_w.T))
    return hidden_state + rms_scale(down_rows, gain_ffn)

def adam_step(weight, gradient, moment, second, step_rate):
    moment = beta_first * moment + (1.0 - beta_first) * gradient
    second = beta_second * second + (1.0 - beta_second) * gradient * gradient
    scaled = moment / (1.0 - beta_first ** STEP) / (jnp.sqrt(second / (1.0 - beta_second ** STEP)) + adam_eps)
    return (moment, second, weight - step_rate * (scaled + decay_rate * weight))

def reference(tokens, cotangent, prefix, query_weight, keyval_weight, output_weight, gateup_weight, down_weight, norm_gains, query_first, keyval_first, output_first, gateup_first, down_first, gains_first, query_second, keyval_second, output_second, gateup_second, down_second, gains_second):
    masters = (query_weight, keyval_weight, output_weight, gateup_weight, down_weight, norm_gains)
    seq_tokens = tokens.astype(jnp.float32).reshape(SEQS, LEN, D)
    seq_cot = cotangent.astype(jnp.float32).reshape(SEQS, LEN, D)

    def per_sequence(totals, batch_item):
        inputs, grad_out, prefix_len = batch_item

        def forward(inputs_f, *weights):
            return layer(inputs_f, *weights, prefix_len)
        outputs, pull_fn = jax.vjp(forward, inputs, *masters)
        gradients = pull_fn(grad_out)
        totals = tuple((running + part_grad for running, part_grad in zip(totals, gradients[1:])))
        return (totals, (outputs.astype(jnp.bfloat16), gradients[0].astype(jnp.bfloat16)))
    zero_grads = tuple((jnp.zeros_like(weight) for weight in masters))
    totals, (block_rows, grad_rows) = lax.scan(per_sequence, zero_grads, (seq_tokens, seq_cot, prefix))
    block_out = block_rows.reshape(TOKENS, D)
    tokens_grad = grad_rows.reshape(TOKENS, D)
    query_moment, query_square, query_master = adam_step(query_weight, totals[0], query_first, query_second, D ** (-0.5))
    keyval_moment, keyval_square, keyval_master = adam_step(keyval_weight, totals[1], keyval_first, keyval_second, D ** (-0.5))
    output_moment, output_square, output_master = adam_step(output_weight, totals[2], output_first, output_second, (HEADS * HEAD_DIM) ** (-0.5))
    gateup_moment, gateup_square, gateup_master = adam_step(gateup_weight, totals[3], gateup_first, gateup_second, D ** (-0.5))
    down_moment, down_square, down_master = adam_step(down_weight, totals[4], down_first, down_second, FF ** (-0.5))
    gains_moment, gains_square, gains_master = adam_step(norm_gains, totals[5], gains_first, gains_second, 0.3)
    return (block_out, tokens_grad, query_moment, query_square, query_master, keyval_moment, keyval_square, keyval_master, output_moment, output_square, output_master, gateup_moment, gateup_square, gateup_master, down_moment, down_square, down_master, gains_moment, gains_square, gains_master)
```

```python
import functools

import jax
import jax.numpy as jnp
import numpy as np
from jax import lax
from jax.experimental import pallas as pl
from jax.experimental.pallas import tpu as pltpu
from jax.sharding import PartitionSpec as P

D = 1152
FF = 6912
HEADS = 4
HEAD_DIM = 256
STEP = 10


eps_norm = 1e-06
query_scale = 0.0625
rope_base = 1000000.0
beta_first = 0.9
beta_second = 0.95
adam_eps = 1e-08
decay_rate = 0.01
masked_fill = -1e30
MESH = pl.DeviceIdType.MESH
low = jnp.bfloat16
full = jnp.float32
CHUNK = 512


def dot_nn(left, right):
    return lax.dot_general(left, right, (((1,), (0,)), ((), ())), preferred_element_type=full)


def dot_nt(left, right):
    return lax.dot_general(left, right, (((1,), (1,)), ((), ())), preferred_element_type=full)


def dot_tn(left, right):
    return lax.dot_general(left, right, (((0,), (0,)), ((), ())), preferred_element_type=full)


def chunks_of(units):
    out = []
    first = 0
    while first < units:
        width = min(CHUNK, units - first)
        out.append((first, width, -(-width // 128) * 128))
        first += width
    return out


def packed_columns(units, head_dim):
    at = 4 * head_dim
    places = []
    for first, width, padded in chunks_of(units):
        places.append((at, at + padded, at + 2 * padded))
        at += 3 * padded
    return places, at


class Place:
    def __init__(self, lines):
        self.lines = lines
        self.dp = lax.axis_index("dp")
        self.tensor = lax.axis_index("tensor")
        self.z = self.dp // 2
        self.x = self.dp % 2
        self.y = self.tensor // 2
        self.core = self.tensor % 2
        self.mate = (self.dp, self.y * 2 + (1 - self.core))
        self.across = (self.dp, (1 - self.y) * 2 + self.core)
        self.side = (self.z * 2 + (1 - self.x), self.tensor)

    def line(self, step):
        return ((lax.rem(self.z + step, self.lines)) * 2 + self.x, self.tensor)

    def peers(self):
        return [self.mate, self.across, self.side] + [self.line(s) for s in range(1, self.lines)]


def meet(place):
    barrier = pltpu.get_barrier_semaphore()
    peers = place.peers()
    for peer in peers:
        pl.semaphore_signal(barrier, inc=1, device_id=peer, device_id_type=MESH)
    pl.semaphore_wait(barrier, len(peers))


def remote(source, target, send_sem, recv_sem, device):
    return pltpu.make_async_remote_copy(
        src_ref=source,
        dst_ref=target,
        send_sem=send_sem,
        recv_sem=recv_sem,
        device_id=device,
        device_id_type=MESH,
    )


class LineGather:
    def __init__(self, place, region, count, send, recv, send_side, recv_side):
        self.place, self.region, self.count = place, region, count
        self.send, self.recv, self.send_side, self.recv_side = send, recv, send_side, recv_side

    def along(self, group, step):
        block = self.region(group, self.place.dp)
        return remote(block, block, self.send.at[group, step], self.recv.at[group, step], self.place.line(step))

    def sideways(self, group, step):
        origin = lax.rem(self.place.z + self.place.lines - step, self.place.lines) * 2 + self.place.x
        block = self.region(group, origin)
        return remote(
            block, block, self.send_side.at[group, step], self.recv_side.at[group, step], self.place.side
        )

    def start(self, group):
        for step in range(1, self.place.lines):
            self.along(group, step).start()
        self.sideways(group, 0).start()

    def pump(self, group):
        for step in range(1, self.place.lines):
            origin = lax.rem(self.place.z + self.place.lines - step, self.place.lines) * 2 + self.place.x
            block = self.region(group, origin)
            remote(
                block, block, self.send.at[group, step], self.recv.at[group, step], self.place.line(step)
            ).wait_recv()
            self.sideways(group, step).start()

    def ready(self, group):
        for step in range(self.place.lines):
            origin = lax.rem(self.place.z + self.place.lines - step, self.place.lines) * 2 + (1 - self.place.x)
            block = self.region(group, origin)
            remote(
                block, block, self.send_side.at[group, step], self.recv_side.at[group, step], self.place.side
            ).wait_recv()

    def finish(self):
        for group in range(self.count):
            for step in range(1, self.place.lines):
                self.along(group, step).wait_send()
            for step in range(self.place.lines):
                self.sideways(group, step).wait_send()


class RowGather:
    def __init__(self, place, source, buffer, rows, send, recv):
        self.place, self.source, self.buffer, self.rows = place, source, buffer, rows
        self.send, self.recv = send, recv

    def slab(self, y, core):
        return self.buffer.at[pl.ds((y * 2 + core) * self.rows, self.rows)]

    def copy(self, index):
        place = self.place
        slab = self.slab(1 - place.y if index == 2 else place.y, place.core)
        source = slab if index == 2 else self.source
        device = place.across if index == 1 else place.mate
        return remote(source, slab, self.send.at[index], self.recv.at[index], device)

    def arrival(self, index, y, core):
        slab = self.slab(y, core)
        remote(slab, slab, self.send.at[index], self.recv.at[index], self.place.mate).wait_recv()

    def start(self):
        self.copy(1).start()
        self.copy(0).start()

    def wait_mate(self):
        self.arrival(0, self.place.y, 1 - self.place.core)

    def wait_across(self):
        self.arrival(1, 1 - self.place.y, self.place.core)
        self.copy(2).start()

    def wait_corner(self):
        self.arrival(2, 1 - self.place.y, 1 - self.place.core)

    def finish(self):
        for index in range(3):
            self.copy(index).wait_send()


class RowScatter:
    def __init__(self, place, part, rows, first, second, mixed, send, recv):
        self.place, self.part, self.rows = place, part, rows
        self.first, self.second, self.mixed = first, second, mixed
        self.send, self.recv = send, recv

    def slab(self, y, core):
        return self.part.at[pl.ds((y * 2 + core) * self.rows, self.rows)]

    def copy(self, index):
        place = self.place
        if index == 2:
            return remote(self.mixed, self.second, self.send.at[2], self.recv.at[2], place.across)
        source = self.slab(1 - place.y if index == 0 else place.y, 1 - place.core)
        return remote(source, self.first.at[index], self.send.at[index], self.recv.at[index], place.mate)

    def order(self):
        place = self.place
        return (
            (1 - place.y) * 2 + (1 - place.core),
            (1 - place.y) * 2 + place.core,
            place.y * 2 + (1 - place.core),
            place.y * 2 + place.core,
        )

    def after(self, step):
        if step == 0:
            self.copy(0).start()
        if step == 1:
            self.copy(0).wait_recv()
            mixed = self.slab(1 - self.place.y, self.place.core)[...].astype(full) + self.first[0].astype(full)
            self.mixed[...] = mixed.astype(low)
            self.copy(2).start()
        if step == 2:
            self.copy(1).start()

    def total(self):
        self.copy(1).wait_recv()
        here = self.slab(self.place.y, self.place.core)[...].astype(full) + self.first[1].astype(full)
        self.copy(2).wait_recv()
        return here + self.second[...].astype(full)

    def finish(self):
        for index in range(3):
            self.copy(index).wait_send()


def inverse_rms(rows):
    return lax.rsqrt(jnp.mean(rows * rows, axis=-1, keepdims=True) + eps_norm)


def rotate_rows(rows, cosine, sine):
    half = rows.shape[-1] // 2
    front, back = rows[:, :half], rows[:, half:]
    return jnp.concatenate([front * cosine - back * sine, back * cosine + front * sine], axis=-1)


def rotate_back(rows, cosine, sine):
    half = rows.shape[-1] // 2
    front, back = rows[:, :half], rows[:, half:]
    return jnp.concatenate([front * cosine + back * sine, back * cosine - front * sine], axis=-1)


def gelu_parts(gate):
    scale = 0.7978845608028654
    square = gate * gate
    bent = jnp.tanh(scale * gate * (1.0 + 0.044715 * square))
    return square, bent


def forward_kernel(
    sizes,
    prefix_ref,
    tokens_ref,
    cot_ref,
    gains_ref,
    shard_ref,
    cos_ref,
    sin_ref,
    wall,
    gvec,
    normed,
    normed_two,
    query_raw,
    keyval_raw,
    attended,
    probs,
    gate_keep,
    up_keep,
    act,
    proj_keep,
    hidden_keep,
    down_keep,
    grad_down,
    dgain_ffn,
    block_out,
    tok_full,
    gains_full,
    key_rot,
    value_low,
    part_one,
    first_one,
    second_one,
    mixed_one,
    first_two,
    second_two,
    mixed_two,
    down_acc,
    line_send,
    line_recv,
    side_send,
    side_recv,
    row_send,
    row_recv,
):
    lines, rows, width, head_dim, units = sizes
    place = Place(lines)
    length = 4 * rows
    shard = shard_ref.shape[0]
    places, _ = packed_columns(units, head_dim)
    chunks = chunks_of(units)
    spans = [(0, 3 * head_dim), (3 * head_dim, 4 * head_dim)]
    spans += [(places[c][0], places[c][0] + 3 * chunks[c][2]) for c in range(len(chunks))]

    def region(group, origin):
        if group == 0:
            return gains_full.at[pl.ds(origin * 8, 8)]
        lo, hi = spans[group - 1]
        return wall.at[pl.ds(origin * shard, shard), lo:hi]

    gather = LineGather(place, region, len(spans) + 1, line_send, line_recv, side_send, side_recv)
    tokens_all = RowGather(place, tokens_ref, tok_full, rows, row_send.at[0], row_recv.at[0])
    own_rows = pl.ds(place.tensor * rows, rows)

    gains_full[pl.ds(place.dp * 8, 8)] = gains_ref[...]
    wall[pl.ds(place.dp * shard, shard)] = shard_ref[...]
    tok_full[own_rows] = tokens_ref[...]
    meet(place)
    tokens_all.start()
    for group in range(3):
        gather.start(group)
    gather.start(3)
    tokens_all.wait_mate()
    tokens_all.wait_across()
    gather.pump(0)
    gather.pump(1)
    tokens_all.wait_corner()
    gather.ready(0)
    for group in range(4, len(spans) + 1):
        gather.start(group)
    step = gains_ref.shape[1]
    for origin in range(2 * lines):
        gvec[:, origin * step : (origin + 1) * step] = gains_full[origin * 8 : origin * 8 + 8]
    gain_in = 1.0 + gvec[0:1, 0:width]
    gain_attn = 1.0 + gvec[0:1, width : 2 * width]
    gain_pre = 1.0 + gvec[0:1, 2 * width : 3 * width]
    gain_ffn = 1.0 + gvec[0:1, 3 * width : 4 * width]
    gain_query = 1.0 + gvec[0:1, 4 * width : 4 * width + head_dim]
    gain_key = 1.0 + gvec[0:1, 4 * width + head_dim : 4 * width + 2 * head_dim]
    gather.pump(2)

    def norm_slab(index, carry):
        at = pl.ds(pl.multiple_of(index * rows, rows), rows)
        x = tok_full[at].astype(full)
        normed[at] = (x * inverse_rms(x) * gain_in).astype(low)
        return carry

    lax.fori_loop(0, 4, norm_slab, 0)
    gather.ready(1)

    def project_slab(index, carry):
        at = pl.ds(pl.multiple_of(index * rows, rows), rows)
        n1 = normed[at]
        query_raw[at] = dot_nn(n1, wall[:, 0:head_dim])
        kv = dot_nn(n1, wall[:, head_dim : 3 * head_dim])
        keyval_raw[at] = kv
        k = kv[:, :head_dim]
        key_rot[at] = rotate_rows(k * inverse_rms(k) * gain_key, cos_ref[at], sin_ref[at]).astype(low)
        value_low[at] = kv[:, head_dim:].astype(low)
        return carry

    lax.fori_loop(0, 4, project_slab, 0)
    gather.pump(3)
    gather.ready(2)

    out_scatter = RowScatter(place, part_one, rows, first_one, second_one, mixed_one, row_send.at[1], row_recv.at[1])

    def attend_slab(index):
        at = pl.ds(pl.multiple_of(index * rows, rows), rows)
        q = query_raw[at]
        qr = rotate_rows(q * inverse_rms(q) * gain_query, cos_ref[at], sin_ref[at]).astype(low)
        scores = dot_nt(qr, key_rot[...]) * query_scale
        row_ids = lax.broadcasted_iota(jnp.int32, (rows, length), 0) + index * rows
        columns = lax.broadcasted_iota(jnp.int32, (rows, length), 1)
        allowed = (columns <= row_ids) | (columns < prefix_ref[0])
        scores = jnp.where(allowed, scores, masked_fill)
        shifted = jnp.exp(scores - jnp.max(scores, axis=-1, keepdims=True))
        soft = (shifted / jnp.sum(shifted, axis=-1, keepdims=True)).astype(low)
        probs[at] = soft
        mixed = dot_nn(soft, value_low[...]).astype(low)
        attended[at] = mixed
        part_one[at] = dot_nt(mixed, wall[:, 3 * head_dim : 4 * head_dim]).astype(low)

    for step, index in enumerate(out_scatter.order()):
        attend_slab(index)
        out_scatter.after(step)
    projected = out_scatter.total()
    out_scatter.finish()
    proj_keep[...] = projected
    hidden = tokens_ref[...].astype(full) + projected * inverse_rms(projected) * gain_attn
    hidden_keep[...] = hidden
    normed_two[own_rows] = (hidden * inverse_rms(hidden) * gain_pre).astype(low)
    two_all = RowGather(place, normed_two.at[own_rows], normed_two, rows, row_send.at[2], row_recv.at[2])
    two_all.start()
    two_all.wait_mate()
    two_all.wait_across()
    two_all.wait_corner()

    down_scatter = RowScatter(place, part_one, rows, first_two, second_two, mixed_two, row_send.at[3], row_recv.at[3])
    for c, (first, wide, padded) in enumerate(chunks):
        at_gate, at_up, at_down = places[c]
        if c + 1 < len(chunks):
            gather.pump(c + 4)
        gather.ready(c + 3)
        block = 2 * rows

        def feed_rows(index, carry):
            at = pl.ds(pl.multiple_of(index * block, block), block)
            n2 = normed_two[at]
            gate = dot_nn(n2, wall[:, at_gate : at_gate + wide])
            up = dot_nn(n2, wall[:, at_up : at_up + wide])
            gate_keep[at, first : first + wide] = gate.astype(low)
            up_keep[at, first : first + wide] = up.astype(low)
            _, bent = gelu_parts(gate)
            z = (0.5 * gate * (1.0 + bent) * up).astype(low)
            act[at, first : first + wide] = z
            if c + 1 < len(chunks):
                more = dot_nt(z, wall[:, at_down : at_down + wide])
                down_acc[at] = more if c == 0 else down_acc[at] + more
            return carry

        lax.fori_loop(0, 2, feed_rows, 0)
    first, wide, _ = chunks[-1]
    at_down = places[-1][2]
    for step, index in enumerate(down_scatter.order()):
        at = pl.ds(pl.multiple_of(index * rows, rows), rows)
        part_one[at] = (
            down_acc[at] + dot_nt(act[at, first : first + wide], wall[:, at_down : at_down + wide])
        ).astype(low)
        down_scatter.after(step)
    f = down_scatter.total()
    down_keep[...] = f
    inv = inverse_rms(f)
    block_out[...] = (hidden_keep[...] + f * inv * gain_ffn).astype(low)
    cot = cot_ref[...].astype(full)
    scaled = cot * gain_ffn
    grad_down[...] = (inv * (scaled - f * (inv * inv) * jnp.mean(f * scaled, axis=-1, keepdims=True))).astype(low)
    dgain_ffn[...] = jnp.broadcast_to(jnp.sum(cot * f * inv, axis=0, keepdims=True), dgain_ffn.shape)
    gather.finish()
    tokens_all.finish()
    two_all.finish()
    down_scatter.finish()


def forward_call(sizes, prefix, tokens, cotangent, gains, shard, cosine, sine):
    lines, rows, width, head_dim, units = sizes
    length = 4 * rows
    columns = shard.shape[1]
    places, _ = packed_columns(units, head_dim)
    padded = sum(c[2] for c in chunks_of(units))
    groups = 3 + len(chunks_of(units))
    vm = pl.BlockSpec(memory_space=pltpu.VMEM)

    def shape(dims, kind):
        return jax.ShapeDtypeStruct(dims, kind)

    outs = (
        shape((2 * lines * shard.shape[0], columns), low),
        shape((8, gains.shape[1] * 2 * lines), full),
        shape((length, width), low),
        shape((length, width), low),
        shape((length, head_dim), full),
        shape((length, 2 * head_dim), full),
        shape((length, head_dim), low),
        shape((length, length), low),
        shape((length, padded), low),
        shape((length, padded), low),
        shape((length, padded), low),
        shape((rows, width), full),
        shape((rows, width), full),
        shape((rows, width), full),
        shape((rows, width), low),
        shape((8, width), full),
        shape((rows, width), low),
    )

    def scatter_set():
        return [
            pltpu.VMEM((2, rows, width), low),
            pltpu.VMEM((rows, width), low),
            pltpu.VMEM((rows, width), low),
        ]

    return pl.pallas_call(
        functools.partial(forward_kernel, sizes),
        out_shape=outs,
        in_specs=[pl.BlockSpec(memory_space=pltpu.SMEM)] + [vm] * 6,
        out_specs=[vm] * len(outs),
        scratch_shapes=[
            pltpu.VMEM((length, width), low),
            pltpu.VMEM((2 * lines * 8, gains.shape[1]), full),
            pltpu.VMEM((length, head_dim), low),
            pltpu.VMEM((length, head_dim), low),
            pltpu.VMEM((length, width), low),
        ]
        + scatter_set()
        + scatter_set()
        + [
            pltpu.VMEM((length, width), full),
            pltpu.SemaphoreType.DMA((groups, lines)),
            pltpu.SemaphoreType.DMA((groups, lines)),
            pltpu.SemaphoreType.DMA((groups, lines)),
            pltpu.SemaphoreType.DMA((groups, lines)),
            pltpu.SemaphoreType.DMA((4, 3)),
            pltpu.SemaphoreType.DMA((4, 3)),
        ],
        compiler_params=pltpu.CompilerParams(
            collective_id=0, has_side_effects=True, vmem_limit_bytes=63 * 1024 * 1024
        ),
        name="forward",
    )(prefix, tokens, cotangent, gains, shard, cosine, sine)


def mixed_dot(left, right):
    return jnp.dot(left, right, preferred_element_type=jnp.float32)


def rms_scale(vector, gain_vec):
    return (
        vector
        * lax.rsqrt(jnp.mean(vector * vector, axis=-1, keepdims=True) + eps_norm)
        * (1.0 + gain_vec)
    )


def rotate(vector, positions):
    half_dim = vector.shape[-1] // 2
    inv_freq = rope_base ** (-2.0 * jnp.arange(half_dim).astype(jnp.float32) / vector.shape[-1])
    angles = positions[:, None] * inv_freq[None, :]
    cosine = jnp.cos(angles)[:, None, :]
    sine_v = jnp.sin(angles)[:, None, :]
    front_half = vector[..., :half_dim]
    back_half = vector[..., half_dim:]
    return jnp.concatenate(
        [front_half * cosine - back_half * sine_v, back_half * cosine + front_half * sine_v],
        axis=-1,
    )


def adam_step(weight, gradient, moment, second, step_rate):
    moment = beta_first * moment + (1.0 - beta_first) * gradient
    second = beta_second * second + (1.0 - beta_second) * gradient * gradient
    scaled = (
        moment
        / (1.0 - beta_first**STEP)
        / (jnp.sqrt(second / (1.0 - beta_second**STEP)) + adam_eps)
    )
    return (moment, second, weight - step_rate * (scaled + decay_rate * weight))


def plain_device(
    tokens,
    cotangent,
    prefix,
    query_weight,
    keyval_weight,
    output_weight,
    gateup_weight,
    down_weight,
    norm_gains,
    query_first,
    keyval_first,
    output_first,
    gateup_first,
    down_first,
    gains_first,
    query_second,
    keyval_second,
    output_second,
    gateup_second,
    down_second,
    gains_second,
):
    rows_dev, width = tokens.shape
    length = rows_dev * lax.axis_size("tensor")
    query_full, keyval_full, output_full, gateup_full, down_full, gains_full = (
        lax.all_gather(query_weight.astype(jnp.bfloat16), "dp", axis=0, tiled=True),
        lax.all_gather(keyval_weight.astype(jnp.bfloat16), "dp", axis=0, tiled=True),
        lax.all_gather(output_weight.astype(jnp.bfloat16), "dp", axis=0, tiled=True),
        lax.all_gather(gateup_weight.astype(jnp.bfloat16), "dp", axis=0, tiled=True),
        lax.all_gather(down_weight.astype(jnp.bfloat16), "dp", axis=0, tiled=True),
        lax.all_gather(norm_gains.astype(jnp.bfloat16), "dp", axis=0, tiled=True),
    )
    head_dim = keyval_full.shape[1] // 2
    heads_dev = query_full.shape[1] // head_dim
    units = down_full.shape[1]
    gain_values = gains_full.astype(jnp.float32)
    gain_input = gain_values[0:width]
    gain_attn = gain_values[width : 2 * width]
    gain_pre = gain_values[2 * width : 3 * width]
    gain_ffn = gain_values[3 * width : 4 * width]
    gain_query = gain_values[4 * width : 4 * width + head_dim]
    gain_key = gain_values[4 * width + head_dim : 4 * width + 2 * head_dim]
    positions = jnp.arange(length).astype(jnp.float32)
    span_rows = min(512, length)
    count_blocks = length // span_rows
    starts = jnp.arange(0, length, span_rows, dtype=jnp.int32)
    columns = jnp.arange(length, dtype=jnp.int32)
    prefix_len = prefix[0]
    gateup_flat = gateup_full.reshape(width, 2 * units)

    def shape_query(raw_rows, gain_vec):
        return rotate(rms_scale(raw_rows, gain_vec), positions)

    def shape_key(raw_rows, gain_vec):
        return rotate(rms_scale(raw_rows[:, None, :], gain_vec), positions)[:, 0]

    token_rows = tokens.astype(jnp.float32)
    normed_local = rms_scale(token_rows, gain_input).astype(jnp.bfloat16)
    normed = lax.all_gather(normed_local, "tensor", axis=0, tiled=True)
    query_raw = mixed_dot(normed, query_full).reshape(length, heads_dev, head_dim)
    keyval_raw = mixed_dot(normed, keyval_full)
    query_rot = shape_query(query_raw, gain_query).astype(jnp.bfloat16)
    key_rot = shape_key(keyval_raw[:, :head_dim], gain_key).astype(jnp.bfloat16)
    value_low = keyval_raw[:, head_dim:].astype(jnp.bfloat16)

    def scores_of(row_start):
        row_ids = row_start + jnp.arange(span_rows, dtype=jnp.int32)
        q_blk = lax.dynamic_slice_in_dim(query_rot, row_start, span_rows, 0)
        raw_scores = (
            jnp.einsum("rhd,kd->hrk", q_blk, key_rot, preferred_element_type=jnp.float32)
            * query_scale
        )
        allowed = (columns[None, :] <= row_ids[:, None]) | (columns[None, :] < prefix_len)
        return (jnp.where(allowed[None], raw_scores, masked_fill), q_blk)

    def forward_block(row_start):
        scores, q_blk = scores_of(row_start)
        row_peak = jnp.max(scores, axis=-1, keepdims=True)
        shifted = jnp.exp(scores - row_peak)
        denom_sum = jnp.sum(shifted, axis=-1, keepdims=True)
        soft_probs = (shifted / denom_sum).astype(jnp.bfloat16)
        mixed_rows = jnp.einsum(
            "hrk,kd->rhd", soft_probs, value_low, preferred_element_type=jnp.float32
        )
        return (mixed_rows, (row_peak + jnp.log(denom_sum))[..., 0])

    attended_blocks, log_sums = lax.map(forward_block, starts)
    attended = attended_blocks.reshape(length, heads_dev * head_dim).astype(jnp.bfloat16)
    attn_part = jnp.einsum("rk,dk->rd", attended, output_full, preferred_element_type=jnp.float32)
    projected = lax.psum_scatter(
        attn_part.astype(jnp.bfloat16), "tensor", scatter_dimension=0, tiled=True
    ).astype(jnp.float32)
    hidden_state = token_rows + rms_scale(projected, gain_attn)
    normed_two = lax.all_gather(
        rms_scale(hidden_state, gain_pre).astype(jnp.bfloat16), "tensor", axis=0, tiled=True
    )
    gateup = mixed_dot(normed_two, gateup_flat)
    gate_part = gateup[:, :units]
    up_part = gateup[:, units:]
    activation = (jax.nn.gelu(gate_part, approximate=True) * up_part).astype(jnp.bfloat16)
    down_part = jnp.einsum("ru,du->rd", activation, down_full, preferred_element_type=jnp.float32)
    down_sum = lax.psum_scatter(
        down_part.astype(jnp.bfloat16), "tensor", scatter_dimension=0, tiled=True
    ).astype(jnp.float32)
    block_out = hidden_state + rms_scale(down_sum, gain_ffn)
    grad_out = cotangent.astype(jnp.float32)
    pull_ffn = jax.vjp(rms_scale, down_sum, gain_ffn)[1]
    grad_down, grad_gain_ffn = pull_ffn(grad_out)
    down_back = lax.all_gather(grad_down.astype(jnp.bfloat16), "tensor", axis=0, tiled=True)
    grad_activation = mixed_dot(down_back, down_full)
    grad_down_w = jnp.einsum("rd,ru->du", down_back, activation, preferred_element_type=jnp.float32)

    def geglu(gate_in, up_in):
        return jax.nn.gelu(gate_in, approximate=True) * up_in

    pull_act = jax.vjp(geglu, gate_part, up_part)[1]
    grad_gate, grad_up = pull_act(grad_activation)
    grad_gateup = jnp.concatenate([grad_gate, grad_up], axis=1).astype(jnp.bfloat16)
    grad_gateup_w = jnp.einsum(
        "rd,ru->du", normed_two, grad_gateup, preferred_element_type=jnp.float32
    ).reshape(width, 2, units)
    grad_normed_two = jnp.einsum(
        "ru,du->rd", grad_gateup, gateup_flat, preferred_element_type=jnp.float32
    )
    grad_pre_rows = lax.psum_scatter(
        grad_normed_two.astype(jnp.bfloat16), "tensor", scatter_dimension=0, tiled=True
    ).astype(jnp.float32)
    pull_pre = jax.vjp(rms_scale, hidden_state, gain_pre)[1]
    grad_hidden_norm, grad_gain_pre = pull_pre(grad_pre_rows)
    grad_hidden = grad_out + grad_hidden_norm
    pull_attn = jax.vjp(rms_scale, projected, gain_attn)[1]
    grad_proj, grad_gain_attn = pull_attn(grad_hidden)
    proj_back = lax.all_gather(grad_proj.astype(jnp.bfloat16), "tensor", axis=0, tiled=True)
    grad_output_w = jnp.einsum("rd,rk->dk", proj_back, attended, preferred_element_type=jnp.float32)
    grad_attended = (
        mixed_dot(proj_back, output_full)
        .astype(jnp.bfloat16)
        .reshape(count_blocks, span_rows, heads_dev, head_dim)
    )

    def backward_block(carry, batch_item):
        key_acc, value_acc = carry
        row_start, grad_att, lse_blk = batch_item
        scores, q_blk = scores_of(row_start)
        soft_full = jnp.exp(scores - lse_blk[..., None])
        grad_probs = jnp.einsum(
            "rhd,kd->hrk", grad_att, value_low, preferred_element_type=jnp.float32
        )
        delta_rows = jnp.sum(soft_full * grad_probs, axis=-1, keepdims=True)
        grad_scores = (soft_full * (grad_probs - delta_rows)).astype(jnp.bfloat16)
        grad_query = (
            jnp.einsum("hrk,kd->rhd", grad_scores, key_rot, preferred_element_type=jnp.float32)
            * query_scale
        )
        key_acc = (
            key_acc
            + jnp.einsum("hrk,rhd->kd", grad_scores, q_blk, preferred_element_type=jnp.float32)
            * query_scale
        )
        value_acc = value_acc + jnp.einsum(
            "hrk,rhd->kd",
            soft_full.astype(jnp.bfloat16),
            grad_att,
            preferred_element_type=jnp.float32,
        )
        return ((key_acc, value_acc), grad_query)

    zero_rows = jnp.zeros((length, head_dim), jnp.float32)
    (grad_key_rot, grad_value), grad_query_blocks = lax.scan(
        backward_block, (zero_rows, zero_rows), (starts, grad_attended, log_sums)
    )
    grad_query_rot = grad_query_blocks.reshape(length, heads_dev, head_dim)
    pull_query = jax.vjp(shape_query, query_raw, gain_query)[1]
    grad_query_raw, grad_gain_query = pull_query(grad_query_rot)
    pull_key = jax.vjp(shape_key, keyval_raw[:, :head_dim], gain_key)[1]
    grad_key_raw, grad_gain_key = pull_key(grad_key_rot)
    grad_query_low = grad_query_raw.reshape(length, heads_dev * head_dim).astype(jnp.bfloat16)
    grad_keyval = jnp.concatenate([grad_key_raw, grad_value], axis=1)
    grad_query_w = jnp.einsum(
        "rd,rk->dk", normed, grad_query_low, preferred_element_type=jnp.float32
    )
    grad_normed_query = jnp.einsum(
        "rk,dk->rd", grad_query_low, query_full, preferred_element_type=jnp.float32
    )
    grad_normed_part, grad_keyval_own = (
        lax.psum_scatter(
            grad_normed_query.astype(jnp.bfloat16), "tensor", scatter_dimension=0, tiled=True
        ).astype(jnp.float32),
        lax.psum_scatter(
            grad_keyval.astype(jnp.bfloat16), "tensor", scatter_dimension=0, tiled=True
        ).astype(jnp.float32),
    )
    grad_keyval_low = grad_keyval_own.astype(jnp.bfloat16)
    grad_keyval_w = jnp.einsum(
        "rd,rk->dk", normed_local, grad_keyval_low, preferred_element_type=jnp.float32
    )
    grad_normed = grad_normed_part + jnp.einsum(
        "rk,dk->rd", grad_keyval_low, keyval_full, preferred_element_type=jnp.float32
    )
    pull_input = jax.vjp(rms_scale, token_rows, gain_input)[1]
    grad_token_norm, grad_gain_input = pull_input(grad_normed)
    tokens_grad = (grad_hidden + grad_token_norm).astype(jnp.bfloat16)
    grad_gains = jnp.concatenate(
        [
            grad_gain_input,
            grad_gain_attn,
            grad_gain_pre,
            grad_gain_ffn,
            grad_gain_query,
            grad_gain_key,
        ]
    )
    keyval_total, gains_total = (
        lax.psum(grad_keyval_w.astype(jnp.bfloat16), "tensor").astype(jnp.float32),
        lax.psum(grad_gains.astype(jnp.bfloat16), "tensor").astype(jnp.float32),
    )
    query_sum, keyval_sum, output_sum, gateup_sum, down_grad_sum, gains_sum = (
        lax.psum_scatter(grad_query_w, "dp", scatter_dimension=0, tiled=True),
        lax.psum_scatter(keyval_total, "dp", scatter_dimension=0, tiled=True),
        lax.psum_scatter(grad_output_w, "dp", scatter_dimension=0, tiled=True),
        lax.psum_scatter(grad_gateup_w, "dp", scatter_dimension=0, tiled=True),
        lax.psum_scatter(grad_down_w, "dp", scatter_dimension=0, tiled=True),
        lax.psum_scatter(gains_total, "dp", scatter_dimension=0, tiled=True),
    )
    query_moment, query_square, query_master = adam_step(
        query_weight, query_sum, query_first, query_second, D ** (-0.5)
    )
    keyval_moment, keyval_square, keyval_master = adam_step(
        keyval_weight, keyval_sum, keyval_first, keyval_second, D ** (-0.5)
    )
    output_moment, output_square, output_master = adam_step(
        output_weight, output_sum, output_first, output_second, (HEADS * HEAD_DIM) ** (-0.5)
    )
    gateup_moment, gateup_square, gateup_master = adam_step(
        gateup_weight, gateup_sum, gateup_first, gateup_second, D ** (-0.5)
    )
    down_moment, down_square, down_master = adam_step(
        down_weight, down_grad_sum, down_first, down_second, FF ** (-0.5)
    )
    gains_moment, gains_square, gains_master = adam_step(
        norm_gains, gains_sum, gains_first, gains_second, 0.3
    )
    return (
        block_out.astype(jnp.bfloat16),
        tokens_grad,
        query_moment,
        query_square,
        query_master,
        keyval_moment,
        keyval_square,
        keyval_master,
        output_moment,
        output_square,
        output_master,
        gateup_moment,
        gateup_square,
        gateup_master,
        down_moment,
        down_square,
        down_master,
        gains_moment,
        gains_square,
        gains_master,
    )


def per_device(
    tokens,
    cotangent,
    prefix,
    query_weight,
    keyval_weight,
    output_weight,
    gateup_weight,
    down_weight,
    norm_gains,
    query_first,
    keyval_first,
    output_first,
    gateup_first,
    down_first,
    gains_first,
    query_second,
    keyval_second,
    output_second,
    gateup_second,
    down_second,
    gains_second,
):
    rows, width = tokens.shape
    lines = lax.axis_size("dp") // 2
    shard = query_weight.shape[0]
    head_dim = keyval_weight.shape[1] // 2
    units = down_weight.shape[1]
    fits = (
        lax.axis_size("tensor") == 4
        and lax.axis_size("dp") == 2 * lines
        and query_weight.shape[1] == head_dim
        and shard % 16 == 0
        and norm_gains.shape[0] % 128 == 0
    )
    if not fits:
        return plain_device(tokens, cotangent, prefix, query_weight, keyval_weight, output_weight, gateup_weight, down_weight, norm_gains, query_first, keyval_first, output_first, gateup_first, down_first, gains_first, query_second, keyval_second, output_second, gateup_second, down_second, gains_second)
    length = 4 * rows
    heads_dev = 1
    flat = [query_weight, keyval_weight, output_weight]
    for first, wide, padded in chunks_of(units):
        for part in (gateup_weight[:, 0], gateup_weight[:, 1], down_weight):
            flat.append(jnp.pad(part[:, first : first + wide], ((0, 0), (0, padded - wide))))
    packed = jnp.concatenate(flat, axis=1).astype(low)
    gains_low = jnp.broadcast_to(norm_gains.astype(low).astype(full), (8, norm_gains.shape[0]))
    angles = np.arange(length)[:, None] * (rope_base ** (-2.0 * np.arange(head_dim // 2) / head_dim))[None, :]
    cosine = jnp.asarray(np.cos(angles), full)
    sine = jnp.asarray(np.sin(angles), full)
    (
        wall, gvec, normed, normed_two, query_raw, keyval_raw, attended, probs, gate_part, up_part, activation,
        projected, hidden_state, down_sum, grad_down, dgain_ffn, block_out,
    ) = forward_call((lines, rows, width, head_dim, units), prefix, tokens, cotangent, gains_low, packed, cosine, sine)
    gain_values = gvec[0]
    gain_input = gain_values[0:width]
    gain_attn = gain_values[width : 2 * width]
    gain_pre = gain_values[2 * width : 3 * width]
    gain_ffn = gain_values[3 * width : 4 * width]
    gain_query = gain_values[4 * width : 4 * width + head_dim]
    gain_key = gain_values[4 * width + head_dim : 4 * width + 2 * head_dim]
    query_full = wall[:, :head_dim]
    keyval_full = wall[:, head_dim : 3 * head_dim]
    output_full = wall[:, 3 * head_dim : 4 * head_dim]
    places, _ = packed_columns(units, head_dim)
    gateup_flat = jnp.concatenate(
        [wall[:, p[i] : p[i] + c[1]] for i in (0, 1) for p, c in zip(places, chunks_of(units))], axis=1
    )
    down_full = jnp.concatenate([wall[:, p[2] : p[2] + c[1]] for p, c in zip(places, chunks_of(units))], axis=1)
    activation = activation[:, :units]
    gate_part = gate_part[:, :units].astype(full)
    up_part = up_part[:, :units].astype(full)
    positions = jnp.arange(length).astype(jnp.float32)
    token_rows = tokens.astype(jnp.float32)
    normed_local = rms_scale(token_rows, gain_input).astype(jnp.bfloat16)
    span_rows = min(512, length)
    count_blocks = length // span_rows
    starts = jnp.arange(0, length, span_rows, dtype=jnp.int32)
    query_raw = query_raw.reshape(length, heads_dev, head_dim)

    def shape_query(raw_rows, gain_vec):
        return rotate(rms_scale(raw_rows, gain_vec), positions)

    def shape_key(raw_rows, gain_vec):
        return rotate(rms_scale(raw_rows[:, None, :], gain_vec), positions)[:, 0]

    query_rot = shape_query(query_raw, gain_query).astype(jnp.bfloat16)
    key_rot = shape_key(keyval_raw[:, :head_dim], gain_key).astype(jnp.bfloat16)
    value_low = keyval_raw[:, head_dim:].astype(jnp.bfloat16)
    block_out = block_out.astype(jnp.float32)
    grad_out = cotangent.astype(jnp.float32)
    pull_ffn = jax.vjp(rms_scale, down_sum, gain_ffn)[1]
    grad_down, grad_gain_ffn = pull_ffn(grad_out)
    down_back = lax.all_gather(grad_down.astype(jnp.bfloat16), "tensor", axis=0, tiled=True)
    grad_activation = mixed_dot(down_back, down_full)
    grad_down_w = jnp.einsum("rd,ru->du", down_back, activation, preferred_element_type=jnp.float32)

    def geglu(gate_in, up_in):
        return jax.nn.gelu(gate_in, approximate=True) * up_in

    pull_act = jax.vjp(geglu, gate_part, up_part)[1]
    grad_gate, grad_up = pull_act(grad_activation)
    grad_gateup = jnp.concatenate([grad_gate, grad_up], axis=1).astype(jnp.bfloat16)
    grad_gateup_w = jnp.einsum(
        "rd,ru->du", normed_two, grad_gateup, preferred_element_type=jnp.float32
    ).reshape(width, 2, units)
    grad_normed_two = jnp.einsum(
        "ru,du->rd", grad_gateup, gateup_flat, preferred_element_type=jnp.float32
    )
    grad_pre_rows = lax.psum_scatter(
        grad_normed_two.astype(jnp.bfloat16), "tensor", scatter_dimension=0, tiled=True
    ).astype(jnp.float32)
    pull_pre = jax.vjp(rms_scale, hidden_state, gain_pre)[1]
    grad_hidden_norm, grad_gain_pre = pull_pre(grad_pre_rows)
    grad_hidden = grad_out + grad_hidden_norm
    pull_attn = jax.vjp(rms_scale, projected, gain_attn)[1]
    grad_proj, grad_gain_attn = pull_attn(grad_hidden)
    proj_back = lax.all_gather(grad_proj.astype(jnp.bfloat16), "tensor", axis=0, tiled=True)
    grad_output_w = jnp.einsum("rd,rk->dk", proj_back, attended, preferred_element_type=jnp.float32)
    grad_attended = (
        mixed_dot(proj_back, output_full)
        .astype(jnp.bfloat16)
        .reshape(count_blocks, span_rows, heads_dev, head_dim)
    )

    def backward_block(carry, batch_item):
        key_acc, value_acc = carry
        row_start, grad_att, lse_blk = batch_item
        q_blk = lax.dynamic_slice_in_dim(query_rot, row_start, span_rows, 0)
        soft_full = lse_blk[None].astype(full)
        grad_probs = jnp.einsum(
            "rhd,kd->hrk", grad_att, value_low, preferred_element_type=jnp.float32
        )
        delta_rows = jnp.sum(soft_full * grad_probs, axis=-1, keepdims=True)
        grad_scores = (soft_full * (grad_probs - delta_rows)).astype(jnp.bfloat16)
        grad_query = (
            jnp.einsum("hrk,kd->rhd", grad_scores, key_rot, preferred_element_type=jnp.float32)
            * query_scale
        )
        key_acc = (
            key_acc
            + jnp.einsum("hrk,rhd->kd", grad_scores, q_blk, preferred_element_type=jnp.float32)
            * query_scale
        )
        value_acc = value_acc + jnp.einsum(
            "hrk,rhd->kd",
            soft_full.astype(jnp.bfloat16),
            grad_att,
            preferred_element_type=jnp.float32,
        )
        return ((key_acc, value_acc), grad_query)

    zero_rows = jnp.zeros((length, head_dim), jnp.float32)
    (grad_key_rot, grad_value), grad_query_blocks = lax.scan(
        backward_block, (zero_rows, zero_rows), (starts, grad_attended, probs.reshape(count_blocks, span_rows, length))
    )
    grad_query_rot = grad_query_blocks.reshape(length, heads_dev, head_dim)
    pull_query = jax.vjp(shape_query, query_raw, gain_query)[1]
    grad_query_raw, grad_gain_query = pull_query(grad_query_rot)
    pull_key = jax.vjp(shape_key, keyval_raw[:, :head_dim], gain_key)[1]
    grad_key_raw, grad_gain_key = pull_key(grad_key_rot)
    grad_query_low = grad_query_raw.reshape(length, heads_dev * head_dim).astype(jnp.bfloat16)
    grad_keyval = jnp.concatenate([grad_key_raw, grad_value], axis=1)
    grad_query_w = jnp.einsum(
        "rd,rk->dk", normed, grad_query_low, preferred_element_type=jnp.float32
    )
    grad_normed_query = jnp.einsum(
        "rk,dk->rd", grad_query_low, query_full, preferred_element_type=jnp.float32
    )
    grad_normed_part, grad_keyval_own = (
        lax.psum_scatter(
            grad_normed_query.astype(jnp.bfloat16), "tensor", scatter_dimension=0, tiled=True
        ).astype(jnp.float32),
        lax.psum_scatter(
            grad_keyval.astype(jnp.bfloat16), "tensor", scatter_dimension=0, tiled=True
        ).astype(jnp.float32),
    )
    grad_keyval_low = grad_keyval_own.astype(jnp.bfloat16)
    grad_keyval_w = jnp.einsum(
        "rd,rk->dk", normed_local, grad_keyval_low, preferred_element_type=jnp.float32
    )
    grad_normed = grad_normed_part + jnp.einsum(
        "rk,dk->rd", grad_keyval_low, keyval_full, preferred_element_type=jnp.float32
    )
    pull_input = jax.vjp(rms_scale, token_rows, gain_input)[1]
    grad_token_norm, grad_gain_input = pull_input(grad_normed)
    tokens_grad = (grad_hidden + grad_token_norm).astype(jnp.bfloat16)
    grad_gains = jnp.concatenate(
        [
            grad_gain_input,
            grad_gain_attn,
            grad_gain_pre,
            grad_gain_ffn,
            grad_gain_query,
            grad_gain_key,
        ]
    )
    keyval_total, gains_total = (
        lax.psum(grad_keyval_w.astype(jnp.bfloat16), "tensor").astype(jnp.float32),
        lax.psum(grad_gains.astype(jnp.bfloat16), "tensor").astype(jnp.float32),
    )
    query_sum, keyval_sum, output_sum, gateup_sum, down_grad_sum, gains_sum = (
        lax.psum_scatter(grad_query_w.astype(low), "dp", scatter_dimension=0, tiled=True),
        lax.psum_scatter(keyval_total, "dp", scatter_dimension=0, tiled=True),
        lax.psum_scatter(grad_output_w.astype(low), "dp", scatter_dimension=0, tiled=True),
        lax.psum_scatter(grad_gateup_w.astype(low), "dp", scatter_dimension=0, tiled=True),
        lax.psum_scatter(grad_down_w.astype(low), "dp", scatter_dimension=0, tiled=True),
        lax.psum_scatter(gains_total, "dp", scatter_dimension=0, tiled=True),
    )
    query_moment, query_square, query_master = adam_step(
        query_weight, query_sum, query_first, query_second, D ** (-0.5)
    )
    keyval_moment, keyval_square, keyval_master = adam_step(
        keyval_weight, keyval_sum, keyval_first, keyval_second, D ** (-0.5)
    )
    output_moment, output_square, output_master = adam_step(
        output_weight, output_sum, output_first, output_second, (HEADS * HEAD_DIM) ** (-0.5)
    )
    gateup_moment, gateup_square, gateup_master = adam_step(
        gateup_weight, gateup_sum, gateup_first, gateup_second, D ** (-0.5)
    )
    down_moment, down_square, down_master = adam_step(
        down_weight, down_grad_sum, down_first, down_second, FF ** (-0.5)
    )
    gains_moment, gains_square, gains_master = adam_step(
        norm_gains, gains_sum, gains_first, gains_second, 0.3
    )
    return (
        block_out.astype(jnp.bfloat16),
        tokens_grad,
        query_moment,
        query_square,
        query_master,
        keyval_moment,
        keyval_square,
        keyval_master,
        output_moment,
        output_square,
        output_master,
        gateup_moment,
        gateup_square,
        gateup_master,
        down_moment,
        down_square,
        down_master,
        gains_moment,
        gains_square,
        gains_master,
    )


def solution(mesh):
    placed = (
        P(("dp", "tensor"), None),
        P(("dp", "tensor"), None),
        P("dp"),
        P("dp", "tensor"),
        P("dp", None),
        P("dp", "tensor"),
        P("dp", None, "tensor"),
        P("dp", "tensor"),
        P("dp"),
        P("dp", "tensor"),
        P("dp", None),
        P("dp", "tensor"),
        P("dp", None, "tensor"),
        P("dp", "tensor"),
        P("dp"),
        P("dp", "tensor"),
        P("dp", None),
        P("dp", "tensor"),
        P("dp", None, "tensor"),
        P("dp", "tensor"),
        P("dp"),
    )
    return jax.shard_map(
        per_device,
        mesh=mesh,
        in_specs=placed,
        out_specs=(
            P(("dp", "tensor"), None),
            P(("dp", "tensor"), None),
            P("dp", "tensor"),
            P("dp", "tensor"),
            P("dp", "tensor"),
            P("dp", None),
            P("dp", None),
            P("dp", None),
            P("dp", "tensor"),
            P("dp", "tensor"),
            P("dp", "tensor"),
            P("dp", None, "tensor"),
            P("dp", None, "tensor"),
            P("dp", None, "tensor"),
            P("dp", "tensor"),
            P("dp", "tensor"),
            P("dp", "tensor"),
            P("dp"),
            P("dp"),
            P("dp"),
        ),
        check_vma=False,
    )
```

```python
import functools

import jax
import jax.numpy as jnp
import numpy as np
from jax import lax
from jax.experimental import pallas as pl
from jax.experimental.pallas import tpu as pltpu
from jax.sharding import PartitionSpec as P

D = 1152
FF = 6912
HEADS = 4
HEAD_DIM = 256
STEP = 10


eps_norm = 1e-06
query_scale = 0.0625
rope_base = 1000000.0
beta_first = 0.9
beta_second = 0.95
adam_eps = 1e-08
decay_rate = 0.01
masked_fill = -1e30
MESH = pl.DeviceIdType.MESH
low = jnp.bfloat16
full = jnp.float32
CHUNK = 512


def dot_nn(left, right):
    return lax.dot_general(left, right, (((1,), (0,)), ((), ())), preferred_element_type=full)


def dot_nt(left, right):
    return lax.dot_general(left, right, (((1,), (1,)), ((), ())), preferred_element_type=full)


def dot_tn(left, right):
    return lax.dot_general(left, right, (((0,), (0,)), ((), ())), preferred_element_type=full)


def chunks_of(units):
    out = []
    first = 0
    while first < units:
        width = min(CHUNK, units - first)
        out.append((first, width, -(-width // 128) * 128))
        first += width
    return out


def small_columns(head_dim):
    quarter = head_dim // 2
    at_query = 2 * head_dim + quarter
    return 2 * head_dim, at_query, at_query + head_dim, at_query + 2 * head_dim


def packed_columns(units, head_dim):
    at = small_columns(head_dim)[3]
    places = []
    for first, width, padded in chunks_of(units):
        places.append((at, at + padded, at + 2 * padded))
        at += 3 * padded
    return places, at


class Place:
    def __init__(self, lines):
        self.lines = lines
        self.dp = lax.axis_index("dp")
        self.tensor = lax.axis_index("tensor")
        self.z = self.dp // 2
        self.x = self.dp % 2
        self.y = self.tensor // 2
        self.core = self.tensor % 2
        self.mate = (self.dp, self.y * 2 + (1 - self.core))
        self.across = (self.dp, (1 - self.y) * 2 + self.core)
        self.side = (self.z * 2 + (1 - self.x), self.tensor)

    def line(self, step):
        return ((lax.rem(self.z + step, self.lines)) * 2 + self.x, self.tensor)

    def peers(self):
        return [self.mate, self.across, self.side] + [self.line(s) for s in range(1, self.lines)]


def meet(place):
    barrier = pltpu.get_barrier_semaphore()
    peers = place.peers()
    for peer in peers:
        pl.semaphore_signal(barrier, inc=1, device_id=peer, device_id_type=MESH)
    pl.semaphore_wait(barrier, len(peers))


def remote(source, target, send_sem, recv_sem, device):
    return pltpu.make_async_remote_copy(
        src_ref=source,
        dst_ref=target,
        send_sem=send_sem,
        recv_sem=recv_sem,
        device_id=device,
        device_id_type=MESH,
    )


class LineGather:
    def __init__(self, place, region, count, send, recv, send_side, recv_side):
        self.place, self.region, self.count = place, region, count
        self.send, self.recv, self.send_side, self.recv_side = send, recv, send_side, recv_side

    def along(self, group, step):
        block = self.region(group, self.place.dp)
        return remote(block, block, self.send.at[group, step], self.recv.at[group, step], self.place.line(step))

    def sideways(self, group, step):
        origin = lax.rem(self.place.z + self.place.lines - step, self.place.lines) * 2 + self.place.x
        block = self.region(group, origin)
        return remote(
            block, block, self.send_side.at[group, step], self.recv_side.at[group, step], self.place.side
        )

    def start(self, group):
        for step in range(1, self.place.lines):
            self.along(group, step).start()
        self.sideways(group, 0).start()

    def pump(self, group):
        for step in range(1, self.place.lines):
            origin = lax.rem(self.place.z + self.place.lines - step, self.place.lines) * 2 + self.place.x
            block = self.region(group, origin)
            remote(
                block, block, self.send.at[group, step], self.recv.at[group, step], self.place.line(step)
            ).wait_recv()
            self.sideways(group, step).start()

    def ready(self, group):
        for step in range(self.place.lines):
            origin = lax.rem(self.place.z + self.place.lines - step, self.place.lines) * 2 + (1 - self.place.x)
            block = self.region(group, origin)
            remote(
                block, block, self.send_side.at[group, step], self.recv_side.at[group, step], self.place.side
            ).wait_recv()

    def finish(self):
        for group in range(self.count):
            for step in range(1, self.place.lines):
                self.along(group, step).wait_send()
            for step in range(self.place.lines):
                self.sideways(group, step).wait_send()


class RowGather:
    def __init__(self, place, source, buffer, rows, send, recv):
        self.place, self.source, self.buffer, self.rows = place, source, buffer, rows
        self.send, self.recv = send, recv

    def slab(self, y, core):
        return self.buffer.at[pl.ds((y * 2 + core) * self.rows, self.rows)]

    def copy(self, index):
        place = self.place
        slab = self.slab(1 - place.y if index == 2 else place.y, place.core)
        source = slab if index == 2 else self.source
        device = place.across if index == 1 else place.mate
        return remote(source, slab, self.send.at[index], self.recv.at[index], device)

    def arrival(self, index, y, core):
        slab = self.slab(y, core)
        remote(slab, slab, self.send.at[index], self.recv.at[index], self.place.mate).wait_recv()

    def start(self):
        self.copy(1).start()
        self.copy(0).start()

    def wait_mate(self):
        self.arrival(0, self.place.y, 1 - self.place.core)

    def wait_across(self):
        self.arrival(1, 1 - self.place.y, self.place.core)
        self.copy(2).start()

    def wait_corner(self):
        self.arrival(2, 1 - self.place.y, 1 - self.place.core)

    def finish(self):
        for index in range(3):
            self.copy(index).wait_send()


class RowScatter:
    def __init__(self, place, part, rows, first, second, mixed, send, recv):
        self.place, self.part, self.rows = place, part, rows
        self.first, self.second, self.mixed = first, second, mixed
        self.send, self.recv = send, recv

    def slab(self, y, core):
        return self.part.at[pl.ds((y * 2 + core) * self.rows, self.rows)]

    def copy(self, index):
        place = self.place
        if index == 2:
            return remote(self.mixed, self.second, self.send.at[2], self.recv.at[2], place.across)
        source = self.slab(1 - place.y if index == 0 else place.y, 1 - place.core)
        return remote(source, self.first.at[index], self.send.at[index], self.recv.at[index], place.mate)

    def order(self):
        place = self.place
        return (
            (1 - place.y) * 2 + (1 - place.core),
            (1 - place.y) * 2 + place.core,
            place.y * 2 + (1 - place.core),
            place.y * 2 + place.core,
        )

    def after(self, step):
        if step == 0:
            self.copy(0).start()
        if step == 1:
            self.copy(0).wait_recv()
            mixed = self.slab(1 - self.place.y, self.place.core)[...].astype(full) + self.first[0].astype(full)
            self.mixed[...] = mixed.astype(low)
            self.copy(2).start()
        if step == 2:
            self.copy(1).start()

    def total(self):
        self.copy(1).wait_recv()
        here = self.slab(self.place.y, self.place.core)[...].astype(full) + self.first[1].astype(full)
        self.copy(2).wait_recv()
        return here + self.second[...].astype(full)

    def finish(self):
        for index in range(3):
            self.copy(index).wait_send()


def inverse_rms(rows):
    return lax.rsqrt(jnp.mean(rows * rows, axis=-1, keepdims=True) + eps_norm)


def rotate_rows(rows, cosine, sine):
    half = rows.shape[-1] // 2
    front, back = rows[:, :half], rows[:, half:]
    return jnp.concatenate([front * cosine - back * sine, back * cosine + front * sine], axis=-1)


def rotate_back(rows, cosine, sine):
    half = rows.shape[-1] // 2
    front, back = rows[:, :half], rows[:, half:]
    return jnp.concatenate([front * cosine + back * sine, back * cosine - front * sine], axis=-1)


def gelu_parts(gate):
    scale = 0.7978845608028654
    square = gate * gate
    bent = jnp.tanh(scale * gate * (1.0 + 0.044715 * square))
    return square, bent


def forward_kernel(
    sizes,
    prefix_ref,
    tokens_ref,
    cot_ref,
    gains_ref,
    shard_ref,
    cos_ref,
    sin_ref,
    wall_out,
    normed_out,
    normed_two_out,
    query_out,
    key_out,
    key_rot_out,
    value_out,
    attended_out,
    probs_out,
    gate_out,
    up_out,
    act_out,
    gvec,
    proj_keep,
    hidden_keep,
    grad_down,
    dgain_ffn,
    block_out,
    wall,
    normed,
    normed_two,
    query_raw,
    key_raw,
    attended,
    probs,
    gate_keep,
    up_keep,
    act,
    tok_full,
    gains_full,
    key_rot,
    value_low,
    part_one,
    first_one,
    second_one,
    mixed_one,
    first_two,
    second_two,
    mixed_two,
    down_acc,
    line_send,
    line_recv,
    side_send,
    side_recv,
    row_send,
    row_recv,
    keep_sem,
):
    lines, rows, width, head_dim, units = sizes
    place = Place(lines)
    length = 4 * rows
    shard = shard_ref.shape[0]
    places, _ = packed_columns(units, head_dim)
    chunks = chunks_of(units)
    kv_end, at_query, at_output, small_end = small_columns(head_dim)
    spans = [(0, kv_end), (at_query, at_output), (at_output, small_end)]
    spans += [(places[c][0], places[c][0] + 3 * chunks[c][2]) for c in range(len(chunks))]

    def region(group, origin):
        if group == 0:
            return gains_full.at[pl.ds(origin * 8, 8)]
        lo, hi = spans[group - 1]
        return wall.at[pl.ds(origin * shard, shard), lo:hi]

    gather = LineGather(place, region, len(spans) + 1, line_send, line_recv, side_send, side_recv)
    tokens_all = RowGather(place, tokens_ref, tok_full, rows, row_send.at[0], row_recv.at[0])
    own_rows = pl.ds(place.tensor * rows, rows)
    kept = []

    def keep(source, target):
        copy = pltpu.make_async_copy(source, target, keep_sem.at[len(kept)])
        copy.start()
        kept.append(copy)

    def keep_span(group):
        lo, hi = spans[group - 1]
        keep(wall.at[:, lo:hi], wall_out.at[:, lo:hi])

    gains_full[pl.ds(place.dp * 8, 8)] = gains_ref[...]
    for lo, hi in spans:
        wall[pl.ds(place.dp * shard, shard), lo:hi] = shard_ref[:, lo:hi]
    tok_full[own_rows] = tokens_ref[...]
    meet(place)
    tokens_all.start()
    for group in range(5):
        gather.start(group)
    tokens_all.wait_mate()
    tokens_all.wait_across()
    gather.pump(0)
    gather.pump(1)
    gather.pump(2)
    tokens_all.wait_corner()
    gather.ready(0)
    for group in range(5, len(spans) + 1):
        gather.start(group)
    step = gains_ref.shape[1]
    for origin in range(2 * lines):
        gvec[:, origin * step : (origin + 1) * step] = gains_full[origin * 8 : origin * 8 + 8]
    gain_in = 1.0 + gvec[0:1, 0:width]
    gain_attn = 1.0 + gvec[0:1, width : 2 * width]
    gain_pre = 1.0 + gvec[0:1, 2 * width : 3 * width]
    gain_ffn = 1.0 + gvec[0:1, 3 * width : 4 * width]
    gain_query = 1.0 + gvec[0:1, 4 * width : 4 * width + head_dim]
    gain_key = 1.0 + gvec[0:1, 4 * width + head_dim : 4 * width + 2 * head_dim]
    gather.pump(3)

    def norm_slab(index, carry):
        at = pl.ds(pl.multiple_of(index * rows, rows), rows)
        x = tok_full[at].astype(full)
        normed[at] = (x * inverse_rms(x) * gain_in).astype(low)
        return carry

    lax.fori_loop(0, 4, norm_slab, 0)
    keep(normed, normed_out)
    gather.ready(1)
    gather.ready(2)

    def project_slab(index, carry):
        at = pl.ds(pl.multiple_of(index * rows, rows), rows)
        n1 = normed[at]
        query_raw[at] = dot_nn(n1, wall[:, at_query:at_output])
        kv = dot_nn(n1, wall[:, 0:kv_end])
        k = kv[:, :head_dim]
        key_raw[at] = k
        key_rot[at] = rotate_rows(k * inverse_rms(k) * gain_key, cos_ref[at], sin_ref[at]).astype(low)
        value_low[at] = kv[:, head_dim:].astype(low)
        return carry

    lax.fori_loop(0, 4, project_slab, 0)
    keep(query_raw, query_out)
    keep(key_raw, key_out)
    keep(key_rot, key_rot_out)
    keep(value_low, value_out)
    keep_span(1)
    keep_span(2)
    gather.pump(4)
    gather.ready(3)
    keep_span(3)

    out_scatter = RowScatter(place, part_one, rows, first_one, second_one, mixed_one, row_send.at[1], row_recv.at[1])

    def attend_slab(index):
        at = pl.ds(pl.multiple_of(index * rows, rows), rows)
        q = query_raw[at]
        qr = rotate_rows(q * inverse_rms(q) * gain_query, cos_ref[at], sin_ref[at]).astype(low)
        scores = dot_nt(qr, key_rot[...]) * query_scale
        row_ids = lax.broadcasted_iota(jnp.int32, (rows, length), 0) + index * rows
        columns = lax.broadcasted_iota(jnp.int32, (rows, length), 1)
        allowed = (columns <= row_ids) | (columns < prefix_ref[0])
        scores = jnp.where(allowed, scores, masked_fill)
        shifted = jnp.exp(scores - jnp.max(scores, axis=-1, keepdims=True))
        soft = (shifted / jnp.sum(shifted, axis=-1, keepdims=True)).astype(low)
        probs[at] = soft
        mixed = dot_nn(soft, value_low[...]).astype(low)
        attended[at] = mixed
        part_one[at] = dot_nt(mixed, wall[:, at_output:small_end]).astype(low)

    for step, index in enumerate(out_scatter.order()):
        attend_slab(index)
        out_scatter.after(step)
    keep(probs, probs_out)
    keep(attended, attended_out)
    projected = out_scatter.total()
    out_scatter.finish()
    proj_keep[...] = projected
    hidden = tokens_ref[...].astype(full) + projected * inverse_rms(projected) * gain_attn
    hidden_keep[...] = hidden
    normed_two[own_rows] = (hidden * inverse_rms(hidden) * gain_pre).astype(low)
    two_all = RowGather(place, normed_two.at[own_rows], normed_two, rows, row_send.at[2], row_recv.at[2])
    two_all.start()
    two_all.wait_mate()
    two_all.wait_across()
    two_all.wait_corner()
    keep(normed_two, normed_two_out)

    down_scatter = RowScatter(place, part_one, rows, first_two, second_two, mixed_two, row_send.at[3], row_recv.at[3])
    for c, (first, wide, padded) in enumerate(chunks):
        at_gate, at_up, at_down = places[c]
        if c + 1 < len(chunks):
            gather.pump(c + 5)
        gather.ready(c + 4)
        keep_span(c + 4)
        block = 2 * rows

        def feed_rows(index, carry):
            at = pl.ds(pl.multiple_of(index * block, block), block)
            n2 = normed_two[at]
            gate = dot_nn(n2, wall[:, at_gate : at_gate + wide])
            up = dot_nn(n2, wall[:, at_up : at_up + wide])
            gate_keep[at, first : first + wide] = gate.astype(low)
            up_keep[at, first : first + wide] = up.astype(low)
            _, bent = gelu_parts(gate)
            z = (0.5 * gate * (1.0 + bent) * up).astype(low)
            act[at, first : first + wide] = z
            if c + 1 < len(chunks):
                more = dot_nt(z, wall[:, at_down : at_down + wide])
                down_acc[at] = more if c == 0 else down_acc[at] + more
            return carry

        lax.fori_loop(0, 2, feed_rows, 0)
        span = slice(first, first + padded)
        keep(gate_keep.at[:, span], gate_out.at[:, span])
        keep(up_keep.at[:, span], up_out.at[:, span])
        keep(act.at[:, span], act_out.at[:, span])
    first, wide, _ = chunks[-1]
    at_down = places[-1][2]
    for step, index in enumerate(down_scatter.order()):
        at = pl.ds(pl.multiple_of(index * rows, rows), rows)
        part_one[at] = (
            down_acc[at] + dot_nt(act[at, first : first + wide], wall[:, at_down : at_down + wide])
        ).astype(low)
        down_scatter.after(step)
    f = down_scatter.total()
    inv = inverse_rms(f)
    block_out[...] = (hidden_keep[...] + f * inv * gain_ffn).astype(low)
    cot = cot_ref[...].astype(full)
    scaled = cot * gain_ffn
    grad_down[...] = (inv * (scaled - f * (inv * inv) * jnp.mean(f * scaled, axis=-1, keepdims=True))).astype(low)
    dgain_ffn[...] = jnp.broadcast_to(jnp.sum(cot * f * inv, axis=0, keepdims=True), dgain_ffn.shape)
    gather.finish()
    tokens_all.finish()
    two_all.finish()
    down_scatter.finish()
    for copy in kept:
        copy.wait()


def forward_call(sizes, prefix, tokens, cotangent, gains, shard, cosine, sine):
    lines, rows, width, head_dim, units = sizes
    length = 4 * rows
    columns = shard.shape[1]
    chunks = chunks_of(units)
    padded = sum(c[2] for c in chunks)
    groups = 4 + len(chunks)
    vm = pl.BlockSpec(memory_space=pltpu.VMEM)
    hbm = pl.BlockSpec(memory_space=pl.ANY)
    large = [
        ((2 * lines * shard.shape[0], columns), low),
        ((length, width), low),
        ((length, width), low),
        ((length, head_dim), full),
        ((length, head_dim), full),
        ((length, head_dim), low),
        ((length, head_dim), low),
        ((length, head_dim), low),
        ((length, length), low),
        ((length, padded), low),
        ((length, padded), low),
        ((length, padded), low),
    ]
    small = [
        ((8, gains.shape[1] * 2 * lines), full),
        ((rows, width), full),
        ((rows, width), full),
        ((rows, width), low),
        ((8, width), full),
        ((rows, width), low),
    ]
    inside = [large[i] for i in (0, 1, 2, 3, 4, 7, 8, 9, 10, 11)]
    scatter_set = [
        pltpu.VMEM((2, rows, width), low),
        pltpu.VMEM((rows, width), low),
        pltpu.VMEM((rows, width), low),
    ]
    return pl.pallas_call(
        functools.partial(forward_kernel, sizes),
        out_shape=[jax.ShapeDtypeStruct(*item) for item in large + small],
        in_specs=[pl.BlockSpec(memory_space=pltpu.SMEM)] + [vm] * 6,
        out_specs=[hbm] * len(large) + [vm] * len(small),
        scratch_shapes=[pltpu.VMEM(*item) for item in inside]
        + [
            pltpu.VMEM((length, width), low),
            pltpu.VMEM((2 * lines * 8, gains.shape[1]), full),
            pltpu.VMEM((length, head_dim), low),
            pltpu.VMEM((length, head_dim), low),
            pltpu.VMEM((length, width), low),
        ]
        + scatter_set
        + scatter_set
        + [
            pltpu.VMEM((length, width), full),
            pltpu.SemaphoreType.DMA((groups, lines)),
            pltpu.SemaphoreType.DMA((groups, lines)),
            pltpu.SemaphoreType.DMA((groups, lines)),
            pltpu.SemaphoreType.DMA((groups, lines)),
            pltpu.SemaphoreType.DMA((4, 3)),
            pltpu.SemaphoreType.DMA((4, 3)),
            pltpu.SemaphoreType.DMA((11 + 4 * len(chunks),)),
        ],
        compiler_params=pltpu.CompilerParams(
            collective_id=0, has_side_effects=True, vmem_limit_bytes=63 * 1024 * 1024
        ),
        name="forward",
    )(prefix, tokens, cotangent, gains, shard, cosine, sine)


class LineScatter:
    def __init__(self, place, block, side_block, line_block, send, recv, kind):
        self.place, self.block, self.side_block, self.line_block = place, block, side_block, line_block
        self.send, self.recv, self.kind = send, recv, kind

    def home(self, step):
        return lax.rem(self.place.z + step, self.place.lines)

    def sideways(self, group, step):
        home = self.home(step)
        return remote(
            self.block(group, home * 2 + (1 - self.place.x)),
            self.side_block(group, home),
            self.send.at[0, group, step],
            self.recv.at[0, group, step],
            self.place.side,
        )

    def along(self, group, step):
        home = self.home(step)
        return remote(
            self.block(group, home * 2 + self.place.x),
            self.line_block(group, step),
            self.send.at[1, group, step],
            self.recv.at[1, group, step],
            self.place.line(step),
        )

    def start(self, group):
        for step in list(range(1, self.place.lines)) + [0]:
            self.sideways(group, step).start()

    def pump(self, group):
        for step in range(1, self.place.lines):
            home = self.home(step)
            self.sideways(group, step).wait_recv()
            block = self.block(group, home * 2 + self.place.x)
            block[...] = (block[...].astype(full) + self.side_block(group, home)[...].astype(full)).astype(self.kind)
            self.along(group, step).start()

    def total(self, group):
        self.sideways(group, 0).wait_recv()
        block = self.block(group, self.place.dp)
        out = block[...].astype(full) + self.side_block(group, self.place.z)[...].astype(full)
        for step in range(1, self.place.lines):
            self.along(group, step).wait_recv()
            out = out + self.line_block(group, step)[...].astype(full)
        return out

    def finish(self, groups):
        for group in groups:
            for step in range(self.place.lines):
                self.sideways(group, step).wait_send()
                if step > 0:
                    self.along(group, step).wait_send()


def norm_back(rows, inv, gain, grad):
    scaled = grad * gain
    back = inv * (scaled - rows * (inv * inv) * jnp.mean(rows * scaled, axis=-1, keepdims=True))
    return back, jnp.sum(grad * rows * inv, axis=0, keepdims=True)


def backward_kernel(
    sizes,
    grad_down_ref,
    cot_ref,
    tokens_ref,
    gvec,
    dgain_ffn,
    proj_ref,
    hidden_ref,
    cos_ref,
    sin_ref,
    wall_in,
    normed_in,
    normed_two_in,
    query_in,
    key_in,
    key_rot_in,
    value_in,
    attended_in,
    probs_in,
    gate_in,
    up_in,
    act_in,
    gate_grad,
    up_grad,
    down_grad,
    small_grad,
    tokens_grad,
    keyval_grad,
    gains_grad,
    wall,
    side_buf,
    line_buf,
    big,
    normed_two,
    row_buf,
    acc,
    first_buf,
    second_buf,
    mixed_buf,
    key_rot,
    value_low,
    dquery,
    dkeyval,
    dhidden,
    dproj,
    kv_first,
    kv_second,
    kv_mixed,
    kv_own,
    dgains,
    gain_part,
    gain_first,
    gain_second,
    gain_side,
    gain_line,
    row_send,
    row_recv,
    line_send,
    line_recv,
    gain_send,
    gain_recv,
    last_send,
    last_recv,
    load_sem,
    store_sem,
):
    lines, rows, width, head_dim, units = sizes
    place = Place(lines)
    length = 4 * rows
    shard = wall.shape[0] // (2 * lines)
    kv_end, at_query, at_output, small_end = small_columns(head_dim)
    quarter = head_dim // 2
    places, _ = packed_columns(units, head_dim)
    chunks = chunks_of(units)
    last = len(chunks) - 1
    spans = [(places[c][0], places[c][0] + 3 * chunks[c][2]) for c in range(len(chunks))] + [(kv_end, small_end)]
    loads = {}

    def load(name, source, target):
        copy = pltpu.make_async_copy(source, target, load_sem.at[len(loads)])
        copy.start()
        loads[name] = copy

    def load_chunk(c):
        lo, hi = spans[c]
        first, _, padded = chunks[c]
        base = (c % 2) * 3 * CHUNK
        load(("wall", c), wall_in.at[:, lo:hi], wall.at[:, lo:hi])
        for k, source in enumerate((gate_in, up_in, act_in)):
            at = base + k * CHUNK
            load((k, c), source.at[:, first : first + padded], big.at[:, at : at + padded])

    load("two", normed_two_in, normed_two)
    load_chunk(0)
    load("kv", wall_in.at[:, 0:kv_end], wall.at[:, 0:kv_end])
    load("qo", wall_in.at[:, at_query:small_end], wall.at[:, at_query:small_end])
    load("key_rot", key_rot_in, key_rot)
    load("value", value_in, value_low)
    gain_in = 1.0 + gvec[0:1, 0:width]
    gain_attn = 1.0 + gvec[0:1, width : 2 * width]
    gain_pre = 1.0 + gvec[0:1, 2 * width : 3 * width]
    gain_query = 1.0 + gvec[0:1, 4 * width : 4 * width + head_dim]
    gain_key = 1.0 + gvec[0:1, 4 * width + head_dim : 4 * width + 2 * head_dim]
    own_rows = pl.ds(place.tensor * rows, rows)
    row_buf[own_rows] = grad_down_ref[...]
    dgains[...] = jnp.zeros_like(dgains)
    dgains[0:1, 3 * width : 4 * width] = dgain_ffn[0:1]
    meet(place)
    down_all = RowGather(place, grad_down_ref, row_buf, rows, row_send.at[0], row_recv.at[0])
    down_all.start()
    load_chunk(1)
    down_all.wait_mate()
    down_all.wait_across()
    down_all.wait_corner()
    loads["two"].wait()

    def block(group, origin):
        lo, hi = spans[group]
        return wall.at[pl.ds(origin * shard, shard), lo:hi]

    def side_block(group, home):
        lo, hi = spans[group]
        return side_buf.at[pl.ds(home * shard, shard), lo - kv_end : hi - kv_end]

    def line_block(group, step):
        lo, hi = spans[group]
        return line_buf.at[pl.ds((step - 1) * shard, shard), lo - kv_end : hi - kv_end]

    scatter = LineScatter(place, block, side_block, line_block, line_send, line_recv, low)
    part = big.at[:, 0:width]
    pre_scatter = RowScatter(place, part, rows, first_buf, second_buf, mixed_buf, row_send.at[1], row_recv.at[1])
    half = 2 * rows
    third = width // 3

    def weight_gradient(lo, wide, left, right):
        for m in range(0, width, third):
            wall[m : m + third, lo : lo + wide] = dot_tn(left[:, m : m + third], right).astype(low)

    for c, (first, wide, padded) in enumerate(chunks):
        at_gate, at_up, at_down = places[c]
        base = (c % 2) * 3 * CHUNK
        loads["wall", c].wait()
        for k in range(3):
            loads[k, c].wait()
        if 1 <= c < last:
            load_chunk(c + 1)
        of_gate = slice(base, base + wide)
        of_up = slice(base + CHUNK, base + CHUNK + wide)
        of_act = slice(base + 2 * CHUNK, base + 2 * CHUNK + wide)

        def unit_rows(index, carry):
            at = pl.ds(pl.multiple_of(index * half, half), half)
            dz = dot_nn(row_buf[at], wall[:, at_down : at_down + wide])
            gate = big[at, of_gate].astype(full)
            up = big[at, of_up].astype(full)
            square, bent = gelu_parts(gate)
            middle = 0.5 * (1.0 + bent)
            slope = middle + 0.5 * gate * (1.0 - bent * bent) * (0.7978845608028654 * (1.0 + 0.134145 * square))
            big[at, of_gate] = (dz * up * slope).astype(low)
            big[at, of_up] = (dz * gate * middle).astype(low)
            return carry

        lax.fori_loop(0, 2, unit_rows, 0)
        weight_gradient(at_down, wide, row_buf, big[:, of_act])

        def back_rows(at):
            more = dot_nt(big[at, of_gate], wall[:, at_gate : at_gate + wide])
            more = more + dot_nt(big[at, of_up], wall[:, at_up : at_up + wide])
            return more if c == 0 else acc[at] + more

        if c < last:

            def collect_rows(index, carry):
                at = pl.ds(pl.multiple_of(index * half, half), half)
                acc[at] = back_rows(at)
                return carry

            lax.fori_loop(0, 2, collect_rows, 0)
        else:
            down_all.finish()
            for step, index in enumerate(pre_scatter.order()):
                at = pl.ds(pl.multiple_of(index * rows, rows), rows)
                part[at] = back_rows(at).astype(low)
                pre_scatter.after(step)
        weight_gradient(at_gate, wide, normed_two, big[:, of_gate])
        weight_gradient(at_up, wide, normed_two, big[:, of_up])
        scatter.start(c)

    at_normed = width
    at_att = at_normed + width
    load("normed", normed_in, big.at[:, at_normed : at_normed + width])
    load("attended", attended_in, big.at[:, at_att : at_att + head_dim])
    load("query", query_in, acc.at[:, 2 * head_dim : 3 * head_dim])
    load("key", key_in, acc.at[:, 3 * head_dim : 4 * head_dim])

    dn2 = pre_scatter.total()
    hidden = hidden_ref[...]
    back, grad = norm_back(hidden, inverse_rms(hidden), gain_pre, dn2)
    dgains[0:1, 2 * width : 3 * width] = grad
    dh = cot_ref[...].astype(full) + back
    dhidden[...] = dh
    proj = proj_ref[...]
    back, grad = norm_back(proj, inverse_rms(proj), gain_attn, dh)
    dgains[0:1, width : 2 * width] = grad
    dproj[...] = back.astype(low)
    row_buf[own_rows] = dproj[...]
    proj_all = RowGather(place, dproj, row_buf, rows, row_send.at[2], row_recv.at[2])
    proj_all.start()
    pre_scatter.finish()
    load("probs", probs_in, big.at[:, 0:length])
    acc[:, 0 : 2 * head_dim] = jnp.zeros((length, 2 * head_dim), full)
    proj_all.wait_mate()
    proj_all.wait_across()
    scatter.pump(0)
    proj_all.wait_corner()
    for name in ("kv", "qo", "key_rot", "value", "normed", "attended", "query", "key", "probs"):
        loads[name].wait()

    def attend_back(index, carry):
        at = pl.ds(pl.multiple_of(index * rows, rows), rows)
        da = dot_nn(row_buf[at], wall[:, at_output:small_end]).astype(low)
        soft = big[at, 0:length]
        wide_soft = soft.astype(full)
        dp = dot_nt(da, value_low[...])
        ds = (wide_soft * (dp - jnp.sum(wide_soft * dp, axis=-1, keepdims=True))).astype(low)
        q = acc[at, 2 * head_dim : 3 * head_dim]
        inv = inverse_rms(q)
        cosine, sine = cos_ref[at], sin_ref[at]
        qr = rotate_rows(q * inv * gain_query, cosine, sine).astype(low)
        dqr = dot_nn(ds, key_rot[...]) * query_scale
        acc[:, 0:head_dim] += dot_tn(ds, qr)
        acc[:, head_dim : 2 * head_dim] += dot_tn(soft, da)
        dq, grad = norm_back(q, inv, gain_query, rotate_back(dqr, cosine, sine))
        dquery[at] = dq.astype(low)
        dgains[0:1, 4 * width : 4 * width + head_dim] += grad
        return carry

    lax.fori_loop(0, 4, attend_back, 0)

    def key_back(index, carry):
        at = pl.ds(pl.multiple_of(index * rows, rows), rows)
        k = acc[at, 3 * head_dim : 4 * head_dim]
        dkr = rotate_back(acc[at, 0:head_dim] * query_scale, cos_ref[at], sin_ref[at])
        dk, grad = norm_back(k, inverse_rms(k), gain_key, dkr)
        dkeyval[at, 0:head_dim] = dk.astype(low)
        dkeyval[at, head_dim : 2 * head_dim] = acc[at, head_dim : 2 * head_dim].astype(low)
        dgains[0:1, 4 * width + head_dim : 4 * width + 2 * head_dim] += grad
        return carry

    lax.fori_loop(0, 4, key_back, 0)
    in_scatter = RowScatter(place, part, rows, first_buf, second_buf, mixed_buf, row_send.at[3], row_recv.at[3])
    for step, index in enumerate(in_scatter.order()):
        at = pl.ds(pl.multiple_of(index * rows, rows), rows)
        more = dot_nt(dquery[at], wall[:, at_query:at_output]) + dot_nt(dkeyval[at], wall[:, 0:kv_end])
        part[at] = more.astype(low)
        in_scatter.after(step)

    normed = big.at[:, at_normed : at_normed + width]
    for m in range(0, width, third):
        wall[m : m + third, 0:kv_end] = dot_tn(normed[:, m : m + third], dkeyval[...]).astype(low)

    def kv_block(y, core):
        return wall.at[:, pl.ds(pl.multiple_of((y * 2 + core) * quarter, quarter), quarter)]

    def kv_copy(index):
        send, recv = last_send.at[index], last_recv.at[index]
        if index == 2:
            return remote(kv_mixed, kv_second, send, recv, place.across)
        return remote(
            kv_block(1 - place.y if index == 0 else place.y, 1 - place.core), kv_first.at[index], send, recv, place.mate
        )

    kv_copy(0).start()
    kv_copy(1).start()
    weight_gradient(at_query, head_dim, normed, dquery[...])
    weight_gradient(at_output, head_dim, row_buf, big[:, at_att : at_att + head_dim])
    kv_copy(0).wait_recv()
    kv_mixed[...] = (kv_block(1 - place.y, place.core)[...].astype(full) + kv_first[0].astype(full)).astype(low)
    kv_copy(2).start()
    scatter.pump(1)

    dn1 = in_scatter.total()
    x = tokens_ref[...].astype(full)
    back, grad = norm_back(x, inverse_rms(x), gain_in, dn1)
    dgains[0:1, 0:width] = grad
    tokens_grad[...] = (dhidden[...] + back).astype(low)
    step = gains_grad.shape[1]
    for origin in range(2 * lines):
        gain_part[origin * 8 : origin * 8 + 8] = dgains[:, origin * step : (origin + 1) * step]

    def gain_copy(index):
        source, target, device = (
            (gain_part, gain_first, place.mate) if index == 0 else (gain_part, gain_second, place.across)
        )
        return remote(source, target, last_send.at[3 + index], last_recv.at[3 + index], device)

    gain_copy(0).start()
    kv_copy(1).wait_recv()
    kv_copy(2).wait_recv()
    wall[:, kv_end:at_query] = (
        kv_block(place.y, place.core)[...].astype(full) + kv_first[1].astype(full) + kv_second[...].astype(full)
    ).astype(low)
    scatter.start(last + 1)
    gain_copy(0).wait_recv()
    gain_copy(0).wait_send()
    gain_part[...] = gain_part[...] + gain_first[...]
    gain_copy(1).start()
    gain_copy(1).wait_recv()
    gain_copy(1).wait_send()
    gain_part[...] = gain_part[...] + gain_second[...]

    gain_scatter = LineScatter(
        place,
        lambda group, origin: gain_part.at[pl.ds(origin * 8, 8)],
        lambda group, home: gain_side.at[pl.ds(home * 8, 8)],
        lambda group, step: gain_line.at[pl.ds((step - 1) * 8, 8)],
        gain_send,
        gain_recv,
        full,
    )
    gain_scatter.start(0)

    stores = []

    def store(group):
        sums = scatter.total(group)
        if group > last:
            pieces = [(sums, small_grad, slice(0, small_end - kv_end))]
            kv_own[...] = sums[:, 0:quarter].astype(low)
        else:
            first, _, padded = chunks[group]
            pieces = [
                (sums[:, k * padded : (k + 1) * padded], target, slice(first, first + padded))
                for k, target in enumerate((gate_grad, up_grad, down_grad))
            ]
        for piece, target, at in pieces:
            slot = len(stores)
            down, right = slot // 2 * shard, slot % 2 * CHUNK
            held = acc.at[down : down + shard, right : right + piece.shape[1]]
            held[...] = piece
            copy = pltpu.make_async_copy(held, target.at[:, at], store_sem.at[slot])
            copy.start()
            stores.append(copy)

    for c in range(2, len(chunks)):
        scatter.pump(c)
        store(c - 2)
    gain_scatter.pump(0)
    scatter.pump(last + 1)
    for c in range(len(chunks) - 2, len(chunks)):
        store(c)
    gains_grad[...] = gain_scatter.total(0)
    store(last + 1)

    def own_block(y, core):
        return keyval_grad.at[:, pl.ds(pl.multiple_of((y * 2 + core) * quarter, quarter), quarter)]

    own_block(place.y, place.core)[...] = kv_own[...]
    targets = (place.mate, place.across, (place.dp, (1 - place.y) * 2 + (1 - place.core)))
    sends = [
        remote(kv_own, own_block(place.y, place.core), last_send.at[5 + i], last_recv.at[5 + i], target)
        for i, target in enumerate(targets)
    ]
    for copy in sends:
        copy.start()
    for i, (y, core) in enumerate(
        ((place.y, 1 - place.core), (1 - place.y, place.core), (1 - place.y, 1 - place.core))
    ):
        remote(kv_own, own_block(y, core), last_send.at[5 + i], last_recv.at[5 + i], targets[i]).wait_recv()
    for copy in sends:
        copy.wait_send()
    for index in range(3):
        kv_copy(index).wait_send()
    scatter.finish(range(len(spans)))
    gain_scatter.finish([0])
    proj_all.finish()
    in_scatter.finish()
    for copy in stores:
        copy.wait()


def backward_call(sizes, vmem_args, hbm_args):
    lines, rows, width, head_dim, units = sizes
    length = 4 * rows
    columns = hbm_args[0].shape[1]
    shard = hbm_args[0].shape[0] // (2 * lines)
    gains = vmem_args[3].shape[1]
    kv_end = small_columns(head_dim)[0]
    quarter = head_dim // 2
    chunks = chunks_of(units)
    groups = len(chunks) + 1
    vm = pl.BlockSpec(memory_space=pltpu.VMEM)
    hbm = pl.BlockSpec(memory_space=pl.ANY)
    padded = sum(c[2] for c in chunks)
    large = [((shard, padded), full)] * 3 + [((shard, 5 * quarter), full)]
    outs = [
        ((rows, width), low),
        ((shard, 2 * head_dim), low),
        ((8, gains // (2 * lines)), full),
    ]
    scratch = [
        (hbm_args[0].shape, low),
        ((lines * shard, columns - kv_end), low),
        (((lines - 1) * shard, columns - kv_end), low),
        ((length, 6 * CHUNK), low),
        ((length, width), low),
        ((length, width), low),
        ((length, width), full),
        ((2, rows, width), low),
        ((rows, width), low),
        ((rows, width), low),
        ((length, head_dim), low),
        ((length, head_dim), low),
        ((length, head_dim), low),
        ((length, 2 * head_dim), low),
        ((rows, width), full),
        ((rows, width), low),
        ((2, width, quarter), low),
        ((width, quarter), low),
        ((width, quarter), low),
        ((shard, quarter), low),
        ((8, gains), full),
        ((2 * lines * 8, gains // (2 * lines)), full),
        ((2 * lines * 8, gains // (2 * lines)), full),
        ((2 * lines * 8, gains // (2 * lines)), full),
        ((lines * 8, gains // (2 * lines)), full),
        (((lines - 1) * 8, gains // (2 * lines)), full),
    ]
    sems = [(4, 3), (4, 3), (2, groups, lines), (2, groups, lines), (2, 1, lines), (2, 1, lines), (8,), (8,)]
    sems += [(10 + 4 * len(chunks),), (1 + 3 * len(chunks),)]
    return pl.pallas_call(
        functools.partial(backward_kernel, sizes),
        out_shape=[jax.ShapeDtypeStruct(*item) for item in large + outs],
        in_specs=[vm] * len(vmem_args) + [hbm] * len(hbm_args),
        out_specs=[hbm] * len(large) + [vm] * len(outs),
        scratch_shapes=[pltpu.VMEM(*item) for item in scratch] + [pltpu.SemaphoreType.DMA(dims) for dims in sems],
        compiler_params=pltpu.CompilerParams(
            collective_id=1, has_side_effects=True, vmem_limit_bytes=63 * 1024 * 1024
        ),
        name="backward",
    )(*vmem_args, *hbm_args)


def mixed_dot(left, right):
    return jnp.dot(left, right, preferred_element_type=jnp.float32)


def rms_scale(vector, gain_vec):
    return (
        vector
        * lax.rsqrt(jnp.mean(vector * vector, axis=-1, keepdims=True) + eps_norm)
        * (1.0 + gain_vec)
    )


def rotate(vector, positions):
    half_dim = vector.shape[-1] // 2
    inv_freq = rope_base ** (-2.0 * jnp.arange(half_dim).astype(jnp.float32) / vector.shape[-1])
    angles = positions[:, None] * inv_freq[None, :]
    cosine = jnp.cos(angles)[:, None, :]
    sine_v = jnp.sin(angles)[:, None, :]
    front_half = vector[..., :half_dim]
    back_half = vector[..., half_dim:]
    return jnp.concatenate(
        [front_half * cosine - back_half * sine_v, back_half * cosine + front_half * sine_v],
        axis=-1,
    )


def adam_step(weight, gradient, moment, second, step_rate):
    moment = beta_first * moment + (1.0 - beta_first) * gradient
    second = beta_second * second + (1.0 - beta_second) * gradient * gradient
    scaled = (
        moment
        / (1.0 - beta_first**STEP)
        / (jnp.sqrt(second / (1.0 - beta_second**STEP)) + adam_eps)
    )
    return (moment, second, weight - step_rate * (scaled + decay_rate * weight))


def plain_device(
    tokens,
    cotangent,
    prefix,
    query_weight,
    keyval_weight,
    output_weight,
    gateup_weight,
    down_weight,
    norm_gains,
    query_first,
    keyval_first,
    output_first,
    gateup_first,
    down_first,
    gains_first,
    query_second,
    keyval_second,
    output_second,
    gateup_second,
    down_second,
    gains_second,
):
    rows_dev, width = tokens.shape
    length = rows_dev * lax.axis_size("tensor")
    query_full, keyval_full, output_full, gateup_full, down_full, gains_full = (
        lax.all_gather(query_weight.astype(jnp.bfloat16), "dp", axis=0, tiled=True),
        lax.all_gather(keyval_weight.astype(jnp.bfloat16), "dp", axis=0, tiled=True),
        lax.all_gather(output_weight.astype(jnp.bfloat16), "dp", axis=0, tiled=True),
        lax.all_gather(gateup_weight.astype(jnp.bfloat16), "dp", axis=0, tiled=True),
        lax.all_gather(down_weight.astype(jnp.bfloat16), "dp", axis=0, tiled=True),
        lax.all_gather(norm_gains.astype(jnp.bfloat16), "dp", axis=0, tiled=True),
    )
    head_dim = keyval_full.shape[1] // 2
    heads_dev = query_full.shape[1] // head_dim
    units = down_full.shape[1]
    gain_values = gains_full.astype(jnp.float32)
    gain_input = gain_values[0:width]
    gain_attn = gain_values[width : 2 * width]
    gain_pre = gain_values[2 * width : 3 * width]
    gain_ffn = gain_values[3 * width : 4 * width]
    gain_query = gain_values[4 * width : 4 * width + head_dim]
    gain_key = gain_values[4 * width + head_dim : 4 * width + 2 * head_dim]
    positions = jnp.arange(length).astype(jnp.float32)
    span_rows = min(512, length)
    count_blocks = length // span_rows
    starts = jnp.arange(0, length, span_rows, dtype=jnp.int32)
    columns = jnp.arange(length, dtype=jnp.int32)
    prefix_len = prefix[0]
    gateup_flat = gateup_full.reshape(width, 2 * units)

    def shape_query(raw_rows, gain_vec):
        return rotate(rms_scale(raw_rows, gain_vec), positions)

    def shape_key(raw_rows, gain_vec):
        return rotate(rms_scale(raw_rows[:, None, :], gain_vec), positions)[:, 0]

    token_rows = tokens.astype(jnp.float32)
    normed_local = rms_scale(token_rows, gain_input).astype(jnp.bfloat16)
    normed = lax.all_gather(normed_local, "tensor", axis=0, tiled=True)
    query_raw = mixed_dot(normed, query_full).reshape(length, heads_dev, head_dim)
    keyval_raw = mixed_dot(normed, keyval_full)
    query_rot = shape_query(query_raw, gain_query).astype(jnp.bfloat16)
    key_rot = shape_key(keyval_raw[:, :head_dim], gain_key).astype(jnp.bfloat16)
    value_low = keyval_raw[:, head_dim:].astype(jnp.bfloat16)

    def scores_of(row_start):
        row_ids = row_start + jnp.arange(span_rows, dtype=jnp.int32)
        q_blk = lax.dynamic_slice_in_dim(query_rot, row_start, span_rows, 0)
        raw_scores = (
            jnp.einsum("rhd,kd->hrk", q_blk, key_rot, preferred_element_type=jnp.float32)
            * query_scale
        )
        allowed = (columns[None, :] <= row_ids[:, None]) | (columns[None, :] < prefix_len)
        return (jnp.where(allowed[None], raw_scores, masked_fill), q_blk)

    def forward_block(row_start):
        scores, q_blk = scores_of(row_start)
        row_peak = jnp.max(scores, axis=-1, keepdims=True)
        shifted = jnp.exp(scores - row_peak)
        denom_sum = jnp.sum(shifted, axis=-1, keepdims=True)
        soft_probs = (shifted / denom_sum).astype(jnp.bfloat16)
        mixed_rows = jnp.einsum(
            "hrk,kd->rhd", soft_probs, value_low, preferred_element_type=jnp.float32
        )
        return (mixed_rows, (row_peak + jnp.log(denom_sum))[..., 0])

    attended_blocks, log_sums = lax.map(forward_block, starts)
    attended = attended_blocks.reshape(length, heads_dev * head_dim).astype(jnp.bfloat16)
    attn_part = jnp.einsum("rk,dk->rd", attended, output_full, preferred_element_type=jnp.float32)
    projected = lax.psum_scatter(
        attn_part.astype(jnp.bfloat16), "tensor", scatter_dimension=0, tiled=True
    ).astype(jnp.float32)
    hidden_state = token_rows + rms_scale(projected, gain_attn)
    normed_two = lax.all_gather(
        rms_scale(hidden_state, gain_pre).astype(jnp.bfloat16), "tensor", axis=0, tiled=True
    )
    gateup = mixed_dot(normed_two, gateup_flat)
    gate_part = gateup[:, :units]
    up_part = gateup[:, units:]
    activation = (jax.nn.gelu(gate_part, approximate=True) * up_part).astype(jnp.bfloat16)
    down_part = jnp.einsum("ru,du->rd", activation, down_full, preferred_element_type=jnp.float32)
    down_sum = lax.psum_scatter(
        down_part.astype(jnp.bfloat16), "tensor", scatter_dimension=0, tiled=True
    ).astype(jnp.float32)
    block_out = hidden_state + rms_scale(down_sum, gain_ffn)
    grad_out = cotangent.astype(jnp.float32)
    pull_ffn = jax.vjp(rms_scale, down_sum, gain_ffn)[1]
    grad_down, grad_gain_ffn = pull_ffn(grad_out)
    down_back = lax.all_gather(grad_down.astype(jnp.bfloat16), "tensor", axis=0, tiled=True)
    grad_activation = mixed_dot(down_back, down_full)
    grad_down_w = jnp.einsum("rd,ru->du", down_back, activation, preferred_element_type=jnp.float32)

    def geglu(gate_in, up_in):
        return jax.nn.gelu(gate_in, approximate=True) * up_in

    pull_act = jax.vjp(geglu, gate_part, up_part)[1]
    grad_gate, grad_up = pull_act(grad_activation)
    grad_gateup = jnp.concatenate([grad_gate, grad_up], axis=1).astype(jnp.bfloat16)
    grad_gateup_w = jnp.einsum(
        "rd,ru->du", normed_two, grad_gateup, preferred_element_type=jnp.float32
    ).reshape(width, 2, units)
    grad_normed_two = jnp.einsum(
        "ru,du->rd", grad_gateup, gateup_flat, preferred_element_type=jnp.float32
    )
    grad_pre_rows = lax.psum_scatter(
        grad_normed_two.astype(jnp.bfloat16), "tensor", scatter_dimension=0, tiled=True
    ).astype(jnp.float32)
    pull_pre = jax.vjp(rms_scale, hidden_state, gain_pre)[1]
    grad_hidden_norm, grad_gain_pre = pull_pre(grad_pre_rows)
    grad_hidden = grad_out + grad_hidden_norm
    pull_attn = jax.vjp(rms_scale, projected, gain_attn)[1]
    grad_proj, grad_gain_attn = pull_attn(grad_hidden)
    proj_back = lax.all_gather(grad_proj.astype(jnp.bfloat16), "tensor", axis=0, tiled=True)
    grad_output_w = jnp.einsum("rd,rk->dk", proj_back, attended, preferred_element_type=jnp.float32)
    grad_attended = (
        mixed_dot(proj_back, output_full)
        .astype(jnp.bfloat16)
        .reshape(count_blocks, span_rows, heads_dev, head_dim)
    )

    def backward_block(carry, batch_item):
        key_acc, value_acc = carry
        row_start, grad_att, lse_blk = batch_item
        scores, q_blk = scores_of(row_start)
        soft_full = jnp.exp(scores - lse_blk[..., None])
        grad_probs = jnp.einsum(
            "rhd,kd->hrk", grad_att, value_low, preferred_element_type=jnp.float32
        )
        delta_rows = jnp.sum(soft_full * grad_probs, axis=-1, keepdims=True)
        grad_scores = (soft_full * (grad_probs - delta_rows)).astype(jnp.bfloat16)
        grad_query = (
            jnp.einsum("hrk,kd->rhd", grad_scores, key_rot, preferred_element_type=jnp.float32)
            * query_scale
        )
        key_acc = (
            key_acc
            + jnp.einsum("hrk,rhd->kd", grad_scores, q_blk, preferred_element_type=jnp.float32)
            * query_scale
        )
        value_acc = value_acc + jnp.einsum(
            "hrk,rhd->kd",
            soft_full.astype(jnp.bfloat16),
            grad_att,
            preferred_element_type=jnp.float32,
        )
        return ((key_acc, value_acc), grad_query)

    zero_rows = jnp.zeros((length, head_dim), jnp.float32)
    (grad_key_rot, grad_value), grad_query_blocks = lax.scan(
        backward_block, (zero_rows, zero_rows), (starts, grad_attended, log_sums)
    )
    grad_query_rot = grad_query_blocks.reshape(length, heads_dev, head_dim)
    pull_query = jax.vjp(shape_query, query_raw, gain_query)[1]
    grad_query_raw, grad_gain_query = pull_query(grad_query_rot)
    pull_key = jax.vjp(shape_key, keyval_raw[:, :head_dim], gain_key)[1]
    grad_key_raw, grad_gain_key = pull_key(grad_key_rot)
    grad_query_low = grad_query_raw.reshape(length, heads_dev * head_dim).astype(jnp.bfloat16)
    grad_keyval = jnp.concatenate([grad_key_raw, grad_value], axis=1)
    grad_query_w = jnp.einsum(
        "rd,rk->dk", normed, grad_query_low, preferred_element_type=jnp.float32
    )
    grad_normed_query = jnp.einsum(
        "rk,dk->rd", grad_query_low, query_full, preferred_element_type=jnp.float32
    )
    grad_normed_part, grad_keyval_own = (
        lax.psum_scatter(
            grad_normed_query.astype(jnp.bfloat16), "tensor", scatter_dimension=0, tiled=True
        ).astype(jnp.float32),
        lax.psum_scatter(
            grad_keyval.astype(jnp.bfloat16), "tensor", scatter_dimension=0, tiled=True
        ).astype(jnp.float32),
    )
    grad_keyval_low = grad_keyval_own.astype(jnp.bfloat16)
    grad_keyval_w = jnp.einsum(
        "rd,rk->dk", normed_local, grad_keyval_low, preferred_element_type=jnp.float32
    )
    grad_normed = grad_normed_part + jnp.einsum(
        "rk,dk->rd", grad_keyval_low, keyval_full, preferred_element_type=jnp.float32
    )
    pull_input = jax.vjp(rms_scale, token_rows, gain_input)[1]
    grad_token_norm, grad_gain_input = pull_input(grad_normed)
    tokens_grad = (grad_hidden + grad_token_norm).astype(jnp.bfloat16)
    grad_gains = jnp.concatenate(
        [
            grad_gain_input,
            grad_gain_attn,
            grad_gain_pre,
            grad_gain_ffn,
            grad_gain_query,
            grad_gain_key,
        ]
    )
    keyval_total, gains_total = (
        lax.psum(grad_keyval_w.astype(jnp.bfloat16), "tensor").astype(jnp.float32),
        lax.psum(grad_gains.astype(jnp.bfloat16), "tensor").astype(jnp.float32),
    )
    query_sum, keyval_sum, output_sum, gateup_sum, down_grad_sum, gains_sum = (
        lax.psum_scatter(grad_query_w, "dp", scatter_dimension=0, tiled=True),
        lax.psum_scatter(keyval_total, "dp", scatter_dimension=0, tiled=True),
        lax.psum_scatter(grad_output_w, "dp", scatter_dimension=0, tiled=True),
        lax.psum_scatter(grad_gateup_w, "dp", scatter_dimension=0, tiled=True),
        lax.psum_scatter(grad_down_w, "dp", scatter_dimension=0, tiled=True),
        lax.psum_scatter(gains_total, "dp", scatter_dimension=0, tiled=True),
    )
    query_moment, query_square, query_master = adam_step(
        query_weight, query_sum, query_first, query_second, D ** (-0.5)
    )
    keyval_moment, keyval_square, keyval_master = adam_step(
        keyval_weight, keyval_sum, keyval_first, keyval_second, D ** (-0.5)
    )
    output_moment, output_square, output_master = adam_step(
        output_weight, output_sum, output_first, output_second, (HEADS * HEAD_DIM) ** (-0.5)
    )
    gateup_moment, gateup_square, gateup_master = adam_step(
        gateup_weight, gateup_sum, gateup_first, gateup_second, D ** (-0.5)
    )
    down_moment, down_square, down_master = adam_step(
        down_weight, down_grad_sum, down_first, down_second, FF ** (-0.5)
    )
    gains_moment, gains_square, gains_master = adam_step(
        norm_gains, gains_sum, gains_first, gains_second, 0.3
    )
    return (
        block_out.astype(jnp.bfloat16),
        tokens_grad,
        query_moment,
        query_square,
        query_master,
        keyval_moment,
        keyval_square,
        keyval_master,
        output_moment,
        output_square,
        output_master,
        gateup_moment,
        gateup_square,
        gateup_master,
        down_moment,
        down_square,
        down_master,
        gains_moment,
        gains_square,
        gains_master,
    )


def per_device(
    tokens,
    cotangent,
    prefix,
    query_weight,
    keyval_weight,
    output_weight,
    gateup_weight,
    down_weight,
    norm_gains,
    query_first,
    keyval_first,
    output_first,
    gateup_first,
    down_first,
    gains_first,
    query_second,
    keyval_second,
    output_second,
    gateup_second,
    down_second,
    gains_second,
):
    rows, width = tokens.shape
    lines = lax.axis_size("dp") // 2
    shard = query_weight.shape[0]
    head_dim = keyval_weight.shape[1] // 2
    units = down_weight.shape[1]
    fits = (
        lax.axis_size("tensor") == 4
        and lax.axis_size("dp") == 2 * lines
        and query_weight.shape[1] == head_dim
        and shard % 16 == 0
        and norm_gains.shape[0] % 128 == 0
        and (3 * len(chunks_of(units)) + 2) // 2 * shard <= 4 * rows
    )
    if not fits:
        return plain_device(
            tokens,
            cotangent,
            prefix,
            query_weight,
            keyval_weight,
            output_weight,
            gateup_weight,
            down_weight,
            norm_gains,
            query_first,
            keyval_first,
            output_first,
            gateup_first,
            down_first,
            gains_first,
            query_second,
            keyval_second,
            output_second,
            gateup_second,
            down_second,
            gains_second,
        )
    length = 4 * rows
    sizes = (lines, rows, width, head_dim, units)
    flat = [keyval_weight, jnp.zeros((shard, head_dim // 2), full), query_weight, output_weight]
    for first, wide, padded in chunks_of(units):
        for part in (gateup_weight[:, 0], gateup_weight[:, 1], down_weight):
            flat.append(jnp.pad(part[:, first : first + wide], ((0, 0), (0, padded - wide))))
    packed = jnp.concatenate(flat, axis=1).astype(low)
    gains_low = jnp.broadcast_to(norm_gains.astype(low).astype(full), (8, norm_gains.shape[0]))
    angles = np.arange(length)[:, None] * (rope_base ** (-2.0 * np.arange(head_dim // 2) / head_dim))[None, :]
    cosine = jnp.asarray(np.cos(angles), full)
    sine = jnp.asarray(np.sin(angles), full)
    *saved, gvec, proj, hidden, grad_down, dgain_ffn, block_out = forward_call(
        sizes, prefix, tokens, cotangent, gains_low, packed, cosine, sine
    )
    gate_sum, up_sum, down_grad_sum, small_sum, tokens_grad, keyval_sum, gains_sum = backward_call(
        sizes, (grad_down, cotangent, tokens, gvec, dgain_ffn, proj, hidden, cosine, sine), saved
    )
    kv_end, at_query, at_output, small_end = small_columns(head_dim)
    query_sum = small_sum[:, at_query - kv_end : at_output - kv_end]
    output_sum = small_sum[:, at_output - kv_end : small_end - kv_end]
    keyval_sum = keyval_sum.astype(full)
    gains_sum = gains_sum[0]
    gateup_sum = jnp.stack([gate_sum[:, :units], up_sum[:, :units]], axis=1)
    down_grad_sum = down_grad_sum[:, :units]
    query_moment, query_square, query_master = adam_step(
        query_weight, query_sum, query_first, query_second, D ** (-0.5)
    )
    keyval_moment, keyval_square, keyval_master = adam_step(
        keyval_weight, keyval_sum, keyval_first, keyval_second, D ** (-0.5)
    )
    output_moment, output_square, output_master = adam_step(
        output_weight, output_sum, output_first, output_second, (HEADS * HEAD_DIM) ** (-0.5)
    )
    gateup_moment, gateup_square, gateup_master = adam_step(
        gateup_weight, gateup_sum, gateup_first, gateup_second, D ** (-0.5)
    )
    down_moment, down_square, down_master = adam_step(
        down_weight, down_grad_sum, down_first, down_second, FF ** (-0.5)
    )
    gains_moment, gains_square, gains_master = adam_step(
        norm_gains, gains_sum, gains_first, gains_second, 0.3
    )
    return (
        block_out,
        tokens_grad,
        query_moment,
        query_square,
        query_master,
        keyval_moment,
        keyval_square,
        keyval_master,
        output_moment,
        output_square,
        output_master,
        gateup_moment,
        gateup_square,
        gateup_master,
        down_moment,
        down_square,
        down_master,
        gains_moment,
        gains_square,
        gains_master,
    )


def solution(mesh):
    placed = (
        P(("dp", "tensor"), None),
        P(("dp", "tensor"), None),
        P("dp"),
        P("dp", "tensor"),
        P("dp", None),
        P("dp", "tensor"),
        P("dp", None, "tensor"),
        P("dp", "tensor"),
        P("dp"),
        P("dp", "tensor"),
        P("dp", None),
        P("dp", "tensor"),
        P("dp", None, "tensor"),
        P("dp", "tensor"),
        P("dp"),
        P("dp", "tensor"),
        P("dp", None),
        P("dp", "tensor"),
        P("dp", None, "tensor"),
        P("dp", "tensor"),
        P("dp"),
    )
    return jax.shard_map(
        per_device,
        mesh=mesh,
        in_specs=placed,
        out_specs=(
            P(("dp", "tensor"), None),
            P(("dp", "tensor"), None),
            P("dp", "tensor"),
            P("dp", "tensor"),
            P("dp", "tensor"),
            P("dp", None),
            P("dp", None),
            P("dp", None),
            P("dp", "tensor"),
            P("dp", "tensor"),
            P("dp", "tensor"),
            P("dp", None, "tensor"),
            P("dp", None, "tensor"),
            P("dp", None, "tensor"),
            P("dp", "tensor"),
            P("dp", "tensor"),
            P("dp", "tensor"),
            P("dp"),
            P("dp"),
            P("dp"),
        ),
        check_vma=False,
    )
```

```python
import functools

import jax
import jax.numpy as jnp
import numpy as np
from jax import lax
from jax.experimental import pallas as pl
from jax.experimental.pallas import tpu as pltpu
from jax.sharding import PartitionSpec as P

D = 1152
FF = 6912
HEADS = 4
HEAD_DIM = 256
STEP = 10


eps_norm = 1e-06
query_scale = 0.0625
rope_base = 1000000.0
beta_first = 0.9
beta_second = 0.95
adam_eps = 1e-08
decay_rate = 0.01
masked_fill = -1e30
MESH = pl.DeviceIdType.MESH
low = jnp.bfloat16
full = jnp.float32
CHUNK = 512


def dot_nn(left, right):
    return lax.dot_general(left, right, (((1,), (0,)), ((), ())), preferred_element_type=full)


def dot_nt(left, right):
    return lax.dot_general(left, right, (((1,), (1,)), ((), ())), preferred_element_type=full)


def dot_tn(left, right):
    return lax.dot_general(left, right, (((0,), (0,)), ((), ())), preferred_element_type=full)


def chunks_of(units):
    out = []
    first = 0
    while first < units:
        width = min(CHUNK, units - first)
        out.append((first, width, -(-width // 128) * 128))
        first += width
    return out


def small_columns(head_dim):
    return 2 * head_dim, 3 * head_dim, 4 * head_dim


def packed_columns(units, head_dim):
    at = small_columns(head_dim)[2]
    places = []
    for first, width, padded in chunks_of(units):
        places.append((at, at + padded, at + 2 * padded))
        at += 3 * padded
    return places, at


class Place:
    def __init__(self):
        self.dp = lax.axis_index("dp")
        self.tensor = lax.axis_index("tensor")
        self.z = self.dp // 2
        self.x = self.dp % 2
        self.y = self.tensor // 2
        self.core = self.tensor % 2
        self.homes = (self.z, self.z + 1 - 2 * (self.z % 2), (self.z + 2) % 4, 3 - self.z)
        self.end = ((self.z + 1) // 2 + 1) % 2
        self.middle = self.end == 0
        self.mate = (self.dp, self.y * 2 + (1 - self.core))
        self.across = (self.dp, (1 - self.y) * 2 + self.core)
        self.side = (self.z * 2 + (1 - self.x), self.tensor)
        self.inner = ((1 + self.z % 2) * 2 + self.x, self.tensor)

    def line(self, step):
        return (self.homes[step] * 2 + self.x, self.tensor)

    def peers(self):
        return [self.mate, self.across, self.side] + [self.line(s) for s in (1, 2, 3)]


def meet(place):
    barrier = pltpu.get_barrier_semaphore()
    peers = place.peers()
    for peer in peers:
        pl.semaphore_signal(barrier, inc=1, device_id=peer, device_id_type=MESH)
    pl.semaphore_wait(barrier, len(peers))


def remote(source, target, send_sem, recv_sem, device):
    return pltpu.make_async_remote_copy(
        src_ref=source,
        dst_ref=target,
        send_sem=send_sem,
        recv_sem=recv_sem,
        device_id=device,
        device_id_type=MESH,
    )


class LineGather:
    def __init__(self, place, region, wide, send, recv, relay_send, side_send, side_recv):
        self.place, self.region, self.wide = place, region, wide
        self.send, self.recv, self.relay_send = send, recv, relay_send
        self.side_send, self.side_recv = side_send, side_recv

    def columns(self, group):
        return (0, 1) if self.wide[group] else (0,)

    def origin(self, column, step):
        place = self.place
        return place.homes[step] * 2 + (place.x if column == 0 else 1 - place.x)

    def along(self, group, column, step):
        block = self.region(group, self.origin(column, 0))
        return remote(
            block, block, self.send.at[group, column, step], self.recv.at[group, column, step], self.place.line(step)
        )

    def arrive(self, group, column, step):
        block = self.region(group, self.origin(column, step))
        remote(
            block, block, self.send.at[group, column, step], self.recv.at[group, column, step], self.place.line(step)
        ).wait_recv()

    def relay(self, group, column):
        block = self.region(group, self.origin(column, 2))
        return remote(
            block, block, self.relay_send.at[group, column], self.recv.at[group, column, 3], self.place.line(1)
        )

    def sideways(self, group, step):
        block = self.region(group, self.origin(0, step))
        return remote(
            block, block, self.side_send.at[group, step], self.side_recv.at[group, step], self.place.side
        )

    def arrive_side(self, group, step):
        block = self.region(group, self.origin(1, step))
        remote(
            block, block, self.side_send.at[group, step], self.side_recv.at[group, step], self.place.side
        ).wait_recv()

    def start_line(self, group, column):
        self.along(group, column, 2).start()
        self.along(group, column, 1).start()

        @pl.when(self.place.middle)
        def _():
            self.along(group, column, 3).start()

    def start(self, group):
        self.sideways(group, 0).start()
        self.start_line(group, 0)

    def widen(self, group):
        self.arrive_side(group, 0)
        self.start_line(group, 1)

    def pass_on(self, group):
        for column in self.columns(group):
            self.arrive(group, column, 2)

            @pl.when(self.place.middle)
            def _():
                self.relay(group, column).start()

            if not self.wide[group]:
                self.sideways(group, 2).start()

    def collect(self, group):
        for column in self.columns(group):
            for step in (1, 3):
                self.arrive(group, column, step)
                if not self.wide[group]:
                    self.sideways(group, step).start()

    def ready(self, group):
        if not self.wide[group]:
            for step in (0, 2, 1, 3):
                self.arrive_side(group, step)

    def finish(self):
        for group in range(len(self.wide)):
            for column in self.columns(group):
                self.along(group, column, 1).wait_send()
                self.along(group, column, 2).wait_send()

                @pl.when(self.place.middle)
                def _():
                    self.along(group, column, 3).wait_send()
                    self.relay(group, column).wait_send()

            for step in (0,) if self.wide[group] else (0, 1, 2, 3):
                self.sideways(group, step).wait_send()


class RowGather:
    def __init__(self, place, source, buffer, rows, send, recv):
        self.place, self.source, self.buffer, self.rows = place, source, buffer, rows
        self.send, self.recv = send, recv

    def slab(self, y, core):
        return self.buffer.at[pl.ds((y * 2 + core) * self.rows, self.rows)]

    def copy(self, index):
        place = self.place
        slab = self.slab(1 - place.y if index == 2 else place.y, place.core)
        source = slab if index == 2 else self.source
        device = place.across if index == 1 else place.mate
        return remote(source, slab, self.send.at[index], self.recv.at[index], device)

    def arrival(self, index, y, core):
        slab = self.slab(y, core)
        remote(slab, slab, self.send.at[index], self.recv.at[index], self.place.mate).wait_recv()

    def start(self):
        self.copy(1).start()
        self.copy(0).start()

    def wait_mate(self):
        self.arrival(0, self.place.y, 1 - self.place.core)

    def wait_across(self):
        self.arrival(1, 1 - self.place.y, self.place.core)
        self.copy(2).start()

    def wait_corner(self):
        self.arrival(2, 1 - self.place.y, 1 - self.place.core)

    def finish(self):
        for index in range(3):
            self.copy(index).wait_send()


class RowScatter:
    def __init__(self, place, part, rows, first, second, mixed, send, recv):
        self.place, self.part, self.rows = place, part, rows
        self.first, self.second, self.mixed = first, second, mixed
        self.send, self.recv = send, recv

    def slab(self, y, core):
        return self.part.at[pl.ds((y * 2 + core) * self.rows, self.rows)]

    def copy(self, index):
        place = self.place
        if index == 2:
            return remote(self.mixed, self.second, self.send.at[2], self.recv.at[2], place.across)
        source = self.slab(1 - place.y if index == 0 else place.y, 1 - place.core)
        return remote(source, self.first.at[index], self.send.at[index], self.recv.at[index], place.mate)

    def order(self):
        place = self.place
        return (
            (1 - place.y) * 2 + (1 - place.core),
            (1 - place.y) * 2 + place.core,
            place.y * 2 + (1 - place.core),
            place.y * 2 + place.core,
        )

    def after(self, step):
        if step == 0:
            self.copy(0).start()
        if step == 1:
            self.copy(0).wait_recv()
            mixed = self.slab(1 - self.place.y, self.place.core)[...].astype(full) + self.first[0].astype(full)
            self.mixed[...] = mixed.astype(low)
            self.copy(2).start()
        if step == 2:
            self.copy(1).start()

    def total(self):
        self.copy(1).wait_recv()
        here = self.slab(self.place.y, self.place.core)[...].astype(full) + self.first[1].astype(full)
        self.copy(2).wait_recv()
        return here + self.second[...].astype(full)

    def finish(self):
        for index in range(3):
            self.copy(index).wait_send()


def inverse_rms(rows):
    return lax.rsqrt(jnp.mean(rows * rows, axis=-1, keepdims=True) + eps_norm)


def rotate_rows(rows, cosine, sine):
    half = rows.shape[-1] // 2
    front, back = rows[:, :half], rows[:, half:]
    return jnp.concatenate([front * cosine - back * sine, back * cosine + front * sine], axis=-1)


def rotate_back(rows, cosine, sine):
    half = rows.shape[-1] // 2
    front, back = rows[:, :half], rows[:, half:]
    return jnp.concatenate([front * cosine + back * sine, back * cosine - front * sine], axis=-1)


def gelu_parts(gate):
    scale = 0.7978845608028654
    square = gate * gate
    bent = jnp.tanh(scale * gate * (1.0 + 0.044715 * square))
    return square, bent


def forward_kernel(
    sizes,
    prefix_ref,
    tokens_ref,
    cot_ref,
    gains_ref,
    keyval_ref,
    query_ref,
    output_ref,
    gate_ref,
    up_ref,
    down_ref,
    cos_ref,
    sin_ref,
    wall_out,
    normed_out,
    normed_two_out,
    query_out,
    key_out,
    key_rot_out,
    value_out,
    attended_out,
    probs_out,
    gate_out,
    up_out,
    act_out,
    gvec,
    proj_keep,
    hidden_keep,
    grad_down,
    dgain_ffn,
    block_out,
    wall,
    normed,
    normed_two,
    query_raw,
    key_raw,
    attended,
    probs,
    gate_keep,
    up_keep,
    act,
    tok_full,
    gains_full,
    key_rot,
    value_low,
    part_one,
    first_one,
    second_one,
    mixed_one,
    first_two,
    second_two,
    mixed_two,
    down_acc,
    line_send,
    line_recv,
    relay_send,
    side_send,
    side_recv,
    row_send,
    row_recv,
    keep_sem,
):
    lines, rows, width, head_dim, units = sizes
    place = Place()
    length = 4 * rows
    shard = keyval_ref.shape[0]
    places, columns = packed_columns(units, head_dim)
    chunks = chunks_of(units)
    last = len(chunks) - 1
    kv_end, query_end, output_end = small_columns(head_dim)
    split = places[last - 1][2]
    spans = [(0, query_end), (query_end, output_end)]
    spans += [(places[c][0], places[c][0] + 3 * chunks[c][2]) for c in range(last - 1)]
    spans += [(places[last - 1][0], split), (split, columns)]
    tail = len(spans)

    def region(group, origin):
        if group == 0:
            return gains_full.at[pl.ds(origin * 8, 8)]
        lo, hi = spans[group - 1]
        return wall.at[pl.ds(origin * shard, shard), lo:hi]

    wide_groups = [False] * tail + [True]
    gather = LineGather(place, region, wide_groups, line_send, line_recv, relay_send, side_send, side_recv)
    tokens_all = RowGather(place, tokens_ref, tok_full, rows, row_send.at[0], row_recv.at[0])
    own_rows = pl.ds(place.tensor * rows, rows)
    kept = []

    def keep(source, target):
        copy = pltpu.make_async_copy(source, target, keep_sem.at[len(kept)])
        copy.start()
        kept.append(copy)

    def keep_span(group):
        lo, hi = spans[group - 1]
        keep(wall.at[:, lo:hi], wall_out.at[:, lo:hi])

    own_gains = gains_ref[...].astype(low).astype(full)
    gains_full[pl.ds(place.dp * 8, 8)] = jnp.broadcast_to(own_gains, (8, own_gains.shape[1]))
    own = pl.ds(place.dp * shard, shard)
    wall[own, 0:kv_end] = keyval_ref[...].astype(low)
    wall[own, kv_end:query_end] = query_ref[...].astype(low)
    wall[own, query_end:output_end] = output_ref[...].astype(low)
    meet(place)
    tokens_all.start()
    for group in range(3):
        gather.start(group)
    for (first, wide, padded), at in zip(chunks, places):
        for source, lo in zip((gate_ref, up_ref, down_ref), at):
            wall[own, lo : lo + wide] = source[:, first : first + wide].astype(low)
            if padded > wide:
                wall[own, lo + wide : lo + padded] = jnp.zeros((shard, padded - wide), low)
    gather.start(3)
    gather.start(4)
    tok_full[own_rows] = tokens_ref[...]
    tokens_all.wait_mate()
    tokens_all.wait_across()
    gather.pass_on(0)
    gather.pass_on(1)
    gather.collect(0)
    gather.collect(1)
    tokens_all.wait_corner()
    gather.pass_on(2)
    gather.collect(2)
    for group in range(5, tail + 1):
        gather.start(group)
    gather.ready(0)
    step = gains_ref.shape[1]
    for origin in range(2 * lines):
        gvec[:, origin * step : (origin + 1) * step] = gains_full[origin * 8 : origin * 8 + 8]
    gain_in = 1.0 + gvec[0:1, 0:width]
    gain_attn = 1.0 + gvec[0:1, width : 2 * width]
    gain_pre = 1.0 + gvec[0:1, 2 * width : 3 * width]
    gain_ffn = 1.0 + gvec[0:1, 3 * width : 4 * width]
    gain_query = 1.0 + gvec[0:1, 4 * width : 4 * width + head_dim]
    gain_key = 1.0 + gvec[0:1, 4 * width + head_dim : 4 * width + 2 * head_dim]

    def norm_slab(index, carry):
        at = pl.ds(pl.multiple_of(index * rows, rows), rows)
        x = tok_full[at].astype(full)
        normed[at] = (x * inverse_rms(x) * gain_in).astype(low)
        return carry

    lax.fori_loop(0, 4, norm_slab, 0)
    keep(normed, normed_out)
    gather.ready(1)

    def project_slab(index, carry):
        at = pl.ds(pl.multiple_of(index * rows, rows), rows)
        n1 = normed[at]
        query_raw[at] = dot_nn(n1, wall[:, kv_end:query_end])
        kv = dot_nn(n1, wall[:, 0:kv_end])
        k = kv[:, :head_dim]
        key_raw[at] = k
        key_rot[at] = rotate_rows(k * inverse_rms(k) * gain_key, cos_ref[at], sin_ref[at]).astype(low)
        value_low[at] = kv[:, head_dim:].astype(low)
        return carry

    lax.fori_loop(0, 4, project_slab, 0)
    keep(query_raw, query_out)
    keep(key_raw, key_out)
    keep(key_rot, key_rot_out)
    keep(value_low, value_out)
    keep_span(1)
    gather.ready(2)
    keep_span(2)

    out_scatter = RowScatter(place, part_one, rows, first_one, second_one, mixed_one, row_send.at[1], row_recv.at[1])

    def attend_slab(index):
        at = pl.ds(pl.multiple_of(index * rows, rows), rows)
        q = query_raw[at]
        qr = rotate_rows(q * inverse_rms(q) * gain_query, cos_ref[at], sin_ref[at]).astype(low)
        scores = dot_nt(qr, key_rot[...]) * query_scale
        row_ids = lax.broadcasted_iota(jnp.int32, (rows, length), 0) + index * rows
        columns = lax.broadcasted_iota(jnp.int32, (rows, length), 1)
        allowed = (columns <= row_ids) | (columns < prefix_ref[0])
        scores = jnp.where(allowed, scores, masked_fill)
        shifted = jnp.exp(scores - jnp.max(scores, axis=-1, keepdims=True))
        soft = (shifted / jnp.sum(shifted, axis=-1, keepdims=True)).astype(low)
        probs[at] = soft
        mixed = dot_nn(soft, value_low[...]).astype(low)
        attended[at] = mixed
        part_one[at] = dot_nt(mixed, wall[:, query_end:output_end]).astype(low)

    for step, index in enumerate(out_scatter.order()):
        attend_slab(index)
        out_scatter.after(step)
    keep(probs, probs_out)
    keep(attended, attended_out)
    gather.pass_on(3)
    gather.collect(3)
    gather.widen(tail)
    projected = out_scatter.total()
    out_scatter.finish()
    proj_keep[...] = projected
    hidden = tokens_ref[...].astype(full) + projected * inverse_rms(projected) * gain_attn
    hidden_keep[...] = hidden
    normed_two[own_rows] = (hidden * inverse_rms(hidden) * gain_pre).astype(low)
    two_all = RowGather(place, normed_two.at[own_rows], normed_two, rows, row_send.at[2], row_recv.at[2])
    two_all.start()
    two_all.wait_mate()
    two_all.wait_across()
    two_all.wait_corner()
    keep(normed_two, normed_two_out)

    down_scatter = RowScatter(place, part_one, rows, first_two, second_two, mixed_two, row_send.at[3], row_recv.at[3])
    block = 2 * rows

    def feed(c):
        first, wide, padded = chunks[c]
        at_gate, at_up, _ = places[c]

        def feed_rows(index, carry):
            at = pl.ds(pl.multiple_of(index * block, block), block)
            n2 = normed_two[at]
            gate = dot_nn(n2, wall[:, at_gate : at_gate + wide])
            up = dot_nn(n2, wall[:, at_up : at_up + wide])
            gate_keep[at, first : first + wide] = gate.astype(low)
            up_keep[at, first : first + wide] = up.astype(low)
            _, bent = gelu_parts(gate)
            act[at, first : first + wide] = (0.5 * gate * (1.0 + bent) * up).astype(low)
            return carry

        lax.fori_loop(0, 2, feed_rows, 0)
        span = slice(first, first + padded)
        keep(gate_keep.at[:, span], gate_out.at[:, span])
        keep(up_keep.at[:, span], up_out.at[:, span])
        keep(act.at[:, span], act_out.at[:, span])

    def lower(c):
        first, wide, _ = chunks[c]
        at_down = places[c][2]

        def lower_rows(index, carry):
            at = pl.ds(pl.multiple_of(index * block, block), block)
            more = dot_nt(act[at, first : first + wide], wall[:, at_down : at_down + wide])
            down_acc[at] = more if c == 0 else down_acc[at] + more
            return carry

        lax.fori_loop(0, 2, lower_rows, 0)

    for c in range(last - 1):
        gather.pass_on(c + 4)
        gather.collect(c + 4)
        gather.ready(c + 3)
        feed(c)
        lower(c)
        keep_span(c + 3)
    gather.pass_on(tail)
    gather.ready(tail - 1)
    feed(last - 1)
    keep_span(tail - 1)
    gather.collect(tail)
    feed(last)
    lower(last - 1)
    keep_span(tail)
    first, wide, _ = chunks[last]
    at_down = places[last][2]
    for step, index in enumerate(down_scatter.order()):
        at = pl.ds(pl.multiple_of(index * rows, rows), rows)
        part_one[at] = (
            down_acc[at] + dot_nt(act[at, first : first + wide], wall[:, at_down : at_down + wide])
        ).astype(low)
        down_scatter.after(step)
    f = down_scatter.total()
    inv = inverse_rms(f)
    block_out[...] = (hidden_keep[...] + f * inv * gain_ffn).astype(low)
    cot = cot_ref[...].astype(full)
    scaled = cot * gain_ffn
    grad_down[...] = (inv * (scaled - f * (inv * inv) * jnp.mean(f * scaled, axis=-1, keepdims=True))).astype(low)
    dgain_ffn[...] = jnp.broadcast_to(jnp.sum(cot * f * inv, axis=0, keepdims=True), dgain_ffn.shape)
    gather.finish()
    tokens_all.finish()
    two_all.finish()
    down_scatter.finish()
    for copy in kept:
        copy.wait()


def forward_call(sizes, prefix, tokens, cotangent, gains, weights, cosine, sine):
    lines, rows, width, head_dim, units = sizes
    length = 4 * rows
    shard = weights[0].shape[0]
    columns = packed_columns(units, head_dim)[1]
    chunks = chunks_of(units)
    padded = sum(c[2] for c in chunks)
    groups = 4 + len(chunks)
    vm = pl.BlockSpec(memory_space=pltpu.VMEM)
    hbm = pl.BlockSpec(memory_space=pl.ANY)
    large = [
        ((2 * lines * shard, columns), low),
        ((length, width), low),
        ((length, width), low),
        ((length, head_dim), full),
        ((length, head_dim), full),
        ((length, head_dim), low),
        ((length, head_dim), low),
        ((length, head_dim), low),
        ((length, length), low),
        ((length, padded), low),
        ((length, padded), low),
        ((length, padded), low),
    ]
    small = [
        ((8, gains.shape[1] * 2 * lines), full),
        ((rows, width), full),
        ((rows, width), full),
        ((rows, width), low),
        ((8, width), full),
        ((rows, width), low),
    ]
    inside = [large[i] for i in (0, 1, 2, 3, 4, 7, 8, 9, 10, 11)]
    scatter_set = [
        pltpu.VMEM((2, rows, width), low),
        pltpu.VMEM((rows, width), low),
        pltpu.VMEM((rows, width), low),
    ]
    return pl.pallas_call(
        functools.partial(forward_kernel, sizes),
        out_shape=[jax.ShapeDtypeStruct(*item) for item in large + small],
        in_specs=[pl.BlockSpec(memory_space=pltpu.SMEM)] + [vm] * 11,
        out_specs=[hbm] * len(large) + [vm] * len(small),
        scratch_shapes=[pltpu.VMEM(*item) for item in inside]
        + [
            pltpu.VMEM((length, width), low),
            pltpu.VMEM((2 * lines * 8, gains.shape[1]), full),
            pltpu.VMEM((length, head_dim), low),
            pltpu.VMEM((length, head_dim), low),
            pltpu.VMEM((length, width), low),
        ]
        + scatter_set
        + scatter_set
        + [
            pltpu.VMEM((length, width), full),
            pltpu.SemaphoreType.DMA((groups, 2, lines)),
            pltpu.SemaphoreType.DMA((groups, 2, lines)),
            pltpu.SemaphoreType.DMA((groups, 2)),
            pltpu.SemaphoreType.DMA((groups, lines)),
            pltpu.SemaphoreType.DMA((groups, lines)),
            pltpu.SemaphoreType.DMA((4, 3)),
            pltpu.SemaphoreType.DMA((4, 3)),
            pltpu.SemaphoreType.DMA((12 + 4 * len(chunks),)),
        ],
        compiler_params=pltpu.CompilerParams(
            collective_id=0, has_side_effects=True, vmem_limit_bytes=63 * 1024 * 1024
        ),
        name="forward",
    )(prefix, tokens, cotangent, gains, *weights, cosine, sine)


class LineScatter:
    def __init__(self, place, block, side_block, line_block, wide, side_send, side_recv, line_send, line_recv, kind):
        self.place, self.block, self.side_block, self.line_block = place, block, side_block, line_block
        self.wide, self.kind = wide, kind
        self.side_send, self.side_recv, self.line_send, self.line_recv = side_send, side_recv, line_send, line_recv

    def columns(self, group):
        return (0, 1) if self.wide[group] else (0,)

    def own(self, group, column, step):
        place = self.place
        return self.block(group, place.homes[step] * 2 + (place.x if column == 0 else 1 - place.x))

    def sideways(self, group, step):
        home = 0 if self.wide[group] else self.place.homes[step]
        return remote(
            self.own(group, 1, step),
            self.side_block(group, home),
            self.side_send.at[group, step],
            self.side_recv.at[group, step],
            self.place.side,
        )

    def along(self, group, column, step):
        slot = step - 1 if step < 3 else 2 + self.place.end
        return remote(
            self.own(group, column, step),
            self.line_block(group, column, slot),
            self.line_send.at[group, column, step],
            self.line_recv.at[group, column, slot],
            self.place.line(step) if step < 3 else self.place.inner,
        )

    def arrive(self, group, column, slot):
        here = self.line_block(group, column, slot)
        remote(
            here, here, self.line_send.at[group, column, 1], self.line_recv.at[group, column, slot], self.place.line(1)
        ).wait_recv()
        return here[...].astype(full)

    def start(self, group):
        if not self.wide[group]:
            for step in (3, 1, 2, 0):
                self.sideways(group, step).start()
            return
        for column in (0, 1):
            self.along(group, column, 3).start()
            self.along(group, column, 1).start()

            @pl.when(self.place.end == 1)
            def _():
                self.along(group, column, 2).start()

    def with_side(self, group, step):
        self.sideways(group, step).wait_recv()
        return self.own(group, 0, step)[...].astype(full) + self.side_block(group, self.place.homes[step])[...].astype(
            full
        )

    def pump(self, group):
        place = self.place
        if self.wide[group]:
            for column in (0, 1):

                @pl.when(place.middle)
                def _():
                    block = self.own(group, column, 2)
                    block[...] = (block[...].astype(full) + self.arrive(group, column, 3)).astype(self.kind)
                    self.along(group, column, 2).start()

            return
        for step in (3, 1):
            self.own(group, 0, step)[...] = self.with_side(group, step).astype(self.kind)
            self.along(group, 0, step).start()
        block = self.own(group, 0, 2)
        both = self.with_side(group, 2)

        @pl.when(place.middle)
        def _():
            block[...] = (both + self.arrive(group, 0, 3)).astype(self.kind)

        @pl.when(place.end == 1)
        def _():
            block[...] = both.astype(self.kind)

        self.along(group, 0, 2).start()

    def hand_over(self, group):
        block = self.own(group, 1, 0)
        both = block[...].astype(full) + self.arrive(group, 1, 0) + self.arrive(group, 1, 1)

        @pl.when(self.place.middle)
        def _():
            block[...] = (both + self.arrive(group, 1, 2)).astype(self.kind)

        @pl.when(self.place.end == 1)
        def _():
            block[...] = both.astype(self.kind)

        self.sideways(group, 0).start()

    def settle(self, group):
        self.sideways(group, 0).wait_recv()
        self.arrive(group, 0, 0)
        self.arrive(group, 0, 1)

        @pl.when(self.place.middle)
        def _():
            self.arrive(group, 0, 2)

    def total(self, group, lo, hi, held):
        parts = [
            self.own(group, 0, 0),
            self.side_block(group, 0 if self.wide[group] else self.place.z),
            self.line_block(group, 0, 0),
            self.line_block(group, 0, 1),
        ]
        first, *others = [part[:, lo:hi].astype(full) for part in parts]
        for other in others:
            first = first + other
        held[...] = first

        @pl.when(self.place.middle)
        def _():
            held[...] = first + self.line_block(group, 0, 2)[:, lo:hi].astype(full)

    def finish(self):
        for group in range(len(self.wide)):
            for step in (0,) if self.wide[group] else (0, 1, 2, 3):
                self.sideways(group, step).wait_send()
            for column in self.columns(group):
                for step in (1, 2, 3):
                    self.along(group, column, step).wait_send()


def norm_back(rows, inv, gain, grad):
    scaled = grad * gain
    back = inv * (scaled - rows * (inv * inv) * jnp.mean(rows * scaled, axis=-1, keepdims=True))
    return back, jnp.sum(grad * rows * inv, axis=0, keepdims=True)


def backward_kernel(
    sizes,
    grad_down_ref,
    cot_ref,
    tokens_ref,
    gvec,
    dgain_ffn,
    proj_ref,
    hidden_ref,
    cos_ref,
    sin_ref,
    wall_in,
    normed_in,
    normed_two_in,
    query_in,
    key_in,
    key_rot_in,
    value_in,
    attended_in,
    probs_in,
    gate_in,
    up_in,
    act_in,
    gate_grad,
    up_grad,
    down_grad,
    small_grad,
    tokens_grad,
    keyval_grad,
    gains_grad,
    wall,
    side_buf,
    side_wide,
    line_buf,
    line_wide,
    big,
    normed_two,
    row_buf,
    acc,
    first_buf,
    second_buf,
    mixed_buf,
    key_rot,
    value_low,
    dquery,
    dkeyval,
    dhidden,
    dproj,
    kv_first,
    kv_second,
    kv_mixed,
    kv_own,
    dgains,
    gain_part,
    gain_first,
    gain_second,
    gain_side,
    gain_line,
    row_send,
    row_recv,
    side_send,
    side_recv,
    line_send,
    line_recv,
    gain_side_send,
    gain_side_recv,
    gain_line_send,
    gain_line_recv,
    last_send,
    last_recv,
    load_sem,
    store_sem,
):
    lines, rows, width, head_dim, units = sizes
    place = Place()
    length = 4 * rows
    shard = wall.shape[0] // (2 * lines)
    kv_end, query_end, output_end = small_columns(head_dim)
    quarter = head_dim // 2
    places, _ = packed_columns(units, head_dim)
    chunks = chunks_of(units)
    last = len(chunks) - 1
    order = [last] + list(range(last))
    base_column = kv_end - quarter
    spans = [(places[c][0], places[c][0] + 3 * chunks[c][2]) for c in range(len(chunks))] + [(base_column, output_end)]
    loads = {}

    def load(name, source, target):
        copy = pltpu.make_async_copy(source, target, load_sem.at[len(loads)])
        copy.start()
        loads[name] = copy

    def load_chunk(c):
        lo, hi = spans[c]
        first, _, padded = chunks[c]
        base = (order.index(c) % 2) * 3 * CHUNK
        load(("wall", c), wall_in.at[:, lo:hi], wall.at[:, lo:hi])
        for k, source in enumerate((gate_in, up_in, act_in)):
            at = base + k * CHUNK
            load((k, c), source.at[:, first : first + padded], big.at[:, at : at + padded])

    load("two", normed_two_in, normed_two)
    load_chunk(order[0])
    load("kv", wall_in.at[:, 0:kv_end], wall.at[:, 0:kv_end])
    load("qo", wall_in.at[:, kv_end:output_end], wall.at[:, kv_end:output_end])
    load("key_rot", key_rot_in, key_rot)
    load("value", value_in, value_low)
    gain_in = 1.0 + gvec[0:1, 0:width]
    gain_attn = 1.0 + gvec[0:1, width : 2 * width]
    gain_pre = 1.0 + gvec[0:1, 2 * width : 3 * width]
    gain_query = 1.0 + gvec[0:1, 4 * width : 4 * width + head_dim]
    gain_key = 1.0 + gvec[0:1, 4 * width + head_dim : 4 * width + 2 * head_dim]
    own_rows = pl.ds(place.tensor * rows, rows)
    row_buf[own_rows] = grad_down_ref[...]
    dgains[...] = jnp.zeros_like(dgains)
    dgains[0:1, 3 * width : 4 * width] = dgain_ffn[0:1]
    meet(place)
    down_all = RowGather(place, grad_down_ref, row_buf, rows, row_send.at[0], row_recv.at[0])
    down_all.start()
    load_chunk(order[1])
    down_all.wait_mate()
    down_all.wait_across()
    down_all.wait_corner()
    loads["two"].wait()

    def block(group, origin):
        lo, hi = spans[group]
        return wall.at[pl.ds(origin * shard, shard), lo:hi]

    def side_block(group, home):
        if wide_groups[group]:
            return side_wide
        lo, hi = spans[group]
        return side_buf.at[pl.ds(home * shard, shard), lo - base_column : hi - base_column]

    def line_block(group, column, slot):
        lo, hi = spans[group]
        if wide_groups[group]:
            return line_wide.at[pl.ds((column * 4 + slot) * shard, shard)]
        return line_buf.at[pl.ds(slot * shard, shard), lo - base_column : hi - base_column]

    wide_groups = [c == last for c in range(last + 2)]
    scatter = LineScatter(
        place, block, side_block, line_block, wide_groups, side_send, side_recv, line_send, line_recv, low
    )
    part = big.at[:, 0:width]
    pre_scatter = RowScatter(place, part, rows, first_buf, second_buf, mixed_buf, row_send.at[1], row_recv.at[1])
    half = 2 * rows
    third = width // 3

    def weight_gradient(lo, wide, left, right):
        for m in range(0, width, third):
            wall[m : m + third, lo : lo + wide] = dot_tn(left[:, m : m + third], right).astype(low)

    for position, c in enumerate(order):
        first, wide, padded = chunks[c]
        at_gate, at_up, at_down = places[c]
        base = (position % 2) * 3 * CHUNK
        loads["wall", c].wait()
        for k in range(3):
            loads[k, c].wait()
        if 1 <= position < last:
            load_chunk(order[position + 1])
        of_gate = slice(base, base + wide)
        of_up = slice(base + CHUNK, base + CHUNK + wide)
        of_act = slice(base + 2 * CHUNK, base + 2 * CHUNK + wide)

        def unit_rows(index, carry):
            at = pl.ds(pl.multiple_of(index * half, half), half)
            dz = dot_nn(row_buf[at], wall[:, at_down : at_down + wide])
            gate = big[at, of_gate].astype(full)
            up = big[at, of_up].astype(full)
            square, bent = gelu_parts(gate)
            middle = 0.5 * (1.0 + bent)
            slope = middle + 0.5 * gate * (1.0 - bent * bent) * (0.7978845608028654 * (1.0 + 0.134145 * square))
            big[at, of_gate] = (dz * up * slope).astype(low)
            big[at, of_up] = (dz * gate * middle).astype(low)
            return carry

        lax.fori_loop(0, 2, unit_rows, 0)
        weight_gradient(at_down, wide, row_buf, big[:, of_act])

        def back_rows(at):
            more = dot_nt(big[at, of_gate], wall[:, at_gate : at_gate + wide])
            more = more + dot_nt(big[at, of_up], wall[:, at_up : at_up + wide])
            return more if position == 0 else acc[at] + more

        if position < last:

            def collect_rows(index, carry):
                at = pl.ds(pl.multiple_of(index * half, half), half)
                acc[at] = back_rows(at)
                return carry

            lax.fori_loop(0, 2, collect_rows, 0)
        else:
            down_all.finish()
            for step, index in enumerate(pre_scatter.order()):
                at = pl.ds(pl.multiple_of(index * rows, rows), rows)
                part[at] = back_rows(at).astype(low)
                pre_scatter.after(step)
        weight_gradient(at_gate, wide, normed_two, big[:, of_gate])
        weight_gradient(at_up, wide, normed_two, big[:, of_up])
        scatter.start(c)
        if position == 2:
            scatter.pump(last)

    at_normed = width
    at_att = at_normed + width
    load("normed", normed_in, big.at[:, at_normed : at_normed + width])
    load("attended", attended_in, big.at[:, at_att : at_att + head_dim])
    load("query", query_in, acc.at[:, 2 * head_dim : 3 * head_dim])
    load("key", key_in, acc.at[:, 3 * head_dim : 4 * head_dim])

    scatter.hand_over(last)
    scatter.pump(order[1])
    dn2 = pre_scatter.total()
    hidden = hidden_ref[...]
    back, grad = norm_back(hidden, inverse_rms(hidden), gain_pre, dn2)
    dgains[0:1, 2 * width : 3 * width] = grad
    dh = cot_ref[...].astype(full) + back
    dhidden[...] = dh
    proj = proj_ref[...]
    back, grad = norm_back(proj, inverse_rms(proj), gain_attn, dh)
    dgains[0:1, width : 2 * width] = grad
    dproj[...] = back.astype(low)
    row_buf[own_rows] = dproj[...]
    proj_all = RowGather(place, dproj, row_buf, rows, row_send.at[2], row_recv.at[2])
    proj_all.start()
    pre_scatter.finish()
    load("probs", probs_in, big.at[:, 0:length])
    acc[:, 0 : 2 * head_dim] = jnp.zeros((length, 2 * head_dim), full)
    proj_all.wait_mate()
    proj_all.wait_across()
    proj_all.wait_corner()
    for name in ("kv", "qo", "key_rot", "value", "normed", "attended", "query", "key", "probs"):
        loads[name].wait()

    def attend_back(index, carry):
        at = pl.ds(pl.multiple_of(index * rows, rows), rows)
        da = dot_nn(row_buf[at], wall[:, query_end:output_end]).astype(low)
        soft = big[at, 0:length]
        wide_soft = soft.astype(full)
        dp = dot_nt(da, value_low[...])
        ds = (wide_soft * (dp - jnp.sum(wide_soft * dp, axis=-1, keepdims=True))).astype(low)
        q = acc[at, 2 * head_dim : 3 * head_dim]
        inv = inverse_rms(q)
        cosine, sine = cos_ref[at], sin_ref[at]
        qr = rotate_rows(q * inv * gain_query, cosine, sine).astype(low)
        dqr = dot_nn(ds, key_rot[...]) * query_scale
        acc[:, 0:head_dim] += dot_tn(ds, qr)
        acc[:, head_dim : 2 * head_dim] += dot_tn(soft, da)
        dq, grad = norm_back(q, inv, gain_query, rotate_back(dqr, cosine, sine))
        dquery[at] = dq.astype(low)
        dgains[0:1, 4 * width : 4 * width + head_dim] += grad
        return carry

    lax.fori_loop(0, 4, attend_back, 0)

    def key_back(index, carry):
        at = pl.ds(pl.multiple_of(index * rows, rows), rows)
        k = acc[at, 3 * head_dim : 4 * head_dim]
        dkr = rotate_back(acc[at, 0:head_dim] * query_scale, cos_ref[at], sin_ref[at])
        dk, grad = norm_back(k, inverse_rms(k), gain_key, dkr)
        dkeyval[at, 0:head_dim] = dk.astype(low)
        dkeyval[at, head_dim : 2 * head_dim] = acc[at, head_dim : 2 * head_dim].astype(low)
        dgains[0:1, 4 * width + head_dim : 4 * width + 2 * head_dim] += grad
        return carry

    lax.fori_loop(0, 4, key_back, 0)
    scatter.pump(order[2])
    in_scatter = RowScatter(place, part, rows, first_buf, second_buf, mixed_buf, row_send.at[3], row_recv.at[3])
    for step, index in enumerate(in_scatter.order()):
        at = pl.ds(pl.multiple_of(index * rows, rows), rows)
        more = dot_nt(dquery[at], wall[:, kv_end:query_end]) + dot_nt(dkeyval[at], wall[:, 0:kv_end])
        part[at] = more.astype(low)
        in_scatter.after(step)

    normed = big.at[:, at_normed : at_normed + width]
    for m in range(0, width, third):
        wall[m : m + third, 0:kv_end] = dot_tn(normed[:, m : m + third], dkeyval[...]).astype(low)

    def kv_block(y, core):
        return wall.at[:, pl.ds(pl.multiple_of((y * 2 + core) * quarter, quarter), quarter)]

    def kv_copy(index):
        send, recv = last_send.at[index], last_recv.at[index]
        if index == 2:
            return remote(kv_mixed, kv_second, send, recv, place.across)
        return remote(
            kv_block(1 - place.y if index == 0 else place.y, 1 - place.core), kv_first.at[index], send, recv, place.mate
        )

    kv_copy(0).start()
    kv_copy(1).start()
    weight_gradient(kv_end, head_dim, normed, dquery[...])
    weight_gradient(query_end, head_dim, row_buf, big[:, at_att : at_att + head_dim])
    kv_copy(0).wait_recv()
    kv_mixed[...] = (kv_block(1 - place.y, place.core)[...].astype(full) + kv_first[0].astype(full)).astype(low)
    kv_copy(2).start()

    dn1 = in_scatter.total()
    x = tokens_ref[...].astype(full)
    back, grad = norm_back(x, inverse_rms(x), gain_in, dn1)
    dgains[0:1, 0:width] = grad
    tokens_grad[...] = (dhidden[...] + back).astype(low)
    step = gains_grad.shape[1]
    for origin in range(2 * lines):
        gain_part[origin * 8 : origin * 8 + 8] = dgains[:, origin * step : (origin + 1) * step]

    def gain_copy(index):
        source, target, device = (
            (gain_part, gain_first, place.mate) if index == 0 else (gain_part, gain_second, place.across)
        )
        return remote(source, target, last_send.at[3 + index], last_recv.at[3 + index], device)

    gain_copy(0).start()
    kv_copy(1).wait_recv()
    kv_copy(2).wait_recv()
    kv_copy(0).wait_send()
    kv_copy(1).wait_send()
    wall[:, base_column:kv_end] = (
        kv_block(place.y, place.core)[...].astype(full) + kv_first[1].astype(full) + kv_second[...].astype(full)
    ).astype(low)
    scatter.start(last + 1)
    gain_copy(0).wait_recv()
    gain_copy(0).wait_send()
    gain_part[...] = gain_part[...] + gain_first[...]
    gain_copy(1).start()
    gain_copy(1).wait_recv()
    gain_copy(1).wait_send()
    gain_part[...] = gain_part[...] + gain_second[...]

    gain_scatter = LineScatter(
        place,
        lambda group, origin: gain_part.at[pl.ds(origin * 8, 8)],
        lambda group, home: gain_side.at[pl.ds(home * 8, 8)],
        lambda group, column, slot: gain_line.at[pl.ds(slot * 8, 8)],
        [False],
        gain_side_send,
        gain_side_recv,
        gain_line_send,
        gain_line_recv,
        full,
    )
    gain_scatter.start(0)

    stores = []

    def store(group):
        first, _, padded = (0, 0, 0) if group > last else chunks[group]
        wide = output_end - base_column if group > last else padded
        scatter.settle(group)
        for k, target in enumerate((small_grad,) if group > last else (gate_grad, up_grad, down_grad)):
            slot = len(stores)
            down, right = slot // 2 * shard, slot % 2 * CHUNK
            held = acc.at[down : down + shard, right : right + wide]
            scatter.total(group, k * wide, (k + 1) * wide, held)
            copy = pltpu.make_async_copy(held, target.at[:, first : first + wide], store_sem.at[slot])
            copy.start()
            stores.append(copy)
            if group > last:
                kv_own[...] = held[:, 0:quarter].astype(low)

    scatter.pump(order[3])
    store(order[0])
    store(order[1])
    gain_scatter.pump(0)
    scatter.pump(last + 1)
    store(order[2])
    store(order[3])
    gain_scatter.settle(0)
    gain_scatter.total(0, 0, gains_grad.shape[1], gains_grad)
    store(last + 1)

    def own_block(y, core):
        return keyval_grad.at[:, pl.ds(pl.multiple_of((y * 2 + core) * quarter, quarter), quarter)]

    own_block(place.y, place.core)[...] = kv_own[...]
    targets = (place.mate, place.across, (place.dp, (1 - place.y) * 2 + (1 - place.core)))
    sends = [
        remote(kv_own, own_block(place.y, place.core), last_send.at[5 + i], last_recv.at[5 + i], target)
        for i, target in enumerate(targets)
    ]
    for copy in sends:
        copy.start()
    for i, (y, core) in enumerate(
        ((place.y, 1 - place.core), (1 - place.y, place.core), (1 - place.y, 1 - place.core))
    ):
        remote(kv_own, own_block(y, core), last_send.at[5 + i], last_recv.at[5 + i], targets[i]).wait_recv()
    for copy in sends:
        copy.wait_send()
    kv_copy(2).wait_send()
    scatter.finish()
    gain_scatter.finish()
    proj_all.finish()
    in_scatter.finish()
    for copy in stores:
        copy.wait()


def backward_call(sizes, vmem_args, hbm_args):
    lines, rows, width, head_dim, units = sizes
    length = 4 * rows
    columns = hbm_args[0].shape[1]
    shard = hbm_args[0].shape[0] // (2 * lines)
    gains = vmem_args[3].shape[1]
    quarter = head_dim // 2
    base_column = 2 * head_dim - quarter
    chunks = chunks_of(units)
    groups = len(chunks) + 1
    vm = pl.BlockSpec(memory_space=pltpu.VMEM)
    hbm = pl.BlockSpec(memory_space=pl.ANY)
    padded = sum(c[2] for c in chunks)
    large = [((shard, padded), full)] * 3 + [((shard, 5 * quarter), full)]
    outs = [
        ((rows, width), low),
        ((shard, 2 * head_dim), low),
        ((8, gains // (2 * lines)), full),
    ]
    scratch = [
        (hbm_args[0].shape, low),
        ((lines * shard, columns - base_column - 3 * chunks[-1][2]), low),
        ((shard, 3 * chunks[-1][2]), low),
        ((lines * shard, columns - base_column - 3 * chunks[-1][2]), low),
        ((2 * lines * shard, 3 * chunks[-1][2]), low),
        ((length, 6 * CHUNK), low),
        ((length, width), low),
        ((length, width), low),
        ((length, width), full),
        ((2, rows, width), low),
        ((rows, width), low),
        ((rows, width), low),
        ((length, head_dim), low),
        ((length, head_dim), low),
        ((length, head_dim), low),
        ((length, 2 * head_dim), low),
        ((rows, width), full),
        ((rows, width), low),
        ((2, width, quarter), low),
        ((width, quarter), low),
        ((width, quarter), low),
        ((shard, quarter), low),
        ((8, gains), full),
        ((2 * lines * 8, gains // (2 * lines)), full),
        ((2 * lines * 8, gains // (2 * lines)), full),
        ((2 * lines * 8, gains // (2 * lines)), full),
        ((lines * 8, gains // (2 * lines)), full),
        ((lines * 8, gains // (2 * lines)), full),
    ]
    sems = [(4, 3), (4, 3), (groups, 4), (groups, 4), (groups, 2, 4), (groups, 2, 4)]
    sems += [(1, 4), (1, 4), (1, 1, 4), (1, 1, 4), (8,), (8,)]
    sems += [(10 + 4 * len(chunks),), (1 + 3 * len(chunks),)]
    return pl.pallas_call(
        functools.partial(backward_kernel, sizes),
        out_shape=[jax.ShapeDtypeStruct(*item) for item in large + outs],
        in_specs=[vm] * len(vmem_args) + [hbm] * len(hbm_args),
        out_specs=[hbm] * len(large) + [vm] * len(outs),
        scratch_shapes=[pltpu.VMEM(*item) for item in scratch] + [pltpu.SemaphoreType.DMA(dims) for dims in sems],
        compiler_params=pltpu.CompilerParams(
            collective_id=1, has_side_effects=True, vmem_limit_bytes=63 * 1024 * 1024
        ),
        name="backward",
    )(*vmem_args, *hbm_args)


def mixed_dot(left, right):
    return jnp.dot(left, right, preferred_element_type=jnp.float32)


def rms_scale(vector, gain_vec):
    return (
        vector
        * lax.rsqrt(jnp.mean(vector * vector, axis=-1, keepdims=True) + eps_norm)
        * (1.0 + gain_vec)
    )


def rotate(vector, positions):
    half_dim = vector.shape[-1] // 2
    inv_freq = rope_base ** (-2.0 * jnp.arange(half_dim).astype(jnp.float32) / vector.shape[-1])
    angles = positions[:, None] * inv_freq[None, :]
    cosine = jnp.cos(angles)[:, None, :]
    sine_v = jnp.sin(angles)[:, None, :]
    front_half = vector[..., :half_dim]
    back_half = vector[..., half_dim:]
    return jnp.concatenate(
        [front_half * cosine - back_half * sine_v, back_half * cosine + front_half * sine_v],
        axis=-1,
    )


def adam_step(weight, gradient, moment, second, step_rate):
    moment = beta_first * moment + (1.0 - beta_first) * gradient
    second = beta_second * second + (1.0 - beta_second) * gradient * gradient
    scaled = (
        moment
        / (1.0 - beta_first**STEP)
        / (jnp.sqrt(second / (1.0 - beta_second**STEP)) + adam_eps)
    )
    return (moment, second, weight - step_rate * (scaled + decay_rate * weight))


def plain_device(
    tokens,
    cotangent,
    prefix,
    query_weight,
    keyval_weight,
    output_weight,
    gateup_weight,
    down_weight,
    norm_gains,
    query_first,
    keyval_first,
    output_first,
    gateup_first,
    down_first,
    gains_first,
    query_second,
    keyval_second,
    output_second,
    gateup_second,
    down_second,
    gains_second,
):
    rows_dev, width = tokens.shape
    length = rows_dev * lax.axis_size("tensor")
    query_full, keyval_full, output_full, gateup_full, down_full, gains_full = (
        lax.all_gather(query_weight.astype(jnp.bfloat16), "dp", axis=0, tiled=True),
        lax.all_gather(keyval_weight.astype(jnp.bfloat16), "dp", axis=0, tiled=True),
        lax.all_gather(output_weight.astype(jnp.bfloat16), "dp", axis=0, tiled=True),
        lax.all_gather(gateup_weight.astype(jnp.bfloat16), "dp", axis=0, tiled=True),
        lax.all_gather(down_weight.astype(jnp.bfloat16), "dp", axis=0, tiled=True),
        lax.all_gather(norm_gains.astype(jnp.bfloat16), "dp", axis=0, tiled=True),
    )
    head_dim = keyval_full.shape[1] // 2
    heads_dev = query_full.shape[1] // head_dim
    units = down_full.shape[1]
    gain_values = gains_full.astype(jnp.float32)
    gain_input = gain_values[0:width]
    gain_attn = gain_values[width : 2 * width]
    gain_pre = gain_values[2 * width : 3 * width]
    gain_ffn = gain_values[3 * width : 4 * width]
    gain_query = gain_values[4 * width : 4 * width + head_dim]
    gain_key = gain_values[4 * width + head_dim : 4 * width + 2 * head_dim]
    positions = jnp.arange(length).astype(jnp.float32)
    span_rows = min(512, length)
    count_blocks = length // span_rows
    starts = jnp.arange(0, length, span_rows, dtype=jnp.int32)
    columns = jnp.arange(length, dtype=jnp.int32)
    prefix_len = prefix[0]
    gateup_flat = gateup_full.reshape(width, 2 * units)

    def shape_query(raw_rows, gain_vec):
        return rotate(rms_scale(raw_rows, gain_vec), positions)

    def shape_key(raw_rows, gain_vec):
        return rotate(rms_scale(raw_rows[:, None, :], gain_vec), positions)[:, 0]

    token_rows = tokens.astype(jnp.float32)
    normed_local = rms_scale(token_rows, gain_input).astype(jnp.bfloat16)
    normed = lax.all_gather(normed_local, "tensor", axis=0, tiled=True)
    query_raw = mixed_dot(normed, query_full).reshape(length, heads_dev, head_dim)
    keyval_raw = mixed_dot(normed, keyval_full)
    query_rot = shape_query(query_raw, gain_query).astype(jnp.bfloat16)
    key_rot = shape_key(keyval_raw[:, :head_dim], gain_key).astype(jnp.bfloat16)
    value_low = keyval_raw[:, head_dim:].astype(jnp.bfloat16)

    def scores_of(row_start):
        row_ids = row_start + jnp.arange(span_rows, dtype=jnp.int32)
        q_blk = lax.dynamic_slice_in_dim(query_rot, row_start, span_rows, 0)
        raw_scores = (
            jnp.einsum("rhd,kd->hrk", q_blk, key_rot, preferred_element_type=jnp.float32)
            * query_scale
        )
        allowed = (columns[None, :] <= row_ids[:, None]) | (columns[None, :] < prefix_len)
        return (jnp.where(allowed[None], raw_scores, masked_fill), q_blk)

    def forward_block(row_start):
        scores, q_blk = scores_of(row_start)
        row_peak = jnp.max(scores, axis=-1, keepdims=True)
        shifted = jnp.exp(scores - row_peak)
        denom_sum = jnp.sum(shifted, axis=-1, keepdims=True)
        soft_probs = (shifted / denom_sum).astype(jnp.bfloat16)
        mixed_rows = jnp.einsum(
            "hrk,kd->rhd", soft_probs, value_low, preferred_element_type=jnp.float32
        )
        return (mixed_rows, (row_peak + jnp.log(denom_sum))[..., 0])

    attended_blocks, log_sums = lax.map(forward_block, starts)
    attended = attended_blocks.reshape(length, heads_dev * head_dim).astype(jnp.bfloat16)
    attn_part = jnp.einsum("rk,dk->rd", attended, output_full, preferred_element_type=jnp.float32)
    projected = lax.psum_scatter(
        attn_part.astype(jnp.bfloat16), "tensor", scatter_dimension=0, tiled=True
    ).astype(jnp.float32)
    hidden_state = token_rows + rms_scale(projected, gain_attn)
    normed_two = lax.all_gather(
        rms_scale(hidden_state, gain_pre).astype(jnp.bfloat16), "tensor", axis=0, tiled=True
    )
    gateup = mixed_dot(normed_two, gateup_flat)
    gate_part = gateup[:, :units]
    up_part = gateup[:, units:]
    activation = (jax.nn.gelu(gate_part, approximate=True) * up_part).astype(jnp.bfloat16)
    down_part = jnp.einsum("ru,du->rd", activation, down_full, preferred_element_type=jnp.float32)
    down_sum = lax.psum_scatter(
        down_part.astype(jnp.bfloat16), "tensor", scatter_dimension=0, tiled=True
    ).astype(jnp.float32)
    block_out = hidden_state + rms_scale(down_sum, gain_ffn)
    grad_out = cotangent.astype(jnp.float32)
    pull_ffn = jax.vjp(rms_scale, down_sum, gain_ffn)[1]
    grad_down, grad_gain_ffn = pull_ffn(grad_out)
    down_back = lax.all_gather(grad_down.astype(jnp.bfloat16), "tensor", axis=0, tiled=True)
    grad_activation = mixed_dot(down_back, down_full)
    grad_down_w = jnp.einsum("rd,ru->du", down_back, activation, preferred_element_type=jnp.float32)

    def geglu(gate_in, up_in):
        return jax.nn.gelu(gate_in, approximate=True) * up_in

    pull_act = jax.vjp(geglu, gate_part, up_part)[1]
    grad_gate, grad_up = pull_act(grad_activation)
    grad_gateup = jnp.concatenate([grad_gate, grad_up], axis=1).astype(jnp.bfloat16)
    grad_gateup_w = jnp.einsum(
        "rd,ru->du", normed_two, grad_gateup, preferred_element_type=jnp.float32
    ).reshape(width, 2, units)
    grad_normed_two = jnp.einsum(
        "ru,du->rd", grad_gateup, gateup_flat, preferred_element_type=jnp.float32
    )
    grad_pre_rows = lax.psum_scatter(
        grad_normed_two.astype(jnp.bfloat16), "tensor", scatter_dimension=0, tiled=True
    ).astype(jnp.float32)
    pull_pre = jax.vjp(rms_scale, hidden_state, gain_pre)[1]
    grad_hidden_norm, grad_gain_pre = pull_pre(grad_pre_rows)
    grad_hidden = grad_out + grad_hidden_norm
    pull_attn = jax.vjp(rms_scale, projected, gain_attn)[1]
    grad_proj, grad_gain_attn = pull_attn(grad_hidden)
    proj_back = lax.all_gather(grad_proj.astype(jnp.bfloat16), "tensor", axis=0, tiled=True)
    grad_output_w = jnp.einsum("rd,rk->dk", proj_back, attended, preferred_element_type=jnp.float32)
    grad_attended = (
        mixed_dot(proj_back, output_full)
        .astype(jnp.bfloat16)
        .reshape(count_blocks, span_rows, heads_dev, head_dim)
    )

    def backward_block(carry, batch_item):
        key_acc, value_acc = carry
        row_start, grad_att, lse_blk = batch_item
        scores, q_blk = scores_of(row_start)
        soft_full = jnp.exp(scores - lse_blk[..., None])
        grad_probs = jnp.einsum(
            "rhd,kd->hrk", grad_att, value_low, preferred_element_type=jnp.float32
        )
        delta_rows = jnp.sum(soft_full * grad_probs, axis=-1, keepdims=True)
        grad_scores = (soft_full * (grad_probs - delta_rows)).astype(jnp.bfloat16)
        grad_query = (
            jnp.einsum("hrk,kd->rhd", grad_scores, key_rot, preferred_element_type=jnp.float32)
            * query_scale
        )
        key_acc = (
            key_acc
            + jnp.einsum("hrk,rhd->kd", grad_scores, q_blk, preferred_element_type=jnp.float32)
            * query_scale
        )
        value_acc = value_acc + jnp.einsum(
            "hrk,rhd->kd",
            soft_full.astype(jnp.bfloat16),
            grad_att,
            preferred_element_type=jnp.float32,
        )
        return ((key_acc, value_acc), grad_query)

    zero_rows = jnp.zeros((length, head_dim), jnp.float32)
    (grad_key_rot, grad_value), grad_query_blocks = lax.scan(
        backward_block, (zero_rows, zero_rows), (starts, grad_attended, log_sums)
    )
    grad_query_rot = grad_query_blocks.reshape(length, heads_dev, head_dim)
    pull_query = jax.vjp(shape_query, query_raw, gain_query)[1]
    grad_query_raw, grad_gain_query = pull_query(grad_query_rot)
    pull_key = jax.vjp(shape_key, keyval_raw[:, :head_dim], gain_key)[1]
    grad_key_raw, grad_gain_key = pull_key(grad_key_rot)
    grad_query_low = grad_query_raw.reshape(length, heads_dev * head_dim).astype(jnp.bfloat16)
    grad_keyval = jnp.concatenate([grad_key_raw, grad_value], axis=1)
    grad_query_w = jnp.einsum(
        "rd,rk->dk", normed, grad_query_low, preferred_element_type=jnp.float32
    )
    grad_normed_query = jnp.einsum(
        "rk,dk->rd", grad_query_low, query_full, preferred_element_type=jnp.float32
    )
    grad_normed_part, grad_keyval_own = (
        lax.psum_scatter(
            grad_normed_query.astype(jnp.bfloat16), "tensor", scatter_dimension=0, tiled=True
        ).astype(jnp.float32),
        lax.psum_scatter(
            grad_keyval.astype(jnp.bfloat16), "tensor", scatter_dimension=0, tiled=True
        ).astype(jnp.float32),
    )
    grad_keyval_low = grad_keyval_own.astype(jnp.bfloat16)
    grad_keyval_w = jnp.einsum(
        "rd,rk->dk", normed_local, grad_keyval_low, preferred_element_type=jnp.float32
    )
    grad_normed = grad_normed_part + jnp.einsum(
        "rk,dk->rd", grad_keyval_low, keyval_full, preferred_element_type=jnp.float32
    )
    pull_input = jax.vjp(rms_scale, token_rows, gain_input)[1]
    grad_token_norm, grad_gain_input = pull_input(grad_normed)
    tokens_grad = (grad_hidden + grad_token_norm).astype(jnp.bfloat16)
    grad_gains = jnp.concatenate(
        [
            grad_gain_input,
            grad_gain_attn,
            grad_gain_pre,
            grad_gain_ffn,
            grad_gain_query,
            grad_gain_key,
        ]
    )
    keyval_total, gains_total = (
        lax.psum(grad_keyval_w.astype(jnp.bfloat16), "tensor").astype(jnp.float32),
        lax.psum(grad_gains.astype(jnp.bfloat16), "tensor").astype(jnp.float32),
    )
    query_sum, keyval_sum, output_sum, gateup_sum, down_grad_sum, gains_sum = (
        lax.psum_scatter(grad_query_w, "dp", scatter_dimension=0, tiled=True),
        lax.psum_scatter(keyval_total, "dp", scatter_dimension=0, tiled=True),
        lax.psum_scatter(grad_output_w, "dp", scatter_dimension=0, tiled=True),
        lax.psum_scatter(grad_gateup_w, "dp", scatter_dimension=0, tiled=True),
        lax.psum_scatter(grad_down_w, "dp", scatter_dimension=0, tiled=True),
        lax.psum_scatter(gains_total, "dp", scatter_dimension=0, tiled=True),
    )
    query_moment, query_square, query_master = adam_step(
        query_weight, query_sum, query_first, query_second, D ** (-0.5)
    )
    keyval_moment, keyval_square, keyval_master = adam_step(
        keyval_weight, keyval_sum, keyval_first, keyval_second, D ** (-0.5)
    )
    output_moment, output_square, output_master = adam_step(
        output_weight, output_sum, output_first, output_second, (HEADS * HEAD_DIM) ** (-0.5)
    )
    gateup_moment, gateup_square, gateup_master = adam_step(
        gateup_weight, gateup_sum, gateup_first, gateup_second, D ** (-0.5)
    )
    down_moment, down_square, down_master = adam_step(
        down_weight, down_grad_sum, down_first, down_second, FF ** (-0.5)
    )
    gains_moment, gains_square, gains_master = adam_step(
        norm_gains, gains_sum, gains_first, gains_second, 0.3
    )
    return (
        block_out.astype(jnp.bfloat16),
        tokens_grad,
        query_moment,
        query_square,
        query_master,
        keyval_moment,
        keyval_square,
        keyval_master,
        output_moment,
        output_square,
        output_master,
        gateup_moment,
        gateup_square,
        gateup_master,
        down_moment,
        down_square,
        down_master,
        gains_moment,
        gains_square,
        gains_master,
    )


def per_device(
    tokens,
    cotangent,
    prefix,
    query_weight,
    keyval_weight,
    output_weight,
    gateup_weight,
    down_weight,
    norm_gains,
    query_first,
    keyval_first,
    output_first,
    gateup_first,
    down_first,
    gains_first,
    query_second,
    keyval_second,
    output_second,
    gateup_second,
    down_second,
    gains_second,
):
    rows, width = tokens.shape
    lines = lax.axis_size("dp") // 2
    shard = query_weight.shape[0]
    head_dim = keyval_weight.shape[1] // 2
    units = down_weight.shape[1]
    fits = (
        lax.axis_size("tensor") == 4
        and lax.axis_size("dp") == 8
        and len(chunks_of(units)) == 4
        and query_weight.shape[1] == head_dim
        and shard % 16 == 0
        and norm_gains.shape[0] % 128 == 0
        and (3 * len(chunks_of(units)) + 2) // 2 * shard <= 4 * rows
    )
    if not fits:
        return plain_device(
            tokens,
            cotangent,
            prefix,
            query_weight,
            keyval_weight,
            output_weight,
            gateup_weight,
            down_weight,
            norm_gains,
            query_first,
            keyval_first,
            output_first,
            gateup_first,
            down_first,
            gains_first,
            query_second,
            keyval_second,
            output_second,
            gateup_second,
            down_second,
            gains_second,
        )
    length = 4 * rows
    sizes = (lines, rows, width, head_dim, units)
    gate_low = gateup_weight[:, 0].astype(low)
    up_low = gateup_weight[:, 1].astype(low)
    weights = (keyval_weight, query_weight, output_weight, gate_low, up_low, down_weight)
    angles = np.arange(length)[:, None] * (rope_base ** (-2.0 * np.arange(head_dim // 2) / head_dim))[None, :]
    cosine = jnp.asarray(np.cos(angles), full)
    sine = jnp.asarray(np.sin(angles), full)
    *saved, gvec, proj, hidden, grad_down, dgain_ffn, block_out = forward_call(
        sizes, prefix, tokens, cotangent, norm_gains[None], weights, cosine, sine
    )
    gate_sum, up_sum, down_grad_sum, small_sum, tokens_grad, keyval_sum, gains_sum = backward_call(
        sizes, (grad_down, cotangent, tokens, gvec, dgain_ffn, proj, hidden, cosine, sine), saved
    )
    quarter = head_dim // 2
    query_sum = small_sum[:, quarter : quarter + head_dim]
    output_sum = small_sum[:, quarter + head_dim :]
    keyval_sum = keyval_sum.astype(full)
    gains_sum = gains_sum[0]
    gateup_sum = jnp.stack([gate_sum[:, :units], up_sum[:, :units]], axis=1)
    down_grad_sum = down_grad_sum[:, :units]
    query_moment, query_square, query_master = adam_step(
        query_weight, query_sum, query_first, query_second, D ** (-0.5)
    )
    keyval_moment, keyval_square, keyval_master = adam_step(
        keyval_weight, keyval_sum, keyval_first, keyval_second, D ** (-0.5)
    )
    output_moment, output_square, output_master = adam_step(
        output_weight, output_sum, output_first, output_second, (HEADS * HEAD_DIM) ** (-0.5)
    )
    gateup_moment, gateup_square, gateup_master = adam_step(
        gateup_weight, gateup_sum, gateup_first, gateup_second, D ** (-0.5)
    )
    down_moment, down_square, down_master = adam_step(
        down_weight, down_grad_sum, down_first, down_second, FF ** (-0.5)
    )
    gains_moment, gains_square, gains_master = adam_step(
        norm_gains, gains_sum, gains_first, gains_second, 0.3
    )
    return (
        block_out,
        tokens_grad,
        query_moment,
        query_square,
        query_master,
        keyval_moment,
        keyval_square,
        keyval_master,
        output_moment,
        output_square,
        output_master,
        gateup_moment,
        gateup_square,
        gateup_master,
        down_moment,
        down_square,
        down_master,
        gains_moment,
        gains_square,
        gains_master,
    )


def solution(mesh):
    placed = (
        P(("dp", "tensor"), None),
        P(("dp", "tensor"), None),
        P("dp"),
        P("dp", "tensor"),
        P("dp", None),
        P("dp", "tensor"),
        P("dp", None, "tensor"),
        P("dp", "tensor"),
        P("dp"),
        P("dp", "tensor"),
        P("dp", None),
        P("dp", "tensor"),
        P("dp", None, "tensor"),
        P("dp", "tensor"),
        P("dp"),
        P("dp", "tensor"),
        P("dp", None),
        P("dp", "tensor"),
        P("dp", None, "tensor"),
        P("dp", "tensor"),
        P("dp"),
    )
    return jax.shard_map(
        per_device,
        mesh=mesh,
        in_specs=placed,
        out_specs=(
            P(("dp", "tensor"), None),
            P(("dp", "tensor"), None),
            P("dp", "tensor"),
            P("dp", "tensor"),
            P("dp", "tensor"),
            P("dp", None),
            P("dp", None),
            P("dp", None),
            P("dp", "tensor"),
            P("dp", "tensor"),
            P("dp", "tensor"),
            P("dp", None, "tensor"),
            P("dp", None, "tensor"),
            P("dp", None, "tensor"),
            P("dp", "tensor"),
            P("dp", "tensor"),
            P("dp", "tensor"),
            P("dp"),
            P("dp"),
            P("dp"),
        ),
        check_vma=False,
    )
```

```python
import functools

import jax
import jax.numpy as jnp
import numpy as np
from jax import lax
from jax.experimental import pallas as pl
from jax.experimental.pallas import tpu as pltpu
from jax.sharding import PartitionSpec as P

D = 1152
FF = 6912
HEADS = 4
HEAD_DIM = 256
STEP = 10


eps_norm = 1e-06
query_scale = 0.0625
rope_base = 1000000.0
beta_first = 0.9
beta_second = 0.95
adam_eps = 1e-08
decay_rate = 0.01
masked_fill = -1e30
MESH = pl.DeviceIdType.MESH
low = jnp.bfloat16
full = jnp.float32
CHUNK = 512


def dot_nn(left, right):
    return lax.dot_general(left, right, (((1,), (0,)), ((), ())), preferred_element_type=full)


def dot_nt(left, right):
    return lax.dot_general(left, right, (((1,), (1,)), ((), ())), preferred_element_type=full)


def dot_tn(left, right):
    return lax.dot_general(left, right, (((0,), (0,)), ((), ())), preferred_element_type=full)


def chunks_of(units):
    out = []
    first = 0
    while first < units:
        width = min(CHUNK, units - first)
        out.append((first, width, -(-width // 128) * 128))
        first += width
    return out


def small_columns(head_dim):
    return 2 * head_dim, 3 * head_dim, 4 * head_dim


def packed_columns(units, head_dim):
    at = small_columns(head_dim)[2]
    places = []
    for first, width, padded in chunks_of(units):
        places.append((at, at + padded, at + 2 * padded))
        at += 3 * padded
    return places, at


class Place:
    def __init__(self):
        self.dp = lax.axis_index("dp")
        self.tensor = lax.axis_index("tensor")
        self.z = self.dp // 2
        self.x = self.dp % 2
        self.y = self.tensor // 2
        self.core = self.tensor % 2
        self.homes = (self.z, self.z + 1 - 2 * (self.z % 2), (self.z + 2) % 4, 3 - self.z)
        self.end = ((self.z + 1) // 2 + 1) % 2
        self.middle = self.end == 0
        self.mate = (self.dp, self.y * 2 + (1 - self.core))
        self.across = (self.dp, (1 - self.y) * 2 + self.core)
        self.side = (self.z * 2 + (1 - self.x), self.tensor)
        self.inner = ((1 + self.z % 2) * 2 + self.x, self.tensor)

    def line(self, step):
        return (self.homes[step] * 2 + self.x, self.tensor)

    def peers(self):
        return [self.mate, self.across, self.side] + [self.line(s) for s in (1, 2, 3)]


def meet(place):
    barrier = pltpu.get_barrier_semaphore()
    peers = place.peers()
    for peer in peers:
        pl.semaphore_signal(barrier, inc=1, device_id=peer, device_id_type=MESH)
    pl.semaphore_wait(barrier, len(peers))


def remote(source, target, send_sem, recv_sem, device):
    return pltpu.make_async_remote_copy(
        src_ref=source,
        dst_ref=target,
        send_sem=send_sem,
        recv_sem=recv_sem,
        device_id=device,
        device_id_type=MESH,
    )


class LineGather:
    def __init__(self, place, region, wide, send, recv, relay_send, side_send, side_recv):
        self.place, self.region, self.wide = place, region, wide
        self.send, self.recv, self.relay_send = send, recv, relay_send
        self.side_send, self.side_recv = side_send, side_recv

    def columns(self, group):
        return (0, 1) if self.wide[group] else (0,)

    def origin(self, column, step):
        place = self.place
        return place.homes[step] * 2 + (place.x if column == 0 else 1 - place.x)

    def along(self, group, column, step):
        block = self.region(group, self.origin(column, 0))
        return remote(
            block, block, self.send.at[group, column, step], self.recv.at[group, column, step], self.place.line(step)
        )

    def arrive(self, group, column, step):
        block = self.region(group, self.origin(column, step))
        remote(
            block, block, self.send.at[group, column, step], self.recv.at[group, column, step], self.place.line(step)
        ).wait_recv()

    def relay(self, group, column):
        block = self.region(group, self.origin(column, 2))
        return remote(
            block, block, self.relay_send.at[group, column], self.recv.at[group, column, 3], self.place.line(1)
        )

    def sideways(self, group, step):
        block = self.region(group, self.origin(0, step))
        return remote(
            block, block, self.side_send.at[group, step], self.side_recv.at[group, step], self.place.side
        )

    def arrive_side(self, group, step):
        block = self.region(group, self.origin(1, step))
        remote(
            block, block, self.side_send.at[group, step], self.side_recv.at[group, step], self.place.side
        ).wait_recv()

    def start_line(self, group, column):
        self.along(group, column, 2).start()
        self.along(group, column, 1).start()

        @pl.when(self.place.middle)
        def _():
            self.along(group, column, 3).start()

    def start(self, group):
        self.sideways(group, 0).start()
        self.start_line(group, 0)

    def widen(self, group):
        self.arrive_side(group, 0)
        self.start_line(group, 1)

    def pass_on(self, group):
        for column in self.columns(group):
            self.arrive(group, column, 2)

            @pl.when(self.place.middle)
            def _():
                self.relay(group, column).start()

            if not self.wide[group]:
                self.sideways(group, 2).start()

    def collect(self, group):
        for column in self.columns(group):
            for step in (1, 3):
                self.arrive(group, column, step)
                if not self.wide[group]:
                    self.sideways(group, step).start()

    def ready(self, group):
        if not self.wide[group]:
            for step in (0, 2, 1, 3):
                self.arrive_side(group, step)

    def finish(self):
        for group in range(len(self.wide)):
            for column in self.columns(group):
                self.along(group, column, 1).wait_send()
                self.along(group, column, 2).wait_send()

                @pl.when(self.place.middle)
                def _():
                    self.along(group, column, 3).wait_send()
                    self.relay(group, column).wait_send()

            for step in (0,) if self.wide[group] else (0, 1, 2, 3):
                self.sideways(group, step).wait_send()


def row_slabs(buffer, rows):
    return lambda y, core: buffer.at[pl.ds((y * 2 + core) * rows, rows)]


def column_slabs(buffer, wide):
    return lambda y, core: buffer.at[:, pl.ds(pl.multiple_of((y * 2 + core) * wide, wide), wide)]


class RowGather:
    def __init__(self, place, source, slab, send, recv):
        self.place, self.source, self.slab = place, source, slab
        self.send, self.recv = send, recv

    def copy(self, index):
        place = self.place
        slab = self.slab(1 - place.y if index == 2 else place.y, place.core)
        source = slab if index == 2 else self.source
        device = place.across if index == 1 else place.mate
        return remote(source, slab, self.send.at[index], self.recv.at[index], device)

    def arrival(self, index, y, core):
        slab = self.slab(y, core)
        remote(slab, slab, self.send.at[index], self.recv.at[index], self.place.mate).wait_recv()

    def start(self):
        self.copy(1).start()
        self.copy(0).start()

    def wait_mate(self):
        self.arrival(0, self.place.y, 1 - self.place.core)

    def wait_across(self):
        self.arrival(1, 1 - self.place.y, self.place.core)
        self.copy(2).start()

    def wait_corner(self):
        self.arrival(2, 1 - self.place.y, 1 - self.place.core)

    def finish(self):
        for index in range(3):
            self.copy(index).wait_send()


class RowScatter:
    def __init__(self, place, part, rows, first, second, mixed, send, recv):
        self.place, self.part, self.rows = place, part, rows
        self.first, self.second, self.mixed = first, second, mixed
        self.send, self.recv = send, recv

    def slab(self, y, core):
        return self.part.at[pl.ds((y * 2 + core) * self.rows, self.rows)]

    def copy(self, index):
        place = self.place
        if index == 2:
            return remote(self.mixed, self.second, self.send.at[2], self.recv.at[2], place.across)
        source = self.slab(1 - place.y if index == 0 else place.y, 1 - place.core)
        return remote(source, self.first.at[index], self.send.at[index], self.recv.at[index], place.mate)

    def order(self):
        place = self.place
        return (
            (1 - place.y) * 2 + (1 - place.core),
            (1 - place.y) * 2 + place.core,
            place.y * 2 + (1 - place.core),
            place.y * 2 + place.core,
        )

    def after(self, step):
        if step == 0:
            self.copy(0).start()
        if step == 1:
            self.copy(0).wait_recv()
            mixed = self.slab(1 - self.place.y, self.place.core)[...].astype(full) + self.first[0].astype(full)
            self.mixed[...] = mixed.astype(low)
            self.copy(2).start()
        if step == 2:
            self.copy(1).start()

    def total(self):
        self.copy(1).wait_recv()
        here = self.slab(self.place.y, self.place.core)[...].astype(full) + self.first[1].astype(full)
        self.copy(2).wait_recv()
        return here + self.second[...].astype(full)

    def finish(self):
        for index in range(3):
            self.copy(index).wait_send()


def inverse_rms(rows):
    return lax.rsqrt(jnp.mean(rows * rows, axis=-1, keepdims=True) + eps_norm)


def rotate_rows(rows, cosine, sine):
    half = rows.shape[-1] // 2
    front, back = rows[:, :half], rows[:, half:]
    return jnp.concatenate([front * cosine - back * sine, back * cosine + front * sine], axis=-1)


def rotate_back(rows, cosine, sine):
    half = rows.shape[-1] // 2
    front, back = rows[:, :half], rows[:, half:]
    return jnp.concatenate([front * cosine + back * sine, back * cosine - front * sine], axis=-1)


def gelu_parts(gate):
    scale = 0.7978845608028654
    square = gate * gate
    bent = jnp.tanh(scale * gate * (1.0 + 0.044715 * square))
    return square, bent


def forward_kernel(
    sizes,
    prefix_ref,
    tokens_ref,
    cot_ref,
    gains_ref,
    keyval_ref,
    query_ref,
    output_ref,
    gateup_ref,
    down_ref,
    cos_ref,
    sin_ref,
    wall_out,
    normed_out,
    normed_two_out,
    query_out,
    key_out,
    key_rot_out,
    value_out,
    attended_out,
    probs_out,
    gate_out,
    up_out,
    act_out,
    gvec,
    proj_keep,
    hidden_keep,
    grad_down,
    dgain_ffn,
    block_out,
    wall,
    normed,
    normed_two,
    query_raw,
    key_raw,
    attended,
    probs,
    gate_keep,
    up_keep,
    act,
    tok_full,
    gains_full,
    key_rot,
    value_low,
    part_one,
    first_one,
    second_one,
    mixed_one,
    first_two,
    second_two,
    mixed_two,
    down_acc,
    line_send,
    line_recv,
    relay_send,
    side_send,
    side_recv,
    row_send,
    row_recv,
    keep_sem,
):
    lines, rows, width, head_dim, units = sizes
    place = Place()
    length = 4 * rows
    shard = keyval_ref.shape[0]
    places, columns = packed_columns(units, head_dim)
    chunks = chunks_of(units)
    last = len(chunks) - 1
    kv_end, query_end, output_end = small_columns(head_dim)
    split = places[last - 1][2]
    quarter = kv_end // 4
    own_quarter = pl.ds(pl.multiple_of(place.tensor * quarter, quarter), quarter)
    spans = [(0, kv_end), (kv_end, output_end)]
    spans += [(places[c][0], places[c][0] + 3 * chunks[c][2]) for c in range(last - 1)]
    spans += [(places[last - 1][0], split), (split, columns)]
    tail = len(spans)

    def region(group, origin):
        if group == 0:
            return gains_full.at[pl.ds(origin * 8, 8)]
        if group == 1:
            return wall.at[pl.ds(origin * shard, shard), own_quarter]
        lo, hi = spans[group - 1]
        return wall.at[pl.ds(origin * shard, shard), lo:hi]

    wide_groups = [False] * tail + [True]
    gather = LineGather(place, region, wide_groups, line_send, line_recv, relay_send, side_send, side_recv)
    tokens_all = RowGather(place, tokens_ref, row_slabs(tok_full, rows), row_send.at[0], row_recv.at[0])
    own_rows = pl.ds(place.tensor * rows, rows)
    kept = []

    def keep(source, target):
        copy = pltpu.make_async_copy(source, target, keep_sem.at[len(kept)])
        copy.start()
        kept.append(copy)

    def keep_span(group):
        lo, hi = spans[group - 1]
        keep(wall.at[:, lo:hi], wall_out.at[:, lo:hi])

    own_gains = gains_ref[...].astype(low).astype(full).reshape(1, -1)
    gains_full[pl.ds(place.dp * 8, 8)] = jnp.broadcast_to(own_gains, (8, own_gains.shape[1]))
    own = pl.ds(place.dp * shard, shard)
    wall[own, own_quarter] = keyval_ref[:, own_quarter].astype(low)
    wall[own, kv_end:query_end] = query_ref[...].astype(low)
    wall[own, query_end:output_end] = output_ref[...].astype(low)
    meet(place)
    tokens_all.start()
    for group in range(3):
        gather.start(group)
    for (first, wide, padded), at in zip(chunks, places):
        for kind, lo in enumerate(at):
            units_here = slice(first, first + wide)
            piece = down_ref[:, units_here] if kind == 2 else gateup_ref[:, kind, units_here]
            wall[own, lo : lo + wide] = piece.astype(low)
            if padded > wide:
                wall[own, lo + wide : lo + padded] = jnp.zeros((shard, padded - wide), low)
    gather.start(3)
    gather.start(4)
    tok_full[own_rows] = tokens_ref[...]
    tokens_all.wait_mate()
    tokens_all.wait_across()
    gather.pass_on(0)
    gather.pass_on(1)
    gather.collect(0)
    gather.collect(1)
    tokens_all.wait_corner()
    gather.pass_on(2)
    gather.ready(1)
    quarters = column_slabs(wall, quarter)
    keyval_all = RowGather(
        place, quarters(place.y, place.core), quarters, row_send.at[4], row_recv.at[4]
    )
    keyval_all.start()
    gather.collect(2)
    for group in range(5, tail + 1):
        gather.start(group)
    gather.ready(0)
    step = gains_ref.shape[0]
    for origin in range(2 * lines):
        gvec[:, origin * step : (origin + 1) * step] = gains_full[origin * 8 : origin * 8 + 8]
    gain_in = 1.0 + gvec[0:1, 0:width]
    gain_attn = 1.0 + gvec[0:1, width : 2 * width]
    gain_pre = 1.0 + gvec[0:1, 2 * width : 3 * width]
    gain_ffn = 1.0 + gvec[0:1, 3 * width : 4 * width]
    gain_query = 1.0 + gvec[0:1, 4 * width : 4 * width + head_dim]
    gain_key = 1.0 + gvec[0:1, 4 * width + head_dim : 4 * width + 2 * head_dim]

    def norm_slab(index, carry):
        at = pl.ds(pl.multiple_of(index * rows, rows), rows)
        x = tok_full[at].astype(full)
        normed[at] = (x * inverse_rms(x) * gain_in).astype(low)
        return carry

    lax.fori_loop(0, 4, norm_slab, 0)
    keep(normed, normed_out)
    keyval_all.wait_mate()
    keyval_all.wait_across()
    gather.ready(2)
    keyval_all.wait_corner()

    def project_slab(index, carry):
        at = pl.ds(pl.multiple_of(index * rows, rows), rows)
        n1 = normed[at]
        query_raw[at] = dot_nn(n1, wall[:, kv_end:query_end])
        kv = dot_nn(n1, wall[:, 0:kv_end])
        k = kv[:, :head_dim]
        key_raw[at] = k
        key_rot[at] = rotate_rows(k * inverse_rms(k) * gain_key, cos_ref[at], sin_ref[at]).astype(low)
        value_low[at] = kv[:, head_dim:].astype(low)
        return carry

    lax.fori_loop(0, 4, project_slab, 0)
    keep(query_raw, query_out)
    keep(key_raw, key_out)
    keep(key_rot, key_rot_out)
    keep(value_low, value_out)
    keep_span(1)
    keep_span(2)

    out_scatter = RowScatter(place, part_one, rows, first_one, second_one, mixed_one, row_send.at[1], row_recv.at[1])

    def attend_slab(index):
        at = pl.ds(pl.multiple_of(index * rows, rows), rows)
        q = query_raw[at]
        qr = rotate_rows(q * inverse_rms(q) * gain_query, cos_ref[at], sin_ref[at]).astype(low)
        scores = dot_nt(qr, key_rot[...]) * query_scale
        row_ids = lax.broadcasted_iota(jnp.int32, (rows, length), 0) + index * rows
        columns = lax.broadcasted_iota(jnp.int32, (rows, length), 1)
        allowed = (columns <= row_ids) | (columns < prefix_ref[0])
        scores = jnp.where(allowed, scores, masked_fill)
        shifted = jnp.exp(scores - jnp.max(scores, axis=-1, keepdims=True))
        soft = (shifted / jnp.sum(shifted, axis=-1, keepdims=True)).astype(low)
        probs[at] = soft
        mixed = dot_nn(soft, value_low[...]).astype(low)
        attended[at] = mixed
        part_one[at] = dot_nt(mixed, wall[:, query_end:output_end]).astype(low)

    for step, index in enumerate(out_scatter.order()):
        attend_slab(index)
        out_scatter.after(step)
    keep(probs, probs_out)
    keep(attended, attended_out)
    gather.pass_on(3)
    gather.collect(3)
    gather.widen(tail)
    projected = out_scatter.total()
    out_scatter.finish()
    proj_keep[...] = projected
    hidden = tokens_ref[...].astype(full) + projected * inverse_rms(projected) * gain_attn
    hidden_keep[...] = hidden
    normed_two[own_rows] = (hidden * inverse_rms(hidden) * gain_pre).astype(low)
    two_all = RowGather(place, normed_two.at[own_rows], row_slabs(normed_two, rows), row_send.at[2], row_recv.at[2])
    two_all.start()
    two_all.wait_mate()
    two_all.wait_across()
    two_all.wait_corner()
    keep(normed_two, normed_two_out)

    down_scatter = RowScatter(place, part_one, rows, first_two, second_two, mixed_two, row_send.at[3], row_recv.at[3])
    block = 2 * rows

    def feed(c):
        first, wide, padded = chunks[c]
        at_gate, at_up, _ = places[c]

        def feed_rows(index, carry):
            at = pl.ds(pl.multiple_of(index * block, block), block)
            n2 = normed_two[at]
            gate = dot_nn(n2, wall[:, at_gate : at_gate + wide])
            up = dot_nn(n2, wall[:, at_up : at_up + wide])
            gate_keep[at, first : first + wide] = gate.astype(low)
            up_keep[at, first : first + wide] = up.astype(low)
            _, bent = gelu_parts(gate)
            act[at, first : first + wide] = (0.5 * gate * (1.0 + bent) * up).astype(low)
            return carry

        lax.fori_loop(0, 2, feed_rows, 0)
        span = slice(first, first + padded)
        keep(gate_keep.at[:, span], gate_out.at[:, span])
        keep(up_keep.at[:, span], up_out.at[:, span])
        keep(act.at[:, span], act_out.at[:, span])

    def lower(c):
        first, wide, _ = chunks[c]
        at_down = places[c][2]

        def lower_rows(index, carry):
            at = pl.ds(pl.multiple_of(index * block, block), block)
            more = dot_nt(act[at, first : first + wide], wall[:, at_down : at_down + wide])
            down_acc[at] = more if c == 0 else down_acc[at] + more
            return carry

        lax.fori_loop(0, 2, lower_rows, 0)

    for c in range(last - 1):
        gather.pass_on(c + 4)
        gather.collect(c + 4)
        gather.ready(c + 3)
        feed(c)
        lower(c)
        keep_span(c + 3)
    gather.pass_on(tail)
    gather.ready(tail - 1)
    feed(last - 1)
    keep_span(tail - 1)
    gather.collect(tail)
    feed(last)
    lower(last - 1)
    keep_span(tail)
    first, wide, _ = chunks[last]
    at_down = places[last][2]
    for step, index in enumerate(down_scatter.order()):
        at = pl.ds(pl.multiple_of(index * rows, rows), rows)
        part_one[at] = (
            down_acc[at] + dot_nt(act[at, first : first + wide], wall[:, at_down : at_down + wide])
        ).astype(low)
        down_scatter.after(step)
    f = down_scatter.total()
    inv = inverse_rms(f)
    block_out[...] = (hidden_keep[...] + f * inv * gain_ffn).astype(low)
    cot = cot_ref[...].astype(full)
    scaled = cot * gain_ffn
    grad_down[...] = (inv * (scaled - f * (inv * inv) * jnp.mean(f * scaled, axis=-1, keepdims=True))).astype(low)
    dgain_ffn[...] = jnp.broadcast_to(jnp.sum(cot * f * inv, axis=0, keepdims=True), dgain_ffn.shape)
    gather.finish()
    tokens_all.finish()
    keyval_all.finish()
    two_all.finish()
    down_scatter.finish()
    for copy in kept:
        copy.wait()


def forward_call(sizes, prefix, tokens, cotangent, gains, weights, cosine, sine):
    lines, rows, width, head_dim, units = sizes
    length = 4 * rows
    shard = weights[0].shape[0]
    columns = packed_columns(units, head_dim)[1]
    chunks = chunks_of(units)
    padded = sum(c[2] for c in chunks)
    groups = 4 + len(chunks)
    vm = pl.BlockSpec(memory_space=pltpu.VMEM)
    hbm = pl.BlockSpec(memory_space=pl.ANY)
    large = [
        ((2 * lines * shard, columns), low),
        ((length, width), low),
        ((length, width), low),
        ((length, head_dim), full),
        ((length, head_dim), full),
        ((length, head_dim), low),
        ((length, head_dim), low),
        ((length, head_dim), low),
        ((length, length), low),
        ((length, padded), low),
        ((length, padded), low),
        ((length, padded), low),
    ]
    small = [
        ((8, gains.shape[0] * 2 * lines), full),
        ((rows, width), full),
        ((rows, width), full),
        ((rows, width), low),
        ((8, width), full),
        ((rows, width), low),
    ]
    inside = [large[i] for i in (0, 1, 2, 3, 4, 7, 8, 9, 10, 11)]
    scatter_set = [
        pltpu.VMEM((2, rows, width), low),
        pltpu.VMEM((rows, width), low),
        pltpu.VMEM((rows, width), low),
    ]
    return pl.pallas_call(
        functools.partial(forward_kernel, sizes),
        out_shape=[jax.ShapeDtypeStruct(*item) for item in large + small],
        in_specs=[pl.BlockSpec(memory_space=pltpu.SMEM)] + [vm] * 10,
        out_specs=[hbm] * len(large) + [vm] * len(small),
        scratch_shapes=[pltpu.VMEM(*item) for item in inside]
        + [
            pltpu.VMEM((length, width), low),
            pltpu.VMEM((2 * lines * 8, gains.shape[0]), full),
            pltpu.VMEM((length, head_dim), low),
            pltpu.VMEM((length, head_dim), low),
            pltpu.VMEM((length, width), low),
        ]
        + scatter_set
        + scatter_set
        + [
            pltpu.VMEM((length, width), full),
            pltpu.SemaphoreType.DMA((groups, 2, lines)),
            pltpu.SemaphoreType.DMA((groups, 2, lines)),
            pltpu.SemaphoreType.DMA((groups, 2)),
            pltpu.SemaphoreType.DMA((groups, lines)),
            pltpu.SemaphoreType.DMA((groups, lines)),
            pltpu.SemaphoreType.DMA((5, 3)),
            pltpu.SemaphoreType.DMA((5, 3)),
            pltpu.SemaphoreType.DMA((12 + 4 * len(chunks),)),
        ],
        compiler_params=pltpu.CompilerParams(
            collective_id=0, has_side_effects=True, vmem_limit_bytes=63 * 1024 * 1024
        ),
        name="forward",
    )(prefix, tokens, cotangent, gains, *weights, cosine, sine)


class LineScatter:
    def __init__(self, place, block, side_block, line_block, wide, side_send, side_recv, line_send, line_recv, kind):
        self.place, self.block, self.side_block, self.line_block = place, block, side_block, line_block
        self.wide, self.kind = wide, kind
        self.side_send, self.side_recv, self.line_send, self.line_recv = side_send, side_recv, line_send, line_recv

    def columns(self, group):
        return (0, 1) if self.wide[group] else (0,)

    def own(self, group, column, step):
        place = self.place
        return self.block(group, place.homes[step] * 2 + (place.x if column == 0 else 1 - place.x))

    def sideways(self, group, step):
        home = 0 if self.wide[group] else self.place.homes[step]
        return remote(
            self.own(group, 1, step),
            self.side_block(group, home),
            self.side_send.at[group, step],
            self.side_recv.at[group, step],
            self.place.side,
        )

    def along(self, group, column, step):
        slot = step - 1 if step < 3 else 2 + self.place.end
        return remote(
            self.own(group, column, step),
            self.line_block(group, column, slot),
            self.line_send.at[group, column, step],
            self.line_recv.at[group, column, slot],
            self.place.line(step) if step < 3 else self.place.inner,
        )

    def arrive(self, group, column, slot):
        here = self.line_block(group, column, slot)
        remote(
            here, here, self.line_send.at[group, column, 1], self.line_recv.at[group, column, slot], self.place.line(1)
        ).wait_recv()
        return here[...].astype(full)

    def start(self, group):
        if not self.wide[group]:
            for step in (3, 1, 2, 0):
                self.sideways(group, step).start()
            return
        for column in (0, 1):
            self.along(group, column, 3).start()
            self.along(group, column, 1).start()

            @pl.when(self.place.end == 1)
            def _():
                self.along(group, column, 2).start()

    def with_side(self, group, step):
        self.sideways(group, step).wait_recv()
        return self.own(group, 0, step)[...].astype(full) + self.side_block(group, self.place.homes[step])[...].astype(
            full
        )

    def pump(self, group, *steps):
        place = self.place
        if self.wide[group]:
            for column in (0, 1):

                @pl.when(place.middle)
                def _():
                    block = self.own(group, column, 2)
                    block[...] = (block[...].astype(full) + self.arrive(group, column, 3)).astype(self.kind)
                    self.along(group, column, 2).start()

            return
        for step in steps or (3, 1, 2):
            block = self.own(group, 0, step)
            both = self.with_side(group, step)
            if step != 2:
                block[...] = both.astype(self.kind)
            else:

                @pl.when(place.middle)
                def _():
                    block[...] = (both + self.arrive(group, 0, 3)).astype(self.kind)

                @pl.when(place.end == 1)
                def _():
                    block[...] = both.astype(self.kind)

            self.along(group, 0, step).start()

    def hand_over(self, group):
        block = self.own(group, 1, 0)
        both = block[...].astype(full) + self.arrive(group, 1, 0) + self.arrive(group, 1, 1)

        @pl.when(self.place.middle)
        def _():
            block[...] = (both + self.arrive(group, 1, 2)).astype(self.kind)

        @pl.when(self.place.end == 1)
        def _():
            block[...] = both.astype(self.kind)

        self.sideways(group, 0).start()

    def settle(self, group):
        self.sideways(group, 0).wait_recv()
        self.arrive(group, 0, 0)
        self.arrive(group, 0, 1)

        @pl.when(self.place.middle)
        def _():
            self.arrive(group, 0, 2)

    def total(self, group, lo, hi, held):
        parts = [
            self.own(group, 0, 0),
            self.side_block(group, 0 if self.wide[group] else self.place.z),
            self.line_block(group, 0, 0),
            self.line_block(group, 0, 1),
        ]
        first, *others = [part[:, lo:hi].astype(full) for part in parts]
        for other in others:
            first = first + other
        held[...] = first

        @pl.when(self.place.middle)
        def _():
            held[...] = first + self.line_block(group, 0, 2)[:, lo:hi].astype(full)

    def finish(self):
        for group in range(len(self.wide)):
            for step in (0,) if self.wide[group] else (0, 1, 2, 3):
                self.sideways(group, step).wait_send()
            for column in self.columns(group):
                for step in (1, 2, 3):
                    self.along(group, column, step).wait_send()


def norm_back(rows, inv, gain, grad):
    scaled = grad * gain
    back = inv * (scaled - rows * (inv * inv) * jnp.mean(rows * scaled, axis=-1, keepdims=True))
    return back, jnp.sum(grad * rows * inv, axis=0, keepdims=True)


def backward_kernel(
    sizes,
    grad_down_ref,
    cot_ref,
    tokens_ref,
    gvec,
    dgain_ffn,
    proj_ref,
    hidden_ref,
    cos_ref,
    sin_ref,
    wall_in,
    normed_in,
    normed_two_in,
    query_in,
    key_in,
    key_rot_in,
    value_in,
    attended_in,
    probs_in,
    gate_in,
    up_in,
    act_in,
    gate_grad,
    up_grad,
    down_grad,
    small_grad,
    tokens_grad,
    keyval_grad,
    gains_grad,
    wall,
    side_buf,
    side_wide,
    line_buf,
    line_wide,
    big,
    normed_two,
    row_buf,
    acc,
    first_buf,
    second_buf,
    mixed_buf,
    key_rot,
    value_low,
    dquery,
    dkeyval,
    dhidden,
    dproj,
    kv_first,
    kv_second,
    kv_mixed,
    kv_own,
    dgains,
    gain_part,
    gain_first,
    gain_second,
    gain_side,
    gain_line,
    row_send,
    row_recv,
    side_send,
    side_recv,
    line_send,
    line_recv,
    gain_side_send,
    gain_side_recv,
    gain_line_send,
    gain_line_recv,
    last_send,
    last_recv,
    load_sem,
    store_sem,
):
    lines, rows, width, head_dim, units = sizes
    place = Place()
    length = 4 * rows
    shard = wall.shape[0] // (2 * lines)
    kv_end, query_end, output_end = small_columns(head_dim)
    quarter = head_dim // 2
    places, _ = packed_columns(units, head_dim)
    chunks = chunks_of(units)
    last = len(chunks) - 1
    order = [0, last] + list(range(1, last))
    base_column = kv_end - quarter
    spans = []
    for c in range(last):
        spans += [(places[c][2], places[c][2] + chunks[c][2]), (places[c][0], places[c][2])]
    group_last, group_small = len(spans), len(spans) + 1
    spans += [(places[last][0], places[last][0] + 3 * chunks[last][2]), (base_column, output_end)]
    loads = {}

    def load(name, source, target):
        copy = pltpu.make_async_copy(source, target, load_sem.at[len(loads)])
        copy.start()
        loads[name] = copy

    def load_chunk(c):
        first, _, padded = chunks[c]
        lo, hi = places[c][0], places[c][0] + 3 * padded
        base = (order.index(c) % 2) * 3 * CHUNK
        load(("wall", c), wall_in.at[:, lo:hi], wall.at[:, lo:hi])
        for k, source in enumerate((gate_in, up_in, act_in)):
            at = base + k * CHUNK
            load((k, c), source.at[:, first : first + padded], big.at[:, at : at + padded])

    load("two", normed_two_in, normed_two)
    load_chunk(order[0])
    load("kv", wall_in.at[:, 0:kv_end], wall.at[:, 0:kv_end])
    load("qo", wall_in.at[:, kv_end:output_end], wall.at[:, kv_end:output_end])
    load("key_rot", key_rot_in, key_rot)
    load("value", value_in, value_low)
    gain_in = 1.0 + gvec[0:1, 0:width]
    gain_attn = 1.0 + gvec[0:1, width : 2 * width]
    gain_pre = 1.0 + gvec[0:1, 2 * width : 3 * width]
    gain_query = 1.0 + gvec[0:1, 4 * width : 4 * width + head_dim]
    gain_key = 1.0 + gvec[0:1, 4 * width + head_dim : 4 * width + 2 * head_dim]
    own_rows = pl.ds(place.tensor * rows, rows)
    row_buf[own_rows] = grad_down_ref[...]
    dgains[...] = jnp.zeros_like(dgains)
    dgains[0:1, 3 * width : 4 * width] = dgain_ffn[0:1]
    meet(place)
    down_all = RowGather(place, grad_down_ref, row_slabs(row_buf, rows), row_send.at[0], row_recv.at[0])
    down_all.start()
    load_chunk(order[1])
    down_all.wait_mate()
    down_all.wait_across()
    down_all.wait_corner()
    loads["two"].wait()

    def block(group, origin):
        lo, hi = spans[group]
        return wall.at[pl.ds(origin * shard, shard), lo:hi]

    def side_block(group, home):
        if wide_groups[group]:
            return side_wide
        lo, hi = spans[group]
        return side_buf.at[pl.ds(home * shard, shard), lo - base_column : hi - base_column]

    def line_block(group, column, slot):
        lo, hi = spans[group]
        if wide_groups[group]:
            return line_wide.at[pl.ds((column * 4 + slot) * shard, shard)]
        return line_buf.at[pl.ds(slot * shard, shard), lo - base_column : hi - base_column]

    wide_groups = [group == group_last for group in range(len(spans))]
    scatter = LineScatter(
        place, block, side_block, line_block, wide_groups, side_send, side_recv, line_send, line_recv, low
    )
    part = big.at[:, 0:width]
    pre_scatter = RowScatter(place, part, rows, first_buf, second_buf, mixed_buf, row_send.at[1], row_recv.at[1])
    half = 2 * rows
    third = width // 3

    def weight_gradient(lo, wide, left, right):
        for m in range(0, width, third):
            wall[m : m + third, lo : lo + wide] = dot_tn(left[:, m : m + third], right).astype(low)

    for position, c in enumerate(order):
        first, wide, padded = chunks[c]
        at_gate, at_up, at_down = places[c]
        base = (position % 2) * 3 * CHUNK
        loads["wall", c].wait()
        for k in range(3):
            loads[k, c].wait()
        if 1 <= position < last:
            load_chunk(order[position + 1])
        of_gate = slice(base, base + wide)
        of_up = slice(base + CHUNK, base + CHUNK + wide)
        of_act = slice(base + 2 * CHUNK, base + 2 * CHUNK + wide)

        def unit_rows(index, carry):
            at = pl.ds(pl.multiple_of(index * half, half), half)
            dz = dot_nn(row_buf[at], wall[:, at_down : at_down + wide])
            gate = big[at, of_gate].astype(full)
            up = big[at, of_up].astype(full)
            square, bent = gelu_parts(gate)
            middle = 0.5 * (1.0 + bent)
            slope = middle + 0.5 * gate * (1.0 - bent * bent) * (0.7978845608028654 * (1.0 + 0.134145 * square))
            big[at, of_gate] = (dz * up * slope).astype(low)
            big[at, of_up] = (dz * gate * middle).astype(low)
            return carry

        lax.fori_loop(0, 2, unit_rows, 0)
        weight_gradient(at_down, wide, row_buf, big[:, of_act])
        if c < last:
            scatter.start(2 * c)

        def back_rows(at):
            more = dot_nt(big[at, of_gate], wall[:, at_gate : at_gate + wide])
            more = more + dot_nt(big[at, of_up], wall[:, at_up : at_up + wide])
            return more if position == 0 else acc[at] + more

        if position < last:

            def collect_rows(index, carry):
                at = pl.ds(pl.multiple_of(index * half, half), half)
                acc[at] = back_rows(at)
                return carry

            lax.fori_loop(0, 2, collect_rows, 0)
        else:
            down_all.finish()
            for step, index in enumerate(pre_scatter.order()):
                at = pl.ds(pl.multiple_of(index * rows, rows), rows)
                part[at] = back_rows(at).astype(low)
                pre_scatter.after(step)
        weight_gradient(at_gate, wide, normed_two, big[:, of_gate])
        weight_gradient(at_up, wide, normed_two, big[:, of_up])
        if c < last:
            scatter.start(2 * c + 1)
        else:
            scatter.start(group_last)
            scatter.pump(0)
        if position == 2:
            scatter.pump(group_last)

    at_normed = width
    at_att = at_normed + width
    load("normed", normed_in, big.at[:, at_normed : at_normed + width])
    load("attended", attended_in, big.at[:, at_att : at_att + head_dim])
    load("query", query_in, acc.at[:, 2 * head_dim : 3 * head_dim])
    load("key", key_in, acc.at[:, 3 * head_dim : 4 * head_dim])

    scatter.pump(1)
    dn2 = pre_scatter.total()
    hidden = hidden_ref[...]
    back, grad = norm_back(hidden, inverse_rms(hidden), gain_pre, dn2)
    dgains[0:1, 2 * width : 3 * width] = grad
    dh = cot_ref[...].astype(full) + back
    dhidden[...] = dh
    proj = proj_ref[...]
    back, grad = norm_back(proj, inverse_rms(proj), gain_attn, dh)
    dgains[0:1, width : 2 * width] = grad
    dproj[...] = back.astype(low)
    row_buf[own_rows] = dproj[...]
    proj_all = RowGather(place, dproj, row_slabs(row_buf, rows), row_send.at[2], row_recv.at[2])
    proj_all.start()
    pre_scatter.finish()
    load("probs", probs_in, big.at[:, 0:length])
    acc[:, 0 : 2 * head_dim] = jnp.zeros((length, 2 * head_dim), full)
    proj_all.wait_mate()
    scatter.pump(2)
    scatter.hand_over(group_last)
    scatter.pump(3, 3)
    proj_all.wait_across()
    proj_all.wait_corner()
    for name in ("kv", "qo", "key_rot", "value", "normed", "attended", "query", "key", "probs"):
        loads[name].wait()

    def attend_back(index, carry):
        at = pl.ds(pl.multiple_of(index * rows, rows), rows)
        da = dot_nn(row_buf[at], wall[:, query_end:output_end]).astype(low)
        soft = big[at, 0:length]
        wide_soft = soft.astype(full)
        dp = dot_nt(da, value_low[...])
        ds = (wide_soft * (dp - jnp.sum(wide_soft * dp, axis=-1, keepdims=True))).astype(low)
        q = acc[at, 2 * head_dim : 3 * head_dim]
        inv = inverse_rms(q)
        cosine, sine = cos_ref[at], sin_ref[at]
        qr = rotate_rows(q * inv * gain_query, cosine, sine).astype(low)
        dqr = dot_nn(ds, key_rot[...]) * query_scale
        acc[:, 0:head_dim] += dot_tn(ds, qr)
        acc[:, head_dim : 2 * head_dim] += dot_tn(soft, da)
        dq, grad = norm_back(q, inv, gain_query, rotate_back(dqr, cosine, sine))
        dquery[at] = dq.astype(low)
        dgains[0:1, 4 * width : 4 * width + head_dim] += grad
        return carry

    lax.fori_loop(0, 2, attend_back, 0)
    scatter.pump(3, 1)
    lax.fori_loop(2, 3, attend_back, 0)
    scatter.pump(3, 2)
    lax.fori_loop(3, 4, attend_back, 0)

    def key_back(index, carry):
        at = pl.ds(pl.multiple_of(index * rows, rows), rows)
        k = acc[at, 3 * head_dim : 4 * head_dim]
        dkr = rotate_back(acc[at, 0:head_dim] * query_scale, cos_ref[at], sin_ref[at])
        dk, grad = norm_back(k, inverse_rms(k), gain_key, dkr)
        dkeyval[at, 0:head_dim] = dk.astype(low)
        dkeyval[at, head_dim : 2 * head_dim] = acc[at, head_dim : 2 * head_dim].astype(low)
        dgains[0:1, 4 * width + head_dim : 4 * width + 2 * head_dim] += grad
        return carry

    lax.fori_loop(0, 4, key_back, 0)
    in_scatter = RowScatter(place, part, rows, first_buf, second_buf, mixed_buf, row_send.at[3], row_recv.at[3])
    for step, index in enumerate(in_scatter.order()):
        at = pl.ds(pl.multiple_of(index * rows, rows), rows)
        more = dot_nt(dquery[at], wall[:, kv_end:query_end]) + dot_nt(dkeyval[at], wall[:, 0:kv_end])
        part[at] = more.astype(low)
        in_scatter.after(step)

    normed = big.at[:, at_normed : at_normed + width]
    for m in range(0, width, third):
        wall[m : m + third, 0:kv_end] = dot_tn(normed[:, m : m + third], dkeyval[...]).astype(low)

    def kv_block(y, core):
        return wall.at[:, pl.ds(pl.multiple_of((y * 2 + core) * quarter, quarter), quarter)]

    def kv_copy(index):
        send, recv = last_send.at[index], last_recv.at[index]
        if index == 2:
            return remote(kv_mixed, kv_second, send, recv, place.across)
        return remote(
            kv_block(1 - place.y if index == 0 else place.y, 1 - place.core), kv_first.at[index], send, recv, place.mate
        )

    kv_copy(0).start()
    kv_copy(1).start()
    weight_gradient(kv_end, head_dim, normed, dquery[...])
    weight_gradient(query_end, head_dim, row_buf, big[:, at_att : at_att + head_dim])
    kv_copy(0).wait_recv()
    kv_mixed[...] = (kv_block(1 - place.y, place.core)[...].astype(full) + kv_first[0].astype(full)).astype(low)
    kv_copy(2).start()
    scatter.pump(4)
    scatter.pump(5, 3)

    dn1 = in_scatter.total()
    x = tokens_ref[...].astype(full)
    back, grad = norm_back(x, inverse_rms(x), gain_in, dn1)
    dgains[0:1, 0:width] = grad
    tokens_grad[...] = (dhidden[...] + back).astype(low)
    step = gains_grad.shape[1]
    for origin in range(2 * lines):
        gain_part[origin * 8 : origin * 8 + 8] = dgains[:, origin * step : (origin + 1) * step]

    def gain_copy(index):
        source, target, device = (
            (gain_part, gain_first, place.mate) if index == 0 else (gain_part, gain_second, place.across)
        )
        return remote(source, target, last_send.at[3 + index], last_recv.at[3 + index], device)

    gain_copy(0).start()
    kv_copy(1).wait_recv()
    kv_copy(2).wait_recv()
    kv_copy(0).wait_send()
    kv_copy(1).wait_send()
    wall[:, base_column:kv_end] = (
        kv_block(place.y, place.core)[...].astype(full) + kv_first[1].astype(full) + kv_second[...].astype(full)
    ).astype(low)
    scatter.start(group_small)
    gain_copy(0).wait_recv()
    gain_copy(0).wait_send()
    gain_part[...] = gain_part[...] + gain_first[...]
    gain_copy(1).start()
    gain_copy(1).wait_recv()
    gain_copy(1).wait_send()
    gain_part[...] = gain_part[...] + gain_second[...]

    gain_scatter = LineScatter(
        place,
        lambda group, origin: gain_part.at[pl.ds(origin * 8, 8)],
        lambda group, home: gain_side.at[pl.ds(home * 8, 8)],
        lambda group, column, slot: gain_line.at[pl.ds(slot * 8, 8)],
        [False],
        gain_side_send,
        gain_side_recv,
        gain_line_send,
        gain_line_recv,
        full,
    )
    gain_scatter.start(0)

    stores = []

    def store(group, kinds, c):
        first, _, padded = chunks[c] if kinds else (0, 0, 0)
        wide = padded if kinds else output_end - base_column
        scatter.settle(group)
        for k, target in enumerate(kinds or (small_grad,)):
            slot = len(stores)
            down, right = slot // 2 * shard, slot % 2 * CHUNK
            held = acc.at[down : down + shard, right : right + wide]
            scatter.total(group, k * wide, (k + 1) * wide, held)
            copy = pltpu.make_async_copy(held, target.at[:, first : first + wide], store_sem.at[slot])
            copy.start()
            stores.append(copy)
            if not kinds:
                kv_own[...] = held[:, 0:quarter].astype(low)

    scatter.pump(5, 1)
    for c in range(last - 1):
        store(2 * c, (down_grad,), c)
        store(2 * c + 1, (gate_grad, up_grad), c)
    scatter.pump(5, 2)
    scatter.pump(group_small)
    gain_scatter.pump(0)
    store(group_last, (gate_grad, up_grad, down_grad), last)
    store(2 * last - 2, (down_grad,), last - 1)
    store(2 * last - 1, (gate_grad, up_grad), last - 1)
    store(group_small, (), 0)
    gain_scatter.settle(0)
    gain_scatter.total(0, 0, gains_grad.shape[1], gains_grad)

    def own_block(y, core):
        return keyval_grad.at[:, pl.ds(pl.multiple_of((y * 2 + core) * quarter, quarter), quarter)]

    own_block(place.y, place.core)[...] = kv_own[...]
    targets = (place.mate, place.across, (place.dp, (1 - place.y) * 2 + (1 - place.core)))
    sends = [
        remote(kv_own, own_block(place.y, place.core), last_send.at[5 + i], last_recv.at[5 + i], target)
        for i, target in enumerate(targets)
    ]
    for copy in sends:
        copy.start()
    for i, (y, core) in enumerate(
        ((place.y, 1 - place.core), (1 - place.y, place.core), (1 - place.y, 1 - place.core))
    ):
        remote(kv_own, own_block(y, core), last_send.at[5 + i], last_recv.at[5 + i], targets[i]).wait_recv()
    for copy in sends:
        copy.wait_send()
    kv_copy(2).wait_send()
    scatter.finish()
    gain_scatter.finish()
    proj_all.finish()
    in_scatter.finish()
    for copy in stores:
        copy.wait()


def backward_call(sizes, vmem_args, hbm_args):
    lines, rows, width, head_dim, units = sizes
    length = 4 * rows
    columns = hbm_args[0].shape[1]
    shard = hbm_args[0].shape[0] // (2 * lines)
    gains = vmem_args[3].shape[1]
    quarter = head_dim // 2
    base_column = 2 * head_dim - quarter
    chunks = chunks_of(units)
    groups = 2 * len(chunks)
    vm = pl.BlockSpec(memory_space=pltpu.VMEM)
    hbm = pl.BlockSpec(memory_space=pl.ANY)
    padded = sum(c[2] for c in chunks)
    large = [((shard, padded), full)] * 3 + [((shard, 5 * quarter), full)]
    outs = [
        ((rows, width), low),
        ((shard, 2 * head_dim), low),
        ((8, gains // (2 * lines)), full),
    ]
    scratch = [
        (hbm_args[0].shape, low),
        ((lines * shard, columns - base_column - 3 * chunks[-1][2]), low),
        ((shard, 3 * chunks[-1][2]), low),
        ((lines * shard, columns - base_column - 3 * chunks[-1][2]), low),
        ((2 * lines * shard, 3 * chunks[-1][2]), low),
        ((length, 6 * CHUNK), low),
        ((length, width), low),
        ((length, width), low),
        ((length, width), full),
        ((2, rows, width), low),
        ((rows, width), low),
        ((rows, width), low),
        ((length, head_dim), low),
        ((length, head_dim), low),
        ((length, head_dim), low),
        ((length, 2 * head_dim), low),
        ((rows, width), full),
        ((rows, width), low),
        ((2, width, quarter), low),
        ((width, quarter), low),
        ((width, quarter), low),
        ((shard, quarter), low),
        ((8, gains), full),
        ((2 * lines * 8, gains // (2 * lines)), full),
        ((2 * lines * 8, gains // (2 * lines)), full),
        ((2 * lines * 8, gains // (2 * lines)), full),
        ((lines * 8, gains // (2 * lines)), full),
        ((lines * 8, gains // (2 * lines)), full),
    ]
    sems = [(4, 3), (4, 3), (groups, 4), (groups, 4), (groups, 2, 4), (groups, 2, 4)]
    sems += [(1, 4), (1, 4), (1, 1, 4), (1, 1, 4), (8,), (8,)]
    sems += [(10 + 4 * len(chunks),), (1 + 3 * len(chunks),)]
    return pl.pallas_call(
        functools.partial(backward_kernel, sizes),
        out_shape=[jax.ShapeDtypeStruct(*item) for item in large + outs],
        in_specs=[vm] * len(vmem_args) + [hbm] * len(hbm_args),
        out_specs=[hbm] * len(large) + [vm] * len(outs),
        scratch_shapes=[pltpu.VMEM(*item) for item in scratch] + [pltpu.SemaphoreType.DMA(dims) for dims in sems],
        compiler_params=pltpu.CompilerParams(
            collective_id=1, has_side_effects=True, vmem_limit_bytes=63 * 1024 * 1024
        ),
        name="backward",
    )(*vmem_args, *hbm_args)


def adam_values(weight, gradient, first, second, step_rate):
    moment = beta_first * first + (1.0 - beta_first) * gradient
    square = beta_second * second + (1.0 - beta_second) * gradient * gradient
    scaled = moment / (1.0 - beta_first**STEP) / (jnp.sqrt(square / (1.0 - beta_second**STEP)) + adam_eps)
    return moment, square, weight - step_rate * (scaled + decay_rate * weight)


def update_kernel(units, head_dim, *refs):
    block_in, tokens_in, gate_grad, up_grad, down_grad, small_grad, keyval_grad, gains_grad = refs[:8]
    old, new = refs[8:26], refs[26:]
    new[0][...] = block_in[...]
    new[1][...] = tokens_in[...]
    quarter = head_dim // 2
    wide = D ** (-0.5)
    flat = (
        (0, small_grad[:, quarter : quarter + head_dim], wide),
        (1, keyval_grad[...].astype(full), wide),
        (2, small_grad[:, quarter + head_dim : quarter + 2 * head_dim], (HEADS * HEAD_DIM) ** (-0.5)),
        (4, down_grad[:, 0:units], FF ** (-0.5)),
    )
    for index, gradient, rate in flat:
        weight, first, second = (ref[...] for ref in old[3 * index : 3 * index + 3])
        values = adam_values(weight, gradient, first, second, rate)
        for target, value in zip(new[2 + 3 * index : 5 + 3 * index], values):
            target[...] = value
    for kind, grad in enumerate((gate_grad, up_grad)):
        weight, first, second = (ref[:, kind, :] for ref in old[9:12])
        values = adam_values(weight, grad[:, 0:units], first, second, wide)
        for target, value in zip(new[11:14], values):
            target[:, kind, :] = value

    @pl.when(pl.program_id(0) == 0)
    def _():
        weight, first, second = (ref[...] for ref in old[15:18])
        values = adam_values(weight, gains_grad[0], first, second, 0.3)
        for target, value in zip(new[17:20], values):
            target[...] = value


def update_call(units, head_dim, passed, grads, old, steps):
    def passing(array):
        return pl.BlockSpec((array.shape[0] // (steps - 1), array.shape[1]), lambda i: (jnp.minimum(i, steps - 2), 0))

    def spec(array, fixed=False):
        rows = array.shape[0] if fixed else array.shape[0] // steps
        rest = array.shape[1:]
        if fixed:
            return pl.BlockSpec(array.shape, lambda i: (0,) * array.ndim)
        return pl.BlockSpec((rows, *rest), lambda i: (i,) + (0,) * (array.ndim - 1))

    ins = [passing(a) for a in passed] + [spec(a) for a in grads[:-1]] + [spec(grads[-1], True)]
    olds = [spec(a, i >= 15) for i, a in enumerate(old)]
    outs = [(a, passing(a)) for a in passed]
    for index in range(6):
        for kind in (1, 2, 0):
            array = old[3 * index + kind]
            outs.append((array, spec(array, index == 5)))
    return pl.pallas_call(
        functools.partial(update_kernel, units, head_dim),
        grid=(steps,),
        out_shape=[jax.ShapeDtypeStruct(a.shape, a.dtype) for a, _ in outs],
        in_specs=ins + olds,
        out_specs=[s for _, s in outs],
        compiler_params=pltpu.CompilerParams(vmem_limit_bytes=60 * 1024 * 1024),
        name="update",
    )(*passed, *grads, *old)


def mixed_dot(left, right):
    return jnp.dot(left, right, preferred_element_type=jnp.float32)


def rms_scale(vector, gain_vec):
    return (
        vector
        * lax.rsqrt(jnp.mean(vector * vector, axis=-1, keepdims=True) + eps_norm)
        * (1.0 + gain_vec)
    )


def rotate(vector, positions):
    half_dim = vector.shape[-1] // 2
    inv_freq = rope_base ** (-2.0 * jnp.arange(half_dim).astype(jnp.float32) / vector.shape[-1])
    angles = positions[:, None] * inv_freq[None, :]
    cosine = jnp.cos(angles)[:, None, :]
    sine_v = jnp.sin(angles)[:, None, :]
    front_half = vector[..., :half_dim]
    back_half = vector[..., half_dim:]
    return jnp.concatenate(
        [front_half * cosine - back_half * sine_v, back_half * cosine + front_half * sine_v],
        axis=-1,
    )


def adam_step(weight, gradient, moment, second, step_rate):
    moment = beta_first * moment + (1.0 - beta_first) * gradient
    second = beta_second * second + (1.0 - beta_second) * gradient * gradient
    scaled = (
        moment
        / (1.0 - beta_first**STEP)
        / (jnp.sqrt(second / (1.0 - beta_second**STEP)) + adam_eps)
    )
    return (moment, second, weight - step_rate * (scaled + decay_rate * weight))


def plain_device(
    tokens,
    cotangent,
    prefix,
    query_weight,
    keyval_weight,
    output_weight,
    gateup_weight,
    down_weight,
    norm_gains,
    query_first,
    keyval_first,
    output_first,
    gateup_first,
    down_first,
    gains_first,
    query_second,
    keyval_second,
    output_second,
    gateup_second,
    down_second,
    gains_second,
):
    rows_dev, width = tokens.shape
    length = rows_dev * lax.axis_size("tensor")
    query_full, keyval_full, output_full, gateup_full, down_full, gains_full = (
        lax.all_gather(query_weight.astype(jnp.bfloat16), "dp", axis=0, tiled=True),
        lax.all_gather(keyval_weight.astype(jnp.bfloat16), "dp", axis=0, tiled=True),
        lax.all_gather(output_weight.astype(jnp.bfloat16), "dp", axis=0, tiled=True),
        lax.all_gather(gateup_weight.astype(jnp.bfloat16), "dp", axis=0, tiled=True),
        lax.all_gather(down_weight.astype(jnp.bfloat16), "dp", axis=0, tiled=True),
        lax.all_gather(norm_gains.astype(jnp.bfloat16), "dp", axis=0, tiled=True),
    )
    head_dim = keyval_full.shape[1] // 2
    heads_dev = query_full.shape[1] // head_dim
    units = down_full.shape[1]
    gain_values = gains_full.astype(jnp.float32)
    gain_input = gain_values[0:width]
    gain_attn = gain_values[width : 2 * width]
    gain_pre = gain_values[2 * width : 3 * width]
    gain_ffn = gain_values[3 * width : 4 * width]
    gain_query = gain_values[4 * width : 4 * width + head_dim]
    gain_key = gain_values[4 * width + head_dim : 4 * width + 2 * head_dim]
    positions = jnp.arange(length).astype(jnp.float32)
    span_rows = min(512, length)
    count_blocks = length // span_rows
    starts = jnp.arange(0, length, span_rows, dtype=jnp.int32)
    columns = jnp.arange(length, dtype=jnp.int32)
    prefix_len = prefix[0]
    gateup_flat = gateup_full.reshape(width, 2 * units)

    def shape_query(raw_rows, gain_vec):
        return rotate(rms_scale(raw_rows, gain_vec), positions)

    def shape_key(raw_rows, gain_vec):
        return rotate(rms_scale(raw_rows[:, None, :], gain_vec), positions)[:, 0]

    token_rows = tokens.astype(jnp.float32)
    normed_local = rms_scale(token_rows, gain_input).astype(jnp.bfloat16)
    normed = lax.all_gather(normed_local, "tensor", axis=0, tiled=True)
    query_raw = mixed_dot(normed, query_full).reshape(length, heads_dev, head_dim)
    keyval_raw = mixed_dot(normed, keyval_full)
    query_rot = shape_query(query_raw, gain_query).astype(jnp.bfloat16)
    key_rot = shape_key(keyval_raw[:, :head_dim], gain_key).astype(jnp.bfloat16)
    value_low = keyval_raw[:, head_dim:].astype(jnp.bfloat16)

    def scores_of(row_start):
        row_ids = row_start + jnp.arange(span_rows, dtype=jnp.int32)
        q_blk = lax.dynamic_slice_in_dim(query_rot, row_start, span_rows, 0)
        raw_scores = (
            jnp.einsum("rhd,kd->hrk", q_blk, key_rot, preferred_element_type=jnp.float32)
            * query_scale
        )
        allowed = (columns[None, :] <= row_ids[:, None]) | (columns[None, :] < prefix_len)
        return (jnp.where(allowed[None], raw_scores, masked_fill), q_blk)

    def forward_block(row_start):
        scores, q_blk = scores_of(row_start)
        row_peak = jnp.max(scores, axis=-1, keepdims=True)
        shifted = jnp.exp(scores - row_peak)
        denom_sum = jnp.sum(shifted, axis=-1, keepdims=True)
        soft_probs = (shifted / denom_sum).astype(jnp.bfloat16)
        mixed_rows = jnp.einsum(
            "hrk,kd->rhd", soft_probs, value_low, preferred_element_type=jnp.float32
        )
        return (mixed_rows, (row_peak + jnp.log(denom_sum))[..., 0])

    attended_blocks, log_sums = lax.map(forward_block, starts)
    attended = attended_blocks.reshape(length, heads_dev * head_dim).astype(jnp.bfloat16)
    attn_part = jnp.einsum("rk,dk->rd", attended, output_full, preferred_element_type=jnp.float32)
    projected = lax.psum_scatter(
        attn_part.astype(jnp.bfloat16), "tensor", scatter_dimension=0, tiled=True
    ).astype(jnp.float32)
    hidden_state = token_rows + rms_scale(projected, gain_attn)
    normed_two = lax.all_gather(
        rms_scale(hidden_state, gain_pre).astype(jnp.bfloat16), "tensor", axis=0, tiled=True
    )
    gateup = mixed_dot(normed_two, gateup_flat)
    gate_part = gateup[:, :units]
    up_part = gateup[:, units:]
    activation = (jax.nn.gelu(gate_part, approximate=True) * up_part).astype(jnp.bfloat16)
    down_part = jnp.einsum("ru,du->rd", activation, down_full, preferred_element_type=jnp.float32)
    down_sum = lax.psum_scatter(
        down_part.astype(jnp.bfloat16), "tensor", scatter_dimension=0, tiled=True
    ).astype(jnp.float32)
    block_out = hidden_state + rms_scale(down_sum, gain_ffn)
    grad_out = cotangent.astype(jnp.float32)
    pull_ffn = jax.vjp(rms_scale, down_sum, gain_ffn)[1]
    grad_down, grad_gain_ffn = pull_ffn(grad_out)
    down_back = lax.all_gather(grad_down.astype(jnp.bfloat16), "tensor", axis=0, tiled=True)
    grad_activation = mixed_dot(down_back, down_full)
    grad_down_w = jnp.einsum("rd,ru->du", down_back, activation, preferred_element_type=jnp.float32)

    def geglu(gate_in, up_in):
        return jax.nn.gelu(gate_in, approximate=True) * up_in

    pull_act = jax.vjp(geglu, gate_part, up_part)[1]
    grad_gate, grad_up = pull_act(grad_activation)
    grad_gateup = jnp.concatenate([grad_gate, grad_up], axis=1).astype(jnp.bfloat16)
    grad_gateup_w = jnp.einsum(
        "rd,ru->du", normed_two, grad_gateup, preferred_element_type=jnp.float32
    ).reshape(width, 2, units)
    grad_normed_two = jnp.einsum(
        "ru,du->rd", grad_gateup, gateup_flat, preferred_element_type=jnp.float32
    )
    grad_pre_rows = lax.psum_scatter(
        grad_normed_two.astype(jnp.bfloat16), "tensor", scatter_dimension=0, tiled=True
    ).astype(jnp.float32)
    pull_pre = jax.vjp(rms_scale, hidden_state, gain_pre)[1]
    grad_hidden_norm, grad_gain_pre = pull_pre(grad_pre_rows)
    grad_hidden = grad_out + grad_hidden_norm
    pull_attn = jax.vjp(rms_scale, projected, gain_attn)[1]
    grad_proj, grad_gain_attn = pull_attn(grad_hidden)
    proj_back = lax.all_gather(grad_proj.astype(jnp.bfloat16), "tensor", axis=0, tiled=True)
    grad_output_w = jnp.einsum("rd,rk->dk", proj_back, attended, preferred_element_type=jnp.float32)
    grad_attended = (
        mixed_dot(proj_back, output_full)
        .astype(jnp.bfloat16)
        .reshape(count_blocks, span_rows, heads_dev, head_dim)
    )

    def backward_block(carry, batch_item):
        key_acc, value_acc = carry
        row_start, grad_att, lse_blk = batch_item
        scores, q_blk = scores_of(row_start)
        soft_full = jnp.exp(scores - lse_blk[..., None])
        grad_probs = jnp.einsum(
            "rhd,kd->hrk", grad_att, value_low, preferred_element_type=jnp.float32
        )
        delta_rows = jnp.sum(soft_full * grad_probs, axis=-1, keepdims=True)
        grad_scores = (soft_full * (grad_probs - delta_rows)).astype(jnp.bfloat16)
        grad_query = (
            jnp.einsum("hrk,kd->rhd", grad_scores, key_rot, preferred_element_type=jnp.float32)
            * query_scale
        )
        key_acc = (
            key_acc
            + jnp.einsum("hrk,rhd->kd", grad_scores, q_blk, preferred_element_type=jnp.float32)
            * query_scale
        )
        value_acc = value_acc + jnp.einsum(
            "hrk,rhd->kd",
            soft_full.astype(jnp.bfloat16),
            grad_att,
            preferred_element_type=jnp.float32,
        )
        return ((key_acc, value_acc), grad_query)

    zero_rows = jnp.zeros((length, head_dim), jnp.float32)
    (grad_key_rot, grad_value), grad_query_blocks = lax.scan(
        backward_block, (zero_rows, zero_rows), (starts, grad_attended, log_sums)
    )
    grad_query_rot = grad_query_blocks.reshape(length, heads_dev, head_dim)
    pull_query = jax.vjp(shape_query, query_raw, gain_query)[1]
    grad_query_raw, grad_gain_query = pull_query(grad_query_rot)
    pull_key = jax.vjp(shape_key, keyval_raw[:, :head_dim], gain_key)[1]
    grad_key_raw, grad_gain_key = pull_key(grad_key_rot)
    grad_query_low = grad_query_raw.reshape(length, heads_dev * head_dim).astype(jnp.bfloat16)
    grad_keyval = jnp.concatenate([grad_key_raw, grad_value], axis=1)
    grad_query_w = jnp.einsum(
        "rd,rk->dk", normed, grad_query_low, preferred_element_type=jnp.float32
    )
    grad_normed_query = jnp.einsum(
        "rk,dk->rd", grad_query_low, query_full, preferred_element_type=jnp.float32
    )
    grad_normed_part, grad_keyval_own = (
        lax.psum_scatter(
            grad_normed_query.astype(jnp.bfloat16), "tensor", scatter_dimension=0, tiled=True
        ).astype(jnp.float32),
        lax.psum_scatter(
            grad_keyval.astype(jnp.bfloat16), "tensor", scatter_dimension=0, tiled=True
        ).astype(jnp.float32),
    )
    grad_keyval_low = grad_keyval_own.astype(jnp.bfloat16)
    grad_keyval_w = jnp.einsum(
        "rd,rk->dk", normed_local, grad_keyval_low, preferred_element_type=jnp.float32
    )
    grad_normed = grad_normed_part + jnp.einsum(
        "rk,dk->rd", grad_keyval_low, keyval_full, preferred_element_type=jnp.float32
    )
    pull_input = jax.vjp(rms_scale, token_rows, gain_input)[1]
    grad_token_norm, grad_gain_input = pull_input(grad_normed)
    tokens_grad = (grad_hidden + grad_token_norm).astype(jnp.bfloat16)
    grad_gains = jnp.concatenate(
        [
            grad_gain_input,
            grad_gain_attn,
            grad_gain_pre,
            grad_gain_ffn,
            grad_gain_query,
            grad_gain_key,
        ]
    )
    keyval_total, gains_total = (
        lax.psum(grad_keyval_w.astype(jnp.bfloat16), "tensor").astype(jnp.float32),
        lax.psum(grad_gains.astype(jnp.bfloat16), "tensor").astype(jnp.float32),
    )
    query_sum, keyval_sum, output_sum, gateup_sum, down_grad_sum, gains_sum = (
        lax.psum_scatter(grad_query_w, "dp", scatter_dimension=0, tiled=True),
        lax.psum_scatter(keyval_total, "dp", scatter_dimension=0, tiled=True),
        lax.psum_scatter(grad_output_w, "dp", scatter_dimension=0, tiled=True),
        lax.psum_scatter(grad_gateup_w, "dp", scatter_dimension=0, tiled=True),
        lax.psum_scatter(grad_down_w, "dp", scatter_dimension=0, tiled=True),
        lax.psum_scatter(gains_total, "dp", scatter_dimension=0, tiled=True),
    )
    query_moment, query_square, query_master = adam_step(
        query_weight, query_sum, query_first, query_second, D ** (-0.5)
    )
    keyval_moment, keyval_square, keyval_master = adam_step(
        keyval_weight, keyval_sum, keyval_first, keyval_second, D ** (-0.5)
    )
    output_moment, output_square, output_master = adam_step(
        output_weight, output_sum, output_first, output_second, (HEADS * HEAD_DIM) ** (-0.5)
    )
    gateup_moment, gateup_square, gateup_master = adam_step(
        gateup_weight, gateup_sum, gateup_first, gateup_second, D ** (-0.5)
    )
    down_moment, down_square, down_master = adam_step(
        down_weight, down_grad_sum, down_first, down_second, FF ** (-0.5)
    )
    gains_moment, gains_square, gains_master = adam_step(
        norm_gains, gains_sum, gains_first, gains_second, 0.3
    )
    return (
        block_out.astype(jnp.bfloat16),
        tokens_grad,
        query_moment,
        query_square,
        query_master,
        keyval_moment,
        keyval_square,
        keyval_master,
        output_moment,
        output_square,
        output_master,
        gateup_moment,
        gateup_square,
        gateup_master,
        down_moment,
        down_square,
        down_master,
        gains_moment,
        gains_square,
        gains_master,
    )


def per_device(
    tokens,
    cotangent,
    prefix,
    query_weight,
    keyval_weight,
    output_weight,
    gateup_weight,
    down_weight,
    norm_gains,
    query_first,
    keyval_first,
    output_first,
    gateup_first,
    down_first,
    gains_first,
    query_second,
    keyval_second,
    output_second,
    gateup_second,
    down_second,
    gains_second,
):
    rows, width = tokens.shape
    lines = lax.axis_size("dp") // 2
    shard = query_weight.shape[0]
    head_dim = keyval_weight.shape[1] // 2
    units = down_weight.shape[1]
    fits = (
        lax.axis_size("tensor") == 4
        and lax.axis_size("dp") == 8
        and len(chunks_of(units)) == 4
        and query_weight.shape[1] == head_dim
        and shard % 16 == 0
        and norm_gains.shape[0] % 128 == 0
        and (3 * len(chunks_of(units)) + 2) // 2 * shard <= 4 * rows
    )
    if not fits:
        return plain_device(
            tokens,
            cotangent,
            prefix,
            query_weight,
            keyval_weight,
            output_weight,
            gateup_weight,
            down_weight,
            norm_gains,
            query_first,
            keyval_first,
            output_first,
            gateup_first,
            down_first,
            gains_first,
            query_second,
            keyval_second,
            output_second,
            gateup_second,
            down_second,
            gains_second,
        )
    length = 4 * rows
    sizes = (lines, rows, width, head_dim, units)
    weights = (keyval_weight, query_weight, output_weight, gateup_weight, down_weight)
    angles = np.arange(length)[:, None] * (rope_base ** (-2.0 * np.arange(head_dim // 2) / head_dim))[None, :]
    cosine = jnp.asarray(np.cos(angles), full)
    sine = jnp.asarray(np.sin(angles), full)
    *saved, gvec, proj, hidden, grad_down, dgain_ffn, block_out = forward_call(
        sizes, prefix, tokens, cotangent, norm_gains, weights, cosine, sine
    )
    *grads, tokens_grad, keyval_sum, gains_sum = backward_call(
        sizes, (grad_down, cotangent, tokens, gvec, dgain_ffn, proj, hidden, cosine, sine), saved
    )
    old = (
        query_weight,
        query_first,
        query_second,
        keyval_weight,
        keyval_first,
        keyval_second,
        output_weight,
        output_first,
        output_second,
        gateup_weight,
        gateup_first,
        gateup_second,
        down_weight,
        down_first,
        down_second,
        norm_gains,
        gains_first,
        gains_second,
    )
    return tuple(update_call(units, head_dim, (block_out, tokens_grad), (*grads, keyval_sum, gains_sum), old, 3))


def solution(mesh):
    placed = (
        P(("dp", "tensor"), None),
        P(("dp", "tensor"), None),
        P("dp"),
        P("dp", "tensor"),
        P("dp", None),
        P("dp", "tensor"),
        P("dp", None, "tensor"),
        P("dp", "tensor"),
        P("dp"),
        P("dp", "tensor"),
        P("dp", None),
        P("dp", "tensor"),
        P("dp", None, "tensor"),
        P("dp", "tensor"),
        P("dp"),
        P("dp", "tensor"),
        P("dp", None),
        P("dp", "tensor"),
        P("dp", None, "tensor"),
        P("dp", "tensor"),
        P("dp"),
    )
    return jax.shard_map(
        per_device,
        mesh=mesh,
        in_specs=placed,
        out_specs=(
            P(("dp", "tensor"), None),
            P(("dp", "tensor"), None),
            P("dp", "tensor"),
            P("dp", "tensor"),
            P("dp", "tensor"),
            P("dp", None),
            P("dp", None),
            P("dp", None),
            P("dp", "tensor"),
            P("dp", "tensor"),
            P("dp", "tensor"),
            P("dp", None, "tensor"),
            P("dp", None, "tensor"),
            P("dp", None, "tensor"),
            P("dp", "tensor"),
            P("dp", "tensor"),
            P("dp", "tensor"),
            P("dp"),
            P("dp"),
            P("dp"),
        ),
        check_vma=False,
    )
```

```python
import functools

import jax
import jax.numpy as jnp
import numpy as np
from jax import lax
from jax.experimental import pallas as pl
from jax.experimental.pallas import tpu as pltpu
from jax.sharding import PartitionSpec as P

D = 1152
FF = 6912
HEADS = 4
HEAD_DIM = 256
STEP = 10


eps_norm = 1e-06
query_scale = 0.0625
rope_base = 1000000.0
beta_first = 0.9
beta_second = 0.95
adam_eps = 1e-08
decay_rate = 0.01
masked_fill = -1e30
MESH = pl.DeviceIdType.MESH
low = jnp.bfloat16
full = jnp.float32
CHUNK = 512


def dot_nn(left, right):
    return lax.dot_general(left, right, (((1,), (0,)), ((), ())), preferred_element_type=full)


def dot_nt(left, right):
    return lax.dot_general(left, right, (((1,), (1,)), ((), ())), preferred_element_type=full)


def dot_tn(left, right):
    return lax.dot_general(left, right, (((0,), (0,)), ((), ())), preferred_element_type=full)


def chunks_of(units):
    out = []
    first = 0
    while first < units:
        width = min(CHUNK, units - first)
        out.append((first, width, -(-width // 128) * 128))
        first += width
    return out


def small_columns(head_dim):
    return 2 * head_dim, 3 * head_dim, 4 * head_dim


def packed_columns(units, head_dim):
    at = small_columns(head_dim)[2]
    places = []
    for first, width, _ in chunks_of(units):
        places.append((at, at + width, at + 2 * width))
        at += -(-3 * width // 128) * 128
    return places, at


class Place:
    def __init__(self):
        self.dp = lax.axis_index("dp")
        self.tensor = lax.axis_index("tensor")
        self.z = self.dp // 2
        self.x = self.dp % 2
        self.y = self.tensor // 2
        self.core = self.tensor % 2
        self.homes = (self.z, self.z + 1 - 2 * (self.z % 2), (self.z + 2) % 4, 3 - self.z)
        self.end = ((self.z + 1) // 2 + 1) % 2
        self.middle = self.end == 0
        self.mate = (self.dp, self.y * 2 + (1 - self.core))
        self.across = (self.dp, (1 - self.y) * 2 + self.core)
        self.side = (self.z * 2 + (1 - self.x), self.tensor)
        self.inner = ((1 + self.z % 2) * 2 + self.x, self.tensor)

    def line(self, step):
        return (self.homes[step] * 2 + self.x, self.tensor)

    def peers(self):
        return [self.mate, self.across, self.side] + [self.line(s) for s in (1, 2, 3)]


def meet(place):
    barrier = pltpu.get_barrier_semaphore()
    peers = place.peers()
    for peer in peers:
        pl.semaphore_signal(barrier, inc=1, device_id=peer, device_id_type=MESH)
    pl.semaphore_wait(barrier, len(peers))


def remote(source, target, send_sem, recv_sem, device):
    return pltpu.make_async_remote_copy(
        src_ref=source,
        dst_ref=target,
        send_sem=send_sem,
        recv_sem=recv_sem,
        device_id=device,
        device_id_type=MESH,
    )


class LineGather:
    def __init__(self, place, region, wide, send, recv, relay_send, side_send, side_recv):
        self.place, self.region, self.wide = place, region, wide
        self.send, self.recv, self.relay_send = send, recv, relay_send
        self.side_send, self.side_recv = side_send, side_recv

    def columns(self, group):
        return (0, 1) if self.wide[group] else (0,)

    def origin(self, column, step):
        place = self.place
        return place.homes[step] * 2 + (place.x if column == 0 else 1 - place.x)

    def along(self, group, column, step):
        block = self.region(group, self.origin(column, 0))
        return remote(
            block, block, self.send.at[group, column, step], self.recv.at[group, column, step], self.place.line(step)
        )

    def arrive(self, group, column, step):
        block = self.region(group, self.origin(column, step))
        remote(
            block, block, self.send.at[group, column, step], self.recv.at[group, column, step], self.place.line(step)
        ).wait_recv()

    def relay(self, group, column):
        block = self.region(group, self.origin(column, 2))
        return remote(
            block, block, self.relay_send.at[group, column], self.recv.at[group, column, 3], self.place.line(1)
        )

    def sideways(self, group, step):
        block = self.region(group, self.origin(0, step))
        return remote(
            block, block, self.side_send.at[group, step], self.side_recv.at[group, step], self.place.side
        )

    def arrive_side(self, group, step):
        block = self.region(group, self.origin(1, step))
        remote(
            block, block, self.side_send.at[group, step], self.side_recv.at[group, step], self.place.side
        ).wait_recv()

    def start_line(self, group, column):
        self.along(group, column, 2).start()
        self.along(group, column, 1).start()

        @pl.when(self.place.middle)
        def _():
            self.along(group, column, 3).start()

    def start(self, group):
        self.sideways(group, 0).start()
        self.start_line(group, 0)

    def widen(self, group):
        self.arrive_side(group, 0)
        self.start_line(group, 1)

    def pass_on(self, group):
        for column in self.columns(group):
            self.arrive(group, column, 2)

            @pl.when(self.place.middle)
            def _():
                self.relay(group, column).start()

            if not self.wide[group]:
                self.sideways(group, 2).start()

    def collect(self, group):
        for column in self.columns(group):
            for step in (1, 3):
                self.arrive(group, column, step)
                if not self.wide[group]:
                    self.sideways(group, step).start()

    def ready(self, group):
        if not self.wide[group]:
            for step in (0, 2, 1, 3):
                self.arrive_side(group, step)

    def finish(self):
        for group in range(len(self.wide)):
            for column in self.columns(group):
                self.along(group, column, 1).wait_send()
                self.along(group, column, 2).wait_send()

                @pl.when(self.place.middle)
                def _():
                    self.along(group, column, 3).wait_send()
                    self.relay(group, column).wait_send()

            for step in (0,) if self.wide[group] else (0, 1, 2, 3):
                self.sideways(group, step).wait_send()


def row_slabs(buffer, rows):
    return lambda y, core: buffer.at[pl.ds((y * 2 + core) * rows, rows)]


def column_slabs(buffer, wide):
    return lambda y, core: buffer.at[:, pl.ds(pl.multiple_of((y * 2 + core) * wide, wide), wide)]


class RowGather:
    def __init__(self, place, source, slab, send, recv):
        self.place, self.source, self.slab = place, source, slab
        self.send, self.recv = send, recv

    def copy(self, index):
        place = self.place
        slab = self.slab(1 - place.y if index == 2 else place.y, place.core)
        source = slab if index == 2 else self.source
        device = place.across if index == 1 else place.mate
        return remote(source, slab, self.send.at[index], self.recv.at[index], device)

    def arrival(self, index, y, core):
        slab = self.slab(y, core)
        remote(slab, slab, self.send.at[index], self.recv.at[index], self.place.mate).wait_recv()

    def start(self):
        self.copy(1).start()
        self.copy(0).start()

    def wait_mate(self):
        self.arrival(0, self.place.y, 1 - self.place.core)

    def wait_across(self):
        self.arrival(1, 1 - self.place.y, self.place.core)
        self.copy(2).start()

    def wait_corner(self):
        self.arrival(2, 1 - self.place.y, 1 - self.place.core)

    def finish(self):
        for index in range(3):
            self.copy(index).wait_send()


class RowScatter:
    def __init__(self, place, part, rows, first, second, mixed, send, recv):
        self.place, self.part, self.rows = place, part, rows
        self.first, self.second, self.mixed = first, second, mixed
        self.send, self.recv = send, recv

    def slab(self, y, core):
        return self.part.at[pl.ds((y * 2 + core) * self.rows, self.rows)]

    def copy(self, index):
        place = self.place
        if index == 2:
            return remote(self.mixed, self.second, self.send.at[2], self.recv.at[2], place.across)
        source = self.slab(1 - place.y if index == 0 else place.y, 1 - place.core)
        return remote(source, self.first.at[index], self.send.at[index], self.recv.at[index], place.mate)

    def order(self):
        place = self.place
        return (
            (1 - place.y) * 2 + (1 - place.core),
            (1 - place.y) * 2 + place.core,
            place.y * 2 + (1 - place.core),
            place.y * 2 + place.core,
        )

    def after(self, step):
        if step == 0:
            self.copy(0).start()
        if step == 1:
            self.copy(0).wait_recv()
            mixed = self.slab(1 - self.place.y, self.place.core)[...].astype(full) + self.first[0].astype(full)
            self.mixed[...] = mixed.astype(low)
            self.copy(2).start()
        if step == 2:
            self.copy(1).start()

    def total(self):
        self.copy(1).wait_recv()
        here = self.slab(self.place.y, self.place.core)[...].astype(full) + self.first[1].astype(full)
        self.copy(2).wait_recv()
        return here + self.second[...].astype(full)

    def finish(self):
        for index in range(3):
            self.copy(index).wait_send()


def inverse_rms(rows):
    return lax.rsqrt(jnp.mean(rows * rows, axis=-1, keepdims=True) + eps_norm)


def rotate_rows(rows, cosine, sine):
    half = rows.shape[-1] // 2
    front, back = rows[:, :half], rows[:, half:]
    return jnp.concatenate([front * cosine - back * sine, back * cosine + front * sine], axis=-1)


def rotate_back(rows, cosine, sine):
    half = rows.shape[-1] // 2
    front, back = rows[:, :half], rows[:, half:]
    return jnp.concatenate([front * cosine + back * sine, back * cosine - front * sine], axis=-1)


def gelu_parts(gate):
    scale = 0.7978845608028654
    square = gate * gate
    bent = jnp.tanh(scale * gate * (1.0 + 0.044715 * square))
    return square, bent


def forward_kernel(
    sizes,
    prefix_ref,
    tokens_ref,
    cot_ref,
    gains_ref,
    keyval_ref,
    query_ref,
    output_ref,
    gateup_ref,
    down_ref,
    cos_ref,
    sin_ref,
    wall_out,
    normed_out,
    normed_two_out,
    query_out,
    key_out,
    key_rot_out,
    value_out,
    attended_out,
    probs_out,
    gate_out,
    up_out,
    act_out,
    gvec,
    proj_keep,
    hidden_keep,
    grad_down,
    dgain_ffn,
    block_out,
    wall,
    normed,
    normed_two,
    query_raw,
    key_raw,
    attended,
    probs,
    gate_keep,
    up_keep,
    act,
    tok_full,
    gains_full,
    key_rot,
    value_low,
    part_one,
    first_one,
    second_one,
    mixed_one,
    first_two,
    second_two,
    mixed_two,
    down_acc,
    line_send,
    line_recv,
    relay_send,
    side_send,
    side_recv,
    row_send,
    row_recv,
    keep_sem,
):
    lines, rows, width, head_dim, units = sizes
    place = Place()
    length = 4 * rows
    shard = keyval_ref.shape[0]
    places, columns = packed_columns(units, head_dim)
    chunks = chunks_of(units)
    last = len(chunks) - 1
    kv_end, query_end, output_end = small_columns(head_dim)
    split, split_last = places[last - 1][2] + 128, places[last][2] // 128 * 128
    quarter = kv_end // 4
    own_quarter = pl.ds(pl.multiple_of(place.tensor * quarter, quarter), quarter)
    spans = [(0, kv_end), (kv_end, output_end)]
    spans += [(places[c][0], places[c + 1][0]) for c in range(last - 1)]
    spans += [(places[last - 1][0], split), (split, split_last), (split_last, columns)]
    tail = len(spans)

    def region(group, origin):
        if group == 0:
            return gains_full.at[pl.ds(origin * 8, 8)]
        if group == 1:
            return wall.at[pl.ds(origin * shard, shard), own_quarter]
        lo, hi = spans[group - 1]
        return wall.at[pl.ds(origin * shard, shard), lo:hi]

    wide_groups = [False] * (tail - 1) + [True] * 2
    gather = LineGather(place, region, wide_groups, line_send, line_recv, relay_send, side_send, side_recv)
    tokens_all = RowGather(place, tokens_ref, row_slabs(tok_full, rows), row_send.at[0], row_recv.at[0])
    own_rows = pl.ds(place.tensor * rows, rows)
    kept = []

    def keep(source, target):
        copy = pltpu.make_async_copy(source, target, keep_sem.at[len(kept)])
        copy.start()
        kept.append(copy)

    def keep_span(group):
        lo, hi = spans[group - 1]
        keep(wall.at[:, lo:hi], wall_out.at[:, lo:hi])

    own_gains = gains_ref[...].astype(low).astype(full).reshape(1, -1)
    gains_full[pl.ds(place.dp * 8, 8)] = jnp.broadcast_to(own_gains, (8, own_gains.shape[1]))
    own = pl.ds(place.dp * shard, shard)
    wall[own, own_quarter] = keyval_ref[:, own_quarter].astype(low)
    wall[own, kv_end:query_end] = query_ref[...].astype(low)
    wall[own, query_end:output_end] = output_ref[...].astype(low)
    meet(place)
    tokens_all.start()
    for group in range(3):
        gather.start(group)
    for (first, wide, _), at in zip(chunks, places):
        for kind, lo in enumerate(at):
            units_here = slice(first, first + wide)
            piece = down_ref[:, units_here] if kind == 2 else gateup_ref[:, kind, units_here]
            wall[own, lo : lo + wide] = piece.astype(low)
    filled = places[last][2] + chunks[last][1]
    if filled < columns:
        wall[own, filled:columns] = jnp.zeros((shard, columns - filled), low)
    gather.start(3)
    gather.start(4)
    tok_full[own_rows] = tokens_ref[...]
    tokens_all.wait_mate()
    tokens_all.wait_across()
    gather.pass_on(0)
    gather.pass_on(1)
    gather.collect(0)
    gather.collect(1)
    tokens_all.wait_corner()
    gather.pass_on(2)
    gather.ready(1)
    quarters = column_slabs(wall, quarter)
    keyval_all = RowGather(
        place, quarters(place.y, place.core), quarters, row_send.at[4], row_recv.at[4]
    )
    keyval_all.start()
    gather.collect(2)
    for group in range(5, tail + 1):
        gather.start(group)
    gather.ready(0)
    step = gains_ref.shape[0]
    for origin in range(2 * lines):
        gvec[:, origin * step : (origin + 1) * step] = gains_full[origin * 8 : origin * 8 + 8]
    gain_in = 1.0 + gvec[0:1, 0:width]
    gain_attn = 1.0 + gvec[0:1, width : 2 * width]
    gain_pre = 1.0 + gvec[0:1, 2 * width : 3 * width]
    gain_ffn = 1.0 + gvec[0:1, 3 * width : 4 * width]
    gain_query = 1.0 + gvec[0:1, 4 * width : 4 * width + head_dim]
    gain_key = 1.0 + gvec[0:1, 4 * width + head_dim : 4 * width + 2 * head_dim]

    def norm_slab(index, carry):
        at = pl.ds(pl.multiple_of(index * rows, rows), rows)
        x = tok_full[at].astype(full)
        normed[at] = (x * inverse_rms(x) * gain_in).astype(low)
        return carry

    lax.fori_loop(0, 4, norm_slab, 0)
    keep(normed, normed_out)
    keyval_all.wait_mate()
    keyval_all.wait_across()
    gather.ready(2)
    keyval_all.wait_corner()

    def project_slab(index, carry):
        at = pl.ds(pl.multiple_of(index * rows, rows), rows)
        n1 = normed[at]
        query_raw[at] = dot_nn(n1, wall[:, kv_end:query_end])
        kv = dot_nn(n1, wall[:, 0:kv_end])
        k = kv[:, :head_dim]
        key_raw[at] = k
        key_rot[at] = rotate_rows(k * inverse_rms(k) * gain_key, cos_ref[at], sin_ref[at]).astype(low)
        value_low[at] = kv[:, head_dim:].astype(low)
        return carry

    lax.fori_loop(0, 4, project_slab, 0)
    keep(query_raw, query_out)
    keep(key_raw, key_out)
    keep(key_rot, key_rot_out)
    keep(value_low, value_out)
    keep_span(1)
    keep_span(2)

    out_scatter = RowScatter(place, part_one, rows, first_one, second_one, mixed_one, row_send.at[1], row_recv.at[1])

    def attend_slab(index):
        at = pl.ds(pl.multiple_of(index * rows, rows), rows)
        q = query_raw[at]
        qr = rotate_rows(q * inverse_rms(q) * gain_query, cos_ref[at], sin_ref[at]).astype(low)
        scores = dot_nt(qr, key_rot[...]) * query_scale
        row_ids = lax.broadcasted_iota(jnp.int32, (rows, length), 0) + index * rows
        columns = lax.broadcasted_iota(jnp.int32, (rows, length), 1)
        allowed = (columns <= row_ids) | (columns < prefix_ref[0])
        scores = jnp.where(allowed, scores, masked_fill)
        shifted = jnp.exp(scores - jnp.max(scores, axis=-1, keepdims=True))
        soft = (shifted / jnp.sum(shifted, axis=-1, keepdims=True)).astype(low)
        probs[at] = soft
        mixed = dot_nn(soft, value_low[...]).astype(low)
        attended[at] = mixed
        part_one[at] = dot_nt(mixed, wall[:, query_end:output_end]).astype(low)

    for step, index in enumerate(out_scatter.order()):
        attend_slab(index)
        out_scatter.after(step)
    keep(probs, probs_out)
    keep(attended, attended_out)
    gather.pass_on(3)
    gather.collect(3)
    gather.widen(tail - 1)
    gather.widen(tail)
    projected = out_scatter.total()
    out_scatter.finish()
    proj_keep[...] = projected
    hidden = tokens_ref[...].astype(full) + projected * inverse_rms(projected) * gain_attn
    hidden_keep[...] = hidden
    normed_two[own_rows] = (hidden * inverse_rms(hidden) * gain_pre).astype(low)
    two_all = RowGather(place, normed_two.at[own_rows], row_slabs(normed_two, rows), row_send.at[2], row_recv.at[2])
    two_all.start()
    two_all.wait_mate()
    two_all.wait_across()
    two_all.wait_corner()
    keep(normed_two, normed_two_out)

    down_scatter = RowScatter(place, part_one, rows, first_two, second_two, mixed_two, row_send.at[3], row_recv.at[3])
    block = 2 * rows

    def feed(c):
        first, wide, padded = chunks[c]
        at_gate, at_up, _ = places[c]

        def feed_rows(index, carry):
            at = pl.ds(pl.multiple_of(index * block, block), block)
            n2 = normed_two[at]
            gate = dot_nn(n2, wall[:, at_gate : at_gate + wide])
            up = dot_nn(n2, wall[:, at_up : at_up + wide])
            gate_keep[at, first : first + wide] = gate.astype(low)
            up_keep[at, first : first + wide] = up.astype(low)
            _, bent = gelu_parts(gate)
            act[at, first : first + wide] = (0.5 * gate * (1.0 + bent) * up).astype(low)
            return carry

        lax.fori_loop(0, 2, feed_rows, 0)
        span = slice(first, first + padded)
        keep(gate_keep.at[:, span], gate_out.at[:, span])
        keep(up_keep.at[:, span], up_out.at[:, span])
        keep(act.at[:, span], act_out.at[:, span])

    def lower(c):
        first, wide, _ = chunks[c]
        at_down = places[c][2]

        def lower_rows(index, carry):
            at = pl.ds(pl.multiple_of(index * block, block), block)
            more = dot_nt(act[at, first : first + wide], wall[:, at_down : at_down + wide])
            down_acc[at] = more if c == 0 else down_acc[at] + more
            return carry

        lax.fori_loop(0, 2, lower_rows, 0)

    for c in range(last - 1):
        gather.pass_on(c + 4)
        gather.collect(c + 4)
        gather.ready(c + 3)
        feed(c)
        lower(c)
        keep_span(c + 3)
    gather.pass_on(tail - 1)
    gather.ready(tail - 2)
    feed(last - 1)
    keep_span(tail - 2)
    gather.collect(tail - 1)
    gather.pass_on(tail)
    lower(last - 1)
    feed(last)
    keep_span(tail - 1)
    gather.collect(tail)
    keep_span(tail)
    first, wide, _ = chunks[last]
    at_down = places[last][2]
    for step, index in enumerate(down_scatter.order()):
        at = pl.ds(pl.multiple_of(index * rows, rows), rows)
        part_one[at] = (
            down_acc[at] + dot_nt(act[at, first : first + wide], wall[:, at_down : at_down + wide])
        ).astype(low)
        down_scatter.after(step)
    f = down_scatter.total()
    inv = inverse_rms(f)
    block_out[...] = (hidden_keep[...] + f * inv * gain_ffn).astype(low)
    cot = cot_ref[...].astype(full)
    scaled = cot * gain_ffn
    grad_down[...] = (inv * (scaled - f * (inv * inv) * jnp.mean(f * scaled, axis=-1, keepdims=True))).astype(low)
    dgain_ffn[...] = jnp.broadcast_to(jnp.sum(cot * f * inv, axis=0, keepdims=True), dgain_ffn.shape)
    gather.finish()
    tokens_all.finish()
    keyval_all.finish()
    two_all.finish()
    down_scatter.finish()
    for copy in kept:
        copy.wait()


def forward_call(sizes, prefix, tokens, cotangent, gains, weights, cosine, sine):
    lines, rows, width, head_dim, units = sizes
    length = 4 * rows
    shard = weights[0].shape[0]
    columns = packed_columns(units, head_dim)[1]
    chunks = chunks_of(units)
    padded = sum(c[2] for c in chunks)
    groups = 5 + len(chunks)
    vm = pl.BlockSpec(memory_space=pltpu.VMEM)
    hbm = pl.BlockSpec(memory_space=pl.ANY)
    large = [
        ((2 * lines * shard, columns), low),
        ((length, width), low),
        ((length, width), low),
        ((length, head_dim), full),
        ((length, head_dim), full),
        ((length, head_dim), low),
        ((length, head_dim), low),
        ((length, head_dim), low),
        ((length, length), low),
        ((length, padded), low),
        ((length, padded), low),
        ((length, padded), low),
    ]
    small = [
        ((8, gains.shape[0] * 2 * lines), full),
        ((rows, width), full),
        ((rows, width), full),
        ((rows, width), low),
        ((8, width), full),
        ((rows, width), low),
    ]
    inside = [large[i] for i in (0, 1, 2, 3, 4, 7, 8, 9, 10, 11)]
    scatter_set = [
        pltpu.VMEM((2, rows, width), low),
        pltpu.VMEM((rows, width), low),
        pltpu.VMEM((rows, width), low),
    ]
    return pl.pallas_call(
        functools.partial(forward_kernel, sizes),
        out_shape=[jax.ShapeDtypeStruct(*item) for item in large + small],
        in_specs=[pl.BlockSpec(memory_space=pltpu.SMEM)] + [vm] * 10,
        out_specs=[hbm] * len(large) + [vm] * len(small),
        scratch_shapes=[pltpu.VMEM(*item) for item in inside]
        + [
            pltpu.VMEM((length, width), low),
            pltpu.VMEM((2 * lines * 8, gains.shape[0]), full),
            pltpu.VMEM((length, head_dim), low),
            pltpu.VMEM((length, head_dim), low),
            pltpu.VMEM((length, width), low),
        ]
        + scatter_set
        + scatter_set
        + [
            pltpu.VMEM((length, width), full),
            pltpu.SemaphoreType.DMA((groups, 2, lines)),
            pltpu.SemaphoreType.DMA((groups, 2, lines)),
            pltpu.SemaphoreType.DMA((groups, 2)),
            pltpu.SemaphoreType.DMA((groups, lines)),
            pltpu.SemaphoreType.DMA((groups, lines)),
            pltpu.SemaphoreType.DMA((5, 3)),
            pltpu.SemaphoreType.DMA((5, 3)),
            pltpu.SemaphoreType.DMA((13 + 4 * len(chunks),)),
        ],
        compiler_params=pltpu.CompilerParams(
            collective_id=0, has_side_effects=True, vmem_limit_bytes=63 * 1024 * 1024
        ),
        name="forward",
    )(prefix, tokens, cotangent, gains, *weights, cosine, sine)


class LineScatter:
    def __init__(self, place, block, side_block, line_block, wide, side_send, side_recv, line_send, line_recv, kind):
        self.place, self.block, self.side_block, self.line_block = place, block, side_block, line_block
        self.wide, self.kind = wide, kind
        self.side_send, self.side_recv, self.line_send, self.line_recv = side_send, side_recv, line_send, line_recv

    def columns(self, group):
        return (0, 1) if self.wide[group] else (0,)

    def own(self, group, column, step):
        place = self.place
        return self.block(group, place.homes[step] * 2 + (place.x if column == 0 else 1 - place.x))

    def sideways(self, group, step):
        home = 0 if self.wide[group] else self.place.homes[step]
        return remote(
            self.own(group, 1, step),
            self.side_block(group, home),
            self.side_send.at[group, step],
            self.side_recv.at[group, step],
            self.place.side,
        )

    def along(self, group, column, step):
        slot = step - 1 if step < 3 else 2 + self.place.end
        return remote(
            self.own(group, column, step),
            self.line_block(group, column, slot),
            self.line_send.at[group, column, step],
            self.line_recv.at[group, column, slot],
            self.place.line(step) if step < 3 else self.place.inner,
        )

    def arrive(self, group, column, slot):
        here = self.line_block(group, column, slot)
        remote(
            here, here, self.line_send.at[group, column, 1], self.line_recv.at[group, column, slot], self.place.line(1)
        ).wait_recv()
        return here[...].astype(full)

    def start(self, group):
        if not self.wide[group]:
            for step in (3, 1, 2, 0):
                self.sideways(group, step).start()
            return
        for step in (3, 1):
            for column in (0, 1):
                self.along(group, column, step).start()

        @pl.when(self.place.end == 1)
        def _():
            for column in (0, 1):
                self.along(group, column, 2).start()

    def with_side(self, group, step):
        self.sideways(group, step).wait_recv()
        return self.own(group, 0, step)[...].astype(full) + self.side_block(group, self.place.homes[step])[...].astype(
            full
        )

    def pump(self, group, *steps):
        for step in steps or (3, 1, 2):
            self.own(group, 0, step)[...] = self.with_side(group, step).astype(self.kind)
            if step != 2:
                self.along(group, 0, step).start()
                continue

            @pl.when(self.place.end == 1)
            def _():
                self.along(group, 0, 2).start()

    def relay(self, group):
        for column in self.columns(group):

            @pl.when(self.place.middle)
            def _():
                block = self.own(group, column, 2)
                block[...] = (block[...].astype(full) + self.arrive(group, column, 3)).astype(self.kind)
                self.along(group, column, 2).start()

    def hand_over(self, group):
        block = self.own(group, 1, 0)
        both = block[...].astype(full) + self.arrive(group, 1, 0) + self.arrive(group, 1, 1)

        @pl.when(self.place.middle)
        def _():
            block[...] = (both + self.arrive(group, 1, 2)).astype(self.kind)

        @pl.when(self.place.end == 1)
        def _():
            block[...] = both.astype(self.kind)

        self.sideways(group, 0).start()

    def settle(self, group):
        self.sideways(group, 0).wait_recv()
        self.arrive(group, 0, 0)
        self.arrive(group, 0, 1)

        @pl.when(self.place.middle)
        def _():
            self.arrive(group, 0, 2)

    def total(self, group, lo, hi, held):
        parts = [
            self.own(group, 0, 0),
            self.side_block(group, 0 if self.wide[group] else self.place.z),
            self.line_block(group, 0, 0),
            self.line_block(group, 0, 1),
        ]
        first, *others = [part[:, lo:hi].astype(full) for part in parts]
        for other in others:
            first = first + other
        held[...] = first

        @pl.when(self.place.middle)
        def _():
            held[...] = first + self.line_block(group, 0, 2)[:, lo:hi].astype(full)

    def finish(self):
        for group in range(len(self.wide)):
            for step in (0,) if self.wide[group] else (0, 1, 2, 3):
                self.sideways(group, step).wait_send()
            for column in self.columns(group):
                for step in (1, 2, 3):
                    self.along(group, column, step).wait_send()


def norm_back(rows, inv, gain, grad):
    scaled = grad * gain
    back = inv * (scaled - rows * (inv * inv) * jnp.mean(rows * scaled, axis=-1, keepdims=True))
    return back, jnp.sum(grad * rows * inv, axis=0, keepdims=True)


def backward_kernel(
    sizes,
    grad_down_ref,
    cot_ref,
    tokens_ref,
    gvec,
    dgain_ffn,
    proj_ref,
    hidden_ref,
    cos_ref,
    sin_ref,
    wall_in,
    normed_in,
    normed_two_in,
    query_in,
    key_in,
    key_rot_in,
    value_in,
    attended_in,
    probs_in,
    gate_in,
    up_in,
    act_in,
    gate_grad,
    up_grad,
    down_grad,
    small_grad,
    tokens_grad,
    keyval_grad,
    gains_grad,
    wall,
    side_buf,
    side_wide,
    line_buf,
    line_wide,
    big,
    normed_two,
    row_buf,
    acc,
    first_buf,
    second_buf,
    mixed_buf,
    key_rot,
    value_low,
    dquery,
    dkeyval,
    dhidden,
    dproj,
    kv_first,
    kv_second,
    kv_mixed,
    kv_own,
    dgains,
    gain_part,
    gain_first,
    gain_second,
    gain_side,
    gain_line,
    row_send,
    row_recv,
    side_send,
    side_recv,
    line_send,
    line_recv,
    gain_side_send,
    gain_side_recv,
    gain_line_send,
    gain_line_recv,
    last_send,
    last_recv,
    load_sem,
    store_sem,
):
    lines, rows, width, head_dim, units = sizes
    place = Place()
    length = 4 * rows
    shard = wall.shape[0] // (2 * lines)
    kv_end, query_end, output_end = small_columns(head_dim)
    quarter = head_dim // 2
    places, columns = packed_columns(units, head_dim)
    chunks = chunks_of(units)
    last = len(chunks) - 1
    order = [0, last] + list(range(1, last))
    base_column = kv_end - quarter
    spans = []
    for c in range(last):
        spans += [(places[c][2], places[c + 1][0]), (places[c][0], places[c][2])]
    group_gate, group_up, group_last, group_small = range(len(spans) - 1, len(spans) + 3)
    spans[-1:] = [(places[last - 1][0], places[last - 1][1]), (places[last - 1][1], places[last - 1][2])]
    spans += [(places[last][0], columns), (base_column, output_end)]
    loads = {}

    def load(name, source, target):
        copy = pltpu.make_async_copy(source, target, load_sem.at[len(loads)])
        copy.start()
        loads[name] = copy

    def load_chunk(c):
        first, _, padded = chunks[c]
        lo, hi = places[c][0], columns if c == last else places[c + 1][0]
        base = (order.index(c) % 2) * 3 * CHUNK
        load(("wall", c), wall_in.at[:, lo:hi], wall.at[:, lo:hi])
        for k, source in enumerate((gate_in, up_in, act_in)):
            at = base + k * CHUNK
            load((k, c), source.at[:, first : first + padded], big.at[:, at : at + padded])

    load("two", normed_two_in, normed_two)
    load_chunk(order[0])
    load("kv", wall_in.at[:, 0:kv_end], wall.at[:, 0:kv_end])
    load("qo", wall_in.at[:, kv_end:output_end], wall.at[:, kv_end:output_end])
    load("key_rot", key_rot_in, key_rot)
    load("value", value_in, value_low)
    gain_in = 1.0 + gvec[0:1, 0:width]
    gain_attn = 1.0 + gvec[0:1, width : 2 * width]
    gain_pre = 1.0 + gvec[0:1, 2 * width : 3 * width]
    gain_query = 1.0 + gvec[0:1, 4 * width : 4 * width + head_dim]
    gain_key = 1.0 + gvec[0:1, 4 * width + head_dim : 4 * width + 2 * head_dim]
    own_rows = pl.ds(place.tensor * rows, rows)
    row_buf[own_rows] = grad_down_ref[...]
    dgains[...] = jnp.zeros_like(dgains)
    dgains[0:1, 3 * width : 4 * width] = dgain_ffn[0:1]
    meet(place)
    down_all = RowGather(place, grad_down_ref, row_slabs(row_buf, rows), row_send.at[0], row_recv.at[0])
    down_all.start()
    load_chunk(order[1])
    down_all.wait_mate()
    down_all.wait_across()
    down_all.wait_corner()
    loads["two"].wait()

    def block(group, origin):
        lo, hi = spans[group]
        return wall.at[pl.ds(origin * shard, shard), lo:hi]

    def side_block(group, home):
        if wide_groups[group]:
            return side_wide
        lo, hi = spans[group]
        return side_buf.at[pl.ds(home * shard, shard), lo - base_column : hi - base_column]

    def line_block(group, column, slot):
        lo, hi = spans[group]
        if wide_groups[group]:
            return line_wide.at[pl.ds((column * 4 + slot) * shard, shard)]
        return line_buf.at[pl.ds(slot * shard, shard), lo - base_column : hi - base_column]

    wide_groups = [group == group_last for group in range(len(spans))]
    scatter = LineScatter(
        place, block, side_block, line_block, wide_groups, side_send, side_recv, line_send, line_recv, low
    )
    part = big.at[:, 0:width]
    pre_scatter = RowScatter(place, part, rows, first_buf, second_buf, mixed_buf, row_send.at[1], row_recv.at[1])
    half = 2 * rows
    third = width // 3

    def weight_gradient(lo, wide, left, right):
        for m in range(0, width, third):
            wall[m : m + third, lo : lo + wide] = dot_tn(left[:, m : m + third], right).astype(low)

    for position, c in enumerate(order):
        first, wide, padded = chunks[c]
        at_gate, at_up, at_down = places[c]
        base = (position % 2) * 3 * CHUNK
        loads["wall", c].wait()
        for k in range(3):
            loads[k, c].wait()
        if 1 <= position < last:
            load_chunk(order[position + 1])
        of_gate = slice(base, base + wide)
        of_up = slice(base + CHUNK, base + CHUNK + wide)
        of_act = slice(base + 2 * CHUNK, base + 2 * CHUNK + wide)

        def unit_rows(index, carry):
            at = pl.ds(pl.multiple_of(index * half, half), half)
            dz = dot_nn(row_buf[at], wall[:, at_down : at_down + wide])
            gate = big[at, of_gate].astype(full)
            up = big[at, of_up].astype(full)
            square, bent = gelu_parts(gate)
            middle = 0.5 * (1.0 + bent)
            slope = middle + 0.5 * gate * (1.0 - bent * bent) * (0.7978845608028654 * (1.0 + 0.134145 * square))
            big[at, of_gate] = (dz * up * slope).astype(low)
            big[at, of_up] = (dz * gate * middle).astype(low)
            return carry

        lax.fori_loop(0, 2, unit_rows, 0)
        weight_gradient(at_down, wide, row_buf, big[:, of_act])
        if c < last:
            scatter.start(2 * c)

        def back_rows(at):
            more = dot_nt(big[at, of_gate], wall[:, at_gate : at_gate + wide])
            more = more + dot_nt(big[at, of_up], wall[:, at_up : at_up + wide])
            return more if position == 0 else acc[at] + more

        if position < last:

            def collect_rows(index, carry):
                at = pl.ds(pl.multiple_of(index * half, half), half)
                acc[at] = back_rows(at)
                return carry

            lax.fori_loop(0, 2, collect_rows, 0)
        else:
            down_all.finish()
            for step, index in enumerate(pre_scatter.order()):
                at = pl.ds(pl.multiple_of(index * rows, rows), rows)
                part[at] = back_rows(at).astype(low)
                pre_scatter.after(step)
        weight_gradient(at_gate, wide, normed_two, big[:, of_gate])
        weight_gradient(at_up, wide, normed_two, big[:, of_up])
        if c < last:
            scatter.start(2 * c + 1)
        else:
            scatter.pump(0)
            scatter.start(group_last)
        if position == 2:
            scatter.relay(0)
        if position == 3:
            scatter.relay(group_last)
            scatter.pump(1, 3, 1)

    at_normed = width
    at_att = at_normed + width
    load("normed", normed_in, big.at[:, at_normed : at_normed + width])
    load("attended", attended_in, big.at[:, at_att : at_att + head_dim])
    load("query", query_in, acc.at[:, 2 * head_dim : 3 * head_dim])
    load("key", key_in, acc.at[:, 3 * head_dim : 4 * head_dim])

    scatter.pump(1, 2)
    dn2 = pre_scatter.total()
    hidden = hidden_ref[...]
    back, grad = norm_back(hidden, inverse_rms(hidden), gain_pre, dn2)
    dgains[0:1, 2 * width : 3 * width] = grad
    dh = cot_ref[...].astype(full) + back
    dhidden[...] = dh
    proj = proj_ref[...]
    back, grad = norm_back(proj, inverse_rms(proj), gain_attn, dh)
    dgains[0:1, width : 2 * width] = grad
    dproj[...] = back.astype(low)
    row_buf[own_rows] = dproj[...]
    proj_all = RowGather(place, dproj, row_slabs(row_buf, rows), row_send.at[2], row_recv.at[2])
    proj_all.start()
    pre_scatter.finish()
    load("probs", probs_in, big.at[:, 0:length])
    acc[:, 0 : 2 * head_dim] = jnp.zeros((length, 2 * head_dim), full)
    proj_all.wait_mate()
    scatter.pump(2)
    proj_all.wait_across()
    scatter.relay(1)
    proj_all.wait_corner()
    for name in ("kv", "qo", "key_rot", "value", "normed", "attended", "query", "key", "probs"):
        loads[name].wait()

    def attend_back(index, carry):
        at = pl.ds(pl.multiple_of(index * rows, rows), rows)
        da = dot_nn(row_buf[at], wall[:, query_end:output_end]).astype(low)
        soft = big[at, 0:length]
        wide_soft = soft.astype(full)
        dp = dot_nt(da, value_low[...])
        ds = (wide_soft * (dp - jnp.sum(wide_soft * dp, axis=-1, keepdims=True))).astype(low)
        q = acc[at, 2 * head_dim : 3 * head_dim]
        inv = inverse_rms(q)
        cosine, sine = cos_ref[at], sin_ref[at]
        qr = rotate_rows(q * inv * gain_query, cosine, sine).astype(low)
        dqr = dot_nn(ds, key_rot[...]) * query_scale
        acc[:, 0:head_dim] += dot_tn(ds, qr)
        acc[:, head_dim : 2 * head_dim] += dot_tn(soft, da)
        dq, grad = norm_back(q, inv, gain_query, rotate_back(dqr, cosine, sine))
        dquery[at] = dq.astype(low)
        dgains[0:1, 4 * width : 4 * width + head_dim] += grad
        return carry

    scatter.hand_over(group_last)
    scatter.pump(3, 3)
    lax.fori_loop(0, 4, attend_back, 0)

    def key_back(index, carry):
        at = pl.ds(pl.multiple_of(index * rows, rows), rows)
        k = acc[at, 3 * head_dim : 4 * head_dim]
        dkr = rotate_back(acc[at, 0:head_dim] * query_scale, cos_ref[at], sin_ref[at])
        dk, grad = norm_back(k, inverse_rms(k), gain_key, dkr)
        dkeyval[at, 0:head_dim] = dk.astype(low)
        dkeyval[at, head_dim : 2 * head_dim] = acc[at, head_dim : 2 * head_dim].astype(low)
        dgains[0:1, 4 * width + head_dim : 4 * width + 2 * head_dim] += grad
        return carry

    lax.fori_loop(0, 4, key_back, 0)
    scatter.pump(3, 1)
    in_scatter = RowScatter(place, part, rows, first_buf, second_buf, mixed_buf, row_send.at[3], row_recv.at[3])
    for step, index in enumerate(in_scatter.order()):
        at = pl.ds(pl.multiple_of(index * rows, rows), rows)
        more = dot_nt(dquery[at], wall[:, kv_end:query_end]) + dot_nt(dkeyval[at], wall[:, 0:kv_end])
        part[at] = more.astype(low)
        in_scatter.after(step)
    scatter.pump(3, 2)
    scatter.relay(2)

    normed = big.at[:, at_normed : at_normed + width]
    for m in range(0, width, third):
        wall[m : m + third, 0:kv_end] = dot_tn(normed[:, m : m + third], dkeyval[...]).astype(low)

    def kv_block(y, core):
        return wall.at[:, pl.ds(pl.multiple_of((y * 2 + core) * quarter, quarter), quarter)]

    def kv_copy(index):
        send, recv = last_send.at[index], last_recv.at[index]
        if index == 2:
            return remote(kv_mixed, kv_second, send, recv, place.across)
        return remote(
            kv_block(1 - place.y if index == 0 else place.y, 1 - place.core), kv_first.at[index], send, recv, place.mate
        )

    kv_copy(0).start()
    kv_copy(1).start()
    weight_gradient(kv_end, head_dim, normed, dquery[...])
    weight_gradient(query_end, head_dim, row_buf, big[:, at_att : at_att + head_dim])
    kv_copy(0).wait_recv()
    kv_mixed[...] = (kv_block(1 - place.y, place.core)[...].astype(full) + kv_first[0].astype(full)).astype(low)
    kv_copy(2).start()
    scatter.pump(4, 3, 1)
    scatter.relay(3)

    dn1 = in_scatter.total()
    x = tokens_ref[...].astype(full)
    back, grad = norm_back(x, inverse_rms(x), gain_in, dn1)
    dgains[0:1, 0:width] = grad
    tokens_grad[...] = (dhidden[...] + back).astype(low)
    step = gains_grad.shape[1]
    for origin in range(2 * lines):
        gain_part[origin * 8 : origin * 8 + 8] = dgains[:, origin * step : (origin + 1) * step]

    def gain_copy(index):
        source, target, device = (
            (gain_part, gain_first, place.mate) if index == 0 else (gain_part, gain_second, place.across)
        )
        return remote(source, target, last_send.at[3 + index], last_recv.at[3 + index], device)

    gain_copy(0).start()
    scatter.pump(4, 2)
    kv_copy(1).wait_recv()
    kv_copy(2).wait_recv()
    kv_copy(0).wait_send()
    kv_copy(1).wait_send()
    wall[:, base_column:kv_end] = (
        kv_block(place.y, place.core)[...].astype(full) + kv_first[1].astype(full) + kv_second[...].astype(full)
    ).astype(low)
    scatter.relay(4)
    gain_copy(0).wait_recv()
    gain_copy(0).wait_send()
    gain_part[...] = gain_part[...] + gain_first[...]
    gain_copy(1).start()
    scatter.pump(group_gate, 3)
    gain_copy(1).wait_recv()
    gain_copy(1).wait_send()
    gain_part[...] = gain_part[...] + gain_second[...]

    gain_scatter = LineScatter(
        place,
        lambda group, origin: gain_part.at[pl.ds(origin * 8, 8)],
        lambda group, home: gain_side.at[pl.ds(home * 8, 8)],
        lambda group, column, slot: gain_line.at[pl.ds(slot * 8, 8)],
        [False],
        gain_side_send,
        gain_side_recv,
        gain_line_send,
        gain_line_recv,
        full,
    )
    gain_scatter.start(0)
    scatter.start(group_small)
    scatter.start(group_up)
    scatter.pump(group_gate, 1, 2)

    stores = []

    def store(group, kinds, c):
        first, wide, padded = chunks[c] if kinds else (0, output_end - base_column, output_end - base_column)
        scatter.settle(group)
        for k, target in enumerate(kinds or (small_grad,)):
            slot = 3 * len(chunks) if not kinds else len([done for done in stores if done[1]])
            down, right = slot // 2 * shard, slot % 2 * CHUNK
            held = acc.at[down : down + shard, right : right + padded]
            scatter.total(group, k * wide, (k + 1) * wide, held.at[:, 0:wide])
            copy = pltpu.make_async_copy(held, target.at[:, first : first + padded], store_sem.at[slot])
            copy.start()
            stores.append((copy, bool(kinds)))
            if not kinds:
                kv_own[...] = held[:, 0:quarter].astype(low)

    for c in range(last - 1):
        store(2 * c, (down_grad,), c)
        store(2 * c + 1, (gate_grad, up_grad), c)
    scatter.relay(group_gate)
    store(group_last, (gate_grad, up_grad, down_grad), last)
    gain_scatter.pump(0)
    store(2 * last - 2, (down_grad,), last - 1)
    scatter.pump(group_small)
    gain_scatter.relay(0)
    scatter.relay(group_small)
    store(group_gate, (gate_grad,), last - 1)
    scatter.pump(group_up, 3, 1)
    store(group_small, (), 0)

    def own_block(y, core):
        return keyval_grad.at[:, pl.ds(pl.multiple_of((y * 2 + core) * quarter, quarter), quarter)]

    own_block(place.y, place.core)[...] = kv_own[...]
    targets = (place.mate, place.across, (place.dp, (1 - place.y) * 2 + (1 - place.core)))
    sends = [
        remote(kv_own, own_block(place.y, place.core), last_send.at[5 + i], last_recv.at[5 + i], target)
        for i, target in enumerate(targets)
    ]
    for copy in sends:
        copy.start()
    scatter.pump(group_up, 2)
    scatter.relay(group_up)
    gain_scatter.settle(0)
    gain_scatter.total(0, 0, gains_grad.shape[1], gains_grad)
    store(group_up, (up_grad,), last - 1)
    for i, (y, core) in enumerate(
        ((place.y, 1 - place.core), (1 - place.y, place.core), (1 - place.y, 1 - place.core))
    ):
        remote(kv_own, own_block(y, core), last_send.at[5 + i], last_recv.at[5 + i], targets[i]).wait_recv()
    for copy in sends:
        copy.wait_send()
    kv_copy(2).wait_send()
    scatter.finish()
    gain_scatter.finish()
    proj_all.finish()
    in_scatter.finish()
    for copy, _ in stores:
        copy.wait()


def backward_call(sizes, vmem_args, hbm_args):
    lines, rows, width, head_dim, units = sizes
    length = 4 * rows
    columns = hbm_args[0].shape[1]
    shard = hbm_args[0].shape[0] // (2 * lines)
    gains = vmem_args[3].shape[1]
    quarter = head_dim // 2
    base_column = 2 * head_dim - quarter
    chunks = chunks_of(units)
    groups = 2 * len(chunks) + 1
    last_wide = columns - packed_columns(units, head_dim)[0][-1][0]
    vm = pl.BlockSpec(memory_space=pltpu.VMEM)
    hbm = pl.BlockSpec(memory_space=pl.ANY)
    padded = sum(c[2] for c in chunks)
    large = [((shard, padded), full)] * 3 + [((shard, 5 * quarter), full)]
    outs = [
        ((rows, width), low),
        ((shard, 2 * head_dim), low),
        ((8, gains // (2 * lines)), full),
    ]
    scratch = [
        (hbm_args[0].shape, low),
        ((lines * shard, packed_columns(units, head_dim)[0][-1][0] - base_column), low),
        ((shard, last_wide), low),
        ((lines * shard, packed_columns(units, head_dim)[0][-1][0] - base_column), low),
        ((2 * lines * shard, last_wide), low),
        ((length, 6 * CHUNK), low),
        ((length, width), low),
        ((length, width), low),
        ((length, width), full),
        ((2, rows, width), low),
        ((rows, width), low),
        ((rows, width), low),
        ((length, head_dim), low),
        ((length, head_dim), low),
        ((length, head_dim), low),
        ((length, 2 * head_dim), low),
        ((rows, width), full),
        ((rows, width), low),
        ((2, width, quarter), low),
        ((width, quarter), low),
        ((width, quarter), low),
        ((shard, quarter), low),
        ((8, gains), full),
        ((2 * lines * 8, gains // (2 * lines)), full),
        ((2 * lines * 8, gains // (2 * lines)), full),
        ((2 * lines * 8, gains // (2 * lines)), full),
        ((lines * 8, gains // (2 * lines)), full),
        ((lines * 8, gains // (2 * lines)), full),
    ]
    sems = [(4, 3), (4, 3), (groups, 4), (groups, 4), (groups, 2, 4), (groups, 2, 4)]
    sems += [(1, 4), (1, 4), (1, 1, 4), (1, 1, 4), (8,), (8,)]
    sems += [(10 + 4 * len(chunks),), (1 + 3 * len(chunks),)]
    return pl.pallas_call(
        functools.partial(backward_kernel, sizes),
        out_shape=[jax.ShapeDtypeStruct(*item) for item in large + outs],
        in_specs=[vm] * len(vmem_args) + [hbm] * len(hbm_args),
        out_specs=[hbm] * len(large) + [vm] * len(outs),
        scratch_shapes=[pltpu.VMEM(*item) for item in scratch] + [pltpu.SemaphoreType.DMA(dims) for dims in sems],
        compiler_params=pltpu.CompilerParams(
            collective_id=1, has_side_effects=True, vmem_limit_bytes=63 * 1024 * 1024
        ),
        name="backward",
    )(*vmem_args, *hbm_args)


def adam_values(weight, gradient, first, second, step_rate):
    moment = beta_first * first + (1.0 - beta_first) * gradient
    square = beta_second * second + (1.0 - beta_second) * gradient * gradient
    scaled = moment / (1.0 - beta_first**STEP) / (jnp.sqrt(square / (1.0 - beta_second**STEP)) + adam_eps)
    return moment, square, weight - step_rate * (scaled + decay_rate * weight)


def update_kernel(units, head_dim, cut, *refs):
    passed, grads, old = refs[:2], refs[2:8], refs[8:26]
    passed_out, new = refs[26:28], refs[28:46]
    held_passed, held_grads, held, load_sem, store_sem = refs[46:48], refs[48:54], refs[54:72], refs[72], refs[73]
    gate_grad, up_grad, down_grad, small_grad, keyval_grad, gains_grad = held_grads
    quarter = head_dim // 2
    shard = old[0].shape[0]
    rows = shard // cut
    wide = D ** (-0.5)
    count = [0, 0]

    def load(source, target, part):
        at = slice(None) if part is None else pl.ds(part * rows, rows)
        copy = pltpu.make_async_copy(source.at[at], target.at[at], load_sem.at[count[0]])
        count[0] += 1
        copy.start()
        return copy

    def store(source, target, part):
        at = slice(None) if part is None else pl.ds(part * rows, rows)
        copy = pltpu.make_async_copy(source.at[at], target.at[at], store_sem.at[count[1]])
        count[1] += 1
        copy.start()
        return copy

    jobs = [(3, part, (0, 1)) for part in range(cut)] + [(4, part, (2,)) for part in range(cut)]
    jobs += [(1, None, (4,)), (0, None, (3,)), (2, None, ()), (5, None, (5,))]
    waits = []
    for index, part, needs in jobs:
        own = range(3 * index, 3 * index + 3)
        waits.append(
            [load(old[i], held[i], part) for i in own] + [load(grads[i], held_grads[i], part) for i in needs]
        )
    through = [load(source, target, None) for source, target in zip(passed, held_passed)]
    waiting = []

    def work(index, part):
        weight, first, second = held[3 * index : 3 * index + 3]
        if index == 5:
            values = adam_values(weight[...], gains_grad[0], first[...], second[...], 0.3)
            for target, value in zip((first, second, weight), values):
                target[...] = value
            return
        step = rows if part is not None else shard // 3

        def some_rows(at):
            if index == 3:
                for kind, grad in enumerate((gate_grad, up_grad)):
                    values = adam_values(
                        weight[at, kind, :], grad[at, 0:units], first[at, kind, :], second[at, kind, :], wide
                    )
                    for target, value in zip((first, second, weight), values):
                        target[at, kind, :] = value
                return
            if index == 4:
                gradient, rate = down_grad[at, 0:units], FF ** (-0.5)
            elif index == 1:
                gradient, rate = keyval_grad[at].astype(full), wide
            elif index == 0:
                gradient, rate = small_grad[at, quarter : quarter + head_dim], wide
            else:
                gradient = small_grad[at, quarter + head_dim : quarter + 2 * head_dim]
                rate = (HEADS * HEAD_DIM) ** (-0.5)
            values = adam_values(weight[at], gradient, first[at], second[at], rate)
            for target, value in zip((first, second, weight), values):
                target[at] = value

        if part is not None:
            some_rows(pl.ds(part * rows, rows))
        else:

            def body(i, carry):
                some_rows(pl.ds(pl.multiple_of(i * step, step), step))
                return carry

            lax.fori_loop(0, 3, body, 0)

    for (index, part, _), copies in zip(jobs, waits):
        if index == 1:
            for copy, source, target in zip(through, held_passed, passed_out):
                copy.wait()
                waiting.append(store(source, target, None))
        for copy in copies:
            copy.wait()
        work(index, part)
        for kind, place in ((1, 0), (2, 1), (0, 2)):
            waiting.append(store(held[3 * index + kind], new[3 * index + place], part))
    for copy in waiting:
        copy.wait()


def update_call(units, head_dim, passed, grads, old, cut):
    hbm = pl.BlockSpec(memory_space=pl.ANY)
    outs = list(passed)
    for index in range(6):
        outs += [old[3 * index + kind] for kind in (1, 2, 0)]
    loads = 9 * cut + 18
    return pl.pallas_call(
        functools.partial(update_kernel, units, head_dim, cut),
        out_shape=[jax.ShapeDtypeStruct(a.shape, a.dtype) for a in outs],
        in_specs=[hbm] * (len(passed) + len(grads) + len(old)),
        out_specs=[hbm] * len(outs),
        scratch_shapes=[pltpu.VMEM(a.shape, a.dtype) for a in (*passed, *grads, *old)]
        + [pltpu.SemaphoreType.DMA((loads,)), pltpu.SemaphoreType.DMA((2 + 6 * cut + 12,))],
        compiler_params=pltpu.CompilerParams(vmem_limit_bytes=60 * 1024 * 1024),
        name="update",
    )(*passed, *grads, *old)


def mixed_dot(left, right):
    return jnp.dot(left, right, preferred_element_type=jnp.float32)


def rms_scale(vector, gain_vec):
    return (
        vector
        * lax.rsqrt(jnp.mean(vector * vector, axis=-1, keepdims=True) + eps_norm)
        * (1.0 + gain_vec)
    )


def rotate(vector, positions):
    half_dim = vector.shape[-1] // 2
    inv_freq = rope_base ** (-2.0 * jnp.arange(half_dim).astype(jnp.float32) / vector.shape[-1])
    angles = positions[:, None] * inv_freq[None, :]
    cosine = jnp.cos(angles)[:, None, :]
    sine_v = jnp.sin(angles)[:, None, :]
    front_half = vector[..., :half_dim]
    back_half = vector[..., half_dim:]
    return jnp.concatenate(
        [front_half * cosine - back_half * sine_v, back_half * cosine + front_half * sine_v],
        axis=-1,
    )


def adam_step(weight, gradient, moment, second, step_rate):
    moment = beta_first * moment + (1.0 - beta_first) * gradient
    second = beta_second * second + (1.0 - beta_second) * gradient * gradient
    scaled = (
        moment
        / (1.0 - beta_first**STEP)
        / (jnp.sqrt(second / (1.0 - beta_second**STEP)) + adam_eps)
    )
    return (moment, second, weight - step_rate * (scaled + decay_rate * weight))


def plain_device(
    tokens,
    cotangent,
    prefix,
    query_weight,
    keyval_weight,
    output_weight,
    gateup_weight,
    down_weight,
    norm_gains,
    query_first,
    keyval_first,
    output_first,
    gateup_first,
    down_first,
    gains_first,
    query_second,
    keyval_second,
    output_second,
    gateup_second,
    down_second,
    gains_second,
):
    rows_dev, width = tokens.shape
    length = rows_dev * lax.axis_size("tensor")
    query_full, keyval_full, output_full, gateup_full, down_full, gains_full = (
        lax.all_gather(query_weight.astype(jnp.bfloat16), "dp", axis=0, tiled=True),
        lax.all_gather(keyval_weight.astype(jnp.bfloat16), "dp", axis=0, tiled=True),
        lax.all_gather(output_weight.astype(jnp.bfloat16), "dp", axis=0, tiled=True),
        lax.all_gather(gateup_weight.astype(jnp.bfloat16), "dp", axis=0, tiled=True),
        lax.all_gather(down_weight.astype(jnp.bfloat16), "dp", axis=0, tiled=True),
        lax.all_gather(norm_gains.astype(jnp.bfloat16), "dp", axis=0, tiled=True),
    )
    head_dim = keyval_full.shape[1] // 2
    heads_dev = query_full.shape[1] // head_dim
    units = down_full.shape[1]
    gain_values = gains_full.astype(jnp.float32)
    gain_input = gain_values[0:width]
    gain_attn = gain_values[width : 2 * width]
    gain_pre = gain_values[2 * width : 3 * width]
    gain_ffn = gain_values[3 * width : 4 * width]
    gain_query = gain_values[4 * width : 4 * width + head_dim]
    gain_key = gain_values[4 * width + head_dim : 4 * width + 2 * head_dim]
    positions = jnp.arange(length).astype(jnp.float32)
    span_rows = min(512, length)
    count_blocks = length // span_rows
    starts = jnp.arange(0, length, span_rows, dtype=jnp.int32)
    columns = jnp.arange(length, dtype=jnp.int32)
    prefix_len = prefix[0]
    gateup_flat = gateup_full.reshape(width, 2 * units)

    def shape_query(raw_rows, gain_vec):
        return rotate(rms_scale(raw_rows, gain_vec), positions)

    def shape_key(raw_rows, gain_vec):
        return rotate(rms_scale(raw_rows[:, None, :], gain_vec), positions)[:, 0]

    token_rows = tokens.astype(jnp.float32)
    normed_local = rms_scale(token_rows, gain_input).astype(jnp.bfloat16)
    normed = lax.all_gather(normed_local, "tensor", axis=0, tiled=True)
    query_raw = mixed_dot(normed, query_full).reshape(length, heads_dev, head_dim)
    keyval_raw = mixed_dot(normed, keyval_full)
    query_rot = shape_query(query_raw, gain_query).astype(jnp.bfloat16)
    key_rot = shape_key(keyval_raw[:, :head_dim], gain_key).astype(jnp.bfloat16)
    value_low = keyval_raw[:, head_dim:].astype(jnp.bfloat16)

    def scores_of(row_start):
        row_ids = row_start + jnp.arange(span_rows, dtype=jnp.int32)
        q_blk = lax.dynamic_slice_in_dim(query_rot, row_start, span_rows, 0)
        raw_scores = (
            jnp.einsum("rhd,kd->hrk", q_blk, key_rot, preferred_element_type=jnp.float32)
            * query_scale
        )
        allowed = (columns[None, :] <= row_ids[:, None]) | (columns[None, :] < prefix_len)
        return (jnp.where(allowed[None], raw_scores, masked_fill), q_blk)

    def forward_block(row_start):
        scores, q_blk = scores_of(row_start)
        row_peak = jnp.max(scores, axis=-1, keepdims=True)
        shifted = jnp.exp(scores - row_peak)
        denom_sum = jnp.sum(shifted, axis=-1, keepdims=True)
        soft_probs = (shifted / denom_sum).astype(jnp.bfloat16)
        mixed_rows = jnp.einsum(
            "hrk,kd->rhd", soft_probs, value_low, preferred_element_type=jnp.float32
        )
        return (mixed_rows, (row_peak + jnp.log(denom_sum))[..., 0])

    attended_blocks, log_sums = lax.map(forward_block, starts)
    attended = attended_blocks.reshape(length, heads_dev * head_dim).astype(jnp.bfloat16)
    attn_part = jnp.einsum("rk,dk->rd", attended, output_full, preferred_element_type=jnp.float32)
    projected = lax.psum_scatter(
        attn_part.astype(jnp.bfloat16), "tensor", scatter_dimension=0, tiled=True
    ).astype(jnp.float32)
    hidden_state = token_rows + rms_scale(projected, gain_attn)
    normed_two = lax.all_gather(
        rms_scale(hidden_state, gain_pre).astype(jnp.bfloat16), "tensor", axis=0, tiled=True
    )
    gateup = mixed_dot(normed_two, gateup_flat)
    gate_part = gateup[:, :units]
    up_part = gateup[:, units:]
    activation = (jax.nn.gelu(gate_part, approximate=True) * up_part).astype(jnp.bfloat16)
    down_part = jnp.einsum("ru,du->rd", activation, down_full, preferred_element_type=jnp.float32)
    down_sum = lax.psum_scatter(
        down_part.astype(jnp.bfloat16), "tensor", scatter_dimension=0, tiled=True
    ).astype(jnp.float32)
    block_out = hidden_state + rms_scale(down_sum, gain_ffn)
    grad_out = cotangent.astype(jnp.float32)
    pull_ffn = jax.vjp(rms_scale, down_sum, gain_ffn)[1]
    grad_down, grad_gain_ffn = pull_ffn(grad_out)
    down_back = lax.all_gather(grad_down.astype(jnp.bfloat16), "tensor", axis=0, tiled=True)
    grad_activation = mixed_dot(down_back, down_full)
    grad_down_w = jnp.einsum("rd,ru->du", down_back, activation, preferred_element_type=jnp.float32)

    def geglu(gate_in, up_in):
        return jax.nn.gelu(gate_in, approximate=True) * up_in

    pull_act = jax.vjp(geglu, gate_part, up_part)[1]
    grad_gate, grad_up = pull_act(grad_activation)
    grad_gateup = jnp.concatenate([grad_gate, grad_up], axis=1).astype(jnp.bfloat16)
    grad_gateup_w = jnp.einsum(
        "rd,ru->du", normed_two, grad_gateup, preferred_element_type=jnp.float32
    ).reshape(width, 2, units)
    grad_normed_two = jnp.einsum(
        "ru,du->rd", grad_gateup, gateup_flat, preferred_element_type=jnp.float32
    )
    grad_pre_rows = lax.psum_scatter(
        grad_normed_two.astype(jnp.bfloat16), "tensor", scatter_dimension=0, tiled=True
    ).astype(jnp.float32)
    pull_pre = jax.vjp(rms_scale, hidden_state, gain_pre)[1]
    grad_hidden_norm, grad_gain_pre = pull_pre(grad_pre_rows)
    grad_hidden = grad_out + grad_hidden_norm
    pull_attn = jax.vjp(rms_scale, projected, gain_attn)[1]
    grad_proj, grad_gain_attn = pull_attn(grad_hidden)
    proj_back = lax.all_gather(grad_proj.astype(jnp.bfloat16), "tensor", axis=0, tiled=True)
    grad_output_w = jnp.einsum("rd,rk->dk", proj_back, attended, preferred_element_type=jnp.float32)
    grad_attended = (
        mixed_dot(proj_back, output_full)
        .astype(jnp.bfloat16)
        .reshape(count_blocks, span_rows, heads_dev, head_dim)
    )

    def backward_block(carry, batch_item):
        key_acc, value_acc = carry
        row_start, grad_att, lse_blk = batch_item
        scores, q_blk = scores_of(row_start)
        soft_full = jnp.exp(scores - lse_blk[..., None])
        grad_probs = jnp.einsum(
            "rhd,kd->hrk", grad_att, value_low, preferred_element_type=jnp.float32
        )
        delta_rows = jnp.sum(soft_full * grad_probs, axis=-1, keepdims=True)
        grad_scores = (soft_full * (grad_probs - delta_rows)).astype(jnp.bfloat16)
        grad_query = (
            jnp.einsum("hrk,kd->rhd", grad_scores, key_rot, preferred_element_type=jnp.float32)
            * query_scale
        )
        key_acc = (
            key_acc
            + jnp.einsum("hrk,rhd->kd", grad_scores, q_blk, preferred_element_type=jnp.float32)
            * query_scale
        )
        value_acc = value_acc + jnp.einsum(
            "hrk,rhd->kd",
            soft_full.astype(jnp.bfloat16),
            grad_att,
            preferred_element_type=jnp.float32,
        )
        return ((key_acc, value_acc), grad_query)

    zero_rows = jnp.zeros((length, head_dim), jnp.float32)
    (grad_key_rot, grad_value), grad_query_blocks = lax.scan(
        backward_block, (zero_rows, zero_rows), (starts, grad_attended, log_sums)
    )
    grad_query_rot = grad_query_blocks.reshape(length, heads_dev, head_dim)
    pull_query = jax.vjp(shape_query, query_raw, gain_query)[1]
    grad_query_raw, grad_gain_query = pull_query(grad_query_rot)
    pull_key = jax.vjp(shape_key, keyval_raw[:, :head_dim], gain_key)[1]
    grad_key_raw, grad_gain_key = pull_key(grad_key_rot)
    grad_query_low = grad_query_raw.reshape(length, heads_dev * head_dim).astype(jnp.bfloat16)
    grad_keyval = jnp.concatenate([grad_key_raw, grad_value], axis=1)
    grad_query_w = jnp.einsum(
        "rd,rk->dk", normed, grad_query_low, preferred_element_type=jnp.float32
    )
    grad_normed_query = jnp.einsum(
        "rk,dk->rd", grad_query_low, query_full, preferred_element_type=jnp.float32
    )
    grad_normed_part, grad_keyval_own = (
        lax.psum_scatter(
            grad_normed_query.astype(jnp.bfloat16), "tensor", scatter_dimension=0, tiled=True
        ).astype(jnp.float32),
        lax.psum_scatter(
            grad_keyval.astype(jnp.bfloat16), "tensor", scatter_dimension=0, tiled=True
        ).astype(jnp.float32),
    )
    grad_keyval_low = grad_keyval_own.astype(jnp.bfloat16)
    grad_keyval_w = jnp.einsum(
        "rd,rk->dk", normed_local, grad_keyval_low, preferred_element_type=jnp.float32
    )
    grad_normed = grad_normed_part + jnp.einsum(
        "rk,dk->rd", grad_keyval_low, keyval_full, preferred_element_type=jnp.float32
    )
    pull_input = jax.vjp(rms_scale, token_rows, gain_input)[1]
    grad_token_norm, grad_gain_input = pull_input(grad_normed)
    tokens_grad = (grad_hidden + grad_token_norm).astype(jnp.bfloat16)
    grad_gains = jnp.concatenate(
        [
            grad_gain_input,
            grad_gain_attn,
            grad_gain_pre,
            grad_gain_ffn,
            grad_gain_query,
            grad_gain_key,
        ]
    )
    keyval_total, gains_total = (
        lax.psum(grad_keyval_w.astype(jnp.bfloat16), "tensor").astype(jnp.float32),
        lax.psum(grad_gains.astype(jnp.bfloat16), "tensor").astype(jnp.float32),
    )
    query_sum, keyval_sum, output_sum, gateup_sum, down_grad_sum, gains_sum = (
        lax.psum_scatter(grad_query_w, "dp", scatter_dimension=0, tiled=True),
        lax.psum_scatter(keyval_total, "dp", scatter_dimension=0, tiled=True),
        lax.psum_scatter(grad_output_w, "dp", scatter_dimension=0, tiled=True),
        lax.psum_scatter(grad_gateup_w, "dp", scatter_dimension=0, tiled=True),
        lax.psum_scatter(grad_down_w, "dp", scatter_dimension=0, tiled=True),
        lax.psum_scatter(gains_total, "dp", scatter_dimension=0, tiled=True),
    )
    query_moment, query_square, query_master = adam_step(
        query_weight, query_sum, query_first, query_second, D ** (-0.5)
    )
    keyval_moment, keyval_square, keyval_master = adam_step(
        keyval_weight, keyval_sum, keyval_first, keyval_second, D ** (-0.5)
    )
    output_moment, output_square, output_master = adam_step(
        output_weight, output_sum, output_first, output_second, (HEADS * HEAD_DIM) ** (-0.5)
    )
    gateup_moment, gateup_square, gateup_master = adam_step(
        gateup_weight, gateup_sum, gateup_first, gateup_second, D ** (-0.5)
    )
    down_moment, down_square, down_master = adam_step(
        down_weight, down_grad_sum, down_first, down_second, FF ** (-0.5)
    )
    gains_moment, gains_square, gains_master = adam_step(
        norm_gains, gains_sum, gains_first, gains_second, 0.3
    )
    return (
        block_out.astype(jnp.bfloat16),
        tokens_grad,
        query_moment,
        query_square,
        query_master,
        keyval_moment,
        keyval_square,
        keyval_master,
        output_moment,
        output_square,
        output_master,
        gateup_moment,
        gateup_square,
        gateup_master,
        down_moment,
        down_square,
        down_master,
        gains_moment,
        gains_square,
        gains_master,
    )


def per_device(
    tokens,
    cotangent,
    prefix,
    query_weight,
    keyval_weight,
    output_weight,
    gateup_weight,
    down_weight,
    norm_gains,
    query_first,
    keyval_first,
    output_first,
    gateup_first,
    down_first,
    gains_first,
    query_second,
    keyval_second,
    output_second,
    gateup_second,
    down_second,
    gains_second,
):
    rows, width = tokens.shape
    lines = lax.axis_size("dp") // 2
    shard = query_weight.shape[0]
    head_dim = keyval_weight.shape[1] // 2
    units = down_weight.shape[1]
    fits = (
        lax.axis_size("tensor") == 4
        and lax.axis_size("dp") == 8
        and len(chunks_of(units)) == 4
        and query_weight.shape[1] == head_dim
        and shard % 16 == 0
        and norm_gains.shape[0] % 128 == 0
        and (3 * len(chunks_of(units)) + 2) // 2 * shard <= 4 * rows
    )
    if not fits:
        return plain_device(
            tokens,
            cotangent,
            prefix,
            query_weight,
            keyval_weight,
            output_weight,
            gateup_weight,
            down_weight,
            norm_gains,
            query_first,
            keyval_first,
            output_first,
            gateup_first,
            down_first,
            gains_first,
            query_second,
            keyval_second,
            output_second,
            gateup_second,
            down_second,
            gains_second,
        )
    length = 4 * rows
    sizes = (lines, rows, width, head_dim, units)
    weights = (keyval_weight, query_weight, output_weight, gateup_weight, down_weight)
    angles = np.arange(length)[:, None] * (rope_base ** (-2.0 * np.arange(head_dim // 2) / head_dim))[None, :]
    cosine = jnp.asarray(np.cos(angles), full)
    sine = jnp.asarray(np.sin(angles), full)
    *saved, gvec, proj, hidden, grad_down, dgain_ffn, block_out = forward_call(
        sizes, prefix, tokens, cotangent, norm_gains, weights, cosine, sine
    )
    *grads, tokens_grad, keyval_sum, gains_sum = backward_call(
        sizes, (grad_down, cotangent, tokens, gvec, dgain_ffn, proj, hidden, cosine, sine), saved
    )
    old = (
        query_weight,
        query_first,
        query_second,
        keyval_weight,
        keyval_first,
        keyval_second,
        output_weight,
        output_first,
        output_second,
        gateup_weight,
        gateup_first,
        gateup_second,
        down_weight,
        down_first,
        down_second,
        norm_gains,
        gains_first,
        gains_second,
    )
    return tuple(update_call(units, head_dim, (block_out, tokens_grad), (*grads, keyval_sum, gains_sum), old, 3))


def solution(mesh):
    placed = (
        P(("dp", "tensor"), None),
        P(("dp", "tensor"), None),
        P("dp"),
        P("dp", "tensor"),
        P("dp", None),
        P("dp", "tensor"),
        P("dp", None, "tensor"),
        P("dp", "tensor"),
        P("dp"),
        P("dp", "tensor"),
        P("dp", None),
        P("dp", "tensor"),
        P("dp", None, "tensor"),
        P("dp", "tensor"),
        P("dp"),
        P("dp", "tensor"),
        P("dp", None),
        P("dp", "tensor"),
        P("dp", None, "tensor"),
        P("dp", "tensor"),
        P("dp"),
    )
    return jax.shard_map(
        per_device,
        mesh=mesh,
        in_specs=placed,
        out_specs=(
            P(("dp", "tensor"), None),
            P(("dp", "tensor"), None),
            P("dp", "tensor"),
            P("dp", "tensor"),
            P("dp", "tensor"),
            P("dp", None),
            P("dp", None),
            P("dp", None),
            P("dp", "tensor"),
            P("dp", "tensor"),
            P("dp", "tensor"),
            P("dp", None, "tensor"),
            P("dp", None, "tensor"),
            P("dp", None, "tensor"),
            P("dp", "tensor"),
            P("dp", "tensor"),
            P("dp", "tensor"),
            P("dp"),
            P("dp"),
            P("dp"),
        ),
        check_vma=False,
    )
```

```python
import functools

import jax
import jax.numpy as jnp
import numpy as np
from jax import lax
from jax.experimental import pallas as pl
from jax.experimental.pallas import tpu as pltpu
from jax.sharding import PartitionSpec as P

D = 1152
FF = 6912
HEADS = 4
HEAD_DIM = 256
STEP = 10


eps_norm = 1e-06
query_scale = 0.0625
rope_base = 1000000.0
beta_first = 0.9
beta_second = 0.95
adam_eps = 1e-08
decay_rate = 0.01
masked_fill = -1e30
MESH = pl.DeviceIdType.MESH
low = jnp.bfloat16
full = jnp.float32
CHUNK = 512


def dot_nn(left, right):
    return lax.dot_general(left, right, (((1,), (0,)), ((), ())), preferred_element_type=full)


def dot_nt(left, right):
    return lax.dot_general(left, right, (((1,), (1,)), ((), ())), preferred_element_type=full)


def dot_tn(left, right):
    return lax.dot_general(left, right, (((0,), (0,)), ((), ())), preferred_element_type=full)


def chunks_of(units):
    out = []
    first = 0
    while first < units:
        width = min(CHUNK, units - first)
        out.append((first, width, -(-width // 128) * 128))
        first += width
    return out


def small_columns(head_dim):
    return 2 * head_dim, 3 * head_dim, 4 * head_dim


def packed_columns(units, head_dim):
    at = small_columns(head_dim)[2]
    places = []
    for first, width, _ in chunks_of(units):
        places.append((at, at + width, at + 2 * width))
        at += -(-3 * width // 128) * 128
    return places, at


class Place:
    def __init__(self):
        self.dp = lax.axis_index("dp")
        self.tensor = lax.axis_index("tensor")
        self.z = self.dp // 2
        self.x = self.dp % 2
        self.y = self.tensor // 2
        self.core = self.tensor % 2
        self.homes = (self.z, self.z + 1 - 2 * (self.z % 2), (self.z + 2) % 4, 3 - self.z)
        self.end = ((self.z + 1) // 2 + 1) % 2
        self.middle = self.end == 0
        self.mate = (self.dp, self.y * 2 + (1 - self.core))
        self.across = (self.dp, (1 - self.y) * 2 + self.core)
        self.side = (self.z * 2 + (1 - self.x), self.tensor)
        self.inner = ((1 + self.z % 2) * 2 + self.x, self.tensor)

    def line(self, step):
        return (self.homes[step] * 2 + self.x, self.tensor)

    def peers(self):
        return [self.mate, self.across, self.side] + [self.line(s) for s in (1, 2, 3)]


def greet(place):
    for peer in place.peers():
        pl.semaphore_signal(pltpu.get_barrier_semaphore(), inc=1, device_id=peer, device_id_type=MESH)


def meet(place):
    pl.semaphore_wait(pltpu.get_barrier_semaphore(), len(place.peers()))


def remote(source, target, send_sem, recv_sem, device):
    return pltpu.make_async_remote_copy(
        src_ref=source,
        dst_ref=target,
        send_sem=send_sem,
        recv_sem=recv_sem,
        device_id=device,
        device_id_type=MESH,
    )


class LineGather:
    def __init__(self, place, region, wide, send, recv, relay_send, side_send, side_recv):
        self.place, self.region, self.wide = place, region, wide
        self.send, self.recv, self.relay_send = send, recv, relay_send
        self.side_send, self.side_recv = side_send, side_recv

    def columns(self, group):
        return (0, 1) if self.wide[group] else (0,)

    def origin(self, column, step):
        place = self.place
        return place.homes[step] * 2 + (place.x if column == 0 else 1 - place.x)

    def along(self, group, column, step):
        block = self.region(group, self.origin(column, 0))
        return remote(
            block, block, self.send.at[group, column, step], self.recv.at[group, column, step], self.place.line(step)
        )

    def arrive(self, group, column, step):
        block = self.region(group, self.origin(column, step))
        remote(
            block, block, self.send.at[group, column, step], self.recv.at[group, column, step], self.place.line(step)
        ).wait_recv()

    def relay(self, group, column):
        block = self.region(group, self.origin(column, 2))
        return remote(
            block, block, self.relay_send.at[group, column], self.recv.at[group, column, 3], self.place.line(1)
        )

    def sideways(self, group, step):
        block = self.region(group, self.origin(0, step))
        return remote(
            block, block, self.side_send.at[group, step], self.side_recv.at[group, step], self.place.side
        )

    def arrive_side(self, group, step):
        block = self.region(group, self.origin(1, step))
        remote(
            block, block, self.side_send.at[group, step], self.side_recv.at[group, step], self.place.side
        ).wait_recv()

    def start_line(self, group, column):
        self.along(group, column, 2).start()
        self.along(group, column, 1).start()

        @pl.when(self.place.middle)
        def _():
            self.along(group, column, 3).start()

    def start_side(self, group):
        self.sideways(group, 0).start()

    def start(self, group):
        self.start_side(group)
        self.start_line(group, 0)

    def widen(self, group):
        self.arrive_side(group, 0)
        self.start_line(group, 1)

    def pass_on(self, group, *columns):
        for column in columns or self.columns(group):
            self.arrive(group, column, 2)

            @pl.when(self.place.middle)
            def _():
                self.relay(group, column).start()

            if not self.wide[group]:
                self.sideways(group, 2).start()

    def collect(self, group):
        for column in self.columns(group):
            for step in (1, 3):
                self.arrive(group, column, step)
                if not self.wide[group]:
                    self.sideways(group, step).start()

    def ready(self, group):
        if not self.wide[group]:
            for step in (0, 2, 1, 3):
                self.arrive_side(group, step)

    def finish(self):
        for group in range(len(self.wide)):
            for column in self.columns(group):
                self.along(group, column, 1).wait_send()
                self.along(group, column, 2).wait_send()

                @pl.when(self.place.middle)
                def _():
                    self.along(group, column, 3).wait_send()
                    self.relay(group, column).wait_send()

            for step in (0,) if self.wide[group] else (0, 1, 2, 3):
                self.sideways(group, step).wait_send()


def row_slabs(buffer, rows):
    return lambda y, core: buffer.at[pl.ds((y * 2 + core) * rows, rows)]


def column_slabs(buffer, wide):
    return lambda y, core: buffer.at[:, pl.ds(pl.multiple_of((y * 2 + core) * wide, wide), wide)]


class RowGather:
    def __init__(self, place, source, slab, send, recv):
        self.place, self.source, self.slab = place, source, slab
        self.send, self.recv = send, recv

    def copy(self, index):
        place = self.place
        slab = self.slab(1 - place.y if index == 2 else place.y, place.core)
        source = slab if index == 2 else self.source
        device = place.across if index == 1 else place.mate
        return remote(source, slab, self.send.at[index], self.recv.at[index], device)

    def arrival(self, index, y, core):
        slab = self.slab(y, core)
        remote(slab, slab, self.send.at[index], self.recv.at[index], self.place.mate).wait_recv()

    def start(self):
        self.copy(1).start()
        self.copy(0).start()

    def wait_mate(self):
        self.arrival(0, self.place.y, 1 - self.place.core)

    def wait_across(self):
        self.arrival(1, 1 - self.place.y, self.place.core)
        self.copy(2).start()

    def wait_corner(self):
        self.arrival(2, 1 - self.place.y, 1 - self.place.core)

    def finish(self):
        for index in range(3):
            self.copy(index).wait_send()


class RowScatter:
    def __init__(self, place, part, rows, first, second, mixed, send, recv):
        self.place, self.part, self.rows = place, part, rows
        self.first, self.second, self.mixed = first, second, mixed
        self.send, self.recv = send, recv

    def slab(self, y, core):
        return self.part.at[pl.ds((y * 2 + core) * self.rows, self.rows)]

    def copy(self, index):
        place = self.place
        if index == 2:
            return remote(self.mixed, self.second, self.send.at[2], self.recv.at[2], place.across)
        source = self.slab(1 - place.y if index == 0 else place.y, 1 - place.core)
        return remote(source, self.first.at[index], self.send.at[index], self.recv.at[index], place.mate)

    def order(self):
        place = self.place
        return (
            (1 - place.y) * 2 + (1 - place.core),
            (1 - place.y) * 2 + place.core,
            place.y * 2 + (1 - place.core),
            place.y * 2 + place.core,
        )

    def after(self, step):
        if step == 0:
            self.copy(0).start()
        if step == 1:
            self.copy(0).wait_recv()
            mixed = self.slab(1 - self.place.y, self.place.core)[...].astype(full) + self.first[0].astype(full)
            self.mixed[...] = mixed.astype(low)
            self.copy(2).start()
        if step == 2:
            self.copy(1).start()

    def total(self):
        self.copy(1).wait_recv()
        here = self.slab(self.place.y, self.place.core)[...].astype(full) + self.first[1].astype(full)
        self.copy(2).wait_recv()
        return here + self.second[...].astype(full)

    def finish(self):
        for index in range(3):
            self.copy(index).wait_send()


def inverse_rms(rows):
    return lax.rsqrt(jnp.mean(rows * rows, axis=-1, keepdims=True) + eps_norm)


def rotate_rows(rows, cosine, sine):
    half = rows.shape[-1] // 2
    front, back = rows[:, :half], rows[:, half:]
    return jnp.concatenate([front * cosine - back * sine, back * cosine + front * sine], axis=-1)


def rotate_back(rows, cosine, sine):
    half = rows.shape[-1] // 2
    front, back = rows[:, :half], rows[:, half:]
    return jnp.concatenate([front * cosine + back * sine, back * cosine - front * sine], axis=-1)


def gelu_parts(gate):
    scale = 0.7978845608028654
    square = gate * gate
    bent = jnp.tanh(scale * gate * (1.0 + 0.044715 * square))
    return square, bent


def forward_kernel(
    sizes,
    prefix_ref,
    tokens_in,
    cot_in,
    gains_in,
    keyval_in,
    query_in,
    output_in,
    gateup_in,
    down_in,
    cos_in,
    sin_in,
    wall_out,
    normed_out,
    normed_two_out,
    query_out,
    key_out,
    key_rot_out,
    value_out,
    attended_out,
    probs_out,
    gate_out,
    up_out,
    act_out,
    gvec_out,
    proj_out,
    hidden_out,
    grad_down_out,
    dgain_ffn_out,
    block_out_out,
    cot_ref,
    gains_ref,
    keyval_ref,
    query_ref,
    output_ref,
    gateup_ref,
    down_ref,
    cos_ref,
    sin_ref,
    gvec,
    proj_keep,
    hidden_keep,
    grad_down,
    dgain_ffn,
    block_out,
    wall,
    normed,
    normed_two,
    query_raw,
    key_raw,
    attended,
    probs,
    gate_keep,
    up_keep,
    act,
    tok_full,
    gains_full,
    key_rot,
    value_low,
    part_one,
    first_one,
    second_one,
    mixed_one,
    down_acc,
    line_send,
    line_recv,
    relay_send,
    side_send,
    side_recv,
    row_send,
    row_recv,
    keep_sem,
    load_sem,
):
    lines, rows, width, head_dim, units = sizes
    place = Place()
    greet(place)
    own_rows = pl.ds(place.tensor * rows, rows)
    loads = {}
    for name, source, target in (
        ("gains", gains_in, gains_ref),
        ("keyval", keyval_in, keyval_ref),
        ("query", query_in, query_ref),
        ("output", output_in, output_ref),
        ("gateup", gateup_in, gateup_ref),
        ("down", down_in, down_ref),
        ("tokens", tokens_in, tok_full.at[own_rows]),
        ("cos", cos_in, cos_ref),
        ("sin", sin_in, sin_ref),
        ("cot", cot_in, cot_ref),
    ):
        loads[name] = pltpu.make_async_copy(source, target, load_sem.at[len(loads)])
        loads[name].start()
    length = 4 * rows
    shard = keyval_ref.shape[0]
    places, columns = packed_columns(units, head_dim)
    chunks = chunks_of(units)
    last = len(chunks) - 1
    kv_end, query_end, output_end = small_columns(head_dim)
    split, split_last = places[last - 1][2] + 128, places[last][2] // 128 * 128
    quarter = kv_end // 4
    own_quarter = pl.ds(pl.multiple_of(place.tensor * quarter, quarter), quarter)
    spans = [(0, kv_end), (kv_end, output_end)]
    spans += [(places[c][0], places[c + 1][0]) for c in range(last - 2)]
    spans += [(places[last - 2][0], places[last - 2][2]), (places[last - 1][0], split)]
    spans += [(places[last - 2][2], places[last - 1][0]), (split, split_last), (split_last, columns)]
    tail = len(spans)

    def region(group, origin):
        if group == 0:
            return gains_full.at[pl.ds(origin * 8, 8)]
        if group == 1:
            return wall.at[pl.ds(origin * shard, shard), own_quarter]
        lo, hi = spans[group - 1]
        return wall.at[pl.ds(origin * shard, shard), lo:hi]

    wide_groups = [False] * (tail - 1) + [True] * 2
    gather = LineGather(place, region, wide_groups, line_send, line_recv, relay_send, side_send, side_recv)
    tokens_all = RowGather(place, tokens_in, row_slabs(tok_full, rows), row_send.at[0], row_recv.at[0])
    kept = []

    def keep(source, target):
        copy = pltpu.make_async_copy(source, target, keep_sem.at[len(kept)])
        copy.start()
        kept.append(copy)

    def keep_span(group):
        lo, hi = spans[group - 1]
        keep(wall.at[:, lo:hi], wall_out.at[:, lo:hi])

    for name in ("gains", "keyval", "query", "output"):
        loads[name].wait()
    own_gains = gains_ref[...].astype(low).astype(full).reshape(1, -1)
    gains_full[pl.ds(place.dp * 8, 8)] = jnp.broadcast_to(own_gains, (8, own_gains.shape[1]))
    own = pl.ds(place.dp * shard, shard)
    wall[own, own_quarter] = keyval_ref[:, own_quarter].astype(low)
    wall[own, kv_end:query_end] = query_ref[...].astype(low)
    wall[own, query_end:output_end] = output_ref[...].astype(low)
    meet(place)
    tokens_all.start()
    for group in range(3):
        gather.start(group)
    loads["gateup"].wait()
    loads["down"].wait()
    for (first, wide, _), at in zip(chunks, places):
        for kind, lo in enumerate(at):
            units_here = slice(first, first + wide)
            piece = down_ref[:, units_here] if kind == 2 else gateup_ref[:, kind, units_here]
            wall[own, lo : lo + wide] = piece.astype(low)
    filled = places[last][2] + chunks[last][1]
    if filled < columns:
        wall[own, filled:columns] = jnp.zeros((shard, columns - filled), low)
    gather.start(3)
    for name in ("tokens", "cos", "sin", "cot"):
        loads[name].wait()
    tokens_all.wait_mate()
    tokens_all.wait_across()
    gather.pass_on(0)
    gather.pass_on(1)
    gather.collect(0)
    gather.collect(1)
    tokens_all.wait_corner()
    gather.pass_on(2)
    gather.ready(1)
    quarters = column_slabs(wall, quarter)
    keyval_all = RowGather(
        place, quarters(place.y, place.core), quarters, row_send.at[4], row_recv.at[4]
    )
    keyval_all.start()
    gather.collect(2)
    for group in range(4, tail + 1):
        gather.start_side(group)
    gather.start_line(4, 0)
    gather.ready(0)
    step = gains_ref.shape[0]
    for origin in range(2 * lines):
        gvec[:, origin * step : (origin + 1) * step] = gains_full[origin * 8 : origin * 8 + 8]
    keep(gvec, gvec_out)
    gain_in = 1.0 + gvec[0:1, 0:width]
    gain_attn = 1.0 + gvec[0:1, width : 2 * width]
    gain_pre = 1.0 + gvec[0:1, 2 * width : 3 * width]
    gain_ffn = 1.0 + gvec[0:1, 3 * width : 4 * width]
    gain_query = 1.0 + gvec[0:1, 4 * width : 4 * width + head_dim]
    gain_key = 1.0 + gvec[0:1, 4 * width + head_dim : 4 * width + 2 * head_dim]

    def norm_slab(index, carry):
        at = pl.ds(pl.multiple_of(index * rows, rows), rows)
        x = tok_full[at].astype(full)
        normed[at] = (x * inverse_rms(x) * gain_in).astype(low)
        return carry

    lax.fori_loop(0, 4, norm_slab, 0)
    keep(normed, normed_out)
    keyval_all.wait_mate()
    keyval_all.wait_across()
    gather.ready(2)
    keyval_all.wait_corner()

    def project_slab(index, carry):
        at = pl.ds(pl.multiple_of(index * rows, rows), rows)
        n1 = normed[at]
        query_raw[at] = dot_nn(n1, wall[:, kv_end:query_end])
        kv = dot_nn(n1, wall[:, 0:kv_end])
        k = kv[:, :head_dim]
        key_raw[at] = k
        key_rot[at] = rotate_rows(k * inverse_rms(k) * gain_key, cos_ref[at], sin_ref[at]).astype(low)
        value_low[at] = kv[:, head_dim:].astype(low)
        return carry

    lax.fori_loop(0, 4, project_slab, 0)
    gather.pass_on(3)
    gather.start_line(5, 0)
    keep(query_raw, query_out)
    keep(key_raw, key_out)
    keep(key_rot, key_rot_out)
    keep(value_low, value_out)
    keep_span(1)
    keep_span(2)

    out_scatter = RowScatter(place, part_one, rows, first_one, second_one, mixed_one, row_send.at[1], row_recv.at[1])

    def attend_slab(index):
        at = pl.ds(pl.multiple_of(index * rows, rows), rows)
        q = query_raw[at]
        qr = rotate_rows(q * inverse_rms(q) * gain_query, cos_ref[at], sin_ref[at]).astype(low)
        scores = dot_nt(qr, key_rot[...]) * query_scale
        row_ids = lax.broadcasted_iota(jnp.int32, (rows, length), 0) + index * rows
        columns = lax.broadcasted_iota(jnp.int32, (rows, length), 1)
        allowed = (columns <= row_ids) | (columns < prefix_ref[0])
        scores = jnp.where(allowed, scores, masked_fill)
        shifted = jnp.exp(scores - jnp.max(scores, axis=-1, keepdims=True))
        soft = (shifted / jnp.sum(shifted, axis=-1, keepdims=True)).astype(low)
        probs[at] = soft
        mixed = dot_nn(soft, value_low[...]).astype(low)
        attended[at] = mixed
        part_one[at] = dot_nt(mixed, wall[:, query_end:output_end]).astype(low)

    for step, index in enumerate(out_scatter.order()):
        attend_slab(index)
        out_scatter.after(step)
    keep(probs, probs_out)
    keep(attended, attended_out)
    gather.collect(3)
    gather.pass_on(4)
    for group in range(6, tail + 1):
        gather.start_line(group, 0)
    projected = out_scatter.total()
    out_scatter.finish()
    proj_keep[...] = projected
    hidden = tok_full[own_rows].astype(full) + projected * inverse_rms(projected) * gain_attn
    hidden_keep[...] = hidden
    keep(proj_keep, proj_out)
    keep(hidden_keep, hidden_out)
    normed_two[own_rows] = (hidden * inverse_rms(hidden) * gain_pre).astype(low)
    two_all = RowGather(place, normed_two.at[own_rows], row_slabs(normed_two, rows), row_send.at[2], row_recv.at[2])
    two_all.start()
    gather.collect(4)
    gather.pass_on(5)
    two_all.wait_mate()
    gather.widen(tail - 1)
    gather.widen(tail)
    two_all.wait_across()
    gather.pass_on(6)
    gather.collect(5)
    two_all.wait_corner()
    keep(normed_two, normed_two_out)

    down_scatter = RowScatter(place, part_one, rows, first_one, second_one, mixed_one, row_send.at[3], row_recv.at[3])
    block = 2 * rows

    def feed(c):
        first, wide, padded = chunks[c]
        at_gate, at_up, _ = places[c]

        def feed_rows(index, carry):
            at = pl.ds(pl.multiple_of(index * block, block), block)
            n2 = normed_two[at]
            gate = dot_nn(n2, wall[:, at_gate : at_gate + wide])
            up = dot_nn(n2, wall[:, at_up : at_up + wide])
            gate_keep[at, first : first + wide] = gate.astype(low)
            up_keep[at, first : first + wide] = up.astype(low)
            _, bent = gelu_parts(gate)
            act[at, first : first + wide] = (0.5 * gate * (1.0 + bent) * up).astype(low)
            return carry

        lax.fori_loop(0, 2, feed_rows, 0)
        span = slice(first, first + padded)
        keep(gate_keep.at[:, span], gate_out.at[:, span])
        keep(up_keep.at[:, span], up_out.at[:, span])
        keep(act.at[:, span], act_out.at[:, span])

    def lower(c):
        first, wide, _ = chunks[c]
        at_down = places[c][2]

        def lower_rows(index, carry):
            at = pl.ds(pl.multiple_of(index * block, block), block)
            more = dot_nt(act[at, first : first + wide], wall[:, at_down : at_down + wide])
            down_acc[at] = more if c == 0 else down_acc[at] + more
            return carry

        lax.fori_loop(0, 2, lower_rows, 0)

    gather.ready(3)
    keep_span(3)
    feed(0)
    gather.pass_on(7, 0)
    gather.pass_on(8, 0)
    gather.collect(6)
    lower(0)
    gather.ready(4)
    keep_span(4)
    feed(1)
    gather.ready(5)
    keep_span(5)
    feed(2)
    gather.pass_on(7, 1)
    gather.collect(7)
    keep_span(7)
    feed(3)
    gather.pass_on(8, 1)
    gather.ready(6)
    keep_span(6)
    lower(1)
    lower(2)
    gather.collect(8)
    keep_span(8)
    first, wide, _ = chunks[last]
    at_down = places[last][2]
    for step, index in enumerate(down_scatter.order()):
        at = pl.ds(pl.multiple_of(index * rows, rows), rows)
        part_one[at] = (
            down_acc[at] + dot_nt(act[at, first : first + wide], wall[:, at_down : at_down + wide])
        ).astype(low)
        down_scatter.after(step)
    f = down_scatter.total()
    inv = inverse_rms(f)
    cot = cot_ref[...].astype(full)
    scaled = cot * gain_ffn
    grad_down[...] = (inv * (scaled - f * (inv * inv) * jnp.mean(f * scaled, axis=-1, keepdims=True))).astype(low)
    keep(grad_down, grad_down_out)
    block_out[...] = (hidden_keep[...] + f * inv * gain_ffn).astype(low)
    keep(block_out, block_out_out)
    dgain_ffn[...] = jnp.broadcast_to(jnp.sum(cot * f * inv, axis=0, keepdims=True), dgain_ffn.shape)
    keep(dgain_ffn, dgain_ffn_out)
    gather.finish()
    tokens_all.finish()
    keyval_all.finish()
    two_all.finish()
    down_scatter.finish()
    for copy in kept:
        copy.wait()


def forward_call(sizes, prefix, tokens, cotangent, gains, weights, cosine, sine):
    lines, rows, width, head_dim, units = sizes
    length = 4 * rows
    shard = weights[0].shape[0]
    columns = packed_columns(units, head_dim)[1]
    chunks = chunks_of(units)
    padded = sum(c[2] for c in chunks)
    groups = 5 + len(chunks)
    inputs = (tokens, cotangent, gains, *weights, cosine, sine)
    hbm = pl.BlockSpec(memory_space=pl.ANY)
    large = [
        ((2 * lines * shard, columns), low),
        ((length, width), low),
        ((length, width), low),
        ((length, head_dim), full),
        ((length, head_dim), full),
        ((length, head_dim), low),
        ((length, head_dim), low),
        ((length, head_dim), low),
        ((length, length), low),
        ((length, padded), low),
        ((length, padded), low),
        ((length, padded), low),
    ]
    small = [
        ((8, gains.shape[0] * 2 * lines), full),
        ((rows, width), full),
        ((rows, width), full),
        ((rows, width), low),
        ((8, width), full),
        ((rows, width), low),
    ]
    inside = [large[i] for i in (0, 1, 2, 3, 4, 7, 8, 9, 10, 11)]
    scatter_set = [
        pltpu.VMEM((2, rows, width), low),
        pltpu.VMEM((rows, width), low),
        pltpu.VMEM((rows, width), low),
    ]
    return pl.pallas_call(
        functools.partial(forward_kernel, sizes),
        out_shape=[jax.ShapeDtypeStruct(*item) for item in large + small],
        in_specs=[pl.BlockSpec(memory_space=pltpu.SMEM)] + [hbm] * len(inputs),
        out_specs=[hbm] * (len(large) + len(small)),
        scratch_shapes=[pltpu.VMEM(a.shape, a.dtype) for a in inputs[1:]]
        + [pltpu.VMEM(*item) for item in small + inside]
        + [
            pltpu.VMEM((length, width), low),
            pltpu.VMEM((2 * lines * 8, gains.shape[0]), full),
            pltpu.VMEM((length, head_dim), low),
            pltpu.VMEM((length, head_dim), low),
            pltpu.VMEM((length, width), low),
        ]
        + scatter_set
        + [
            pltpu.VMEM((length, width), full),
            pltpu.SemaphoreType.DMA((groups, 2, lines)),
            pltpu.SemaphoreType.DMA((groups, 2, lines)),
            pltpu.SemaphoreType.DMA((groups, 2)),
            pltpu.SemaphoreType.DMA((groups, lines)),
            pltpu.SemaphoreType.DMA((groups, lines)),
            pltpu.SemaphoreType.DMA((5, 3)),
            pltpu.SemaphoreType.DMA((5, 3)),
            pltpu.SemaphoreType.DMA((19 + 4 * len(chunks),)),
            pltpu.SemaphoreType.DMA((len(inputs),)),
        ],
        compiler_params=pltpu.CompilerParams(
            collective_id=0, has_side_effects=True, vmem_limit_bytes=63 * 1024 * 1024
        ),
        name="forward",
    )(prefix, *inputs)


class LineScatter:
    def __init__(self, place, block, side_block, line_block, wide, side_send, side_recv, line_send, line_recv, kind):
        self.place, self.block, self.side_block, self.line_block = place, block, side_block, line_block
        self.wide, self.kind = wide, kind
        self.side_send, self.side_recv, self.line_send, self.line_recv = side_send, side_recv, line_send, line_recv

    def columns(self, group):
        return (0, 1) if self.wide[group] else (0,)

    def own(self, group, column, step):
        place = self.place
        return self.block(group, place.homes[step] * 2 + (place.x if column == 0 else 1 - place.x))

    def sideways(self, group, step):
        home = 0 if self.wide[group] else self.place.homes[step]
        return remote(
            self.own(group, 1, step),
            self.side_block(group, home),
            self.side_send.at[group, step],
            self.side_recv.at[group, step],
            self.place.side,
        )

    def along(self, group, column, step):
        slot = step - 1 if step < 3 else 2 + self.place.end
        return remote(
            self.own(group, column, step),
            self.line_block(group, column, slot),
            self.line_send.at[group, column, step],
            self.line_recv.at[group, column, slot],
            self.place.line(step) if step < 3 else self.place.inner,
        )

    def arrive(self, group, column, slot):
        here = self.line_block(group, column, slot)
        remote(
            here, here, self.line_send.at[group, column, 1], self.line_recv.at[group, column, slot], self.place.line(1)
        ).wait_recv()
        return here[...].astype(full)

    def start(self, group):
        if not self.wide[group]:
            for step in (3, 1, 2, 0):
                self.sideways(group, step).start()
            return
        for step in (3, 1):
            for column in (0, 1):
                self.along(group, column, step).start()

        @pl.when(self.place.end == 1)
        def _():
            for column in (0, 1):
                self.along(group, column, 2).start()

    def with_side(self, group, step):
        self.sideways(group, step).wait_recv()
        return self.own(group, 0, step)[...].astype(full) + self.side_block(group, self.place.homes[step])[...].astype(
            full
        )

    def pump(self, group, *steps):
        for step in steps or (3, 1, 2):
            self.own(group, 0, step)[...] = self.with_side(group, step).astype(self.kind)
            if step != 2:
                self.along(group, 0, step).start()
                continue

            @pl.when(self.place.end == 1)
            def _():
                self.along(group, 0, 2).start()

    def relay(self, group):
        for column in self.columns(group):

            @pl.when(self.place.middle)
            def _():
                block = self.own(group, column, 2)
                block[...] = (block[...].astype(full) + self.arrive(group, column, 3)).astype(self.kind)
                self.along(group, column, 2).start()

    def hand_over(self, group):
        block = self.own(group, 1, 0)
        both = block[...].astype(full) + self.arrive(group, 1, 0) + self.arrive(group, 1, 1)

        @pl.when(self.place.middle)
        def _():
            block[...] = (both + self.arrive(group, 1, 2)).astype(self.kind)

        @pl.when(self.place.end == 1)
        def _():
            block[...] = both.astype(self.kind)

        self.sideways(group, 0).start()

    def settle(self, group):
        self.sideways(group, 0).wait_recv()
        self.arrive(group, 0, 0)
        self.arrive(group, 0, 1)

        @pl.when(self.place.middle)
        def _():
            self.arrive(group, 0, 2)

    def total(self, group, lo, hi, held):
        parts = [
            self.own(group, 0, 0),
            self.side_block(group, 0 if self.wide[group] else self.place.z),
            self.line_block(group, 0, 0),
            self.line_block(group, 0, 1),
        ]
        first, *others = [part[:, lo:hi].astype(full) for part in parts]
        for other in others:
            first = first + other
        held[...] = first

        @pl.when(self.place.middle)
        def _():
            held[...] = first + self.line_block(group, 0, 2)[:, lo:hi].astype(full)

    def finish(self):
        for group in range(len(self.wide)):
            for step in (0,) if self.wide[group] else (0, 1, 2, 3):
                self.sideways(group, step).wait_send()
            for column in self.columns(group):
                for step in (1, 2, 3):
                    self.along(group, column, step).wait_send()


def norm_back(rows, inv, gain, grad):
    scaled = grad * gain
    back = inv * (scaled - rows * (inv * inv) * jnp.mean(rows * scaled, axis=-1, keepdims=True))
    return back, jnp.sum(grad * rows * inv, axis=0, keepdims=True)


def backward_kernel(
    sizes,
    grad_down_in,
    cot_in,
    tokens_in,
    gvec_in,
    dgain_ffn_in,
    proj_in,
    hidden_in,
    cos_in,
    sin_in,
    wall_in,
    normed_in,
    normed_two_in,
    query_in,
    key_in,
    key_rot_in,
    value_in,
    attended_in,
    probs_in,
    gate_in,
    up_in,
    act_in,
    gate_grad,
    up_grad,
    down_grad,
    small_grad,
    tokens_grad_out,
    keyval_grad,
    gains_grad,
    tokens_grad,
    cot_ref,
    tokens_ref,
    gvec,
    dgain_ffn,
    proj_ref,
    hidden_ref,
    cos_ref,
    sin_ref,
    wall,
    side_buf,
    side_wide,
    line_buf,
    line_wide,
    big,
    normed_two,
    row_buf,
    acc,
    first_buf,
    second_buf,
    mixed_buf,
    key_rot,
    value_low,
    dquery,
    dkeyval,
    dhidden,
    dproj,
    kv_first,
    kv_second,
    kv_mixed,
    kv_own,
    dgains,
    gain_part,
    gain_first,
    gain_second,
    gain_side,
    gain_line,
    row_send,
    row_recv,
    side_send,
    side_recv,
    line_send,
    line_recv,
    gain_side_send,
    gain_side_recv,
    gain_line_send,
    gain_line_recv,
    last_send,
    last_recv,
    load_sem,
    store_sem,
):
    lines, rows, width, head_dim, units = sizes
    place = Place()
    length = 4 * rows
    shard = wall.shape[0] // (2 * lines)
    kv_end, query_end, output_end = small_columns(head_dim)
    quarter = head_dim // 2
    places, columns = packed_columns(units, head_dim)
    chunks = chunks_of(units)
    last = len(chunks) - 1
    order = [0, last] + list(range(1, last))
    base_column = kv_end - quarter
    spans = []
    for c in range(last):
        spans += [(places[c][2], places[c + 1][0]), (places[c][0], places[c][2])]
    group_gate, group_up, group_last, group_small = range(len(spans) - 1, len(spans) + 3)
    spans[-1:] = [(places[last - 1][0], places[last - 1][1]), (places[last - 1][1], places[last - 1][2])]
    spans += [(places[last][0], columns), (base_column, output_end)]
    loads = {}

    def load(name, source, target):
        copy = pltpu.make_async_copy(source, target, load_sem.at[len(loads)])
        copy.start()
        loads[name] = copy

    def load_chunk(c):
        first, _, padded = chunks[c]
        lo, hi = places[c][0], columns if c == last else places[c + 1][0]
        base = (order.index(c) % 2) * 3 * CHUNK
        load(("wall", c), wall_in.at[:, lo:hi], wall.at[:, lo:hi])
        for k, source in enumerate((gate_in, up_in, act_in)):
            at = base + k * CHUNK
            load((k, c), source.at[:, first : first + padded], big.at[:, at : at + padded])

    greet(place)
    own_rows = pl.ds(place.tensor * rows, rows)
    load("own", grad_down_in, row_buf.at[own_rows])
    load_chunk(order[0])
    load("two", normed_two_in, normed_two)
    load("gvec", gvec_in, gvec)
    load("dgain", dgain_ffn_in, dgain_ffn)
    load_chunk(order[1])
    load("hidden", hidden_in, hidden_ref)
    load("cot", cot_in, cot_ref)
    load("proj", proj_in, proj_ref)
    load("tokens", tokens_in, tokens_ref)
    load("cos", cos_in, cos_ref)
    load("sin", sin_in, sin_ref)
    load("kv", wall_in.at[:, 0:kv_end], wall.at[:, 0:kv_end])
    load("qo", wall_in.at[:, kv_end:output_end], wall.at[:, kv_end:output_end])
    load("key_rot", key_rot_in, key_rot)
    load("value", value_in, value_low)
    meet(place)
    down_all = RowGather(place, grad_down_in, row_slabs(row_buf, rows), row_send.at[0], row_recv.at[0])
    down_all.start()
    loads["gvec"].wait()
    loads["dgain"].wait()
    gain_in = 1.0 + gvec[0:1, 0:width]
    gain_attn = 1.0 + gvec[0:1, width : 2 * width]
    gain_pre = 1.0 + gvec[0:1, 2 * width : 3 * width]
    gain_query = 1.0 + gvec[0:1, 4 * width : 4 * width + head_dim]
    gain_key = 1.0 + gvec[0:1, 4 * width + head_dim : 4 * width + 2 * head_dim]
    dgains[...] = jnp.zeros_like(dgains)
    dgains[0:1, 3 * width : 4 * width] = dgain_ffn[0:1]
    loads["own"].wait()
    down_all.wait_mate()
    down_all.wait_across()
    down_all.wait_corner()
    loads["two"].wait()

    def block(group, origin):
        lo, hi = spans[group]
        return wall.at[pl.ds(origin * shard, shard), lo:hi]

    def side_block(group, home):
        if wide_groups[group]:
            return side_wide
        lo, hi = spans[group]
        return side_buf.at[pl.ds(home * shard, shard), lo - base_column : hi - base_column]

    def line_block(group, column, slot):
        lo, hi = spans[group]
        if wide_groups[group]:
            return line_wide.at[pl.ds((column * 4 + slot) * shard, shard)]
        return line_buf.at[pl.ds(slot * shard, shard), lo - base_column : hi - base_column]

    wide_groups = [group == group_last for group in range(len(spans))]
    scatter = LineScatter(
        place, block, side_block, line_block, wide_groups, side_send, side_recv, line_send, line_recv, low
    )
    part = big.at[:, 0:width]
    pre_scatter = RowScatter(place, part, rows, first_buf, second_buf, mixed_buf, row_send.at[1], row_recv.at[1])
    half = 2 * rows
    third = width // 3

    def weight_gradient(lo, wide, left, right):
        for m in range(0, width, third):
            wall[m : m + third, lo : lo + wide] = dot_tn(left[:, m : m + third], right).astype(low)

    for position, c in enumerate(order):
        first, wide, padded = chunks[c]
        at_gate, at_up, at_down = places[c]
        base = (position % 2) * 3 * CHUNK
        loads["wall", c].wait()
        for k in range(3):
            loads[k, c].wait()
        if 1 <= position < last:
            load_chunk(order[position + 1])
        of_gate = slice(base, base + wide)
        of_up = slice(base + CHUNK, base + CHUNK + wide)
        of_act = slice(base + 2 * CHUNK, base + 2 * CHUNK + wide)

        def unit_rows(index, carry):
            at = pl.ds(pl.multiple_of(index * half, half), half)
            dz = dot_nn(row_buf[at], wall[:, at_down : at_down + wide])
            gate = big[at, of_gate].astype(full)
            up = big[at, of_up].astype(full)
            square, bent = gelu_parts(gate)
            middle = 0.5 * (1.0 + bent)
            slope = middle + 0.5 * gate * (1.0 - bent * bent) * (0.7978845608028654 * (1.0 + 0.134145 * square))
            big[at, of_gate] = (dz * up * slope).astype(low)
            big[at, of_up] = (dz * gate * middle).astype(low)
            return carry

        lax.fori_loop(0, 2, unit_rows, 0)
        weight_gradient(at_down, wide, row_buf, big[:, of_act])
        if c < last:
            scatter.start(2 * c)

        def back_rows(at):
            more = dot_nt(big[at, of_gate], wall[:, at_gate : at_gate + wide])
            more = more + dot_nt(big[at, of_up], wall[:, at_up : at_up + wide])
            return more if position == 0 else acc[at] + more

        if position < last:

            def collect_rows(index, carry):
                at = pl.ds(pl.multiple_of(index * half, half), half)
                acc[at] = back_rows(at)
                return carry

            lax.fori_loop(0, 2, collect_rows, 0)
        else:
            down_all.finish()
            for step, index in enumerate(pre_scatter.order()):
                at = pl.ds(pl.multiple_of(index * rows, rows), rows)
                part[at] = back_rows(at).astype(low)
                pre_scatter.after(step)
        weight_gradient(at_gate, wide, normed_two, big[:, of_gate])
        weight_gradient(at_up, wide, normed_two, big[:, of_up])
        if c < last:
            scatter.start(2 * c + 1)
        else:
            scatter.pump(0)
            scatter.start(group_last)
        if position == 2:
            scatter.relay(0)
        if position == 3:
            scatter.relay(group_last)
            scatter.pump(1, 3, 1)

    at_normed = width
    at_att = at_normed + width
    load("normed", normed_in, big.at[:, at_normed : at_normed + width])
    load("attended", attended_in, big.at[:, at_att : at_att + head_dim])
    load("query", query_in, acc.at[:, 2 * head_dim : 3 * head_dim])
    load("key", key_in, acc.at[:, 3 * head_dim : 4 * head_dim])

    scatter.pump(1, 2)
    dn2 = pre_scatter.total()
    for name in ("hidden", "cot", "proj", "tokens", "cos", "sin"):
        loads[name].wait()
    hidden = hidden_ref[...]
    back, grad = norm_back(hidden, inverse_rms(hidden), gain_pre, dn2)
    dgains[0:1, 2 * width : 3 * width] = grad
    dh = cot_ref[...].astype(full) + back
    dhidden[...] = dh
    proj = proj_ref[...]
    back, grad = norm_back(proj, inverse_rms(proj), gain_attn, dh)
    dgains[0:1, width : 2 * width] = grad
    dproj[...] = back.astype(low)
    row_buf[own_rows] = dproj[...]
    proj_all = RowGather(place, dproj, row_slabs(row_buf, rows), row_send.at[2], row_recv.at[2])
    proj_all.start()
    pre_scatter.finish()
    load("probs", probs_in, big.at[:, 0:length])
    acc[:, 0 : 2 * head_dim] = jnp.zeros((length, 2 * head_dim), full)
    proj_all.wait_mate()
    scatter.pump(2)
    proj_all.wait_across()
    scatter.relay(1)
    proj_all.wait_corner()
    for name in ("kv", "qo", "key_rot", "value", "normed", "attended", "query", "key", "probs"):
        loads[name].wait()

    def attend_back(index, carry):
        at = pl.ds(pl.multiple_of(index * rows, rows), rows)
        da = dot_nn(row_buf[at], wall[:, query_end:output_end]).astype(low)
        soft = big[at, 0:length]
        wide_soft = soft.astype(full)
        dp = dot_nt(da, value_low[...])
        ds = (wide_soft * (dp - jnp.sum(wide_soft * dp, axis=-1, keepdims=True))).astype(low)
        q = acc[at, 2 * head_dim : 3 * head_dim]
        inv = inverse_rms(q)
        cosine, sine = cos_ref[at], sin_ref[at]
        qr = rotate_rows(q * inv * gain_query, cosine, sine).astype(low)
        dqr = dot_nn(ds, key_rot[...]) * query_scale
        acc[:, 0:head_dim] += dot_tn(ds, qr)
        acc[:, head_dim : 2 * head_dim] += dot_tn(soft, da)
        dq, grad = norm_back(q, inv, gain_query, rotate_back(dqr, cosine, sine))
        dquery[at] = dq.astype(low)
        dgains[0:1, 4 * width : 4 * width + head_dim] += grad
        return carry

    scatter.hand_over(group_last)
    scatter.pump(3, 3)
    lax.fori_loop(0, 4, attend_back, 0)

    def key_back(index, carry):
        at = pl.ds(pl.multiple_of(index * rows, rows), rows)
        k = acc[at, 3 * head_dim : 4 * head_dim]
        dkr = rotate_back(acc[at, 0:head_dim] * query_scale, cos_ref[at], sin_ref[at])
        dk, grad = norm_back(k, inverse_rms(k), gain_key, dkr)
        dkeyval[at, 0:head_dim] = dk.astype(low)
        dkeyval[at, head_dim : 2 * head_dim] = acc[at, head_dim : 2 * head_dim].astype(low)
        dgains[0:1, 4 * width + head_dim : 4 * width + 2 * head_dim] += grad
        return carry

    lax.fori_loop(0, 4, key_back, 0)
    scatter.pump(3, 1)
    in_scatter = RowScatter(place, part, rows, first_buf, second_buf, mixed_buf, row_send.at[3], row_recv.at[3])
    for step, index in enumerate(in_scatter.order()):
        at = pl.ds(pl.multiple_of(index * rows, rows), rows)
        more = dot_nt(dquery[at], wall[:, kv_end:query_end]) + dot_nt(dkeyval[at], wall[:, 0:kv_end])
        part[at] = more.astype(low)
        in_scatter.after(step)
    scatter.pump(3, 2)
    scatter.relay(2)

    normed = big.at[:, at_normed : at_normed + width]
    for m in range(0, width, third):
        wall[m : m + third, 0:kv_end] = dot_tn(normed[:, m : m + third], dkeyval[...]).astype(low)

    def kv_block(y, core):
        return wall.at[:, pl.ds(pl.multiple_of((y * 2 + core) * quarter, quarter), quarter)]

    def kv_copy(index):
        send, recv = last_send.at[index], last_recv.at[index]
        if index == 2:
            return remote(kv_mixed, kv_second, send, recv, place.across)
        return remote(
            kv_block(1 - place.y if index == 0 else place.y, 1 - place.core), kv_first.at[index], send, recv, place.mate
        )

    kv_copy(0).start()
    kv_copy(1).start()
    weight_gradient(kv_end, head_dim, normed, dquery[...])
    weight_gradient(query_end, head_dim, row_buf, big[:, at_att : at_att + head_dim])
    kv_copy(0).wait_recv()
    kv_mixed[...] = (kv_block(1 - place.y, place.core)[...].astype(full) + kv_first[0].astype(full)).astype(low)
    kv_copy(2).start()
    scatter.pump(4, 3, 1)
    scatter.relay(3)

    dn1 = in_scatter.total()
    x = tokens_ref[...].astype(full)
    back, grad = norm_back(x, inverse_rms(x), gain_in, dn1)
    dgains[0:1, 0:width] = grad
    tokens_grad[...] = (dhidden[...] + back).astype(low)
    tokens_copy = pltpu.make_async_copy(tokens_grad, tokens_grad_out, store_sem.at[1 + 3 * len(chunks)])
    tokens_copy.start()
    step = gains_grad.shape[1]
    for origin in range(2 * lines):
        gain_part[origin * 8 : origin * 8 + 8] = dgains[:, origin * step : (origin + 1) * step]

    def gain_copy(index):
        source, target, device = (
            (gain_part, gain_first, place.mate) if index == 0 else (gain_part, gain_second, place.across)
        )
        return remote(source, target, last_send.at[3 + index], last_recv.at[3 + index], device)

    gain_copy(0).start()
    scatter.pump(4, 2)
    kv_copy(1).wait_recv()
    kv_copy(2).wait_recv()
    kv_copy(0).wait_send()
    kv_copy(1).wait_send()
    wall[:, base_column:kv_end] = (
        kv_block(place.y, place.core)[...].astype(full) + kv_first[1].astype(full) + kv_second[...].astype(full)
    ).astype(low)
    scatter.relay(4)
    gain_copy(0).wait_recv()
    gain_copy(0).wait_send()
    gain_part[...] = gain_part[...] + gain_first[...]
    gain_copy(1).start()
    scatter.pump(group_gate, 3)
    gain_copy(1).wait_recv()
    gain_copy(1).wait_send()
    gain_part[...] = gain_part[...] + gain_second[...]

    gain_scatter = LineScatter(
        place,
        lambda group, origin: gain_part.at[pl.ds(origin * 8, 8)],
        lambda group, home: gain_side.at[pl.ds(home * 8, 8)],
        lambda group, column, slot: gain_line.at[pl.ds(slot * 8, 8)],
        [False],
        gain_side_send,
        gain_side_recv,
        gain_line_send,
        gain_line_recv,
        full,
    )
    gain_scatter.start(0)
    scatter.start(group_small)
    scatter.start(group_up)
    scatter.pump(group_gate, 1, 2)

    stores = []

    def store(group, kinds, c):
        first, wide, padded = chunks[c] if kinds else (0, output_end - base_column, output_end - base_column)
        scatter.settle(group)
        for k, target in enumerate(kinds or (small_grad,)):
            slot = 3 * len(chunks) if not kinds else len([done for done in stores if done[1]])
            down, right = slot // 2 * shard, slot % 2 * CHUNK
            held = acc.at[down : down + shard, right : right + padded]
            scatter.total(group, k * wide, (k + 1) * wide, held.at[:, 0:wide])
            copy = pltpu.make_async_copy(held, target.at[:, first : first + padded], store_sem.at[slot])
            copy.start()
            stores.append((copy, bool(kinds)))
            if not kinds:
                kv_own[...] = held[:, 0:quarter].astype(low)

    for c in range(last - 1):
        store(2 * c, (down_grad,), c)
        store(2 * c + 1, (gate_grad, up_grad), c)
    scatter.relay(group_gate)
    store(group_last, (gate_grad, up_grad, down_grad), last)
    gain_scatter.pump(0)
    store(2 * last - 2, (down_grad,), last - 1)
    scatter.pump(group_small)
    gain_scatter.relay(0)
    scatter.relay(group_small)
    store(group_gate, (gate_grad,), last - 1)
    scatter.pump(group_up, 3, 1)
    store(group_small, (), 0)

    def own_block(y, core):
        return keyval_grad.at[:, pl.ds(pl.multiple_of((y * 2 + core) * quarter, quarter), quarter)]

    own_block(place.y, place.core)[...] = kv_own[...]
    targets = (place.mate, place.across, (place.dp, (1 - place.y) * 2 + (1 - place.core)))
    sends = [
        remote(kv_own, own_block(place.y, place.core), last_send.at[5 + i], last_recv.at[5 + i], target)
        for i, target in enumerate(targets)
    ]
    for copy in sends:
        copy.start()
    scatter.pump(group_up, 2)
    scatter.relay(group_up)
    gain_scatter.settle(0)
    gain_scatter.total(0, 0, gains_grad.shape[1], gains_grad)
    store(group_up, (up_grad,), last - 1)
    for i, (y, core) in enumerate(
        ((place.y, 1 - place.core), (1 - place.y, place.core), (1 - place.y, 1 - place.core))
    ):
        remote(kv_own, own_block(y, core), last_send.at[5 + i], last_recv.at[5 + i], targets[i]).wait_recv()
    for copy in sends:
        copy.wait_send()
    kv_copy(2).wait_send()
    scatter.finish()
    gain_scatter.finish()
    proj_all.finish()
    in_scatter.finish()
    for copy, _ in stores:
        copy.wait()
    tokens_copy.wait()


def backward_call(sizes, small_args, hbm_args):
    lines, rows, width, head_dim, units = sizes
    length = 4 * rows
    columns = hbm_args[0].shape[1]
    shard = hbm_args[0].shape[0] // (2 * lines)
    gains = small_args[3].shape[1]
    quarter = head_dim // 2
    base_column = 2 * head_dim - quarter
    chunks = chunks_of(units)
    groups = 2 * len(chunks) + 1
    last_wide = columns - packed_columns(units, head_dim)[0][-1][0]
    vm = pl.BlockSpec(memory_space=pltpu.VMEM)
    hbm = pl.BlockSpec(memory_space=pl.ANY)
    padded = sum(c[2] for c in chunks)
    large = [((shard, padded), full)] * 3 + [((shard, 5 * quarter), full), ((rows, width), low)]
    outs = [
        ((shard, 2 * head_dim), low),
        ((8, gains // (2 * lines)), full),
    ]
    scratch = [((rows, width), low)] + [(a.shape, a.dtype) for a in small_args[1:]]
    scratch += [
        (hbm_args[0].shape, low),
        ((lines * shard, packed_columns(units, head_dim)[0][-1][0] - base_column), low),
        ((shard, last_wide), low),
        ((lines * shard, packed_columns(units, head_dim)[0][-1][0] - base_column), low),
        ((2 * lines * shard, last_wide), low),
        ((length, 6 * CHUNK), low),
        ((length, width), low),
        ((length, width), low),
        ((length, width), full),
        ((2, rows, width), low),
        ((rows, width), low),
        ((rows, width), low),
        ((length, head_dim), low),
        ((length, head_dim), low),
        ((length, head_dim), low),
        ((length, 2 * head_dim), low),
        ((rows, width), full),
        ((rows, width), low),
        ((2, width, quarter), low),
        ((width, quarter), low),
        ((width, quarter), low),
        ((shard, quarter), low),
        ((8, gains), full),
        ((2 * lines * 8, gains // (2 * lines)), full),
        ((2 * lines * 8, gains // (2 * lines)), full),
        ((2 * lines * 8, gains // (2 * lines)), full),
        ((lines * 8, gains // (2 * lines)), full),
        ((lines * 8, gains // (2 * lines)), full),
    ]
    sems = [(4, 3), (4, 3), (groups, 4), (groups, 4), (groups, 2, 4), (groups, 2, 4)]
    sems += [(1, 4), (1, 4), (1, 1, 4), (1, 1, 4), (8,), (8,)]
    sems += [(19 + 4 * len(chunks),), (2 + 3 * len(chunks),)]
    return pl.pallas_call(
        functools.partial(backward_kernel, sizes),
        out_shape=[jax.ShapeDtypeStruct(*item) for item in large + outs],
        in_specs=[hbm] * (len(small_args) + len(hbm_args)),
        out_specs=[hbm] * len(large) + [vm] * len(outs),
        scratch_shapes=[pltpu.VMEM(*item) for item in scratch] + [pltpu.SemaphoreType.DMA(dims) for dims in sems],
        compiler_params=pltpu.CompilerParams(
            collective_id=1, has_side_effects=True, vmem_limit_bytes=63 * 1024 * 1024
        ),
        name="backward",
    )(*small_args, *hbm_args)


def adam_values(weight, gradient, first, second, step_rate):
    moment = beta_first * first + (1.0 - beta_first) * gradient
    square = beta_second * second + (1.0 - beta_second) * gradient * gradient
    scaled = moment / (1.0 - beta_first**STEP) / (jnp.sqrt(square / (1.0 - beta_second**STEP)) + adam_eps)
    return moment, square, weight - step_rate * (scaled + decay_rate * weight)


def update_kernel(units, head_dim, cut, *refs):
    passed, grads, old = refs[:2], refs[2:8], refs[8:26]
    passed_out, new = refs[26:28], refs[28:46]
    held_passed, held_grads, held, load_sem, store_sem = refs[46:48], refs[48:54], refs[54:72], refs[72], refs[73]
    gate_grad, up_grad, down_grad, small_grad, keyval_grad, gains_grad = held_grads
    quarter = head_dim // 2
    shard = old[0].shape[0]
    rows = shard // cut
    wide = D ** (-0.5)
    count = [0, 0]

    def load(source, target, part):
        at = slice(None) if part is None else pl.ds(part * rows, rows)
        copy = pltpu.make_async_copy(source.at[at], target.at[at], load_sem.at[count[0]])
        count[0] += 1
        copy.start()
        return copy

    def store(source, target, part):
        at = slice(None) if part is None else pl.ds(part * rows, rows)
        copy = pltpu.make_async_copy(source.at[at], target.at[at], store_sem.at[count[1]])
        count[1] += 1
        copy.start()
        return copy

    jobs = [(3, part, (0, 1)) for part in range(cut)] + [(4, part, (2,)) for part in range(cut)]
    jobs += [(1, None, (4,)), (0, None, (3,)), (2, None, ()), (5, None, (5,))]
    waits = []
    for index, part, needs in jobs:
        own = range(3 * index, 3 * index + 3)
        waits.append(
            [load(old[i], held[i], part) for i in own] + [load(grads[i], held_grads[i], part) for i in needs]
        )
    through = [load(source, target, None) for source, target in zip(passed, held_passed)]
    waiting = []

    def work(index, part):
        weight, first, second = held[3 * index : 3 * index + 3]
        if index == 5:
            values = adam_values(weight[...], gains_grad[0], first[...], second[...], 0.3)
            for target, value in zip((first, second, weight), values):
                target[...] = value
            return
        step = rows if part is not None else shard // 3

        def some_rows(at):
            if index == 3:
                for kind, grad in enumerate((gate_grad, up_grad)):
                    values = adam_values(
                        weight[at, kind, :], grad[at, 0:units], first[at, kind, :], second[at, kind, :], wide
                    )
                    for target, value in zip((first, second, weight), values):
                        target[at, kind, :] = value
                return
            if index == 4:
                gradient, rate = down_grad[at, 0:units], FF ** (-0.5)
            elif index == 1:
                gradient, rate = keyval_grad[at].astype(full), wide
            elif index == 0:
                gradient, rate = small_grad[at, quarter : quarter + head_dim], wide
            else:
                gradient = small_grad[at, quarter + head_dim : quarter + 2 * head_dim]
                rate = (HEADS * HEAD_DIM) ** (-0.5)
            values = adam_values(weight[at], gradient, first[at], second[at], rate)
            for target, value in zip((first, second, weight), values):
                target[at] = value

        if part is not None:
            some_rows(pl.ds(part * rows, rows))
        else:

            def body(i, carry):
                some_rows(pl.ds(pl.multiple_of(i * step, step), step))
                return carry

            lax.fori_loop(0, 3, body, 0)

    for (index, part, _), copies in zip(jobs, waits):
        if index == 1:
            for copy, source, target in zip(through, held_passed, passed_out):
                copy.wait()
                waiting.append(store(source, target, None))
        for copy in copies:
            copy.wait()
        work(index, part)
        for kind, place in ((1, 0), (2, 1), (0, 2)):
            waiting.append(store(held[3 * index + kind], new[3 * index + place], part))
    for copy in waiting:
        copy.wait()


def update_call(units, head_dim, passed, grads, old, cut):
    hbm = pl.BlockSpec(memory_space=pl.ANY)
    outs = list(passed)
    for index in range(6):
        outs += [old[3 * index + kind] for kind in (1, 2, 0)]
    loads = 9 * cut + 18
    return pl.pallas_call(
        functools.partial(update_kernel, units, head_dim, cut),
        out_shape=[jax.ShapeDtypeStruct(a.shape, a.dtype) for a in outs],
        in_specs=[hbm] * (len(passed) + len(grads) + len(old)),
        out_specs=[hbm] * len(outs),
        scratch_shapes=[pltpu.VMEM(a.shape, a.dtype) for a in (*passed, *grads, *old)]
        + [pltpu.SemaphoreType.DMA((loads,)), pltpu.SemaphoreType.DMA((2 + 6 * cut + 12,))],
        compiler_params=pltpu.CompilerParams(vmem_limit_bytes=60 * 1024 * 1024),
        name="update",
    )(*passed, *grads, *old)


def mixed_dot(left, right):
    return jnp.dot(left, right, preferred_element_type=jnp.float32)


def rms_scale(vector, gain_vec):
    return (
        vector
        * lax.rsqrt(jnp.mean(vector * vector, axis=-1, keepdims=True) + eps_norm)
        * (1.0 + gain_vec)
    )


def rotate(vector, positions):
    half_dim = vector.shape[-1] // 2
    inv_freq = rope_base ** (-2.0 * jnp.arange(half_dim).astype(jnp.float32) / vector.shape[-1])
    angles = positions[:, None] * inv_freq[None, :]
    cosine = jnp.cos(angles)[:, None, :]
    sine_v = jnp.sin(angles)[:, None, :]
    front_half = vector[..., :half_dim]
    back_half = vector[..., half_dim:]
    return jnp.concatenate(
        [front_half * cosine - back_half * sine_v, back_half * cosine + front_half * sine_v],
        axis=-1,
    )


def adam_step(weight, gradient, moment, second, step_rate):
    moment = beta_first * moment + (1.0 - beta_first) * gradient
    second = beta_second * second + (1.0 - beta_second) * gradient * gradient
    scaled = (
        moment
        / (1.0 - beta_first**STEP)
        / (jnp.sqrt(second / (1.0 - beta_second**STEP)) + adam_eps)
    )
    return (moment, second, weight - step_rate * (scaled + decay_rate * weight))


def plain_device(
    tokens,
    cotangent,
    prefix,
    query_weight,
    keyval_weight,
    output_weight,
    gateup_weight,
    down_weight,
    norm_gains,
    query_first,
    keyval_first,
    output_first,
    gateup_first,
    down_first,
    gains_first,
    query_second,
    keyval_second,
    output_second,
    gateup_second,
    down_second,
    gains_second,
):
    rows_dev, width = tokens.shape
    length = rows_dev * lax.axis_size("tensor")
    query_full, keyval_full, output_full, gateup_full, down_full, gains_full = (
        lax.all_gather(query_weight.astype(jnp.bfloat16), "dp", axis=0, tiled=True),
        lax.all_gather(keyval_weight.astype(jnp.bfloat16), "dp", axis=0, tiled=True),
        lax.all_gather(output_weight.astype(jnp.bfloat16), "dp", axis=0, tiled=True),
        lax.all_gather(gateup_weight.astype(jnp.bfloat16), "dp", axis=0, tiled=True),
        lax.all_gather(down_weight.astype(jnp.bfloat16), "dp", axis=0, tiled=True),
        lax.all_gather(norm_gains.astype(jnp.bfloat16), "dp", axis=0, tiled=True),
    )
    head_dim = keyval_full.shape[1] // 2
    heads_dev = query_full.shape[1] // head_dim
    units = down_full.shape[1]
    gain_values = gains_full.astype(jnp.float32)
    gain_input = gain_values[0:width]
    gain_attn = gain_values[width : 2 * width]
    gain_pre = gain_values[2 * width : 3 * width]
    gain_ffn = gain_values[3 * width : 4 * width]
    gain_query = gain_values[4 * width : 4 * width + head_dim]
    gain_key = gain_values[4 * width + head_dim : 4 * width + 2 * head_dim]
    positions = jnp.arange(length).astype(jnp.float32)
    span_rows = min(512, length)
    count_blocks = length // span_rows
    starts = jnp.arange(0, length, span_rows, dtype=jnp.int32)
    columns = jnp.arange(length, dtype=jnp.int32)
    prefix_len = prefix[0]
    gateup_flat = gateup_full.reshape(width, 2 * units)

    def shape_query(raw_rows, gain_vec):
        return rotate(rms_scale(raw_rows, gain_vec), positions)

    def shape_key(raw_rows, gain_vec):
        return rotate(rms_scale(raw_rows[:, None, :], gain_vec), positions)[:, 0]

    token_rows = tokens.astype(jnp.float32)
    normed_local = rms_scale(token_rows, gain_input).astype(jnp.bfloat16)
    normed = lax.all_gather(normed_local, "tensor", axis=0, tiled=True)
    query_raw = mixed_dot(normed, query_full).reshape(length, heads_dev, head_dim)
    keyval_raw = mixed_dot(normed, keyval_full)
    query_rot = shape_query(query_raw, gain_query).astype(jnp.bfloat16)
    key_rot = shape_key(keyval_raw[:, :head_dim], gain_key).astype(jnp.bfloat16)
    value_low = keyval_raw[:, head_dim:].astype(jnp.bfloat16)

    def scores_of(row_start):
        row_ids = row_start + jnp.arange(span_rows, dtype=jnp.int32)
        q_blk = lax.dynamic_slice_in_dim(query_rot, row_start, span_rows, 0)
        raw_scores = (
            jnp.einsum("rhd,kd->hrk", q_blk, key_rot, preferred_element_type=jnp.float32)
            * query_scale
        )
        allowed = (columns[None, :] <= row_ids[:, None]) | (columns[None, :] < prefix_len)
        return (jnp.where(allowed[None], raw_scores, masked_fill), q_blk)

    def forward_block(row_start):
        scores, q_blk = scores_of(row_start)
        row_peak = jnp.max(scores, axis=-1, keepdims=True)
        shifted = jnp.exp(scores - row_peak)
        denom_sum = jnp.sum(shifted, axis=-1, keepdims=True)
        soft_probs = (shifted / denom_sum).astype(jnp.bfloat16)
        mixed_rows = jnp.einsum(
            "hrk,kd->rhd", soft_probs, value_low, preferred_element_type=jnp.float32
        )
        return (mixed_rows, (row_peak + jnp.log(denom_sum))[..., 0])

    attended_blocks, log_sums = lax.map(forward_block, starts)
    attended = attended_blocks.reshape(length, heads_dev * head_dim).astype(jnp.bfloat16)
    attn_part = jnp.einsum("rk,dk->rd", attended, output_full, preferred_element_type=jnp.float32)
    projected = lax.psum_scatter(
        attn_part.astype(jnp.bfloat16), "tensor", scatter_dimension=0, tiled=True
    ).astype(jnp.float32)
    hidden_state = token_rows + rms_scale(projected, gain_attn)
    normed_two = lax.all_gather(
        rms_scale(hidden_state, gain_pre).astype(jnp.bfloat16), "tensor", axis=0, tiled=True
    )
    gateup = mixed_dot(normed_two, gateup_flat)
    gate_part = gateup[:, :units]
    up_part = gateup[:, units:]
    activation = (jax.nn.gelu(gate_part, approximate=True) * up_part).astype(jnp.bfloat16)
    down_part = jnp.einsum("ru,du->rd", activation, down_full, preferred_element_type=jnp.float32)
    down_sum = lax.psum_scatter(
        down_part.astype(jnp.bfloat16), "tensor", scatter_dimension=0, tiled=True
    ).astype(jnp.float32)
    block_out = hidden_state + rms_scale(down_sum, gain_ffn)
    grad_out = cotangent.astype(jnp.float32)
    pull_ffn = jax.vjp(rms_scale, down_sum, gain_ffn)[1]
    grad_down, grad_gain_ffn = pull_ffn(grad_out)
    down_back = lax.all_gather(grad_down.astype(jnp.bfloat16), "tensor", axis=0, tiled=True)
    grad_activation = mixed_dot(down_back, down_full)
    grad_down_w = jnp.einsum("rd,ru->du", down_back, activation, preferred_element_type=jnp.float32)

    def geglu(gate_in, up_in):
        return jax.nn.gelu(gate_in, approximate=True) * up_in

    pull_act = jax.vjp(geglu, gate_part, up_part)[1]
    grad_gate, grad_up = pull_act(grad_activation)
    grad_gateup = jnp.concatenate([grad_gate, grad_up], axis=1).astype(jnp.bfloat16)
    grad_gateup_w = jnp.einsum(
        "rd,ru->du", normed_two, grad_gateup, preferred_element_type=jnp.float32
    ).reshape(width, 2, units)
    grad_normed_two = jnp.einsum(
        "ru,du->rd", grad_gateup, gateup_flat, preferred_element_type=jnp.float32
    )
    grad_pre_rows = lax.psum_scatter(
        grad_normed_two.astype(jnp.bfloat16), "tensor", scatter_dimension=0, tiled=True
    ).astype(jnp.float32)
    pull_pre = jax.vjp(rms_scale, hidden_state, gain_pre)[1]
    grad_hidden_norm, grad_gain_pre = pull_pre(grad_pre_rows)
    grad_hidden = grad_out + grad_hidden_norm
    pull_attn = jax.vjp(rms_scale, projected, gain_attn)[1]
    grad_proj, grad_gain_attn = pull_attn(grad_hidden)
    proj_back = lax.all_gather(grad_proj.astype(jnp.bfloat16), "tensor", axis=0, tiled=True)
    grad_output_w = jnp.einsum("rd,rk->dk", proj_back, attended, preferred_element_type=jnp.float32)
    grad_attended = (
        mixed_dot(proj_back, output_full)
        .astype(jnp.bfloat16)
        .reshape(count_blocks, span_rows, heads_dev, head_dim)
    )

    def backward_block(carry, batch_item):
        key_acc, value_acc = carry
        row_start, grad_att, lse_blk = batch_item
        scores, q_blk = scores_of(row_start)
        soft_full = jnp.exp(scores - lse_blk[..., None])
        grad_probs = jnp.einsum(
            "rhd,kd->hrk", grad_att, value_low, preferred_element_type=jnp.float32
        )
        delta_rows = jnp.sum(soft_full * grad_probs, axis=-1, keepdims=True)
        grad_scores = (soft_full * (grad_probs - delta_rows)).astype(jnp.bfloat16)
        grad_query = (
            jnp.einsum("hrk,kd->rhd", grad_scores, key_rot, preferred_element_type=jnp.float32)
            * query_scale
        )
        key_acc = (
            key_acc
            + jnp.einsum("hrk,rhd->kd", grad_scores, q_blk, preferred_element_type=jnp.float32)
            * query_scale
        )
        value_acc = value_acc + jnp.einsum(
            "hrk,rhd->kd",
            soft_full.astype(jnp.bfloat16),
            grad_att,
            preferred_element_type=jnp.float32,
        )
        return ((key_acc, value_acc), grad_query)

    zero_rows = jnp.zeros((length, head_dim), jnp.float32)
    (grad_key_rot, grad_value), grad_query_blocks = lax.scan(
        backward_block, (zero_rows, zero_rows), (starts, grad_attended, log_sums)
    )
    grad_query_rot = grad_query_blocks.reshape(length, heads_dev, head_dim)
    pull_query = jax.vjp(shape_query, query_raw, gain_query)[1]
    grad_query_raw, grad_gain_query = pull_query(grad_query_rot)
    pull_key = jax.vjp(shape_key, keyval_raw[:, :head_dim], gain_key)[1]
    grad_key_raw, grad_gain_key = pull_key(grad_key_rot)
    grad_query_low = grad_query_raw.reshape(length, heads_dev * head_dim).astype(jnp.bfloat16)
    grad_keyval = jnp.concatenate([grad_key_raw, grad_value], axis=1)
    grad_query_w = jnp.einsum(
        "rd,rk->dk", normed, grad_query_low, preferred_element_type=jnp.float32
    )
    grad_normed_query = jnp.einsum(
        "rk,dk->rd", grad_query_low, query_full, preferred_element_type=jnp.float32
    )
    grad_normed_part, grad_keyval_own = (
        lax.psum_scatter(
            grad_normed_query.astype(jnp.bfloat16), "tensor", scatter_dimension=0, tiled=True
        ).astype(jnp.float32),
        lax.psum_scatter(
            grad_keyval.astype(jnp.bfloat16), "tensor", scatter_dimension=0, tiled=True
        ).astype(jnp.float32),
    )
    grad_keyval_low = grad_keyval_own.astype(jnp.bfloat16)
    grad_keyval_w = jnp.einsum(
        "rd,rk->dk", normed_local, grad_keyval_low, preferred_element_type=jnp.float32
    )
    grad_normed = grad_normed_part + jnp.einsum(
        "rk,dk->rd", grad_keyval_low, keyval_full, preferred_element_type=jnp.float32
    )
    pull_input = jax.vjp(rms_scale, token_rows, gain_input)[1]
    grad_token_norm, grad_gain_input = pull_input(grad_normed)
    tokens_grad = (grad_hidden + grad_token_norm).astype(jnp.bfloat16)
    grad_gains = jnp.concatenate(
        [
            grad_gain_input,
            grad_gain_attn,
            grad_gain_pre,
            grad_gain_ffn,
            grad_gain_query,
            grad_gain_key,
        ]
    )
    keyval_total, gains_total = (
        lax.psum(grad_keyval_w.astype(jnp.bfloat16), "tensor").astype(jnp.float32),
        lax.psum(grad_gains.astype(jnp.bfloat16), "tensor").astype(jnp.float32),
    )
    query_sum, keyval_sum, output_sum, gateup_sum, down_grad_sum, gains_sum = (
        lax.psum_scatter(grad_query_w, "dp", scatter_dimension=0, tiled=True),
        lax.psum_scatter(keyval_total, "dp", scatter_dimension=0, tiled=True),
        lax.psum_scatter(grad_output_w, "dp", scatter_dimension=0, tiled=True),
        lax.psum_scatter(grad_gateup_w, "dp", scatter_dimension=0, tiled=True),
        lax.psum_scatter(grad_down_w, "dp", scatter_dimension=0, tiled=True),
        lax.psum_scatter(gains_total, "dp", scatter_dimension=0, tiled=True),
    )
    query_moment, query_square, query_master = adam_step(
        query_weight, query_sum, query_first, query_second, D ** (-0.5)
    )
    keyval_moment, keyval_square, keyval_master = adam_step(
        keyval_weight, keyval_sum, keyval_first, keyval_second, D ** (-0.5)
    )
    output_moment, output_square, output_master = adam_step(
        output_weight, output_sum, output_first, output_second, (HEADS * HEAD_DIM) ** (-0.5)
    )
    gateup_moment, gateup_square, gateup_master = adam_step(
        gateup_weight, gateup_sum, gateup_first, gateup_second, D ** (-0.5)
    )
    down_moment, down_square, down_master = adam_step(
        down_weight, down_grad_sum, down_first, down_second, FF ** (-0.5)
    )
    gains_moment, gains_square, gains_master = adam_step(
        norm_gains, gains_sum, gains_first, gains_second, 0.3
    )
    return (
        block_out.astype(jnp.bfloat16),
        tokens_grad,
        query_moment,
        query_square,
        query_master,
        keyval_moment,
        keyval_square,
        keyval_master,
        output_moment,
        output_square,
        output_master,
        gateup_moment,
        gateup_square,
        gateup_master,
        down_moment,
        down_square,
        down_master,
        gains_moment,
        gains_square,
        gains_master,
    )


def per_device(
    tokens,
    cotangent,
    prefix,
    query_weight,
    keyval_weight,
    output_weight,
    gateup_weight,
    down_weight,
    norm_gains,
    query_first,
    keyval_first,
    output_first,
    gateup_first,
    down_first,
    gains_first,
    query_second,
    keyval_second,
    output_second,
    gateup_second,
    down_second,
    gains_second,
):
    rows, width = tokens.shape
    lines = lax.axis_size("dp") // 2
    shard = query_weight.shape[0]
    head_dim = keyval_weight.shape[1] // 2
    units = down_weight.shape[1]
    fits = (
        lax.axis_size("tensor") == 4
        and lax.axis_size("dp") == 8
        and len(chunks_of(units)) == 4
        and query_weight.shape[1] == head_dim
        and shard % 16 == 0
        and norm_gains.shape[0] % 128 == 0
        and (3 * len(chunks_of(units)) + 2) // 2 * shard <= 4 * rows
    )
    if not fits:
        return plain_device(
            tokens,
            cotangent,
            prefix,
            query_weight,
            keyval_weight,
            output_weight,
            gateup_weight,
            down_weight,
            norm_gains,
            query_first,
            keyval_first,
            output_first,
            gateup_first,
            down_first,
            gains_first,
            query_second,
            keyval_second,
            output_second,
            gateup_second,
            down_second,
            gains_second,
        )
    length = 4 * rows
    sizes = (lines, rows, width, head_dim, units)
    weights = (keyval_weight, query_weight, output_weight, gateup_weight, down_weight)
    angles = np.arange(length)[:, None] * (rope_base ** (-2.0 * np.arange(head_dim // 2) / head_dim))[None, :]
    cosine = jnp.asarray(np.cos(angles), full)
    sine = jnp.asarray(np.sin(angles), full)
    *saved, gvec, proj, hidden, grad_down, dgain_ffn, block_out = forward_call(
        sizes, prefix, tokens, cotangent, norm_gains, weights, cosine, sine
    )
    *grads, tokens_grad, keyval_sum, gains_sum = backward_call(
        sizes, (grad_down, cotangent, tokens, gvec, dgain_ffn, proj, hidden, cosine, sine), saved
    )
    old = (
        query_weight,
        query_first,
        query_second,
        keyval_weight,
        keyval_first,
        keyval_second,
        output_weight,
        output_first,
        output_second,
        gateup_weight,
        gateup_first,
        gateup_second,
        down_weight,
        down_first,
        down_second,
        norm_gains,
        gains_first,
        gains_second,
    )
    return tuple(update_call(units, head_dim, (block_out, tokens_grad), (*grads, keyval_sum, gains_sum), old, 3))


def solution(mesh):
    placed = (
        P(("dp", "tensor"), None),
        P(("dp", "tensor"), None),
        P("dp"),
        P("dp", "tensor"),
        P("dp", None),
        P("dp", "tensor"),
        P("dp", None, "tensor"),
        P("dp", "tensor"),
        P("dp"),
        P("dp", "tensor"),
        P("dp", None),
        P("dp", "tensor"),
        P("dp", None, "tensor"),
        P("dp", "tensor"),
        P("dp"),
        P("dp", "tensor"),
        P("dp", None),
        P("dp", "tensor"),
        P("dp", None, "tensor"),
        P("dp", "tensor"),
        P("dp"),
    )
    return jax.shard_map(
        per_device,
        mesh=mesh,
        in_specs=placed,
        out_specs=(
            P(("dp", "tensor"), None),
            P(("dp", "tensor"), None),
            P("dp", "tensor"),
            P("dp", "tensor"),
            P("dp", "tensor"),
            P("dp", None),
            P("dp", None),
            P("dp", None),
            P("dp", "tensor"),
            P("dp", "tensor"),
            P("dp", "tensor"),
            P("dp", None, "tensor"),
            P("dp", None, "tensor"),
            P("dp", None, "tensor"),
            P("dp", "tensor"),
            P("dp", "tensor"),
            P("dp", "tensor"),
            P("dp"),
            P("dp"),
            P("dp"),
        ),
        check_vma=False,
    )
```

```python
import functools

import jax
import jax.numpy as jnp
import numpy as np
from jax import lax
from jax.experimental import pallas as pl
from jax.experimental.pallas import tpu as pltpu
from jax.sharding import PartitionSpec as P

D = 1152
FF = 6912
HEADS = 4
HEAD_DIM = 256
STEP = 10


eps_norm = 1e-06
query_scale = 0.0625
rope_base = 1000000.0
beta_first = 0.9
beta_second = 0.95
adam_eps = 1e-08
decay_rate = 0.01
masked_fill = -1e30
MESH = pl.DeviceIdType.MESH
low = jnp.bfloat16
full = jnp.float32
CHUNK = 512


def dot_nn(left, right):
    return lax.dot_general(left, right, (((1,), (0,)), ((), ())), preferred_element_type=full)


def dot_nt(left, right):
    return lax.dot_general(left, right, (((1,), (1,)), ((), ())), preferred_element_type=full)


def dot_tn(left, right):
    return lax.dot_general(left, right, (((0,), (0,)), ((), ())), preferred_element_type=full)


def chunks_of(units):
    out = []
    first = 0
    while first < units:
        width = min(CHUNK, units - first)
        out.append((first, width, -(-width // 128) * 128))
        first += width
    return out


def small_columns(head_dim):
    return 2 * head_dim, 3 * head_dim, 4 * head_dim


def packed_columns(units, head_dim):
    at = small_columns(head_dim)[2]
    places = []
    for first, width, _ in chunks_of(units):
        places.append((at, at + width, at + 2 * width))
        at += -(-3 * width // 128) * 128
    return places, at


class Place:
    def __init__(self):
        self.dp = lax.axis_index("dp")
        self.tensor = lax.axis_index("tensor")
        self.z = self.dp // 2
        self.x = self.dp % 2
        self.y = self.tensor // 2
        self.core = self.tensor % 2
        self.homes = (self.z, self.z + 1 - 2 * (self.z % 2), (self.z + 2) % 4, 3 - self.z)
        self.end = ((self.z + 1) // 2 + 1) % 2
        self.middle = self.end == 0
        self.mate = (self.dp, self.y * 2 + (1 - self.core))
        self.across = (self.dp, (1 - self.y) * 2 + self.core)
        self.side = (self.z * 2 + (1 - self.x), self.tensor)
        self.inner = ((1 + self.z % 2) * 2 + self.x, self.tensor)

    def line(self, step):
        return (self.homes[step] * 2 + self.x, self.tensor)

    def peers(self):
        return [self.mate, self.across, self.side] + [self.line(s) for s in (1, 2, 3)]


def greet(place):
    for peer in place.peers():
        pl.semaphore_signal(pltpu.get_barrier_semaphore(), inc=1, device_id=peer, device_id_type=MESH)


def meet(place):
    pl.semaphore_wait(pltpu.get_barrier_semaphore(), len(place.peers()))


def remote(source, target, send_sem, recv_sem, device):
    return pltpu.make_async_remote_copy(
        src_ref=source,
        dst_ref=target,
        send_sem=send_sem,
        recv_sem=recv_sem,
        device_id=device,
        device_id_type=MESH,
    )


class LineGather:
    def __init__(self, place, region, wide, send, recv, relay_send, side_send, side_recv):
        self.place, self.region, self.wide = place, region, wide
        self.send, self.recv, self.relay_send = send, recv, relay_send
        self.side_send, self.side_recv = side_send, side_recv

    def columns(self, group):
        return (0, 1) if self.wide[group] else (0,)

    def origin(self, column, step):
        place = self.place
        return place.homes[step] * 2 + (place.x if column == 0 else 1 - place.x)

    def along(self, group, column, step):
        block = self.region(group, self.origin(column, 0))
        return remote(
            block, block, self.send.at[group, column, step], self.recv.at[group, column, step], self.place.line(step)
        )

    def arrive(self, group, column, step):
        block = self.region(group, self.origin(column, step))
        remote(
            block, block, self.send.at[group, column, step], self.recv.at[group, column, step], self.place.line(step)
        ).wait_recv()

    def relay(self, group, column):
        block = self.region(group, self.origin(column, 2))
        return remote(
            block, block, self.relay_send.at[group, column], self.recv.at[group, column, 3], self.place.line(1)
        )

    def sideways(self, group, step):
        block = self.region(group, self.origin(0, step))
        return remote(
            block, block, self.side_send.at[group, step], self.side_recv.at[group, step], self.place.side
        )

    def arrive_side(self, group, step):
        block = self.region(group, self.origin(1, step))
        remote(
            block, block, self.side_send.at[group, step], self.side_recv.at[group, step], self.place.side
        ).wait_recv()

    def start_line(self, group, column):
        self.along(group, column, 2).start()
        self.along(group, column, 1).start()

        @pl.when(self.place.middle)
        def _():
            self.along(group, column, 3).start()

    def start_side(self, group):
        self.sideways(group, 0).start()

    def start(self, group):
        self.start_side(group)
        self.start_line(group, 0)

    def widen(self, group):
        self.arrive_side(group, 0)
        self.start_line(group, 1)

    def pass_on(self, group, *columns):
        for column in columns or self.columns(group):
            self.arrive(group, column, 2)

            @pl.when(self.place.middle)
            def _():
                self.relay(group, column).start()

            if not self.wide[group]:
                self.sideways(group, 2).start()

    def collect(self, group):
        for column in self.columns(group):
            for step in (1, 3):
                self.arrive(group, column, step)
                if not self.wide[group]:
                    self.sideways(group, step).start()

    def ready(self, group):
        if not self.wide[group]:
            for step in (0, 2, 1, 3):
                self.arrive_side(group, step)

    def finish(self):
        for group in range(len(self.wide)):
            for column in self.columns(group):
                self.along(group, column, 1).wait_send()
                self.along(group, column, 2).wait_send()

                @pl.when(self.place.middle)
                def _():
                    self.along(group, column, 3).wait_send()
                    self.relay(group, column).wait_send()

            for step in (0,) if self.wide[group] else (0, 1, 2, 3):
                self.sideways(group, step).wait_send()


def row_slabs(buffer, rows, first=0, count=None):
    return lambda y, core: buffer.at[pl.ds((y * 2 + core) * rows + first, count or rows)]


def column_slabs(buffer, wide):
    return lambda y, core: buffer.at[:, pl.ds(pl.multiple_of((y * 2 + core) * wide, wide), wide)]


class RowGather:
    def __init__(self, place, source, slab, send, recv):
        self.place, self.source, self.slab = place, source, slab
        self.send, self.recv = send, recv

    def copy(self, index):
        place = self.place
        slab = self.slab(1 - place.y if index == 2 else place.y, place.core)
        source = slab if index == 2 else self.source
        device = place.across if index == 1 else place.mate
        return remote(source, slab, self.send.at[index], self.recv.at[index], device)

    def arrival(self, index, y, core):
        slab = self.slab(y, core)
        remote(slab, slab, self.send.at[index], self.recv.at[index], self.place.mate).wait_recv()

    def start(self):
        self.copy(1).start()
        self.copy(0).start()

    def wait_mate(self):
        self.arrival(0, self.place.y, 1 - self.place.core)

    def wait_across(self):
        self.arrival(1, 1 - self.place.y, self.place.core)
        self.copy(2).start()

    def wait_corner(self):
        self.arrival(2, 1 - self.place.y, 1 - self.place.core)

    def finish(self):
        for index in range(3):
            self.copy(index).wait_send()


class RowScatter:
    def __init__(self, place, slab, first, second, mixed, send, recv):
        self.place, self.slab = place, slab
        self.first, self.second, self.mixed = first, second, mixed
        self.send, self.recv = send, recv

    def copy(self, index):
        place = self.place
        if index == 2:
            return remote(self.mixed, self.second, self.send.at[2], self.recv.at[2], place.across)
        source = self.slab(1 - place.y if index == 0 else place.y, 1 - place.core)
        return remote(source, self.first.at[index], self.send.at[index], self.recv.at[index], place.mate)

    def order(self):
        place = self.place
        return (
            (1 - place.y) * 2 + (1 - place.core),
            (1 - place.y) * 2 + place.core,
            place.y * 2 + (1 - place.core),
            place.y * 2 + place.core,
        )

    def after(self, step):
        if step == 0:
            self.copy(0).start()
        if step == 1:
            self.copy(0).wait_recv()
            mixed = self.slab(1 - self.place.y, self.place.core)[...].astype(full) + self.first[0].astype(full)
            self.mixed[...] = mixed.astype(low)
            self.copy(2).start()
        if step == 2:
            self.copy(1).start()

    def total(self):
        self.copy(1).wait_recv()
        here = self.slab(self.place.y, self.place.core)[...].astype(full) + self.first[1].astype(full)
        self.copy(2).wait_recv()
        return here + self.second[...].astype(full)

    def finish(self):
        for index in range(3):
            self.copy(index).wait_send()


def inverse_rms(rows):
    return lax.rsqrt(jnp.mean(rows * rows, axis=-1, keepdims=True) + eps_norm)


def rotate_rows(rows, cosine, sine):
    half = rows.shape[-1] // 2
    front, back = rows[:, :half], rows[:, half:]
    return jnp.concatenate([front * cosine - back * sine, back * cosine + front * sine], axis=-1)


def rotate_back(rows, cosine, sine):
    half = rows.shape[-1] // 2
    front, back = rows[:, :half], rows[:, half:]
    return jnp.concatenate([front * cosine + back * sine, back * cosine - front * sine], axis=-1)


def gelu_parts(gate):
    scale = 0.7978845608028654
    square = gate * gate
    bent = jnp.tanh(scale * gate * (1.0 + 0.044715 * square))
    return square, bent


def forward_kernel(
    sizes,
    prefix_ref,
    tokens_in,
    cot_in,
    gains_in,
    keyval_in,
    query_in,
    output_in,
    gateup_in,
    down_in,
    cos_in,
    sin_in,
    wall_out,
    normed_out,
    normed_two_out,
    query_out,
    key_out,
    key_rot_out,
    value_out,
    attended_out,
    probs_out,
    gate_out,
    up_out,
    act_out,
    gvec_out,
    proj_out,
    hidden_out,
    grad_down_out,
    dgain_ffn_out,
    block_out_out,
    cot_ref,
    gains_ref,
    keyval_ref,
    query_ref,
    output_ref,
    gateup_ref,
    down_ref,
    cos_ref,
    sin_ref,
    gvec,
    proj_keep,
    hidden_keep,
    dgain_ffn,
    block_out,
    wall,
    normed,
    normed_two,
    query_raw,
    key_raw,
    attended,
    probs,
    gate_keep,
    up_keep,
    act,
    tok_full,
    gains_full,
    key_rot,
    value_low,
    part_one,
    first_one,
    second_one,
    mixed_one,
    down_acc,
    line_send,
    line_recv,
    relay_send,
    side_send,
    side_recv,
    row_send,
    row_recv,
    keep_sem,
    load_sem,
):
    lines, rows, width, head_dim, units = sizes
    place = Place()
    greet(place)
    own_rows = pl.ds(place.tensor * rows, rows)
    loads = {}
    for name, source, target in (
        ("gains", gains_in, gains_ref),
        ("keyval", keyval_in, keyval_ref),
        ("query", query_in, query_ref),
        ("output", output_in, output_ref),
        ("gateup", gateup_in, gateup_ref),
        ("down", down_in, down_ref),
        ("tokens", tokens_in, tok_full.at[own_rows]),
        ("cos", cos_in, cos_ref),
        ("sin", sin_in, sin_ref),
        ("cot", cot_in, cot_ref),
    ):
        loads[name] = pltpu.make_async_copy(source, target, load_sem.at[len(loads)])
        loads[name].start()
    length = 4 * rows
    shard = keyval_ref.shape[0]
    places, columns = packed_columns(units, head_dim)
    chunks = chunks_of(units)
    last = len(chunks) - 1
    kv_end, query_end, output_end = small_columns(head_dim)
    split, split_last = places[last - 1][2] + 128, places[last][2] // 128 * 128
    quarter = kv_end // 4
    own_quarter = pl.ds(pl.multiple_of(place.tensor * quarter, quarter), quarter)
    spans = [(0, kv_end), (kv_end, output_end)]
    spans += [(places[c][0], places[c + 1][0]) for c in range(last - 2)]
    spans += [(places[last - 2][0], places[last - 2][2]), (places[last - 1][0], split)]
    spans += [(places[last - 2][2], places[last - 1][0]), (split, split_last), (split_last, columns)]
    tail = len(spans)

    def region(group, origin):
        if group == 0:
            return gains_full.at[pl.ds(origin * 8, 8)]
        if group == 1:
            return wall.at[pl.ds(origin * shard, shard), own_quarter]
        lo, hi = spans[group - 1]
        return wall.at[pl.ds(origin * shard, shard), lo:hi]

    wide_groups = [False] * (tail - 1) + [True] * 2
    gather = LineGather(place, region, wide_groups, line_send, line_recv, relay_send, side_send, side_recv)
    tokens_all = RowGather(place, tokens_in, row_slabs(tok_full, rows), row_send.at[0], row_recv.at[0])
    kept = []

    def keep(source, target):
        copy = pltpu.make_async_copy(source, target, keep_sem.at[len(kept)])
        copy.start()
        kept.append(copy)

    def keep_span(group):
        lo, hi = spans[group - 1]
        keep(wall.at[:, lo:hi], wall_out.at[:, lo:hi])

    for name in ("gains", "keyval", "query", "output"):
        loads[name].wait()
    own_gains = gains_ref[...].astype(low).astype(full).reshape(1, -1)
    gains_full[pl.ds(place.dp * 8, 8)] = jnp.broadcast_to(own_gains, (8, own_gains.shape[1]))
    own = pl.ds(place.dp * shard, shard)
    wall[own, own_quarter] = keyval_ref[:, own_quarter].astype(low)
    wall[own, kv_end:query_end] = query_ref[...].astype(low)
    wall[own, query_end:output_end] = output_ref[...].astype(low)
    meet(place)
    tokens_all.start()
    for group in range(3):
        gather.start(group)
    loads["gateup"].wait()
    loads["down"].wait()
    for (first, wide, _), at in zip(chunks, places):
        for kind, lo in enumerate(at):
            units_here = slice(first, first + wide)
            piece = down_ref[:, units_here] if kind == 2 else gateup_ref[:, kind, units_here]
            wall[own, lo : lo + wide] = piece.astype(low)
    filled = places[last][2] + chunks[last][1]
    if filled < columns:
        wall[own, filled:columns] = jnp.zeros((shard, columns - filled), low)
    gather.start(3)
    for name in ("tokens", "cos", "sin", "cot"):
        loads[name].wait()
    tokens_all.wait_mate()
    tokens_all.wait_across()
    gather.pass_on(0)
    gather.pass_on(1)
    gather.collect(0)
    gather.collect(1)
    tokens_all.wait_corner()
    gather.pass_on(2)
    gather.ready(1)
    quarters = column_slabs(wall, quarter)
    keyval_all = RowGather(
        place, quarters(place.y, place.core), quarters, row_send.at[7], row_recv.at[7]
    )
    keyval_all.start()
    gather.collect(2)
    for group in range(4, tail + 1):
        gather.start_side(group)
    gather.start_line(4, 0)
    gather.ready(0)
    step = gains_ref.shape[0]
    for origin in range(2 * lines):
        gvec[:, origin * step : (origin + 1) * step] = gains_full[origin * 8 : origin * 8 + 8]
    keep(gvec, gvec_out)
    gain_in = 1.0 + gvec[0:1, 0:width]
    gain_attn = 1.0 + gvec[0:1, width : 2 * width]
    gain_pre = 1.0 + gvec[0:1, 2 * width : 3 * width]
    gain_ffn = 1.0 + gvec[0:1, 3 * width : 4 * width]
    gain_query = 1.0 + gvec[0:1, 4 * width : 4 * width + head_dim]
    gain_key = 1.0 + gvec[0:1, 4 * width + head_dim : 4 * width + 2 * head_dim]

    def norm_slab(index, carry):
        at = pl.ds(pl.multiple_of(index * rows, rows), rows)
        x = tok_full[at].astype(full)
        normed[at] = (x * inverse_rms(x) * gain_in).astype(low)
        return carry

    lax.fori_loop(0, 4, norm_slab, 0)
    keep(normed, normed_out)
    keyval_all.wait_mate()
    keyval_all.wait_across()
    gather.ready(2)
    keyval_all.wait_corner()

    def project_slab(index, carry):
        at = pl.ds(pl.multiple_of(index * rows, rows), rows)
        n1 = normed[at]
        query_raw[at] = dot_nn(n1, wall[:, kv_end:query_end])
        kv = dot_nn(n1, wall[:, 0:kv_end])
        k = kv[:, :head_dim]
        key_raw[at] = k
        key_rot[at] = rotate_rows(k * inverse_rms(k) * gain_key, cos_ref[at], sin_ref[at]).astype(low)
        value_low[at] = kv[:, head_dim:].astype(low)
        return carry

    lax.fori_loop(0, 4, project_slab, 0)
    gather.pass_on(3)
    gather.start_line(5, 0)
    keep(query_raw, query_out)
    keep(key_raw, key_out)
    keep(key_rot, key_rot_out)
    keep(value_low, value_out)
    keep_span(1)
    keep_span(2)

    out_scatter = RowScatter(
        place, row_slabs(part_one, rows), first_one, second_one, mixed_one, row_send.at[1], row_recv.at[1]
    )

    def attend_slab(index):
        at = pl.ds(pl.multiple_of(index * rows, rows), rows)
        q = query_raw[at]
        qr = rotate_rows(q * inverse_rms(q) * gain_query, cos_ref[at], sin_ref[at]).astype(low)
        scores = dot_nt(qr, key_rot[...]) * query_scale
        row_ids = lax.broadcasted_iota(jnp.int32, (rows, length), 0) + index * rows
        columns = lax.broadcasted_iota(jnp.int32, (rows, length), 1)
        allowed = (columns <= row_ids) | (columns < prefix_ref[0])
        scores = jnp.where(allowed, scores, masked_fill)
        shifted = jnp.exp(scores - jnp.max(scores, axis=-1, keepdims=True))
        soft = (shifted / jnp.sum(shifted, axis=-1, keepdims=True)).astype(low)
        probs[at] = soft
        mixed = dot_nn(soft, value_low[...]).astype(low)
        attended[at] = mixed
        part_one[at] = dot_nt(mixed, wall[:, query_end:output_end]).astype(low)

    for step, index in enumerate(out_scatter.order()):
        attend_slab(index)
        out_scatter.after(step)
    keep(probs, probs_out)
    keep(attended, attended_out)
    gather.collect(3)
    gather.pass_on(4)
    for group in range(6, tail + 1):
        gather.start_line(group, 0)
    projected = out_scatter.total()
    out_scatter.finish()
    proj_keep[...] = projected
    hidden = tok_full[own_rows].astype(full) + projected * inverse_rms(projected) * gain_attn
    hidden_keep[...] = hidden
    keep(proj_keep, proj_out)
    keep(hidden_keep, hidden_out)
    normed_two[own_rows] = (hidden * inverse_rms(hidden) * gain_pre).astype(low)
    two_all = RowGather(place, normed_two.at[own_rows], row_slabs(normed_two, rows), row_send.at[2], row_recv.at[2])
    two_all.start()
    gather.collect(4)
    gather.pass_on(5)
    two_all.wait_mate()
    gather.widen(tail - 1)
    gather.widen(tail)
    two_all.wait_across()
    gather.pass_on(6)
    gather.collect(5)
    two_all.wait_corner()
    keep(normed_two, normed_two_out)

    half = rows // 2
    down_scatters, down_gathers = [], []
    for index in range(2):
        piece = slice(index * half, (index + 1) * half)
        down_scatters.append(
            RowScatter(
                place,
                row_slabs(part_one, rows, index * half, half),
                first_one.at[:, piece],
                second_one.at[piece],
                mixed_one.at[piece],
                row_send.at[3 + index],
                row_recv.at[3 + index],
            )
        )
        slabs = row_slabs(tok_full, rows, index * half, half)
        down_gathers.append(
            RowGather(place, slabs(place.y, place.core), slabs, row_send.at[5 + index], row_recv.at[5 + index])
        )
    block = 2 * rows

    def feed(c):
        first, wide, padded = chunks[c]
        at_gate, at_up, _ = places[c]

        def feed_rows(index, carry):
            at = pl.ds(pl.multiple_of(index * block, block), block)
            n2 = normed_two[at]
            gate = dot_nn(n2, wall[:, at_gate : at_gate + wide])
            up = dot_nn(n2, wall[:, at_up : at_up + wide])
            gate_keep[at, first : first + wide] = gate.astype(low)
            up_keep[at, first : first + wide] = up.astype(low)
            _, bent = gelu_parts(gate)
            act[at, first : first + wide] = (0.5 * gate * (1.0 + bent) * up).astype(low)
            return carry

        lax.fori_loop(0, 2, feed_rows, 0)
        span = slice(first, first + padded)
        keep(gate_keep.at[:, span], gate_out.at[:, span])
        keep(up_keep.at[:, span], up_out.at[:, span])
        keep(act.at[:, span], act_out.at[:, span])

    def lower(c):
        first, wide, _ = chunks[c]
        at_down = places[c][2]

        def lower_rows(index, carry):
            at = pl.ds(pl.multiple_of(index * block, block), block)
            more = dot_nt(act[at, first : first + wide], wall[:, at_down : at_down + wide])
            down_acc[at] = more if c == 0 else down_acc[at] + more
            return carry

        lax.fori_loop(0, 2, lower_rows, 0)

    gather.ready(3)
    keep_span(3)
    feed(0)
    gather.pass_on(7, 0)
    gather.pass_on(8, 0)
    gather.collect(6)
    lower(0)
    gather.ready(4)
    keep_span(4)
    feed(1)
    gather.ready(5)
    keep_span(5)
    feed(2)
    gather.pass_on(7, 1)
    gather.collect(7)
    keep_span(7)
    feed(3)
    gather.pass_on(8, 1)
    gather.ready(6)
    keep_span(6)
    lower(1)
    lower(2)
    gather.collect(8)
    keep_span(8)
    first, wide, _ = chunks[last]
    at_down = places[last][2]
    tokens_all.finish()
    for step, index in enumerate(down_scatters[0].order()):
        at = pl.ds(pl.multiple_of(index * rows, rows), rows)
        part_one[at] = (
            down_acc[at] + dot_nt(act[at, first : first + wide], wall[:, at_down : at_down + wide])
        ).astype(low)
        for scatter in down_scatters:
            scatter.after(step)
    for index, (scatter, spread) in enumerate(zip(down_scatters, down_gathers)):
        piece = slice(index * half, (index + 1) * half)
        f = scatter.total()
        inv = inverse_rms(f)
        cot = cot_ref[piece].astype(full)
        scaled = cot * gain_ffn
        back = inv * (scaled - f * (inv * inv) * jnp.mean(f * scaled, axis=-1, keepdims=True))
        tok_full[pl.ds(place.tensor * rows + index * half, half)] = back.astype(low)
        spread.start()
        block_out[piece] = (hidden_keep[piece] + f * inv * gain_ffn).astype(low)
        grad = jnp.broadcast_to(jnp.sum(cot * f * inv, axis=0, keepdims=True), dgain_ffn.shape)
        dgain_ffn[...] = grad if index == 0 else dgain_ffn[...] + grad

    def keep_slab(y, core):
        at = pl.ds((y * 2 + core) * rows, rows)
        keep(tok_full.at[at], grad_down_out.at[at])

    keep(block_out, block_out_out)
    keep(dgain_ffn, dgain_ffn_out)
    keep_slab(place.y, place.core)
    for spread in down_gathers:
        spread.wait_mate()
    keep_slab(place.y, 1 - place.core)
    for spread in down_gathers:
        spread.wait_across()
    keep_slab(1 - place.y, place.core)
    for spread in down_gathers:
        spread.wait_corner()
    keep_slab(1 - place.y, 1 - place.core)
    gather.finish()
    keyval_all.finish()
    two_all.finish()
    for item in down_scatters + down_gathers:
        item.finish()
    for copy in kept:
        copy.wait()


def forward_call(sizes, prefix, tokens, cotangent, gains, weights, cosine, sine):
    lines, rows, width, head_dim, units = sizes
    length = 4 * rows
    shard = weights[0].shape[0]
    columns = packed_columns(units, head_dim)[1]
    chunks = chunks_of(units)
    padded = sum(c[2] for c in chunks)
    groups = 5 + len(chunks)
    inputs = (tokens, cotangent, gains, *weights, cosine, sine)
    hbm = pl.BlockSpec(memory_space=pl.ANY)
    large = [
        ((2 * lines * shard, columns), low),
        ((length, width), low),
        ((length, width), low),
        ((length, head_dim), full),
        ((length, head_dim), full),
        ((length, head_dim), low),
        ((length, head_dim), low),
        ((length, head_dim), low),
        ((length, length), low),
        ((length, padded), low),
        ((length, padded), low),
        ((length, padded), low),
    ]
    small = [
        ((8, gains.shape[0] * 2 * lines), full),
        ((rows, width), full),
        ((rows, width), full),
        ((length, width), low),
        ((8, width), full),
        ((rows, width), low),
    ]
    inside = [large[i] for i in (0, 1, 2, 3, 4, 7, 8, 9, 10, 11)]
    scatter_set = [
        pltpu.VMEM((2, rows, width), low),
        pltpu.VMEM((rows, width), low),
        pltpu.VMEM((rows, width), low),
    ]
    return pl.pallas_call(
        functools.partial(forward_kernel, sizes),
        out_shape=[jax.ShapeDtypeStruct(*item) for item in large + small],
        in_specs=[pl.BlockSpec(memory_space=pltpu.SMEM)] + [hbm] * len(inputs),
        out_specs=[hbm] * (len(large) + len(small)),
        scratch_shapes=[pltpu.VMEM(a.shape, a.dtype) for a in inputs[1:]]
        + [pltpu.VMEM(*item) for item in small[:3] + small[4:] + inside]
        + [
            pltpu.VMEM((length, width), low),
            pltpu.VMEM((2 * lines * 8, gains.shape[0]), full),
            pltpu.VMEM((length, head_dim), low),
            pltpu.VMEM((length, head_dim), low),
            pltpu.VMEM((length, width), low),
        ]
        + scatter_set
        + [
            pltpu.VMEM((length, width), full),
            pltpu.SemaphoreType.DMA((groups, 2, lines)),
            pltpu.SemaphoreType.DMA((groups, 2, lines)),
            pltpu.SemaphoreType.DMA((groups, 2)),
            pltpu.SemaphoreType.DMA((groups, lines)),
            pltpu.SemaphoreType.DMA((groups, lines)),
            pltpu.SemaphoreType.DMA((8, 3)),
            pltpu.SemaphoreType.DMA((8, 3)),
            pltpu.SemaphoreType.DMA((22 + 4 * len(chunks),)),
            pltpu.SemaphoreType.DMA((len(inputs),)),
        ],
        compiler_params=pltpu.CompilerParams(
            collective_id=0, has_side_effects=True, vmem_limit_bytes=63 * 1024 * 1024
        ),
        name="forward",
    )(prefix, *inputs)


class LineScatter:
    def __init__(self, place, block, side_block, line_block, wide, side_send, side_recv, line_send, line_recv, kind):
        self.place, self.block, self.side_block, self.line_block = place, block, side_block, line_block
        self.wide, self.kind = wide, kind
        self.side_send, self.side_recv, self.line_send, self.line_recv = side_send, side_recv, line_send, line_recv

    def columns(self, group):
        return (0, 1) if self.wide[group] else (0,)

    def own(self, group, column, step):
        place = self.place
        return self.block(group, place.homes[step] * 2 + (place.x if column == 0 else 1 - place.x))

    def sideways(self, group, step):
        home = 0 if self.wide[group] else self.place.homes[step]
        return remote(
            self.own(group, 1, step),
            self.side_block(group, home),
            self.side_send.at[group, step],
            self.side_recv.at[group, step],
            self.place.side,
        )

    def along(self, group, column, step):
        slot = step - 1 if step < 3 else 2 + self.place.end
        return remote(
            self.own(group, column, step),
            self.line_block(group, column, slot),
            self.line_send.at[group, column, step],
            self.line_recv.at[group, column, slot],
            self.place.line(step) if step < 3 else self.place.inner,
        )

    def arrive(self, group, column, slot):
        here = self.line_block(group, column, slot)
        remote(
            here, here, self.line_send.at[group, column, 1], self.line_recv.at[group, column, slot], self.place.line(1)
        ).wait_recv()
        return here[...].astype(full)

    def start(self, group):
        if not self.wide[group]:
            for step in (3, 1, 2, 0):
                self.sideways(group, step).start()
            return
        for step in (3, 1):
            for column in (0, 1):
                self.along(group, column, step).start()

        @pl.when(self.place.end == 1)
        def _():
            for column in (0, 1):
                self.along(group, column, 2).start()

    def with_side(self, group, step):
        self.sideways(group, step).wait_recv()
        return self.own(group, 0, step)[...].astype(full) + self.side_block(group, self.place.homes[step])[...].astype(
            full
        )

    def pump(self, group, *steps):
        for step in steps or (3, 1, 2):
            self.own(group, 0, step)[...] = self.with_side(group, step).astype(self.kind)
            if step != 2:
                self.along(group, 0, step).start()
                continue

            @pl.when(self.place.end == 1)
            def _():
                self.along(group, 0, 2).start()

    def relay(self, group):
        for column in self.columns(group):

            @pl.when(self.place.middle)
            def _():
                block = self.own(group, column, 2)
                block[...] = (block[...].astype(full) + self.arrive(group, column, 3)).astype(self.kind)
                self.along(group, column, 2).start()

    def hand_over(self, group):
        block = self.own(group, 1, 0)
        both = block[...].astype(full) + self.arrive(group, 1, 0) + self.arrive(group, 1, 1)

        @pl.when(self.place.middle)
        def _():
            block[...] = (both + self.arrive(group, 1, 2)).astype(self.kind)

        @pl.when(self.place.end == 1)
        def _():
            block[...] = both.astype(self.kind)

        self.sideways(group, 0).start()

    def settle(self, group):
        self.sideways(group, 0).wait_recv()
        self.arrive(group, 0, 0)
        self.arrive(group, 0, 1)

        @pl.when(self.place.middle)
        def _():
            self.arrive(group, 0, 2)

    def total(self, group, lo, hi, held):
        parts = [
            self.own(group, 0, 0),
            self.side_block(group, 0 if self.wide[group] else self.place.z),
            self.line_block(group, 0, 0),
            self.line_block(group, 0, 1),
        ]
        first, *others = [part[:, lo:hi].astype(full) for part in parts]
        for other in others:
            first = first + other
        held[...] = first

        @pl.when(self.place.middle)
        def _():
            held[...] = first + self.line_block(group, 0, 2)[:, lo:hi].astype(full)

    def finish(self):
        for group in range(len(self.wide)):
            for step in (0,) if self.wide[group] else (0, 1, 2, 3):
                self.sideways(group, step).wait_send()
            for column in self.columns(group):
                for step in (1, 2, 3):
                    self.along(group, column, step).wait_send()


def norm_back(rows, inv, gain, grad):
    scaled = grad * gain
    back = inv * (scaled - rows * (inv * inv) * jnp.mean(rows * scaled, axis=-1, keepdims=True))
    return back, jnp.sum(grad * rows * inv, axis=0, keepdims=True)


def backward_kernel(
    sizes,
    grad_down_in,
    cot_in,
    tokens_in,
    gvec_in,
    dgain_ffn_in,
    proj_in,
    hidden_in,
    cos_in,
    sin_in,
    wall_in,
    normed_in,
    normed_two_in,
    query_in,
    key_in,
    key_rot_in,
    value_in,
    attended_in,
    probs_in,
    gate_in,
    up_in,
    act_in,
    gate_grad,
    up_grad,
    down_grad,
    small_grad,
    tokens_grad_out,
    keyval_grad,
    gains_grad,
    tokens_grad,
    cot_ref,
    tokens_ref,
    gvec,
    dgain_ffn,
    proj_ref,
    hidden_ref,
    cos_ref,
    sin_ref,
    wall,
    side_buf,
    side_wide,
    line_buf,
    line_wide,
    big,
    normed_two,
    row_buf,
    acc,
    first_buf,
    second_buf,
    mixed_buf,
    key_rot,
    value_low,
    dquery,
    dkeyval,
    dhidden,
    dproj,
    kv_first,
    kv_second,
    kv_mixed,
    kv_own,
    dgains,
    gain_part,
    gain_first,
    gain_second,
    gain_side,
    gain_line,
    row_send,
    row_recv,
    side_send,
    side_recv,
    line_send,
    line_recv,
    gain_side_send,
    gain_side_recv,
    gain_line_send,
    gain_line_recv,
    last_send,
    last_recv,
    load_sem,
    store_sem,
):
    lines, rows, width, head_dim, units = sizes
    place = Place()
    length = 4 * rows
    shard = wall.shape[0] // (2 * lines)
    kv_end, query_end, output_end = small_columns(head_dim)
    quarter = head_dim // 2
    places, columns = packed_columns(units, head_dim)
    chunks = chunks_of(units)
    last = len(chunks) - 1
    order = [0, last] + list(range(1, last))
    base_column = kv_end - quarter
    spans = []
    for c in range(last):
        spans += [(places[c][2], places[c + 1][0]), (places[c][0], places[c][2])]
    group_gate, group_up, group_last, group_small = range(len(spans) - 1, len(spans) + 3)
    spans[-1:] = [(places[last - 1][0], places[last - 1][1]), (places[last - 1][1], places[last - 1][2])]
    spans += [(places[last][0], columns), (base_column, output_end)]
    loads = {}

    def load(name, source, target):
        copy = pltpu.make_async_copy(source, target, load_sem.at[len(loads)])
        copy.start()
        loads[name] = copy

    def load_chunk(c):
        first, _, padded = chunks[c]
        lo, hi = places[c][0], columns if c == last else places[c + 1][0]
        base = (order.index(c) % 2) * 3 * CHUNK
        load(("wall", c), wall_in.at[:, lo:hi], wall.at[:, lo:hi])
        for k, source in enumerate((gate_in, up_in, act_in)):
            at = base + k * CHUNK
            load((k, c), source.at[:, first : first + padded], big.at[:, at : at + padded])

    greet(place)
    own_rows = pl.ds(place.tensor * rows, rows)
    load("down", grad_down_in, row_buf)
    load_chunk(order[0])
    load("two", normed_two_in, normed_two)
    load("gvec", gvec_in, gvec)
    load("dgain", dgain_ffn_in, dgain_ffn)
    load_chunk(order[1])
    load("hidden", hidden_in, hidden_ref)
    load("cot", cot_in, cot_ref)
    load("proj", proj_in, proj_ref)
    load("tokens", tokens_in, tokens_ref)
    load("cos", cos_in, cos_ref)
    load("sin", sin_in, sin_ref)
    load("kv", wall_in.at[:, 0:kv_end], wall.at[:, 0:kv_end])
    load("qo", wall_in.at[:, kv_end:output_end], wall.at[:, kv_end:output_end])
    load("key_rot", key_rot_in, key_rot)
    load("value", value_in, value_low)
    loads["gvec"].wait()
    loads["dgain"].wait()
    gain_in = 1.0 + gvec[0:1, 0:width]
    gain_attn = 1.0 + gvec[0:1, width : 2 * width]
    gain_pre = 1.0 + gvec[0:1, 2 * width : 3 * width]
    gain_query = 1.0 + gvec[0:1, 4 * width : 4 * width + head_dim]
    gain_key = 1.0 + gvec[0:1, 4 * width + head_dim : 4 * width + 2 * head_dim]
    dgains[...] = jnp.zeros_like(dgains)
    dgains[0:1, 3 * width : 4 * width] = dgain_ffn[0:1]
    loads["down"].wait()
    loads["two"].wait()

    def block(group, origin):
        lo, hi = spans[group]
        return wall.at[pl.ds(origin * shard, shard), lo:hi]

    def side_block(group, home):
        if wide_groups[group]:
            return side_wide
        lo, hi = spans[group]
        return side_buf.at[pl.ds(home * shard, shard), lo - base_column : hi - base_column]

    def line_block(group, column, slot):
        lo, hi = spans[group]
        if wide_groups[group]:
            return line_wide.at[pl.ds((column * 4 + slot) * shard, shard)]
        return line_buf.at[pl.ds(slot * shard, shard), lo - base_column : hi - base_column]

    wide_groups = [group == group_last for group in range(len(spans))]
    scatter = LineScatter(
        place, block, side_block, line_block, wide_groups, side_send, side_recv, line_send, line_recv, low
    )
    part = big.at[:, 0:width]
    pre_scatter = RowScatter(
        place, row_slabs(part, rows), first_buf, second_buf, mixed_buf, row_send.at[1], row_recv.at[1]
    )
    half = 2 * rows
    third = width // 3

    def weight_gradient(lo, wide, left, right):
        for m in range(0, width, third):
            wall[m : m + third, lo : lo + wide] = dot_tn(left[:, m : m + third], right).astype(low)

    for position, c in enumerate(order):
        first, wide, padded = chunks[c]
        at_gate, at_up, at_down = places[c]
        base = (position % 2) * 3 * CHUNK
        loads["wall", c].wait()
        for k in range(3):
            loads[k, c].wait()
        if 1 <= position < last:
            load_chunk(order[position + 1])
        of_gate = slice(base, base + wide)
        of_up = slice(base + CHUNK, base + CHUNK + wide)
        of_act = slice(base + 2 * CHUNK, base + 2 * CHUNK + wide)

        def unit_rows(index, carry):
            at = pl.ds(pl.multiple_of(index * half, half), half)
            dz = dot_nn(row_buf[at], wall[:, at_down : at_down + wide])
            gate = big[at, of_gate].astype(full)
            up = big[at, of_up].astype(full)
            square, bent = gelu_parts(gate)
            middle = 0.5 * (1.0 + bent)
            slope = middle + 0.5 * gate * (1.0 - bent * bent) * (0.7978845608028654 * (1.0 + 0.134145 * square))
            big[at, of_gate] = (dz * up * slope).astype(low)
            big[at, of_up] = (dz * gate * middle).astype(low)
            return carry

        lax.fori_loop(0, 2, unit_rows, 0)
        weight_gradient(at_down, wide, row_buf, big[:, of_act])
        if position == 0:
            meet(place)
        if c < last:
            scatter.start(2 * c)

        def back_rows(at):
            more = dot_nt(big[at, of_gate], wall[:, at_gate : at_gate + wide])
            more = more + dot_nt(big[at, of_up], wall[:, at_up : at_up + wide])
            return more if position == 0 else acc[at] + more

        if position < last:

            def collect_rows(index, carry):
                at = pl.ds(pl.multiple_of(index * half, half), half)
                acc[at] = back_rows(at)
                return carry

            lax.fori_loop(0, 2, collect_rows, 0)
        else:
            for step, index in enumerate(pre_scatter.order()):
                at = pl.ds(pl.multiple_of(index * rows, rows), rows)
                part[at] = back_rows(at).astype(low)
                pre_scatter.after(step)
        weight_gradient(at_gate, wide, normed_two, big[:, of_gate])
        weight_gradient(at_up, wide, normed_two, big[:, of_up])
        if c < last:
            scatter.start(2 * c + 1)
        else:
            scatter.pump(0)
            scatter.start(group_last)
        if position == 2:
            scatter.relay(0)
        if position == 3:
            scatter.relay(group_last)
            scatter.pump(1, 3, 1)

    at_normed = width
    at_att = at_normed + width
    load("normed", normed_in, big.at[:, at_normed : at_normed + width])
    load("attended", attended_in, big.at[:, at_att : at_att + head_dim])
    load("query", query_in, acc.at[:, 2 * head_dim : 3 * head_dim])
    load("key", key_in, acc.at[:, 3 * head_dim : 4 * head_dim])

    scatter.pump(1, 2)
    dn2 = pre_scatter.total()
    for name in ("hidden", "cot", "proj", "tokens", "cos", "sin"):
        loads[name].wait()
    hidden = hidden_ref[...]
    back, grad = norm_back(hidden, inverse_rms(hidden), gain_pre, dn2)
    dgains[0:1, 2 * width : 3 * width] = grad
    dh = cot_ref[...].astype(full) + back
    dhidden[...] = dh
    proj = proj_ref[...]
    back, grad = norm_back(proj, inverse_rms(proj), gain_attn, dh)
    dgains[0:1, width : 2 * width] = grad
    dproj[...] = back.astype(low)
    row_buf[own_rows] = dproj[...]
    proj_all = RowGather(place, dproj, row_slabs(row_buf, rows), row_send.at[2], row_recv.at[2])
    proj_all.start()
    pre_scatter.finish()
    load("probs", probs_in, big.at[:, 0:length])
    acc[:, 0 : 2 * head_dim] = jnp.zeros((length, 2 * head_dim), full)
    proj_all.wait_mate()
    scatter.pump(2)
    proj_all.wait_across()
    scatter.relay(1)
    proj_all.wait_corner()
    for name in ("kv", "qo", "key_rot", "value", "normed", "attended", "query", "key", "probs"):
        loads[name].wait()

    def attend_back(index, carry):
        at = pl.ds(pl.multiple_of(index * rows, rows), rows)
        da = dot_nn(row_buf[at], wall[:, query_end:output_end]).astype(low)
        soft = big[at, 0:length]
        wide_soft = soft.astype(full)
        dp = dot_nt(da, value_low[...])
        ds = (wide_soft * (dp - jnp.sum(wide_soft * dp, axis=-1, keepdims=True))).astype(low)
        q = acc[at, 2 * head_dim : 3 * head_dim]
        inv = inverse_rms(q)
        cosine, sine = cos_ref[at], sin_ref[at]
        qr = rotate_rows(q * inv * gain_query, cosine, sine).astype(low)
        dqr = dot_nn(ds, key_rot[...]) * query_scale
        acc[:, 0:head_dim] += dot_tn(ds, qr)
        acc[:, head_dim : 2 * head_dim] += dot_tn(soft, da)
        dq, grad = norm_back(q, inv, gain_query, rotate_back(dqr, cosine, sine))
        dquery[at] = dq.astype(low)
        dgains[0:1, 4 * width : 4 * width + head_dim] += grad
        return carry

    scatter.hand_over(group_last)
    scatter.pump(3, 3)
    lax.fori_loop(0, 4, attend_back, 0)

    def key_back(index, carry):
        at = pl.ds(pl.multiple_of(index * rows, rows), rows)
        k = acc[at, 3 * head_dim : 4 * head_dim]
        dkr = rotate_back(acc[at, 0:head_dim] * query_scale, cos_ref[at], sin_ref[at])
        dk, grad = norm_back(k, inverse_rms(k), gain_key, dkr)
        dkeyval[at, 0:head_dim] = dk.astype(low)
        dkeyval[at, head_dim : 2 * head_dim] = acc[at, head_dim : 2 * head_dim].astype(low)
        dgains[0:1, 4 * width + head_dim : 4 * width + 2 * head_dim] += grad
        return carry

    lax.fori_loop(0, 4, key_back, 0)
    scatter.pump(3, 1)
    in_scatter = RowScatter(
        place, row_slabs(part, rows), first_buf, second_buf, mixed_buf, row_send.at[3], row_recv.at[3]
    )
    for step, index in enumerate(in_scatter.order()):
        at = pl.ds(pl.multiple_of(index * rows, rows), rows)
        more = dot_nt(dquery[at], wall[:, kv_end:query_end]) + dot_nt(dkeyval[at], wall[:, 0:kv_end])
        part[at] = more.astype(low)
        in_scatter.after(step)
    scatter.pump(3, 2)
    scatter.relay(2)

    normed = big.at[:, at_normed : at_normed + width]
    for m in range(0, width, third):
        wall[m : m + third, 0:kv_end] = dot_tn(normed[:, m : m + third], dkeyval[...]).astype(low)

    def kv_block(y, core):
        return wall.at[:, pl.ds(pl.multiple_of((y * 2 + core) * quarter, quarter), quarter)]

    def kv_copy(index):
        send, recv = last_send.at[index], last_recv.at[index]
        if index == 2:
            return remote(kv_mixed, kv_second, send, recv, place.across)
        return remote(
            kv_block(1 - place.y if index == 0 else place.y, 1 - place.core), kv_first.at[index], send, recv, place.mate
        )

    kv_copy(0).start()
    kv_copy(1).start()
    weight_gradient(kv_end, head_dim, normed, dquery[...])
    weight_gradient(query_end, head_dim, row_buf, big[:, at_att : at_att + head_dim])
    kv_copy(0).wait_recv()
    kv_mixed[...] = (kv_block(1 - place.y, place.core)[...].astype(full) + kv_first[0].astype(full)).astype(low)
    kv_copy(2).start()
    scatter.pump(4, 3, 1)
    scatter.relay(3)

    dn1 = in_scatter.total()
    x = tokens_ref[...].astype(full)
    back, grad = norm_back(x, inverse_rms(x), gain_in, dn1)
    dgains[0:1, 0:width] = grad
    tokens_grad[...] = (dhidden[...] + back).astype(low)
    tokens_copy = pltpu.make_async_copy(tokens_grad, tokens_grad_out, store_sem.at[1 + 3 * len(chunks)])
    tokens_copy.start()
    step = gains_grad.shape[1]
    for origin in range(2 * lines):
        gain_part[origin * 8 : origin * 8 + 8] = dgains[:, origin * step : (origin + 1) * step]

    def gain_copy(index):
        source, target, device = (
            (gain_part, gain_first, place.mate) if index == 0 else (gain_part, gain_second, place.across)
        )
        return remote(source, target, last_send.at[3 + index], last_recv.at[3 + index], device)

    gain_copy(0).start()
    scatter.pump(4, 2)
    kv_copy(1).wait_recv()
    kv_copy(2).wait_recv()
    kv_copy(0).wait_send()
    kv_copy(1).wait_send()
    wall[:, base_column:kv_end] = (
        kv_block(place.y, place.core)[...].astype(full) + kv_first[1].astype(full) + kv_second[...].astype(full)
    ).astype(low)
    scatter.relay(4)
    gain_copy(0).wait_recv()
    gain_copy(0).wait_send()
    gain_part[...] = gain_part[...] + gain_first[...]
    gain_copy(1).start()
    scatter.pump(group_gate, 3)
    gain_copy(1).wait_recv()
    gain_copy(1).wait_send()
    gain_part[...] = gain_part[...] + gain_second[...]

    gain_scatter = LineScatter(
        place,
        lambda group, origin: gain_part.at[pl.ds(origin * 8, 8)],
        lambda group, home: gain_side.at[pl.ds(home * 8, 8)],
        lambda group, column, slot: gain_line.at[pl.ds(slot * 8, 8)],
        [False],
        gain_side_send,
        gain_side_recv,
        gain_line_send,
        gain_line_recv,
        full,
    )
    gain_scatter.start(0)
    scatter.start(group_small)
    scatter.start(group_up)
    scatter.pump(group_gate, 1, 2)

    stores = []

    def store(group, kinds, c):
        first, wide, padded = chunks[c] if kinds else (0, output_end - base_column, output_end - base_column)
        scatter.settle(group)
        for k, target in enumerate(kinds or (small_grad,)):
            slot = 3 * len(chunks) if not kinds else len([done for done in stores if done[1]])
            down, right = slot // 2 * shard, slot % 2 * CHUNK
            held = acc.at[down : down + shard, right : right + padded]
            scatter.total(group, k * wide, (k + 1) * wide, held.at[:, 0:wide])
            copy = pltpu.make_async_copy(held, target.at[:, first : first + padded], store_sem.at[slot])
            copy.start()
            stores.append((copy, bool(kinds)))
            if not kinds:
                kv_own[...] = held[:, 0:quarter].astype(low)

    for c in range(last - 1):
        store(2 * c, (down_grad,), c)
        store(2 * c + 1, (gate_grad, up_grad), c)
    scatter.relay(group_gate)
    store(group_last, (gate_grad, up_grad, down_grad), last)
    gain_scatter.pump(0)
    store(2 * last - 2, (down_grad,), last - 1)
    scatter.pump(group_small)
    gain_scatter.relay(0)
    scatter.relay(group_small)
    store(group_gate, (gate_grad,), last - 1)
    scatter.pump(group_up, 3, 1)
    store(group_small, (), 0)

    def own_block(y, core):
        return keyval_grad.at[:, pl.ds(pl.multiple_of((y * 2 + core) * quarter, quarter), quarter)]

    own_block(place.y, place.core)[...] = kv_own[...]
    targets = (place.mate, place.across, (place.dp, (1 - place.y) * 2 + (1 - place.core)))
    sends = [
        remote(kv_own, own_block(place.y, place.core), last_send.at[5 + i], last_recv.at[5 + i], target)
        for i, target in enumerate(targets)
    ]
    for copy in sends:
        copy.start()
    scatter.pump(group_up, 2)
    scatter.relay(group_up)
    gain_scatter.settle(0)
    gain_scatter.total(0, 0, gains_grad.shape[1], gains_grad)
    store(group_up, (up_grad,), last - 1)
    for i, (y, core) in enumerate(
        ((place.y, 1 - place.core), (1 - place.y, place.core), (1 - place.y, 1 - place.core))
    ):
        remote(kv_own, own_block(y, core), last_send.at[5 + i], last_recv.at[5 + i], targets[i]).wait_recv()
    for copy in sends:
        copy.wait_send()
    kv_copy(2).wait_send()
    scatter.finish()
    gain_scatter.finish()
    proj_all.finish()
    in_scatter.finish()
    for copy, _ in stores:
        copy.wait()
    tokens_copy.wait()


def backward_call(sizes, small_args, hbm_args):
    lines, rows, width, head_dim, units = sizes
    length = 4 * rows
    columns = hbm_args[0].shape[1]
    shard = hbm_args[0].shape[0] // (2 * lines)
    gains = small_args[3].shape[1]
    quarter = head_dim // 2
    base_column = 2 * head_dim - quarter
    chunks = chunks_of(units)
    groups = 2 * len(chunks) + 1
    last_wide = columns - packed_columns(units, head_dim)[0][-1][0]
    vm = pl.BlockSpec(memory_space=pltpu.VMEM)
    hbm = pl.BlockSpec(memory_space=pl.ANY)
    padded = sum(c[2] for c in chunks)
    large = [((shard, padded), full)] * 3 + [((shard, 5 * quarter), full), ((rows, width), low)]
    outs = [
        ((shard, 2 * head_dim), low),
        ((8, gains // (2 * lines)), full),
    ]
    scratch = [((rows, width), low)] + [(a.shape, a.dtype) for a in small_args[1:]]
    scratch += [
        (hbm_args[0].shape, low),
        ((lines * shard, packed_columns(units, head_dim)[0][-1][0] - base_column), low),
        ((shard, last_wide), low),
        ((lines * shard, packed_columns(units, head_dim)[0][-1][0] - base_column), low),
        ((2 * lines * shard, last_wide), low),
        ((length, 6 * CHUNK), low),
        ((length, width), low),
        ((length, width), low),
        ((length, width), full),
        ((2, rows, width), low),
        ((rows, width), low),
        ((rows, width), low),
        ((length, head_dim), low),
        ((length, head_dim), low),
        ((length, head_dim), low),
        ((length, 2 * head_dim), low),
        ((rows, width), full),
        ((rows, width), low),
        ((2, width, quarter), low),
        ((width, quarter), low),
        ((width, quarter), low),
        ((shard, quarter), low),
        ((8, gains), full),
        ((2 * lines * 8, gains // (2 * lines)), full),
        ((2 * lines * 8, gains // (2 * lines)), full),
        ((2 * lines * 8, gains // (2 * lines)), full),
        ((lines * 8, gains // (2 * lines)), full),
        ((lines * 8, gains // (2 * lines)), full),
    ]
    sems = [(4, 3), (4, 3), (groups, 4), (groups, 4), (groups, 2, 4), (groups, 2, 4)]
    sems += [(1, 4), (1, 4), (1, 1, 4), (1, 1, 4), (8,), (8,)]
    sems += [(19 + 4 * len(chunks),), (2 + 3 * len(chunks),)]
    return pl.pallas_call(
        functools.partial(backward_kernel, sizes),
        out_shape=[jax.ShapeDtypeStruct(*item) for item in large + outs],
        in_specs=[hbm] * (len(small_args) + len(hbm_args)),
        out_specs=[hbm] * len(large) + [vm] * len(outs),
        scratch_shapes=[pltpu.VMEM(*item) for item in scratch] + [pltpu.SemaphoreType.DMA(dims) for dims in sems],
        compiler_params=pltpu.CompilerParams(
            collective_id=1, has_side_effects=True, vmem_limit_bytes=63 * 1024 * 1024
        ),
        name="backward",
    )(*small_args, *hbm_args)


def adam_values(weight, gradient, first, second, step_rate):
    moment = beta_first * first + (1.0 - beta_first) * gradient
    square = beta_second * second + (1.0 - beta_second) * gradient * gradient
    scaled = moment / (1.0 - beta_first**STEP) / (jnp.sqrt(square / (1.0 - beta_second**STEP)) + adam_eps)
    return moment, square, weight - step_rate * (scaled + decay_rate * weight)


def update_kernel(units, head_dim, cut, *refs):
    passed, grads, old = refs[:2], refs[2:8], refs[8:26]
    passed_out, new = refs[26:28], refs[28:46]
    held_passed, held_grads, held, load_sem, store_sem = refs[46:48], refs[48:54], refs[54:72], refs[72], refs[73]
    gate_grad, up_grad, down_grad, small_grad, keyval_grad, gains_grad = held_grads
    quarter = head_dim // 2
    shard = old[0].shape[0]
    rows = shard // cut
    wide = D ** (-0.5)
    count = [0, 0]

    def load(source, target, part):
        at = slice(None) if part is None else pl.ds(part * rows, rows)
        copy = pltpu.make_async_copy(source.at[at], target.at[at], load_sem.at[count[0]])
        count[0] += 1
        copy.start()
        return copy

    def store(source, target, part):
        at = slice(None) if part is None else pl.ds(part * rows, rows)
        copy = pltpu.make_async_copy(source.at[at], target.at[at], store_sem.at[count[1]])
        count[1] += 1
        copy.start()
        return copy

    jobs = [(3, part, (0, 1)) for part in range(cut)] + [(4, part, (2,)) for part in range(cut)]
    jobs += [(1, None, (4,)), (0, None, (3,)), (2, None, ()), (5, None, (5,))]
    waits = []
    for index, part, needs in jobs:
        own = range(3 * index, 3 * index + 3)
        waits.append(
            [load(old[i], held[i], part) for i in own] + [load(grads[i], held_grads[i], part) for i in needs]
        )
    through = [load(source, target, None) for source, target in zip(passed, held_passed)]
    waiting = []

    def work(index, part):
        weight, first, second = held[3 * index : 3 * index + 3]
        if index == 5:
            values = adam_values(weight[...], gains_grad[0], first[...], second[...], 0.3)
            for target, value in zip((first, second, weight), values):
                target[...] = value
            return
        step = rows if part is not None else shard // 3

        def some_rows(at):
            if index == 3:
                for kind, grad in enumerate((gate_grad, up_grad)):
                    values = adam_values(
                        weight[at, kind, :], grad[at, 0:units], first[at, kind, :], second[at, kind, :], wide
                    )
                    for target, value in zip((first, second, weight), values):
                        target[at, kind, :] = value
                return
            if index == 4:
                gradient, rate = down_grad[at, 0:units], FF ** (-0.5)
            elif index == 1:
                gradient, rate = keyval_grad[at].astype(full), wide
            elif index == 0:
                gradient, rate = small_grad[at, quarter : quarter + head_dim], wide
            else:
                gradient = small_grad[at, quarter + head_dim : quarter + 2 * head_dim]
                rate = (HEADS * HEAD_DIM) ** (-0.5)
            values = adam_values(weight[at], gradient, first[at], second[at], rate)
            for target, value in zip((first, second, weight), values):
                target[at] = value

        if part is not None:
            some_rows(pl.ds(part * rows, rows))
        else:

            def body(i, carry):
                some_rows(pl.ds(pl.multiple_of(i * step, step), step))
                return carry

            lax.fori_loop(0, 3, body, 0)

    for (index, part, _), copies in zip(jobs, waits):
        if index == 1:
            for copy, source, target in zip(through, held_passed, passed_out):
                copy.wait()
                waiting.append(store(source, target, None))
        for copy in copies:
            copy.wait()
        work(index, part)
        for kind, place in ((1, 0), (2, 1), (0, 2)):
            waiting.append(store(held[3 * index + kind], new[3 * index + place], part))
    for copy in waiting:
        copy.wait()


def update_call(units, head_dim, passed, grads, old, cut):
    hbm = pl.BlockSpec(memory_space=pl.ANY)
    outs = list(passed)
    for index in range(6):
        outs += [old[3 * index + kind] for kind in (1, 2, 0)]
    loads = 9 * cut + 18
    return pl.pallas_call(
        functools.partial(update_kernel, units, head_dim, cut),
        out_shape=[jax.ShapeDtypeStruct(a.shape, a.dtype) for a in outs],
        in_specs=[hbm] * (len(passed) + len(grads) + len(old)),
        out_specs=[hbm] * len(outs),
        scratch_shapes=[pltpu.VMEM(a.shape, a.dtype) for a in (*passed, *grads, *old)]
        + [pltpu.SemaphoreType.DMA((loads,)), pltpu.SemaphoreType.DMA((2 + 6 * cut + 12,))],
        compiler_params=pltpu.CompilerParams(vmem_limit_bytes=60 * 1024 * 1024),
        name="update",
    )(*passed, *grads, *old)


def mixed_dot(left, right):
    return jnp.dot(left, right, preferred_element_type=jnp.float32)


def rms_scale(vector, gain_vec):
    return (
        vector
        * lax.rsqrt(jnp.mean(vector * vector, axis=-1, keepdims=True) + eps_norm)
        * (1.0 + gain_vec)
    )


def rotate(vector, positions):
    half_dim = vector.shape[-1] // 2
    inv_freq = rope_base ** (-2.0 * jnp.arange(half_dim).astype(jnp.float32) / vector.shape[-1])
    angles = positions[:, None] * inv_freq[None, :]
    cosine = jnp.cos(angles)[:, None, :]
    sine_v = jnp.sin(angles)[:, None, :]
    front_half = vector[..., :half_dim]
    back_half = vector[..., half_dim:]
    return jnp.concatenate(
        [front_half * cosine - back_half * sine_v, back_half * cosine + front_half * sine_v],
        axis=-1,
    )


def adam_step(weight, gradient, moment, second, step_rate):
    moment = beta_first * moment + (1.0 - beta_first) * gradient
    second = beta_second * second + (1.0 - beta_second) * gradient * gradient
    scaled = (
        moment
        / (1.0 - beta_first**STEP)
        / (jnp.sqrt(second / (1.0 - beta_second**STEP)) + adam_eps)
    )
    return (moment, second, weight - step_rate * (scaled + decay_rate * weight))


def plain_device(
    tokens,
    cotangent,
    prefix,
    query_weight,
    keyval_weight,
    output_weight,
    gateup_weight,
    down_weight,
    norm_gains,
    query_first,
    keyval_first,
    output_first,
    gateup_first,
    down_first,
    gains_first,
    query_second,
    keyval_second,
    output_second,
    gateup_second,
    down_second,
    gains_second,
):
    rows_dev, width = tokens.shape
    length = rows_dev * lax.axis_size("tensor")
    query_full, keyval_full, output_full, gateup_full, down_full, gains_full = (
        lax.all_gather(query_weight.astype(jnp.bfloat16), "dp", axis=0, tiled=True),
        lax.all_gather(keyval_weight.astype(jnp.bfloat16), "dp", axis=0, tiled=True),
        lax.all_gather(output_weight.astype(jnp.bfloat16), "dp", axis=0, tiled=True),
        lax.all_gather(gateup_weight.astype(jnp.bfloat16), "dp", axis=0, tiled=True),
        lax.all_gather(down_weight.astype(jnp.bfloat16), "dp", axis=0, tiled=True),
        lax.all_gather(norm_gains.astype(jnp.bfloat16), "dp", axis=0, tiled=True),
    )
    head_dim = keyval_full.shape[1] // 2
    heads_dev = query_full.shape[1] // head_dim
    units = down_full.shape[1]
    gain_values = gains_full.astype(jnp.float32)
    gain_input = gain_values[0:width]
    gain_attn = gain_values[width : 2 * width]
    gain_pre = gain_values[2 * width : 3 * width]
    gain_ffn = gain_values[3 * width : 4 * width]
    gain_query = gain_values[4 * width : 4 * width + head_dim]
    gain_key = gain_values[4 * width + head_dim : 4 * width + 2 * head_dim]
    positions = jnp.arange(length).astype(jnp.float32)
    span_rows = min(512, length)
    count_blocks = length // span_rows
    starts = jnp.arange(0, length, span_rows, dtype=jnp.int32)
    columns = jnp.arange(length, dtype=jnp.int32)
    prefix_len = prefix[0]
    gateup_flat = gateup_full.reshape(width, 2 * units)

    def shape_query(raw_rows, gain_vec):
        return rotate(rms_scale(raw_rows, gain_vec), positions)

    def shape_key(raw_rows, gain_vec):
        return rotate(rms_scale(raw_rows[:, None, :], gain_vec), positions)[:, 0]

    token_rows = tokens.astype(jnp.float32)
    normed_local = rms_scale(token_rows, gain_input).astype(jnp.bfloat16)
    normed = lax.all_gather(normed_local, "tensor", axis=0, tiled=True)
    query_raw = mixed_dot(normed, query_full).reshape(length, heads_dev, head_dim)
    keyval_raw = mixed_dot(normed, keyval_full)
    query_rot = shape_query(query_raw, gain_query).astype(jnp.bfloat16)
    key_rot = shape_key(keyval_raw[:, :head_dim], gain_key).astype(jnp.bfloat16)
    value_low = keyval_raw[:, head_dim:].astype(jnp.bfloat16)

    def scores_of(row_start):
        row_ids = row_start + jnp.arange(span_rows, dtype=jnp.int32)
        q_blk = lax.dynamic_slice_in_dim(query_rot, row_start, span_rows, 0)
        raw_scores = (
            jnp.einsum("rhd,kd->hrk", q_blk, key_rot, preferred_element_type=jnp.float32)
            * query_scale
        )
        allowed = (columns[None, :] <= row_ids[:, None]) | (columns[None, :] < prefix_len)
        return (jnp.where(allowed[None], raw_scores, masked_fill), q_blk)

    def forward_block(row_start):
        scores, q_blk = scores_of(row_start)
        row_peak = jnp.max(scores, axis=-1, keepdims=True)
        shifted = jnp.exp(scores - row_peak)
        denom_sum = jnp.sum(shifted, axis=-1, keepdims=True)
        soft_probs = (shifted / denom_sum).astype(jnp.bfloat16)
        mixed_rows = jnp.einsum(
            "hrk,kd->rhd", soft_probs, value_low, preferred_element_type=jnp.float32
        )
        return (mixed_rows, (row_peak + jnp.log(denom_sum))[..., 0])

    attended_blocks, log_sums = lax.map(forward_block, starts)
    attended = attended_blocks.reshape(length, heads_dev * head_dim).astype(jnp.bfloat16)
    attn_part = jnp.einsum("rk,dk->rd", attended, output_full, preferred_element_type=jnp.float32)
    projected = lax.psum_scatter(
        attn_part.astype(jnp.bfloat16), "tensor", scatter_dimension=0, tiled=True
    ).astype(jnp.float32)
    hidden_state = token_rows + rms_scale(projected, gain_attn)
    normed_two = lax.all_gather(
        rms_scale(hidden_state, gain_pre).astype(jnp.bfloat16), "tensor", axis=0, tiled=True
    )
    gateup = mixed_dot(normed_two, gateup_flat)
    gate_part = gateup[:, :units]
    up_part = gateup[:, units:]
    activation = (jax.nn.gelu(gate_part, approximate=True) * up_part).astype(jnp.bfloat16)
    down_part = jnp.einsum("ru,du->rd", activation, down_full, preferred_element_type=jnp.float32)
    down_sum = lax.psum_scatter(
        down_part.astype(jnp.bfloat16), "tensor", scatter_dimension=0, tiled=True
    ).astype(jnp.float32)
    block_out = hidden_state + rms_scale(down_sum, gain_ffn)
    grad_out = cotangent.astype(jnp.float32)
    pull_ffn = jax.vjp(rms_scale, down_sum, gain_ffn)[1]
    grad_down, grad_gain_ffn = pull_ffn(grad_out)
    down_back = lax.all_gather(grad_down.astype(jnp.bfloat16), "tensor", axis=0, tiled=True)
    grad_activation = mixed_dot(down_back, down_full)
    grad_down_w = jnp.einsum("rd,ru->du", down_back, activation, preferred_element_type=jnp.float32)

    def geglu(gate_in, up_in):
        return jax.nn.gelu(gate_in, approximate=True) * up_in

    pull_act = jax.vjp(geglu, gate_part, up_part)[1]
    grad_gate, grad_up = pull_act(grad_activation)
    grad_gateup = jnp.concatenate([grad_gate, grad_up], axis=1).astype(jnp.bfloat16)
    grad_gateup_w = jnp.einsum(
        "rd,ru->du", normed_two, grad_gateup, preferred_element_type=jnp.float32
    ).reshape(width, 2, units)
    grad_normed_two = jnp.einsum(
        "ru,du->rd", grad_gateup, gateup_flat, preferred_element_type=jnp.float32
    )
    grad_pre_rows = lax.psum_scatter(
        grad_normed_two.astype(jnp.bfloat16), "tensor", scatter_dimension=0, tiled=True
    ).astype(jnp.float32)
    pull_pre = jax.vjp(rms_scale, hidden_state, gain_pre)[1]
    grad_hidden_norm, grad_gain_pre = pull_pre(grad_pre_rows)
    grad_hidden = grad_out + grad_hidden_norm
    pull_attn = jax.vjp(rms_scale, projected, gain_attn)[1]
    grad_proj, grad_gain_attn = pull_attn(grad_hidden)
    proj_back = lax.all_gather(grad_proj.astype(jnp.bfloat16), "tensor", axis=0, tiled=True)
    grad_output_w = jnp.einsum("rd,rk->dk", proj_back, attended, preferred_element_type=jnp.float32)
    grad_attended = (
        mixed_dot(proj_back, output_full)
        .astype(jnp.bfloat16)
        .reshape(count_blocks, span_rows, heads_dev, head_dim)
    )

    def backward_block(carry, batch_item):
        key_acc, value_acc = carry
        row_start, grad_att, lse_blk = batch_item
        scores, q_blk = scores_of(row_start)
        soft_full = jnp.exp(scores - lse_blk[..., None])
        grad_probs = jnp.einsum(
            "rhd,kd->hrk", grad_att, value_low, preferred_element_type=jnp.float32
        )
        delta_rows = jnp.sum(soft_full * grad_probs, axis=-1, keepdims=True)
        grad_scores = (soft_full * (grad_probs - delta_rows)).astype(jnp.bfloat16)
        grad_query = (
            jnp.einsum("hrk,kd->rhd", grad_scores, key_rot, preferred_element_type=jnp.float32)
            * query_scale
        )
        key_acc = (
            key_acc
            + jnp.einsum("hrk,rhd->kd", grad_scores, q_blk, preferred_element_type=jnp.float32)
            * query_scale
        )
        value_acc = value_acc + jnp.einsum(
            "hrk,rhd->kd",
            soft_full.astype(jnp.bfloat16),
            grad_att,
            preferred_element_type=jnp.float32,
        )
        return ((key_acc, value_acc), grad_query)

    zero_rows = jnp.zeros((length, head_dim), jnp.float32)
    (grad_key_rot, grad_value), grad_query_blocks = lax.scan(
        backward_block, (zero_rows, zero_rows), (starts, grad_attended, log_sums)
    )
    grad_query_rot = grad_query_blocks.reshape(length, heads_dev, head_dim)
    pull_query = jax.vjp(shape_query, query_raw, gain_query)[1]
    grad_query_raw, grad_gain_query = pull_query(grad_query_rot)
    pull_key = jax.vjp(shape_key, keyval_raw[:, :head_dim], gain_key)[1]
    grad_key_raw, grad_gain_key = pull_key(grad_key_rot)
    grad_query_low = grad_query_raw.reshape(length, heads_dev * head_dim).astype(jnp.bfloat16)
    grad_keyval = jnp.concatenate([grad_key_raw, grad_value], axis=1)
    grad_query_w = jnp.einsum(
        "rd,rk->dk", normed, grad_query_low, preferred_element_type=jnp.float32
    )
    grad_normed_query = jnp.einsum(
        "rk,dk->rd", grad_query_low, query_full, preferred_element_type=jnp.float32
    )
    grad_normed_part, grad_keyval_own = (
        lax.psum_scatter(
            grad_normed_query.astype(jnp.bfloat16), "tensor", scatter_dimension=0, tiled=True
        ).astype(jnp.float32),
        lax.psum_scatter(
            grad_keyval.astype(jnp.bfloat16), "tensor", scatter_dimension=0, tiled=True
        ).astype(jnp.float32),
    )
    grad_keyval_low = grad_keyval_own.astype(jnp.bfloat16)
    grad_keyval_w = jnp.einsum(
        "rd,rk->dk", normed_local, grad_keyval_low, preferred_element_type=jnp.float32
    )
    grad_normed = grad_normed_part + jnp.einsum(
        "rk,dk->rd", grad_keyval_low, keyval_full, preferred_element_type=jnp.float32
    )
    pull_input = jax.vjp(rms_scale, token_rows, gain_input)[1]
    grad_token_norm, grad_gain_input = pull_input(grad_normed)
    tokens_grad = (grad_hidden + grad_token_norm).astype(jnp.bfloat16)
    grad_gains = jnp.concatenate(
        [
            grad_gain_input,
            grad_gain_attn,
            grad_gain_pre,
            grad_gain_ffn,
            grad_gain_query,
            grad_gain_key,
        ]
    )
    keyval_total, gains_total = (
        lax.psum(grad_keyval_w.astype(jnp.bfloat16), "tensor").astype(jnp.float32),
        lax.psum(grad_gains.astype(jnp.bfloat16), "tensor").astype(jnp.float32),
    )
    query_sum, keyval_sum, output_sum, gateup_sum, down_grad_sum, gains_sum = (
        lax.psum_scatter(grad_query_w, "dp", scatter_dimension=0, tiled=True),
        lax.psum_scatter(keyval_total, "dp", scatter_dimension=0, tiled=True),
        lax.psum_scatter(grad_output_w, "dp", scatter_dimension=0, tiled=True),
        lax.psum_scatter(grad_gateup_w, "dp", scatter_dimension=0, tiled=True),
        lax.psum_scatter(grad_down_w, "dp", scatter_dimension=0, tiled=True),
        lax.psum_scatter(gains_total, "dp", scatter_dimension=0, tiled=True),
    )
    query_moment, query_square, query_master = adam_step(
        query_weight, query_sum, query_first, query_second, D ** (-0.5)
    )
    keyval_moment, keyval_square, keyval_master = adam_step(
        keyval_weight, keyval_sum, keyval_first, keyval_second, D ** (-0.5)
    )
    output_moment, output_square, output_master = adam_step(
        output_weight, output_sum, output_first, output_second, (HEADS * HEAD_DIM) ** (-0.5)
    )
    gateup_moment, gateup_square, gateup_master = adam_step(
        gateup_weight, gateup_sum, gateup_first, gateup_second, D ** (-0.5)
    )
    down_moment, down_square, down_master = adam_step(
        down_weight, down_grad_sum, down_first, down_second, FF ** (-0.5)
    )
    gains_moment, gains_square, gains_master = adam_step(
        norm_gains, gains_sum, gains_first, gains_second, 0.3
    )
    return (
        block_out.astype(jnp.bfloat16),
        tokens_grad,
        query_moment,
        query_square,
        query_master,
        keyval_moment,
        keyval_square,
        keyval_master,
        output_moment,
        output_square,
        output_master,
        gateup_moment,
        gateup_square,
        gateup_master,
        down_moment,
        down_square,
        down_master,
        gains_moment,
        gains_square,
        gains_master,
    )


def per_device(
    tokens,
    cotangent,
    prefix,
    query_weight,
    keyval_weight,
    output_weight,
    gateup_weight,
    down_weight,
    norm_gains,
    query_first,
    keyval_first,
    output_first,
    gateup_first,
    down_first,
    gains_first,
    query_second,
    keyval_second,
    output_second,
    gateup_second,
    down_second,
    gains_second,
):
    rows, width = tokens.shape
    lines = lax.axis_size("dp") // 2
    shard = query_weight.shape[0]
    head_dim = keyval_weight.shape[1] // 2
    units = down_weight.shape[1]
    fits = (
        lax.axis_size("tensor") == 4
        and lax.axis_size("dp") == 8
        and len(chunks_of(units)) == 4
        and query_weight.shape[1] == head_dim
        and shard % 16 == 0
        and norm_gains.shape[0] % 128 == 0
        and (3 * len(chunks_of(units)) + 2) // 2 * shard <= 4 * rows
    )
    if not fits:
        return plain_device(
            tokens,
            cotangent,
            prefix,
            query_weight,
            keyval_weight,
            output_weight,
            gateup_weight,
            down_weight,
            norm_gains,
            query_first,
            keyval_first,
            output_first,
            gateup_first,
            down_first,
            gains_first,
            query_second,
            keyval_second,
            output_second,
            gateup_second,
            down_second,
            gains_second,
        )
    length = 4 * rows
    sizes = (lines, rows, width, head_dim, units)
    weights = (keyval_weight, query_weight, output_weight, gateup_weight, down_weight)
    angles = np.arange(length)[:, None] * (rope_base ** (-2.0 * np.arange(head_dim // 2) / head_dim))[None, :]
    cosine = jnp.asarray(np.cos(angles), full)
    sine = jnp.asarray(np.sin(angles), full)
    *saved, gvec, proj, hidden, grad_down, dgain_ffn, block_out = forward_call(
        sizes, prefix, tokens, cotangent, norm_gains, weights, cosine, sine
    )
    *grads, tokens_grad, keyval_sum, gains_sum = backward_call(
        sizes, (grad_down, cotangent, tokens, gvec, dgain_ffn, proj, hidden, cosine, sine), saved
    )
    old = (
        query_weight,
        query_first,
        query_second,
        keyval_weight,
        keyval_first,
        keyval_second,
        output_weight,
        output_first,
        output_second,
        gateup_weight,
        gateup_first,
        gateup_second,
        down_weight,
        down_first,
        down_second,
        norm_gains,
        gains_first,
        gains_second,
    )
    return tuple(update_call(units, head_dim, (block_out, tokens_grad), (*grads, keyval_sum, gains_sum), old, 3))


def solution(mesh):
    placed = (
        P(("dp", "tensor"), None),
        P(("dp", "tensor"), None),
        P("dp"),
        P("dp", "tensor"),
        P("dp", None),
        P("dp", "tensor"),
        P("dp", None, "tensor"),
        P("dp", "tensor"),
        P("dp"),
        P("dp", "tensor"),
        P("dp", None),
        P("dp", "tensor"),
        P("dp", None, "tensor"),
        P("dp", "tensor"),
        P("dp"),
        P("dp", "tensor"),
        P("dp", None),
        P("dp", "tensor"),
        P("dp", None, "tensor"),
        P("dp", "tensor"),
        P("dp"),
    )
    return jax.shard_map(
        per_device,
        mesh=mesh,
        in_specs=placed,
        out_specs=(
            P(("dp", "tensor"), None),
            P(("dp", "tensor"), None),
            P("dp", "tensor"),
            P("dp", "tensor"),
            P("dp", "tensor"),
            P("dp", None),
            P("dp", None),
            P("dp", None),
            P("dp", "tensor"),
            P("dp", "tensor"),
            P("dp", "tensor"),
            P("dp", None, "tensor"),
            P("dp", None, "tensor"),
            P("dp", None, "tensor"),
            P("dp", "tensor"),
            P("dp", "tensor"),
            P("dp", "tensor"),
            P("dp"),
            P("dp"),
            P("dp"),
        ),
        check_vma=False,
    )
```

```python
import functools

import jax
import jax.numpy as jnp
import numpy as np
from jax import lax
from jax.experimental import pallas as pl
from jax.experimental.pallas import tpu as pltpu
from jax.sharding import PartitionSpec as P

D = 1152
FF = 6912
HEADS = 4
HEAD_DIM = 256
STEP = 10


eps_norm = 1e-06
query_scale = 0.0625
rope_base = 1000000.0
beta_first = 0.9
beta_second = 0.95
adam_eps = 1e-08
decay_rate = 0.01
masked_fill = -1e30
MESH = pl.DeviceIdType.MESH
low = jnp.bfloat16
full = jnp.float32
CHUNK = 512


def dot_nn(left, right):
    return lax.dot_general(left, right, (((1,), (0,)), ((), ())), preferred_element_type=full)


def dot_nt(left, right):
    return lax.dot_general(left, right, (((1,), (1,)), ((), ())), preferred_element_type=full)


def dot_tn(left, right):
    return lax.dot_general(left, right, (((0,), (0,)), ((), ())), preferred_element_type=full)


def chunks_of(units):
    out = []
    first = 0
    while first < units:
        width = min(CHUNK, units - first)
        out.append((first, width, -(-width // 128) * 128))
        first += width
    return out


def small_columns(head_dim):
    return 2 * head_dim, 3 * head_dim, 4 * head_dim


def packed_columns(units, head_dim):
    at = small_columns(head_dim)[2]
    places = []
    for first, width, _ in chunks_of(units):
        places.append((at, at + width, at + 2 * width))
        at += -(-3 * width // 128) * 128
    return places, at


class Place:
    def __init__(self):
        self.dp = lax.axis_index("dp")
        self.tensor = lax.axis_index("tensor")
        self.z = self.dp // 2
        self.x = self.dp % 2
        self.y = self.tensor // 2
        self.core = self.tensor % 2
        self.homes = (self.z, self.z + 1 - 2 * (self.z % 2), (self.z + 2) % 4, 3 - self.z)
        self.end = ((self.z + 1) // 2 + 1) % 2
        self.middle = self.end == 0
        self.mate = (self.dp, self.y * 2 + (1 - self.core))
        self.across = (self.dp, (1 - self.y) * 2 + self.core)
        self.side = (self.z * 2 + (1 - self.x), self.tensor)
        self.inner = ((1 + self.z % 2) * 2 + self.x, self.tensor)

    def line(self, step):
        return (self.homes[step] * 2 + self.x, self.tensor)

    def peers(self):
        return [self.mate, self.across, self.side] + [self.line(s) for s in (1, 2, 3)]


def greet(place):
    for peer in place.peers():
        pl.semaphore_signal(pltpu.get_barrier_semaphore(), inc=1, device_id=peer, device_id_type=MESH)


def meet(place):
    pl.semaphore_wait(pltpu.get_barrier_semaphore(), len(place.peers()))


def remote(source, target, send_sem, recv_sem, device):
    return pltpu.make_async_remote_copy(
        src_ref=source,
        dst_ref=target,
        send_sem=send_sem,
        recv_sem=recv_sem,
        device_id=device,
        device_id_type=MESH,
    )


class LineGather:
    def __init__(self, place, region, wide, send, recv, relay_send, side_send, side_recv):
        self.place, self.region, self.wide = place, region, wide
        self.send, self.recv, self.relay_send = send, recv, relay_send
        self.side_send, self.side_recv = side_send, side_recv

    def columns(self, group):
        return (0, 1) if self.wide[group] else (0,)

    def origin(self, column, step):
        place = self.place
        return place.homes[step] * 2 + (place.x if column == 0 else 1 - place.x)

    def along(self, group, column, step):
        block = self.region(group, self.origin(column, 0))
        return remote(
            block, block, self.send.at[group, column, step], self.recv.at[group, column, step], self.place.line(step)
        )

    def arrive(self, group, column, step):
        block = self.region(group, self.origin(column, step))
        remote(
            block, block, self.send.at[group, column, step], self.recv.at[group, column, step], self.place.line(step)
        ).wait_recv()

    def relay(self, group, column):
        block = self.region(group, self.origin(column, 2))
        return remote(
            block, block, self.relay_send.at[group, column], self.recv.at[group, column, 3], self.place.line(1)
        )

    def sideways(self, group, step):
        block = self.region(group, self.origin(0, step))
        return remote(
            block, block, self.side_send.at[group, step], self.side_recv.at[group, step], self.place.side
        )

    def arrive_side(self, group, step):
        block = self.region(group, self.origin(1, step))
        remote(
            block, block, self.side_send.at[group, step], self.side_recv.at[group, step], self.place.side
        ).wait_recv()

    def start_line(self, group, column):
        self.along(group, column, 2).start()
        self.along(group, column, 1).start()

        @pl.when(self.place.middle)
        def _():
            self.along(group, column, 3).start()

    def start_side(self, group):
        self.sideways(group, 0).start()

    def start(self, group):
        self.start_side(group)
        self.start_line(group, 0)

    def widen(self, group):
        self.arrive_side(group, 0)
        self.start_line(group, 1)

    def pass_on(self, group, *columns):
        for column in columns or self.columns(group):
            self.arrive(group, column, 2)

            @pl.when(self.place.middle)
            def _():
                self.relay(group, column).start()

            if not self.wide[group]:
                self.sideways(group, 2).start()

    def collect(self, group):
        for column in self.columns(group):
            for step in (1, 3):
                self.arrive(group, column, step)
                if not self.wide[group]:
                    self.sideways(group, step).start()

    def ready(self, group):
        if not self.wide[group]:
            for step in (0, 2, 1, 3):
                self.arrive_side(group, step)

    def finish(self):
        for group in range(len(self.wide)):
            for column in self.columns(group):
                self.along(group, column, 1).wait_send()
                self.along(group, column, 2).wait_send()

                @pl.when(self.place.middle)
                def _():
                    self.along(group, column, 3).wait_send()
                    self.relay(group, column).wait_send()

            for step in (0,) if self.wide[group] else (0, 1, 2, 3):
                self.sideways(group, step).wait_send()


def row_slabs(buffer, rows, first=0, count=None):
    return lambda y, core: buffer.at[pl.ds((y * 2 + core) * rows + first, count or rows)]


def column_slabs(buffer, wide):
    return lambda y, core: buffer.at[:, pl.ds(pl.multiple_of((y * 2 + core) * wide, wide), wide)]


class RowGather:
    def __init__(self, place, source, slab, send, recv):
        self.place, self.source, self.slab = place, source, slab
        self.send, self.recv = send, recv

    def copy(self, index):
        place = self.place
        slab = self.slab(1 - place.y if index == 2 else place.y, place.core)
        source = slab if index == 2 else self.source
        device = place.across if index == 1 else place.mate
        return remote(source, slab, self.send.at[index], self.recv.at[index], device)

    def arrival(self, index, y, core):
        slab = self.slab(y, core)
        remote(slab, slab, self.send.at[index], self.recv.at[index], self.place.mate).wait_recv()

    def start(self):
        self.copy(1).start()
        self.copy(0).start()

    def wait_mate(self):
        self.arrival(0, self.place.y, 1 - self.place.core)

    def wait_across(self):
        self.arrival(1, 1 - self.place.y, self.place.core)
        self.copy(2).start()

    def wait_corner(self):
        self.arrival(2, 1 - self.place.y, 1 - self.place.core)

    def finish(self):
        for index in range(3):
            self.copy(index).wait_send()


class RowScatter:
    def __init__(self, place, slab, first, second, mixed, send, recv):
        self.place, self.slab = place, slab
        self.first, self.second, self.mixed = first, second, mixed
        self.send, self.recv = send, recv

    def copy(self, index):
        place = self.place
        if index == 2:
            return remote(self.mixed, self.second, self.send.at[2], self.recv.at[2], place.across)
        source = self.slab(1 - place.y if index == 0 else place.y, 1 - place.core)
        return remote(source, self.first.at[index], self.send.at[index], self.recv.at[index], place.mate)

    def order(self):
        place = self.place
        return (
            (1 - place.y) * 2 + (1 - place.core),
            (1 - place.y) * 2 + place.core,
            place.y * 2 + (1 - place.core),
            place.y * 2 + place.core,
        )

    def after(self, step):
        if step == 0:
            self.copy(0).start()
        if step == 1:
            self.copy(0).wait_recv()
            mixed = self.slab(1 - self.place.y, self.place.core)[...].astype(full) + self.first[0].astype(full)
            self.mixed[...] = mixed.astype(low)
            self.copy(2).start()
        if step == 2:
            self.copy(1).start()

    def total(self):
        self.copy(1).wait_recv()
        here = self.slab(self.place.y, self.place.core)[...].astype(full) + self.first[1].astype(full)
        self.copy(2).wait_recv()
        return here + self.second[...].astype(full)

    def finish(self):
        for index in range(3):
            self.copy(index).wait_send()


def inverse_rms(rows):
    return lax.rsqrt(jnp.mean(rows * rows, axis=-1, keepdims=True) + eps_norm)


def rotate_rows(rows, cosine, sine):
    half = rows.shape[-1] // 2
    front, back = rows[:, :half], rows[:, half:]
    return jnp.concatenate([front * cosine - back * sine, back * cosine + front * sine], axis=-1)


def rotate_back(rows, cosine, sine):
    half = rows.shape[-1] // 2
    front, back = rows[:, :half], rows[:, half:]
    return jnp.concatenate([front * cosine + back * sine, back * cosine - front * sine], axis=-1)


def gelu_parts(gate):
    scale = 0.7978845608028654
    square = gate * gate
    bent = jnp.tanh(scale * gate * (1.0 + 0.044715 * square))
    return square, bent


def forward_kernel(
    sizes,
    prefix_ref,
    tokens_in,
    cot_in,
    gains_in,
    keyval_in,
    query_in,
    output_in,
    gateup_in,
    down_in,
    cos_in,
    sin_in,
    wall_out,
    normed_out,
    normed_two_out,
    query_out,
    key_out,
    key_rot_out,
    value_out,
    attended_out,
    probs_out,
    gate_out,
    up_out,
    act_out,
    gvec_out,
    proj_out,
    hidden_out,
    grad_down_out,
    dgain_ffn_out,
    block_out_out,
    cot_ref,
    gains_ref,
    keyval_ref,
    query_ref,
    output_ref,
    gateup_ref,
    down_ref,
    cos_ref,
    sin_ref,
    gvec,
    proj_keep,
    hidden_keep,
    dgain_ffn,
    block_out,
    wall,
    normed,
    normed_two,
    query_raw,
    key_raw,
    attended,
    probs,
    gate_keep,
    up_keep,
    act,
    tok_full,
    gains_full,
    key_rot,
    value_low,
    part_one,
    first_one,
    second_one,
    mixed_one,
    down_acc,
    line_send,
    line_recv,
    relay_send,
    side_send,
    side_recv,
    row_send,
    row_recv,
    keep_sem,
    load_sem,
):
    lines, rows, width, head_dim, units = sizes
    place = Place()
    greet(place)
    own_rows = pl.ds(place.tensor * rows, rows)
    loads = {}
    for name, source, target in (
        ("gains", gains_in, gains_ref),
        ("keyval", keyval_in, keyval_ref),
        ("query", query_in, query_ref),
        ("output", output_in, output_ref),
        ("gateup", gateup_in, gateup_ref),
        ("down", down_in, down_ref),
        ("tokens", tokens_in, tok_full.at[own_rows]),
        ("cos", cos_in, cos_ref),
        ("sin", sin_in, sin_ref),
        ("cot", cot_in, cot_ref),
    ):
        loads[name] = pltpu.make_async_copy(source, target, load_sem.at[len(loads)])
        loads[name].start()
    length = 4 * rows
    shard = keyval_ref.shape[0]
    places, columns = packed_columns(units, head_dim)
    chunks = chunks_of(units)
    last = len(chunks) - 1
    kv_end, query_end, output_end = small_columns(head_dim)
    split, split_last = places[last - 1][2] + 128, places[last][2] // 128 * 128
    quarter = kv_end // 4
    own_quarter = pl.ds(pl.multiple_of(place.tensor * quarter, quarter), quarter)
    spans = [(0, kv_end), (kv_end, output_end)]
    spans += [(places[c][0], places[c + 1][0]) for c in range(last - 2)]
    spans += [(places[last - 2][0], places[last - 2][2]), (places[last - 1][0], split)]
    spans += [(places[last - 2][2], places[last - 1][0]), (split, split_last), (split_last, columns)]
    tail = len(spans)

    def region(group, origin):
        if group == 0:
            return gains_full.at[pl.ds(origin * 8, 8)]
        if group == 1:
            return wall.at[pl.ds(origin * shard, shard), own_quarter]
        lo, hi = spans[group - 1]
        return wall.at[pl.ds(origin * shard, shard), lo:hi]

    wide_groups = [False] * (tail - 1) + [True] * 2
    gather = LineGather(place, region, wide_groups, line_send, line_recv, relay_send, side_send, side_recv)
    tokens_all = RowGather(place, tokens_in, row_slabs(tok_full, rows), row_send.at[0], row_recv.at[0])
    kept = []

    def keep(source, target):
        copy = pltpu.make_async_copy(source, target, keep_sem.at[len(kept)])
        copy.start()
        kept.append(copy)

    def keep_span(group):
        lo, hi = spans[group - 1]
        keep(wall.at[:, lo:hi], wall_out.at[:, lo:hi])

    for name in ("gains", "keyval", "query", "output"):
        loads[name].wait()
    own_gains = gains_ref[...].astype(low).astype(full).reshape(1, -1)
    gains_full[pl.ds(place.dp * 8, 8)] = jnp.broadcast_to(own_gains, (8, own_gains.shape[1]))
    own = pl.ds(place.dp * shard, shard)
    wall[own, own_quarter] = keyval_ref[:, own_quarter].astype(low)
    wall[own, kv_end:query_end] = query_ref[...].astype(low)
    wall[own, query_end:output_end] = output_ref[...].astype(low)
    meet(place)
    tokens_all.start()
    for group in range(3):
        gather.start(group)
    loads["gateup"].wait()
    loads["down"].wait()
    for (first, wide, _), at in zip(chunks, places):
        for kind, lo in enumerate(at):
            units_here = slice(first, first + wide)
            piece = down_ref[:, units_here] if kind == 2 else gateup_ref[:, kind, units_here]
            wall[own, lo : lo + wide] = piece.astype(low)
    filled = places[last][2] + chunks[last][1]
    if filled < columns:
        wall[own, filled:columns] = jnp.zeros((shard, columns - filled), low)
    gather.start(3)
    for name in ("tokens", "cos", "sin", "cot"):
        loads[name].wait()
    tokens_all.wait_mate()
    tokens_all.wait_across()
    gather.pass_on(0)
    gather.pass_on(1)
    gather.collect(0)
    gather.collect(1)
    tokens_all.wait_corner()
    gather.pass_on(2)
    gather.ready(1)
    quarters = column_slabs(wall, quarter)
    keyval_all = RowGather(
        place, quarters(place.y, place.core), quarters, row_send.at[7], row_recv.at[7]
    )
    keyval_all.start()
    gather.collect(2)
    for group in range(4, tail + 1):
        gather.start_side(group)
    gather.start_line(4, 0)
    gather.ready(0)
    step = gains_ref.shape[0]
    for origin in range(2 * lines):
        gvec[:, origin * step : (origin + 1) * step] = gains_full[origin * 8 : origin * 8 + 8]
    keep(gvec, gvec_out)
    gain_in = 1.0 + gvec[0:1, 0:width]
    gain_attn = 1.0 + gvec[0:1, width : 2 * width]
    gain_pre = 1.0 + gvec[0:1, 2 * width : 3 * width]
    gain_ffn = 1.0 + gvec[0:1, 3 * width : 4 * width]
    gain_query = 1.0 + gvec[0:1, 4 * width : 4 * width + head_dim]
    gain_key = 1.0 + gvec[0:1, 4 * width + head_dim : 4 * width + 2 * head_dim]

    def norm_slab(index, carry):
        at = pl.ds(pl.multiple_of(index * rows, rows), rows)
        x = tok_full[at].astype(full)
        normed[at] = (x * inverse_rms(x) * gain_in).astype(low)
        return carry

    lax.fori_loop(0, 4, norm_slab, 0)
    keep(normed, normed_out)
    keyval_all.wait_mate()
    keyval_all.wait_across()
    gather.ready(2)
    keyval_all.wait_corner()

    def project_slab(index, carry):
        at = pl.ds(pl.multiple_of(index * rows, rows), rows)
        n1 = normed[at]
        query_raw[at] = dot_nn(n1, wall[:, kv_end:query_end])
        kv = dot_nn(n1, wall[:, 0:kv_end])
        k = kv[:, :head_dim]
        key_raw[at] = k
        key_rot[at] = rotate_rows(k * inverse_rms(k) * gain_key, cos_ref[at], sin_ref[at]).astype(low)
        value_low[at] = kv[:, head_dim:].astype(low)
        return carry

    lax.fori_loop(0, 4, project_slab, 0)
    gather.pass_on(3)
    gather.start_line(5, 0)
    keep(query_raw, query_out)
    keep(key_raw, key_out)
    keep(key_rot, key_rot_out)
    keep(value_low, value_out)
    keep_span(1)
    keep_span(2)

    out_scatter = RowScatter(
        place, row_slabs(part_one, rows), first_one, second_one, mixed_one, row_send.at[1], row_recv.at[1]
    )

    def attend_slab(index):
        at = pl.ds(pl.multiple_of(index * rows, rows), rows)
        q = query_raw[at]
        qr = rotate_rows(q * inverse_rms(q) * gain_query, cos_ref[at], sin_ref[at]).astype(low)
        scores = dot_nt(qr, key_rot[...]) * query_scale
        row_ids = lax.broadcasted_iota(jnp.int32, (rows, length), 0) + index * rows
        columns = lax.broadcasted_iota(jnp.int32, (rows, length), 1)
        allowed = (columns <= row_ids) | (columns < prefix_ref[0])
        scores = jnp.where(allowed, scores, masked_fill)
        shifted = jnp.exp(scores - jnp.max(scores, axis=-1, keepdims=True))
        soft = (shifted / jnp.sum(shifted, axis=-1, keepdims=True)).astype(low)
        probs[at] = soft
        mixed = dot_nn(soft, value_low[...]).astype(low)
        attended[at] = mixed
        part_one[at] = dot_nt(mixed, wall[:, query_end:output_end]).astype(low)

    for step, index in enumerate(out_scatter.order()):
        attend_slab(index)
        out_scatter.after(step)
    keep(probs, probs_out)
    keep(attended, attended_out)
    gather.collect(3)
    gather.pass_on(4)
    for group in range(6, tail + 1):
        gather.start_line(group, 0)
    projected = out_scatter.total()
    out_scatter.finish()
    proj_keep[...] = projected
    hidden = tok_full[own_rows].astype(full) + projected * inverse_rms(projected) * gain_attn
    hidden_keep[...] = hidden
    keep(proj_keep, proj_out)
    keep(hidden_keep, hidden_out)
    normed_two[own_rows] = (hidden * inverse_rms(hidden) * gain_pre).astype(low)
    two_all = RowGather(place, normed_two.at[own_rows], row_slabs(normed_two, rows), row_send.at[2], row_recv.at[2])
    two_all.start()
    gather.collect(4)
    gather.pass_on(5)
    two_all.wait_mate()
    gather.widen(tail - 1)
    gather.widen(tail)
    two_all.wait_across()
    gather.pass_on(6)
    gather.collect(5)
    two_all.wait_corner()
    keep(normed_two, normed_two_out)

    half = rows // 2
    down_scatters, down_gathers = [], []
    for index in range(2):
        piece = slice(index * half, (index + 1) * half)
        down_scatters.append(
            RowScatter(
                place,
                row_slabs(part_one, rows, index * half, half),
                first_one.at[:, piece],
                second_one.at[piece],
                mixed_one.at[piece],
                row_send.at[3 + index],
                row_recv.at[3 + index],
            )
        )
        slabs = row_slabs(tok_full, rows, index * half, half)
        down_gathers.append(
            RowGather(place, slabs(place.y, place.core), slabs, row_send.at[5 + index], row_recv.at[5 + index])
        )
    block = 2 * rows

    def feed(c):
        first, wide, padded = chunks[c]
        at_gate, at_up, _ = places[c]

        def feed_rows(index, carry):
            at = pl.ds(pl.multiple_of(index * block, block), block)
            n2 = normed_two[at]
            gate = dot_nn(n2, wall[:, at_gate : at_gate + wide])
            up = dot_nn(n2, wall[:, at_up : at_up + wide])
            gate_keep[at, first : first + wide] = gate.astype(low)
            up_keep[at, first : first + wide] = up.astype(low)
            _, bent = gelu_parts(gate)
            act[at, first : first + wide] = (0.5 * gate * (1.0 + bent) * up).astype(low)
            return carry

        lax.fori_loop(0, 2, feed_rows, 0)
        span = slice(first, first + padded)
        keep(gate_keep.at[:, span], gate_out.at[:, span])
        keep(up_keep.at[:, span], up_out.at[:, span])
        keep(act.at[:, span], act_out.at[:, span])

    def lower(c):
        first, wide, _ = chunks[c]
        at_down = places[c][2]

        def lower_rows(index, carry):
            at = pl.ds(pl.multiple_of(index * block, block), block)
            more = dot_nt(act[at, first : first + wide], wall[:, at_down : at_down + wide])
            down_acc[at] = more if c == 0 else down_acc[at] + more
            return carry

        lax.fori_loop(0, 2, lower_rows, 0)

    gather.ready(3)
    keep_span(3)
    feed(0)
    gather.pass_on(7, 0)
    gather.pass_on(8, 0)
    gather.collect(6)
    lower(0)
    gather.ready(4)
    keep_span(4)
    feed(1)
    gather.pass_on(7, 1)
    gather.ready(5)
    keep_span(5)
    feed(2)
    gather.pass_on(8, 1)
    gather.collect(7)
    keep_span(7)
    feed(3)
    lower(2)
    gather.ready(6)
    keep_span(6)
    lower(1)
    gather.collect(8)
    keep_span(8)
    first, wide, _ = chunks[last]
    at_down = places[last][2]
    tokens_all.finish()
    for step, index in enumerate(down_scatters[0].order()):
        at = pl.ds(pl.multiple_of(index * rows, rows), rows)
        part_one[at] = (
            down_acc[at] + dot_nt(act[at, first : first + wide], wall[:, at_down : at_down + wide])
        ).astype(low)
        for scatter in down_scatters:
            scatter.after(step)
    for index, (scatter, spread) in enumerate(zip(down_scatters, down_gathers)):
        piece = slice(index * half, (index + 1) * half)
        f = scatter.total()
        inv = inverse_rms(f)
        cot = cot_ref[piece].astype(full)
        scaled = cot * gain_ffn
        back = inv * (scaled - f * (inv * inv) * jnp.mean(f * scaled, axis=-1, keepdims=True))
        tok_full[pl.ds(place.tensor * rows + index * half, half)] = back.astype(low)
        spread.start()
        block_out[piece] = (hidden_keep[piece] + f * inv * gain_ffn).astype(low)
        grad = jnp.broadcast_to(jnp.sum(cot * f * inv, axis=0, keepdims=True), dgain_ffn.shape)
        dgain_ffn[...] = grad if index == 0 else dgain_ffn[...] + grad

    def keep_slab(y, core):
        at = pl.ds((y * 2 + core) * rows, rows)
        keep(tok_full.at[at], grad_down_out.at[at])

    keep(block_out, block_out_out)
    keep(dgain_ffn, dgain_ffn_out)
    keep_slab(place.y, place.core)
    for spread in down_gathers:
        spread.wait_mate()
    keep_slab(place.y, 1 - place.core)
    for spread in down_gathers:
        spread.wait_across()
    keep_slab(1 - place.y, place.core)
    for spread in down_gathers:
        spread.wait_corner()
    keep_slab(1 - place.y, 1 - place.core)
    gather.finish()
    keyval_all.finish()
    two_all.finish()
    for item in down_scatters + down_gathers:
        item.finish()
    for copy in kept:
        copy.wait()


def forward_call(sizes, prefix, tokens, cotangent, gains, weights, cosine, sine):
    lines, rows, width, head_dim, units = sizes
    length = 4 * rows
    shard = weights[0].shape[0]
    columns = packed_columns(units, head_dim)[1]
    chunks = chunks_of(units)
    padded = sum(c[2] for c in chunks)
    groups = 5 + len(chunks)
    inputs = (tokens, cotangent, gains, *weights, cosine, sine)
    hbm = pl.BlockSpec(memory_space=pl.ANY)
    large = [
        ((2 * lines * shard, columns), low),
        ((length, width), low),
        ((length, width), low),
        ((length, head_dim), full),
        ((length, head_dim), full),
        ((length, head_dim), low),
        ((length, head_dim), low),
        ((length, head_dim), low),
        ((length, length), low),
        ((length, padded), low),
        ((length, padded), low),
        ((length, padded), low),
    ]
    small = [
        ((8, gains.shape[0] * 2 * lines), full),
        ((rows, width), full),
        ((rows, width), full),
        ((length, width), low),
        ((8, width), full),
        ((rows, width), low),
    ]
    inside = [large[i] for i in (0, 1, 2, 3, 4, 7, 8, 9, 10, 11)]
    scatter_set = [
        pltpu.VMEM((2, rows, width), low),
        pltpu.VMEM((rows, width), low),
        pltpu.VMEM((rows, width), low),
    ]
    return pl.pallas_call(
        functools.partial(forward_kernel, sizes),
        out_shape=[jax.ShapeDtypeStruct(*item) for item in large + small],
        in_specs=[pl.BlockSpec(memory_space=pltpu.SMEM)] + [hbm] * len(inputs),
        out_specs=[hbm] * (len(large) + len(small)),
        scratch_shapes=[pltpu.VMEM(a.shape, a.dtype) for a in inputs[1:]]
        + [pltpu.VMEM(*item) for item in small[:3] + small[4:] + inside]
        + [
            pltpu.VMEM((length, width), low),
            pltpu.VMEM((2 * lines * 8, gains.shape[0]), full),
            pltpu.VMEM((length, head_dim), low),
            pltpu.VMEM((length, head_dim), low),
            pltpu.VMEM((length, width), low),
        ]
        + scatter_set
        + [
            pltpu.VMEM((length, width), full),
            pltpu.SemaphoreType.DMA((groups, 2, lines)),
            pltpu.SemaphoreType.DMA((groups, 2, lines)),
            pltpu.SemaphoreType.DMA((groups, 2)),
            pltpu.SemaphoreType.DMA((groups, lines)),
            pltpu.SemaphoreType.DMA((groups, lines)),
            pltpu.SemaphoreType.DMA((8, 3)),
            pltpu.SemaphoreType.DMA((8, 3)),
            pltpu.SemaphoreType.DMA((22 + 4 * len(chunks),)),
            pltpu.SemaphoreType.DMA((len(inputs),)),
        ],
        compiler_params=pltpu.CompilerParams(
            collective_id=0, has_side_effects=True, vmem_limit_bytes=63 * 1024 * 1024
        ),
        name="forward",
    )(prefix, *inputs)


class LineScatter:
    def __init__(self, place, block, side_block, line_block, wide, side_send, side_recv, line_send, line_recv, kind):
        self.place, self.block, self.side_block, self.line_block = place, block, side_block, line_block
        self.wide, self.kind = wide, kind
        self.side_send, self.side_recv, self.line_send, self.line_recv = side_send, side_recv, line_send, line_recv

    def columns(self, group):
        return (0, 1) if self.wide[group] else (0,)

    def own(self, group, column, step):
        place = self.place
        return self.block(group, place.homes[step] * 2 + (place.x if column == 0 else 1 - place.x))

    def sideways(self, group, step):
        home = 0 if self.wide[group] else self.place.homes[step]
        return remote(
            self.own(group, 1, step),
            self.side_block(group, home),
            self.side_send.at[group, step],
            self.side_recv.at[group, step],
            self.place.side,
        )

    def along(self, group, column, step):
        slot = step - 1 if step < 3 else 2 + self.place.end
        return remote(
            self.own(group, column, step),
            self.line_block(group, column, slot),
            self.line_send.at[group, column, step],
            self.line_recv.at[group, column, slot],
            self.place.line(step) if step < 3 else self.place.inner,
        )

    def arrive(self, group, column, slot):
        here = self.line_block(group, column, slot)
        remote(
            here, here, self.line_send.at[group, column, 1], self.line_recv.at[group, column, slot], self.place.line(1)
        ).wait_recv()
        return here[...].astype(full)

    def start(self, group):
        if not self.wide[group]:
            for step in (3, 1, 2, 0):
                self.sideways(group, step).start()
            return
        for step in (3, 1):
            for column in (0, 1):
                self.along(group, column, step).start()

        @pl.when(self.place.end == 1)
        def _():
            for column in (0, 1):
                self.along(group, column, 2).start()

    def with_side(self, group, step):
        self.sideways(group, step).wait_recv()
        return self.own(group, 0, step)[...].astype(full) + self.side_block(group, self.place.homes[step])[...].astype(
            full
        )

    def pump(self, group, *steps):
        for step in steps or (3, 1, 2):
            self.own(group, 0, step)[...] = self.with_side(group, step).astype(self.kind)
            if step != 2:
                self.along(group, 0, step).start()
                continue

            @pl.when(self.place.end == 1)
            def _():
                self.along(group, 0, 2).start()

    def relay(self, group):
        for column in self.columns(group):

            @pl.when(self.place.middle)
            def _():
                block = self.own(group, column, 2)
                block[...] = (block[...].astype(full) + self.arrive(group, column, 3)).astype(self.kind)
                self.along(group, column, 2).start()

    def hand_over(self, group):
        block = self.own(group, 1, 0)
        both = block[...].astype(full) + self.arrive(group, 1, 0) + self.arrive(group, 1, 1)

        @pl.when(self.place.middle)
        def _():
            block[...] = (both + self.arrive(group, 1, 2)).astype(self.kind)

        @pl.when(self.place.end == 1)
        def _():
            block[...] = both.astype(self.kind)

        self.sideways(group, 0).start()

    def settle(self, group):
        self.sideways(group, 0).wait_recv()
        self.arrive(group, 0, 0)
        self.arrive(group, 0, 1)

        @pl.when(self.place.middle)
        def _():
            self.arrive(group, 0, 2)

    def total(self, group, lo, hi, held):
        parts = [
            self.own(group, 0, 0),
            self.side_block(group, 0 if self.wide[group] else self.place.z),
            self.line_block(group, 0, 0),
            self.line_block(group, 0, 1),
        ]
        first, *others = [part[:, lo:hi].astype(full) for part in parts]
        for other in others:
            first = first + other
        held[...] = first

        @pl.when(self.place.middle)
        def _():
            held[...] = first + self.line_block(group, 0, 2)[:, lo:hi].astype(full)

    def finish(self):
        for group in range(len(self.wide)):
            for step in (0,) if self.wide[group] else (0, 1, 2, 3):
                self.sideways(group, step).wait_send()
            for column in self.columns(group):
                for step in (1, 2, 3):
                    self.along(group, column, step).wait_send()


def norm_back(rows, inv, gain, grad):
    scaled = grad * gain
    back = inv * (scaled - rows * (inv * inv) * jnp.mean(rows * scaled, axis=-1, keepdims=True))
    return back, jnp.sum(grad * rows * inv, axis=0, keepdims=True)


def backward_kernel(
    sizes,
    grad_down_in,
    cot_in,
    tokens_in,
    gvec_in,
    dgain_ffn_in,
    proj_in,
    hidden_in,
    cos_in,
    sin_in,
    wall_in,
    normed_in,
    normed_two_in,
    query_in,
    key_in,
    key_rot_in,
    value_in,
    attended_in,
    probs_in,
    gate_in,
    up_in,
    act_in,
    gate_grad,
    up_grad,
    down_grad,
    small_grad,
    tokens_grad_out,
    keyval_grad,
    gains_grad,
    tokens_grad,
    cot_ref,
    tokens_ref,
    gvec,
    dgain_ffn,
    proj_ref,
    hidden_ref,
    cos_ref,
    sin_ref,
    wall,
    side_buf,
    side_wide,
    line_buf,
    line_wide,
    big,
    normed_two,
    row_buf,
    acc,
    first_buf,
    second_buf,
    mixed_buf,
    key_rot,
    value_low,
    dquery,
    dkeyval,
    dhidden,
    dproj,
    kv_first,
    kv_second,
    kv_mixed,
    kv_own,
    dgains,
    gain_part,
    gain_first,
    gain_second,
    gain_side,
    gain_line,
    row_send,
    row_recv,
    side_send,
    side_recv,
    line_send,
    line_recv,
    gain_side_send,
    gain_side_recv,
    gain_line_send,
    gain_line_recv,
    last_send,
    last_recv,
    load_sem,
    store_sem,
):
    lines, rows, width, head_dim, units = sizes
    place = Place()
    length = 4 * rows
    shard = wall.shape[0] // (2 * lines)
    kv_end, query_end, output_end = small_columns(head_dim)
    quarter = head_dim // 2
    places, columns = packed_columns(units, head_dim)
    chunks = chunks_of(units)
    last = len(chunks) - 1
    order = [0, last] + list(range(1, last))
    base_column = kv_end - quarter
    spans = []
    for c in range(last):
        spans += [(places[c][2], places[c + 1][0]), (places[c][0], places[c][2])]
    group_gate, group_up, group_last, group_small = range(len(spans) - 1, len(spans) + 3)
    spans[-1:] = [(places[last - 1][0], places[last - 1][1]), (places[last - 1][1], places[last - 1][2])]
    spans += [(places[last][0], columns), (base_column, output_end)]
    loads = {}

    def load(name, source, target):
        copy = pltpu.make_async_copy(source, target, load_sem.at[len(loads)])
        copy.start()
        loads[name] = copy

    def load_chunk(c):
        first, _, padded = chunks[c]
        lo, hi = places[c][0], columns if c == last else places[c + 1][0]
        base = (order.index(c) % 2) * 3 * CHUNK
        load(("wall", c), wall_in.at[:, lo:hi], wall.at[:, lo:hi])
        for k, source in enumerate((gate_in, up_in, act_in)):
            at = base + k * CHUNK
            load((k, c), source.at[:, first : first + padded], big.at[:, at : at + padded])

    greet(place)
    own_rows = pl.ds(place.tensor * rows, rows)
    load("down", grad_down_in, row_buf)
    load_chunk(order[0])
    load("two", normed_two_in, normed_two)
    load("gvec", gvec_in, gvec)
    load("dgain", dgain_ffn_in, dgain_ffn)
    load_chunk(order[1])
    load("hidden", hidden_in, hidden_ref)
    load("cot", cot_in, cot_ref)
    load("proj", proj_in, proj_ref)
    load("tokens", tokens_in, tokens_ref)
    load("cos", cos_in, cos_ref)
    load("sin", sin_in, sin_ref)
    load("kv", wall_in.at[:, 0:kv_end], wall.at[:, 0:kv_end])
    load("qo", wall_in.at[:, kv_end:output_end], wall.at[:, kv_end:output_end])
    load("key_rot", key_rot_in, key_rot)
    load("value", value_in, value_low)
    loads["gvec"].wait()
    loads["dgain"].wait()
    gain_in = 1.0 + gvec[0:1, 0:width]
    gain_attn = 1.0 + gvec[0:1, width : 2 * width]
    gain_pre = 1.0 + gvec[0:1, 2 * width : 3 * width]
    gain_query = 1.0 + gvec[0:1, 4 * width : 4 * width + head_dim]
    gain_key = 1.0 + gvec[0:1, 4 * width + head_dim : 4 * width + 2 * head_dim]
    dgains[...] = jnp.zeros_like(dgains)
    dgains[0:1, 3 * width : 4 * width] = dgain_ffn[0:1]
    loads["down"].wait()
    loads["two"].wait()

    def block(group, origin):
        lo, hi = spans[group]
        return wall.at[pl.ds(origin * shard, shard), lo:hi]

    def side_block(group, home):
        if wide_groups[group]:
            return side_wide
        lo, hi = spans[group]
        return side_buf.at[pl.ds(home * shard, shard), lo - base_column : hi - base_column]

    def line_block(group, column, slot):
        lo, hi = spans[group]
        if wide_groups[group]:
            return line_wide.at[pl.ds((column * 4 + slot) * shard, shard)]
        return line_buf.at[pl.ds(slot * shard, shard), lo - base_column : hi - base_column]

    wide_groups = [group == group_last for group in range(len(spans))]
    scatter = LineScatter(
        place, block, side_block, line_block, wide_groups, side_send, side_recv, line_send, line_recv, low
    )
    part = big.at[:, 0:width]
    pre_scatter = RowScatter(
        place, row_slabs(part, rows), first_buf, second_buf, mixed_buf, row_send.at[1], row_recv.at[1]
    )
    half = 2 * rows
    third = width // 3

    def weight_gradient(lo, wide, left, right):
        for m in range(0, width, third):
            wall[m : m + third, lo : lo + wide] = dot_tn(left[:, m : m + third], right).astype(low)

    for position, c in enumerate(order):
        first, wide, padded = chunks[c]
        at_gate, at_up, at_down = places[c]
        base = (position % 2) * 3 * CHUNK
        loads["wall", c].wait()
        for k in range(3):
            loads[k, c].wait()
        if 1 <= position < last:
            load_chunk(order[position + 1])
        of_gate = slice(base, base + wide)
        of_up = slice(base + CHUNK, base + CHUNK + wide)
        of_act = slice(base + 2 * CHUNK, base + 2 * CHUNK + wide)

        def unit_rows(index, carry):
            at = pl.ds(pl.multiple_of(index * half, half), half)
            dz = dot_nn(row_buf[at], wall[:, at_down : at_down + wide])
            gate = big[at, of_gate].astype(full)
            up = big[at, of_up].astype(full)
            square, bent = gelu_parts(gate)
            middle = 0.5 * (1.0 + bent)
            slope = middle + 0.5 * gate * (1.0 - bent * bent) * (0.7978845608028654 * (1.0 + 0.134145 * square))
            big[at, of_gate] = (dz * up * slope).astype(low)
            big[at, of_up] = (dz * gate * middle).astype(low)
            return carry

        lax.fori_loop(0, 2, unit_rows, 0)
        weight_gradient(at_down, wide, row_buf, big[:, of_act])
        if position == 0:
            meet(place)
        if c < last:
            scatter.start(2 * c)

        def back_rows(at):
            more = dot_nt(big[at, of_gate], wall[:, at_gate : at_gate + wide])
            more = more + dot_nt(big[at, of_up], wall[:, at_up : at_up + wide])
            return more if position == 0 else acc[at] + more

        if position < last:

            def collect_rows(index, carry):
                at = pl.ds(pl.multiple_of(index * half, half), half)
                acc[at] = back_rows(at)
                return carry

            lax.fori_loop(0, 2, collect_rows, 0)
        else:
            for step, index in enumerate(pre_scatter.order()):
                at = pl.ds(pl.multiple_of(index * rows, rows), rows)
                part[at] = back_rows(at).astype(low)
                pre_scatter.after(step)
        weight_gradient(at_gate, wide, normed_two, big[:, of_gate])
        weight_gradient(at_up, wide, normed_two, big[:, of_up])
        if c < last:
            scatter.start(2 * c + 1)
        else:
            scatter.pump(0)
            scatter.start(group_last)
        if position == 2:
            scatter.relay(0)
        if position == 3:
            scatter.relay(group_last)
            scatter.pump(1, 3, 1)

    at_normed = width
    at_att = at_normed + width
    load("normed", normed_in, big.at[:, at_normed : at_normed + width])
    load("attended", attended_in, big.at[:, at_att : at_att + head_dim])
    load("query", query_in, acc.at[:, 2 * head_dim : 3 * head_dim])
    load("key", key_in, acc.at[:, 3 * head_dim : 4 * head_dim])

    scatter.pump(1, 2)
    dn2 = pre_scatter.total()
    for name in ("hidden", "cot", "proj", "tokens", "cos", "sin"):
        loads[name].wait()
    hidden = hidden_ref[...]
    back, grad = norm_back(hidden, inverse_rms(hidden), gain_pre, dn2)
    dgains[0:1, 2 * width : 3 * width] = grad
    dh = cot_ref[...].astype(full) + back
    dhidden[...] = dh
    proj = proj_ref[...]
    back, grad = norm_back(proj, inverse_rms(proj), gain_attn, dh)
    dgains[0:1, width : 2 * width] = grad
    dproj[...] = back.astype(low)
    row_buf[own_rows] = dproj[...]
    proj_all = RowGather(place, dproj, row_slabs(row_buf, rows), row_send.at[2], row_recv.at[2])
    proj_all.start()
    pre_scatter.finish()
    load("probs", probs_in, big.at[:, 0:length])
    acc[:, 0 : 2 * head_dim] = jnp.zeros((length, 2 * head_dim), full)
    proj_all.wait_mate()
    scatter.pump(2)
    proj_all.wait_across()
    scatter.relay(1)
    proj_all.wait_corner()
    for name in ("kv", "qo", "key_rot", "value", "normed", "attended", "query", "key", "probs"):
        loads[name].wait()

    def attend_back(index, carry):
        at = pl.ds(pl.multiple_of(index * rows, rows), rows)
        da = dot_nn(row_buf[at], wall[:, query_end:output_end]).astype(low)
        soft = big[at, 0:length]
        wide_soft = soft.astype(full)
        dp = dot_nt(da, value_low[...])
        ds = (wide_soft * (dp - jnp.sum(wide_soft * dp, axis=-1, keepdims=True))).astype(low)
        q = acc[at, 2 * head_dim : 3 * head_dim]
        inv = inverse_rms(q)
        cosine, sine = cos_ref[at], sin_ref[at]
        qr = rotate_rows(q * inv * gain_query, cosine, sine).astype(low)
        dqr = dot_nn(ds, key_rot[...]) * query_scale
        acc[:, 0:head_dim] += dot_tn(ds, qr)
        acc[:, head_dim : 2 * head_dim] += dot_tn(soft, da)
        dq, grad = norm_back(q, inv, gain_query, rotate_back(dqr, cosine, sine))
        dquery[at] = dq.astype(low)
        dgains[0:1, 4 * width : 4 * width + head_dim] += grad
        return carry

    scatter.hand_over(group_last)
    scatter.pump(3, 3)
    lax.fori_loop(0, 4, attend_back, 0)

    def key_back(index, carry):
        at = pl.ds(pl.multiple_of(index * rows, rows), rows)
        k = acc[at, 3 * head_dim : 4 * head_dim]
        dkr = rotate_back(acc[at, 0:head_dim] * query_scale, cos_ref[at], sin_ref[at])
        dk, grad = norm_back(k, inverse_rms(k), gain_key, dkr)
        dkeyval[at, 0:head_dim] = dk.astype(low)
        dkeyval[at, head_dim : 2 * head_dim] = acc[at, head_dim : 2 * head_dim].astype(low)
        dgains[0:1, 4 * width + head_dim : 4 * width + 2 * head_dim] += grad
        return carry

    lax.fori_loop(0, 4, key_back, 0)
    scatter.pump(3, 1)
    in_scatter = RowScatter(
        place, row_slabs(part, rows), first_buf, second_buf, mixed_buf, row_send.at[3], row_recv.at[3]
    )
    for step, index in enumerate(in_scatter.order()):
        at = pl.ds(pl.multiple_of(index * rows, rows), rows)
        more = dot_nt(dquery[at], wall[:, kv_end:query_end]) + dot_nt(dkeyval[at], wall[:, 0:kv_end])
        part[at] = more.astype(low)
        in_scatter.after(step)
    scatter.pump(3, 2)
    scatter.relay(2)

    normed = big.at[:, at_normed : at_normed + width]
    for m in range(0, width, third):
        wall[m : m + third, 0:kv_end] = dot_tn(normed[:, m : m + third], dkeyval[...]).astype(low)

    def kv_block(y, core):
        return wall.at[:, pl.ds(pl.multiple_of((y * 2 + core) * quarter, quarter), quarter)]

    def kv_copy(index):
        send, recv = last_send.at[index], last_recv.at[index]
        if index == 2:
            return remote(kv_mixed, kv_second, send, recv, place.across)
        return remote(
            kv_block(1 - place.y if index == 0 else place.y, 1 - place.core), kv_first.at[index], send, recv, place.mate
        )

    kv_copy(0).start()
    kv_copy(1).start()
    weight_gradient(kv_end, head_dim, normed, dquery[...])
    weight_gradient(query_end, head_dim, row_buf, big[:, at_att : at_att + head_dim])
    kv_copy(0).wait_recv()
    kv_mixed[...] = (kv_block(1 - place.y, place.core)[...].astype(full) + kv_first[0].astype(full)).astype(low)
    kv_copy(2).start()
    scatter.pump(4, 3, 1)
    scatter.relay(3)

    dn1 = in_scatter.total()
    x = tokens_ref[...].astype(full)
    back, grad = norm_back(x, inverse_rms(x), gain_in, dn1)
    dgains[0:1, 0:width] = grad
    tokens_grad[...] = (dhidden[...] + back).astype(low)
    tokens_copy = pltpu.make_async_copy(tokens_grad, tokens_grad_out, store_sem.at[1 + 3 * len(chunks)])
    tokens_copy.start()
    step = gains_grad.shape[1]
    for origin in range(2 * lines):
        gain_part[origin * 8 : origin * 8 + 8] = dgains[:, origin * step : (origin + 1) * step]

    def gain_copy(index):
        source, target, device = (
            (gain_part, gain_first, place.mate) if index == 0 else (gain_part, gain_second, place.across)
        )
        return remote(source, target, last_send.at[3 + index], last_recv.at[3 + index], device)

    gain_copy(0).start()
    scatter.pump(4, 2)
    kv_copy(1).wait_recv()
    kv_copy(2).wait_recv()
    kv_copy(0).wait_send()
    kv_copy(1).wait_send()
    wall[:, base_column:kv_end] = (
        kv_block(place.y, place.core)[...].astype(full) + kv_first[1].astype(full) + kv_second[...].astype(full)
    ).astype(low)
    scatter.relay(4)
    gain_copy(0).wait_recv()
    gain_copy(0).wait_send()
    gain_part[...] = gain_part[...] + gain_first[...]
    gain_copy(1).start()
    scatter.pump(group_gate, 3)
    gain_copy(1).wait_recv()
    gain_copy(1).wait_send()
    gain_part[...] = gain_part[...] + gain_second[...]

    gain_scatter = LineScatter(
        place,
        lambda group, origin: gain_part.at[pl.ds(origin * 8, 8)],
        lambda group, home: gain_side.at[pl.ds(home * 8, 8)],
        lambda group, column, slot: gain_line.at[pl.ds(slot * 8, 8)],
        [False],
        gain_side_send,
        gain_side_recv,
        gain_line_send,
        gain_line_recv,
        full,
    )
    gain_scatter.start(0)
    scatter.start(group_small)
    scatter.start(group_up)
    scatter.pump(group_gate, 1, 2)

    stores = []

    def store(group, kinds, c):
        first, wide, padded = chunks[c] if kinds else (0, output_end - base_column, output_end - base_column)
        scatter.settle(group)
        for k, target in enumerate(kinds or (small_grad,)):
            slot = 3 * len(chunks) if not kinds else len([done for done in stores if done[1]])
            down, right = slot // 2 * shard, slot % 2 * CHUNK
            held = acc.at[down : down + shard, right : right + padded]
            scatter.total(group, k * wide, (k + 1) * wide, held.at[:, 0:wide])
            copy = pltpu.make_async_copy(held, target.at[:, first : first + padded], store_sem.at[slot])
            copy.start()
            stores.append((copy, bool(kinds)))
            if not kinds:
                kv_own[...] = held[:, 0:quarter].astype(low)

    for c in range(last - 1):
        store(2 * c, (down_grad,), c)
        store(2 * c + 1, (gate_grad, up_grad), c)
    scatter.relay(group_gate)
    store(group_last, (gate_grad, up_grad, down_grad), last)
    gain_scatter.pump(0)
    store(2 * last - 2, (down_grad,), last - 1)
    scatter.pump(group_small)
    gain_scatter.relay(0)
    scatter.relay(group_small)
    store(group_gate, (gate_grad,), last - 1)
    scatter.pump(group_up, 3, 1)
    store(group_small, (), 0)

    def own_block(y, core):
        return keyval_grad.at[:, pl.ds(pl.multiple_of((y * 2 + core) * quarter, quarter), quarter)]

    own_block(place.y, place.core)[...] = kv_own[...]
    targets = (place.mate, place.across, (place.dp, (1 - place.y) * 2 + (1 - place.core)))
    sends = [
        remote(kv_own, own_block(place.y, place.core), last_send.at[5 + i], last_recv.at[5 + i], target)
        for i, target in enumerate(targets)
    ]
    for copy in sends:
        copy.start()
    scatter.pump(group_up, 2)
    scatter.relay(group_up)
    gain_scatter.settle(0)
    gain_scatter.total(0, 0, gains_grad.shape[1], gains_grad)
    store(group_up, (up_grad,), last - 1)
    for i, (y, core) in enumerate(
        ((place.y, 1 - place.core), (1 - place.y, place.core), (1 - place.y, 1 - place.core))
    ):
        remote(kv_own, own_block(y, core), last_send.at[5 + i], last_recv.at[5 + i], targets[i]).wait_recv()
    for copy in sends:
        copy.wait_send()
    kv_copy(2).wait_send()
    scatter.finish()
    gain_scatter.finish()
    proj_all.finish()
    in_scatter.finish()
    for copy, _ in stores:
        copy.wait()
    tokens_copy.wait()


def backward_call(sizes, small_args, hbm_args):
    lines, rows, width, head_dim, units = sizes
    length = 4 * rows
    columns = hbm_args[0].shape[1]
    shard = hbm_args[0].shape[0] // (2 * lines)
    gains = small_args[3].shape[1]
    quarter = head_dim // 2
    base_column = 2 * head_dim - quarter
    chunks = chunks_of(units)
    groups = 2 * len(chunks) + 1
    last_wide = columns - packed_columns(units, head_dim)[0][-1][0]
    vm = pl.BlockSpec(memory_space=pltpu.VMEM)
    hbm = pl.BlockSpec(memory_space=pl.ANY)
    padded = sum(c[2] for c in chunks)
    large = [((shard, padded), full)] * 3 + [((shard, 5 * quarter), full), ((rows, width), low)]
    outs = [
        ((shard, 2 * head_dim), low),
        ((8, gains // (2 * lines)), full),
    ]
    scratch = [((rows, width), low)] + [(a.shape, a.dtype) for a in small_args[1:]]
    scratch += [
        (hbm_args[0].shape, low),
        ((lines * shard, packed_columns(units, head_dim)[0][-1][0] - base_column), low),
        ((shard, last_wide), low),
        ((lines * shard, packed_columns(units, head_dim)[0][-1][0] - base_column), low),
        ((2 * lines * shard, last_wide), low),
        ((length, 6 * CHUNK), low),
        ((length, width), low),
        ((length, width), low),
        ((length, width), full),
        ((2, rows, width), low),
        ((rows, width), low),
        ((rows, width), low),
        ((length, head_dim), low),
        ((length, head_dim), low),
        ((length, head_dim), low),
        ((length, 2 * head_dim), low),
        ((rows, width), full),
        ((rows, width), low),
        ((2, width, quarter), low),
        ((width, quarter), low),
        ((width, quarter), low),
        ((shard, quarter), low),
        ((8, gains), full),
        ((2 * lines * 8, gains // (2 * lines)), full),
        ((2 * lines * 8, gains // (2 * lines)), full),
        ((2 * lines * 8, gains // (2 * lines)), full),
        ((lines * 8, gains // (2 * lines)), full),
        ((lines * 8, gains // (2 * lines)), full),
    ]
    sems = [(4, 3), (4, 3), (groups, 4), (groups, 4), (groups, 2, 4), (groups, 2, 4)]
    sems += [(1, 4), (1, 4), (1, 1, 4), (1, 1, 4), (8,), (8,)]
    sems += [(19 + 4 * len(chunks),), (2 + 3 * len(chunks),)]
    return pl.pallas_call(
        functools.partial(backward_kernel, sizes),
        out_shape=[jax.ShapeDtypeStruct(*item) for item in large + outs],
        in_specs=[hbm] * (len(small_args) + len(hbm_args)),
        out_specs=[hbm] * len(large) + [vm] * len(outs),
        scratch_shapes=[pltpu.VMEM(*item) for item in scratch] + [pltpu.SemaphoreType.DMA(dims) for dims in sems],
        compiler_params=pltpu.CompilerParams(
            collective_id=1, has_side_effects=True, vmem_limit_bytes=63 * 1024 * 1024
        ),
        name="backward",
    )(*small_args, *hbm_args)


def adam_values(weight, gradient, first, second, step_rate):
    moment = beta_first * first + (1.0 - beta_first) * gradient
    square = beta_second * second + (1.0 - beta_second) * gradient * gradient
    scaled = moment / (1.0 - beta_first**STEP) / (jnp.sqrt(square / (1.0 - beta_second**STEP)) + adam_eps)
    return moment, square, weight - step_rate * (scaled + decay_rate * weight)


def update_kernel(units, head_dim, cut, *refs):
    passed, grads, old = refs[:2], refs[2:8], refs[8:26]
    passed_out, new = refs[26:28], refs[28:46]
    held_passed, held_grads, held, load_sem, store_sem = refs[46:48], refs[48:54], refs[54:72], refs[72], refs[73]
    gate_grad, up_grad, down_grad, small_grad, keyval_grad, gains_grad = held_grads
    quarter = head_dim // 2
    shard = old[0].shape[0]
    rows = shard // cut
    wide = D ** (-0.5)
    count = [0, 0]

    def load(source, target, part):
        at = slice(None) if part is None else pl.ds(part * rows, rows)
        copy = pltpu.make_async_copy(source.at[at], target.at[at], load_sem.at[count[0]])
        count[0] += 1
        copy.start()
        return copy

    def store(source, target, part):
        at = slice(None) if part is None else pl.ds(part * rows, rows)
        copy = pltpu.make_async_copy(source.at[at], target.at[at], store_sem.at[count[1]])
        count[1] += 1
        copy.start()
        return copy

    jobs = [(3, part, (0, 1)) for part in range(cut)] + [(4, part, (2,)) for part in range(cut)]
    jobs += [(1, None, (4,)), (0, None, (3,)), (2, None, ()), (5, None, (5,))]
    waits = []
    for index, part, needs in jobs:
        own = range(3 * index, 3 * index + 3)
        waits.append(
            [load(old[i], held[i], part) for i in own] + [load(grads[i], held_grads[i], part) for i in needs]
        )
    through = [load(source, target, None) for source, target in zip(passed, held_passed)]
    waiting = []

    def work(index, part):
        weight, first, second = held[3 * index : 3 * index + 3]
        if index == 5:
            values = adam_values(weight[...], gains_grad[0], first[...], second[...], 0.3)
            for target, value in zip((first, second, weight), values):
                target[...] = value
            return
        step = rows if part is not None else shard // 3

        def some_rows(at):
            if index == 3:
                for kind, grad in enumerate((gate_grad, up_grad)):
                    values = adam_values(
                        weight[at, kind, :], grad[at, 0:units], first[at, kind, :], second[at, kind, :], wide
                    )
                    for target, value in zip((first, second, weight), values):
                        target[at, kind, :] = value
                return
            if index == 4:
                gradient, rate = down_grad[at, 0:units], FF ** (-0.5)
            elif index == 1:
                gradient, rate = keyval_grad[at].astype(full), wide
            elif index == 0:
                gradient, rate = small_grad[at, quarter : quarter + head_dim], wide
            else:
                gradient = small_grad[at, quarter + head_dim : quarter + 2 * head_dim]
                rate = (HEADS * HEAD_DIM) ** (-0.5)
            values = adam_values(weight[at], gradient, first[at], second[at], rate)
            for target, value in zip((first, second, weight), values):
                target[at] = value

        if part is not None:
            some_rows(pl.ds(part * rows, rows))
        else:

            def body(i, carry):
                some_rows(pl.ds(pl.multiple_of(i * step, step), step))
                return carry

            lax.fori_loop(0, 3, body, 0)

    for (index, part, _), copies in zip(jobs, waits):
        if index == 1:
            for copy, source, target in zip(through, held_passed, passed_out):
                copy.wait()
                waiting.append(store(source, target, None))
        for copy in copies:
            copy.wait()
        work(index, part)
        for kind, place in ((1, 0), (2, 1), (0, 2)):
            waiting.append(store(held[3 * index + kind], new[3 * index + place], part))
    for copy in waiting:
        copy.wait()


def update_call(units, head_dim, passed, grads, old, cut):
    hbm = pl.BlockSpec(memory_space=pl.ANY)
    outs = list(passed)
    for index in range(6):
        outs += [old[3 * index + kind] for kind in (1, 2, 0)]
    loads = 9 * cut + 18
    return pl.pallas_call(
        functools.partial(update_kernel, units, head_dim, cut),
        out_shape=[jax.ShapeDtypeStruct(a.shape, a.dtype) for a in outs],
        in_specs=[hbm] * (len(passed) + len(grads) + len(old)),
        out_specs=[hbm] * len(outs),
        scratch_shapes=[pltpu.VMEM(a.shape, a.dtype) for a in (*passed, *grads, *old)]
        + [pltpu.SemaphoreType.DMA((loads,)), pltpu.SemaphoreType.DMA((2 + 6 * cut + 12,))],
        compiler_params=pltpu.CompilerParams(vmem_limit_bytes=60 * 1024 * 1024),
        name="update",
    )(*passed, *grads, *old)


def mixed_dot(left, right):
    return jnp.dot(left, right, preferred_element_type=jnp.float32)


def rms_scale(vector, gain_vec):
    return (
        vector
        * lax.rsqrt(jnp.mean(vector * vector, axis=-1, keepdims=True) + eps_norm)
        * (1.0 + gain_vec)
    )


def rotate(vector, positions):
    half_dim = vector.shape[-1] // 2
    inv_freq = rope_base ** (-2.0 * jnp.arange(half_dim).astype(jnp.float32) / vector.shape[-1])
    angles = positions[:, None] * inv_freq[None, :]
    cosine = jnp.cos(angles)[:, None, :]
    sine_v = jnp.sin(angles)[:, None, :]
    front_half = vector[..., :half_dim]
    back_half = vector[..., half_dim:]
    return jnp.concatenate(
        [front_half * cosine - back_half * sine_v, back_half * cosine + front_half * sine_v],
        axis=-1,
    )


def adam_step(weight, gradient, moment, second, step_rate):
    moment = beta_first * moment + (1.0 - beta_first) * gradient
    second = beta_second * second + (1.0 - beta_second) * gradient * gradient
    scaled = (
        moment
        / (1.0 - beta_first**STEP)
        / (jnp.sqrt(second / (1.0 - beta_second**STEP)) + adam_eps)
    )
    return (moment, second, weight - step_rate * (scaled + decay_rate * weight))


def plain_device(
    tokens,
    cotangent,
    prefix,
    query_weight,
    keyval_weight,
    output_weight,
    gateup_weight,
    down_weight,
    norm_gains,
    query_first,
    keyval_first,
    output_first,
    gateup_first,
    down_first,
    gains_first,
    query_second,
    keyval_second,
    output_second,
    gateup_second,
    down_second,
    gains_second,
):
    rows_dev, width = tokens.shape
    length = rows_dev * lax.axis_size("tensor")
    query_full, keyval_full, output_full, gateup_full, down_full, gains_full = (
        lax.all_gather(query_weight.astype(jnp.bfloat16), "dp", axis=0, tiled=True),
        lax.all_gather(keyval_weight.astype(jnp.bfloat16), "dp", axis=0, tiled=True),
        lax.all_gather(output_weight.astype(jnp.bfloat16), "dp", axis=0, tiled=True),
        lax.all_gather(gateup_weight.astype(jnp.bfloat16), "dp", axis=0, tiled=True),
        lax.all_gather(down_weight.astype(jnp.bfloat16), "dp", axis=0, tiled=True),
        lax.all_gather(norm_gains.astype(jnp.bfloat16), "dp", axis=0, tiled=True),
    )
    head_dim = keyval_full.shape[1] // 2
    heads_dev = query_full.shape[1] // head_dim
    units = down_full.shape[1]
    gain_values = gains_full.astype(jnp.float32)
    gain_input = gain_values[0:width]
    gain_attn = gain_values[width : 2 * width]
    gain_pre = gain_values[2 * width : 3 * width]
    gain_ffn = gain_values[3 * width : 4 * width]
    gain_query = gain_values[4 * width : 4 * width + head_dim]
    gain_key = gain_values[4 * width + head_dim : 4 * width + 2 * head_dim]
    positions = jnp.arange(length).astype(jnp.float32)
    span_rows = min(512, length)
    count_blocks = length // span_rows
    starts = jnp.arange(0, length, span_rows, dtype=jnp.int32)
    columns = jnp.arange(length, dtype=jnp.int32)
    prefix_len = prefix[0]
    gateup_flat = gateup_full.reshape(width, 2 * units)

    def shape_query(raw_rows, gain_vec):
        return rotate(rms_scale(raw_rows, gain_vec), positions)

    def shape_key(raw_rows, gain_vec):
        return rotate(rms_scale(raw_rows[:, None, :], gain_vec), positions)[:, 0]

    token_rows = tokens.astype(jnp.float32)
    normed_local = rms_scale(token_rows, gain_input).astype(jnp.bfloat16)
    normed = lax.all_gather(normed_local, "tensor", axis=0, tiled=True)
    query_raw = mixed_dot(normed, query_full).reshape(length, heads_dev, head_dim)
    keyval_raw = mixed_dot(normed, keyval_full)
    query_rot = shape_query(query_raw, gain_query).astype(jnp.bfloat16)
    key_rot = shape_key(keyval_raw[:, :head_dim], gain_key).astype(jnp.bfloat16)
    value_low = keyval_raw[:, head_dim:].astype(jnp.bfloat16)

    def scores_of(row_start):
        row_ids = row_start + jnp.arange(span_rows, dtype=jnp.int32)
        q_blk = lax.dynamic_slice_in_dim(query_rot, row_start, span_rows, 0)
        raw_scores = (
            jnp.einsum("rhd,kd->hrk", q_blk, key_rot, preferred_element_type=jnp.float32)
            * query_scale
        )
        allowed = (columns[None, :] <= row_ids[:, None]) | (columns[None, :] < prefix_len)
        return (jnp.where(allowed[None], raw_scores, masked_fill), q_blk)

    def forward_block(row_start):
        scores, q_blk = scores_of(row_start)
        row_peak = jnp.max(scores, axis=-1, keepdims=True)
        shifted = jnp.exp(scores - row_peak)
        denom_sum = jnp.sum(shifted, axis=-1, keepdims=True)
        soft_probs = (shifted / denom_sum).astype(jnp.bfloat16)
        mixed_rows = jnp.einsum(
            "hrk,kd->rhd", soft_probs, value_low, preferred_element_type=jnp.float32
        )
        return (mixed_rows, (row_peak + jnp.log(denom_sum))[..., 0])

    attended_blocks, log_sums = lax.map(forward_block, starts)
    attended = attended_blocks.reshape(length, heads_dev * head_dim).astype(jnp.bfloat16)
    attn_part = jnp.einsum("rk,dk->rd", attended, output_full, preferred_element_type=jnp.float32)
    projected = lax.psum_scatter(
        attn_part.astype(jnp.bfloat16), "tensor", scatter_dimension=0, tiled=True
    ).astype(jnp.float32)
    hidden_state = token_rows + rms_scale(projected, gain_attn)
    normed_two = lax.all_gather(
        rms_scale(hidden_state, gain_pre).astype(jnp.bfloat16), "tensor", axis=0, tiled=True
    )
    gateup = mixed_dot(normed_two, gateup_flat)
    gate_part = gateup[:, :units]
    up_part = gateup[:, units:]
    activation = (jax.nn.gelu(gate_part, approximate=True) * up_part).astype(jnp.bfloat16)
    down_part = jnp.einsum("ru,du->rd", activation, down_full, preferred_element_type=jnp.float32)
    down_sum = lax.psum_scatter(
        down_part.astype(jnp.bfloat16), "tensor", scatter_dimension=0, tiled=True
    ).astype(jnp.float32)
    block_out = hidden_state + rms_scale(down_sum, gain_ffn)
    grad_out = cotangent.astype(jnp.float32)
    pull_ffn = jax.vjp(rms_scale, down_sum, gain_ffn)[1]
    grad_down, grad_gain_ffn = pull_ffn(grad_out)
    down_back = lax.all_gather(grad_down.astype(jnp.bfloat16), "tensor", axis=0, tiled=True)
    grad_activation = mixed_dot(down_back, down_full)
    grad_down_w = jnp.einsum("rd,ru->du", down_back, activation, preferred_element_type=jnp.float32)

    def geglu(gate_in, up_in):
        return jax.nn.gelu(gate_in, approximate=True) * up_in

    pull_act = jax.vjp(geglu, gate_part, up_part)[1]
    grad_gate, grad_up = pull_act(grad_activation)
    grad_gateup = jnp.concatenate([grad_gate, grad_up], axis=1).astype(jnp.bfloat16)
    grad_gateup_w = jnp.einsum(
        "rd,ru->du", normed_two, grad_gateup, preferred_element_type=jnp.float32
    ).reshape(width, 2, units)
    grad_normed_two = jnp.einsum(
        "ru,du->rd", grad_gateup, gateup_flat, preferred_element_type=jnp.float32
    )
    grad_pre_rows = lax.psum_scatter(
        grad_normed_two.astype(jnp.bfloat16), "tensor", scatter_dimension=0, tiled=True
    ).astype(jnp.float32)
    pull_pre = jax.vjp(rms_scale, hidden_state, gain_pre)[1]
    grad_hidden_norm, grad_gain_pre = pull_pre(grad_pre_rows)
    grad_hidden = grad_out + grad_hidden_norm
    pull_attn = jax.vjp(rms_scale, projected, gain_attn)[1]
    grad_proj, grad_gain_attn = pull_attn(grad_hidden)
    proj_back = lax.all_gather(grad_proj.astype(jnp.bfloat16), "tensor", axis=0, tiled=True)
    grad_output_w = jnp.einsum("rd,rk->dk", proj_back, attended, preferred_element_type=jnp.float32)
    grad_attended = (
        mixed_dot(proj_back, output_full)
        .astype(jnp.bfloat16)
        .reshape(count_blocks, span_rows, heads_dev, head_dim)
    )

    def backward_block(carry, batch_item):
        key_acc, value_acc = carry
        row_start, grad_att, lse_blk = batch_item
        scores, q_blk = scores_of(row_start)
        soft_full = jnp.exp(scores - lse_blk[..., None])
        grad_probs = jnp.einsum(
            "rhd,kd->hrk", grad_att, value_low, preferred_element_type=jnp.float32
        )
        delta_rows = jnp.sum(soft_full * grad_probs, axis=-1, keepdims=True)
        grad_scores = (soft_full * (grad_probs - delta_rows)).astype(jnp.bfloat16)
        grad_query = (
            jnp.einsum("hrk,kd->rhd", grad_scores, key_rot, preferred_element_type=jnp.float32)
            * query_scale
        )
        key_acc = (
            key_acc
            + jnp.einsum("hrk,rhd->kd", grad_scores, q_blk, preferred_element_type=jnp.float32)
            * query_scale
        )
        value_acc = value_acc + jnp.einsum(
            "hrk,rhd->kd",
            soft_full.astype(jnp.bfloat16),
            grad_att,
            preferred_element_type=jnp.float32,
        )
        return ((key_acc, value_acc), grad_query)

    zero_rows = jnp.zeros((length, head_dim), jnp.float32)
    (grad_key_rot, grad_value), grad_query_blocks = lax.scan(
        backward_block, (zero_rows, zero_rows), (starts, grad_attended, log_sums)
    )
    grad_query_rot = grad_query_blocks.reshape(length, heads_dev, head_dim)
    pull_query = jax.vjp(shape_query, query_raw, gain_query)[1]
    grad_query_raw, grad_gain_query = pull_query(grad_query_rot)
    pull_key = jax.vjp(shape_key, keyval_raw[:, :head_dim], gain_key)[1]
    grad_key_raw, grad_gain_key = pull_key(grad_key_rot)
    grad_query_low = grad_query_raw.reshape(length, heads_dev * head_dim).astype(jnp.bfloat16)
    grad_keyval = jnp.concatenate([grad_key_raw, grad_value], axis=1)
    grad_query_w = jnp.einsum(
        "rd,rk->dk", normed, grad_query_low, preferred_element_type=jnp.float32
    )
    grad_normed_query = jnp.einsum(
        "rk,dk->rd", grad_query_low, query_full, preferred_element_type=jnp.float32
    )
    grad_normed_part, grad_keyval_own = (
        lax.psum_scatter(
            grad_normed_query.astype(jnp.bfloat16), "tensor", scatter_dimension=0, tiled=True
        ).astype(jnp.float32),
        lax.psum_scatter(
            grad_keyval.astype(jnp.bfloat16), "tensor", scatter_dimension=0, tiled=True
        ).astype(jnp.float32),
    )
    grad_keyval_low = grad_keyval_own.astype(jnp.bfloat16)
    grad_keyval_w = jnp.einsum(
        "rd,rk->dk", normed_local, grad_keyval_low, preferred_element_type=jnp.float32
    )
    grad_normed = grad_normed_part + jnp.einsum(
        "rk,dk->rd", grad_keyval_low, keyval_full, preferred_element_type=jnp.float32
    )
    pull_input = jax.vjp(rms_scale, token_rows, gain_input)[1]
    grad_token_norm, grad_gain_input = pull_input(grad_normed)
    tokens_grad = (grad_hidden + grad_token_norm).astype(jnp.bfloat16)
    grad_gains = jnp.concatenate(
        [
            grad_gain_input,
            grad_gain_attn,
            grad_gain_pre,
            grad_gain_ffn,
            grad_gain_query,
            grad_gain_key,
        ]
    )
    keyval_total, gains_total = (
        lax.psum(grad_keyval_w.astype(jnp.bfloat16), "tensor").astype(jnp.float32),
        lax.psum(grad_gains.astype(jnp.bfloat16), "tensor").astype(jnp.float32),
    )
    query_sum, keyval_sum, output_sum, gateup_sum, down_grad_sum, gains_sum = (
        lax.psum_scatter(grad_query_w, "dp", scatter_dimension=0, tiled=True),
        lax.psum_scatter(keyval_total, "dp", scatter_dimension=0, tiled=True),
        lax.psum_scatter(grad_output_w, "dp", scatter_dimension=0, tiled=True),
        lax.psum_scatter(grad_gateup_w, "dp", scatter_dimension=0, tiled=True),
        lax.psum_scatter(grad_down_w, "dp", scatter_dimension=0, tiled=True),
        lax.psum_scatter(gains_total, "dp", scatter_dimension=0, tiled=True),
    )
    query_moment, query_square, query_master = adam_step(
        query_weight, query_sum, query_first, query_second, D ** (-0.5)
    )
    keyval_moment, keyval_square, keyval_master = adam_step(
        keyval_weight, keyval_sum, keyval_first, keyval_second, D ** (-0.5)
    )
    output_moment, output_square, output_master = adam_step(
        output_weight, output_sum, output_first, output_second, (HEADS * HEAD_DIM) ** (-0.5)
    )
    gateup_moment, gateup_square, gateup_master = adam_step(
        gateup_weight, gateup_sum, gateup_first, gateup_second, D ** (-0.5)
    )
    down_moment, down_square, down_master = adam_step(
        down_weight, down_grad_sum, down_first, down_second, FF ** (-0.5)
    )
    gains_moment, gains_square, gains_master = adam_step(
        norm_gains, gains_sum, gains_first, gains_second, 0.3
    )
    return (
        block_out.astype(jnp.bfloat16),
        tokens_grad,
        query_moment,
        query_square,
        query_master,
        keyval_moment,
        keyval_square,
        keyval_master,
        output_moment,
        output_square,
        output_master,
        gateup_moment,
        gateup_square,
        gateup_master,
        down_moment,
        down_square,
        down_master,
        gains_moment,
        gains_square,
        gains_master,
    )


def per_device(
    tokens,
    cotangent,
    prefix,
    query_weight,
    keyval_weight,
    output_weight,
    gateup_weight,
    down_weight,
    norm_gains,
    query_first,
    keyval_first,
    output_first,
    gateup_first,
    down_first,
    gains_first,
    query_second,
    keyval_second,
    output_second,
    gateup_second,
    down_second,
    gains_second,
):
    rows, width = tokens.shape
    lines = lax.axis_size("dp") // 2
    shard = query_weight.shape[0]
    head_dim = keyval_weight.shape[1] // 2
    units = down_weight.shape[1]
    fits = (
        lax.axis_size("tensor") == 4
        and lax.axis_size("dp") == 8
        and len(chunks_of(units)) == 4
        and query_weight.shape[1] == head_dim
        and shard % 16 == 0
        and norm_gains.shape[0] % 128 == 0
        and (3 * len(chunks_of(units)) + 2) // 2 * shard <= 4 * rows
    )
    if not fits:
        return plain_device(
            tokens,
            cotangent,
            prefix,
            query_weight,
            keyval_weight,
            output_weight,
            gateup_weight,
            down_weight,
            norm_gains,
            query_first,
            keyval_first,
            output_first,
            gateup_first,
            down_first,
            gains_first,
            query_second,
            keyval_second,
            output_second,
            gateup_second,
            down_second,
            gains_second,
        )
    length = 4 * rows
    sizes = (lines, rows, width, head_dim, units)
    weights = (keyval_weight, query_weight, output_weight, gateup_weight, down_weight)
    angles = np.arange(length)[:, None] * (rope_base ** (-2.0 * np.arange(head_dim // 2) / head_dim))[None, :]
    cosine = jnp.asarray(np.cos(angles), full)
    sine = jnp.asarray(np.sin(angles), full)
    *saved, gvec, proj, hidden, grad_down, dgain_ffn, block_out = forward_call(
        sizes, prefix, tokens, cotangent, norm_gains, weights, cosine, sine
    )
    *grads, tokens_grad, keyval_sum, gains_sum = backward_call(
        sizes, (grad_down, cotangent, tokens, gvec, dgain_ffn, proj, hidden, cosine, sine), saved
    )
    old = (
        query_weight,
        query_first,
        query_second,
        keyval_weight,
        keyval_first,
        keyval_second,
        output_weight,
        output_first,
        output_second,
        gateup_weight,
        gateup_first,
        gateup_second,
        down_weight,
        down_first,
        down_second,
        norm_gains,
        gains_first,
        gains_second,
    )
    return tuple(update_call(units, head_dim, (block_out, tokens_grad), (*grads, keyval_sum, gains_sum), old, 3))


def solution(mesh):
    placed = (
        P(("dp", "tensor"), None),
        P(("dp", "tensor"), None),
        P("dp"),
        P("dp", "tensor"),
        P("dp", None),
        P("dp", "tensor"),
        P("dp", None, "tensor"),
        P("dp", "tensor"),
        P("dp"),
        P("dp", "tensor"),
        P("dp", None),
        P("dp", "tensor"),
        P("dp", None, "tensor"),
        P("dp", "tensor"),
        P("dp"),
        P("dp", "tensor"),
        P("dp", None),
        P("dp", "tensor"),
        P("dp", None, "tensor"),
        P("dp", "tensor"),
        P("dp"),
    )
    return jax.shard_map(
        per_device,
        mesh=mesh,
        in_specs=placed,
        out_specs=(
            P(("dp", "tensor"), None),
            P(("dp", "tensor"), None),
            P("dp", "tensor"),
            P("dp", "tensor"),
            P("dp", "tensor"),
            P("dp", None),
            P("dp", None),
            P("dp", None),
            P("dp", "tensor"),
            P("dp", "tensor"),
            P("dp", "tensor"),
            P("dp", None, "tensor"),
            P("dp", None, "tensor"),
            P("dp", None, "tensor"),
            P("dp", "tensor"),
            P("dp", "tensor"),
            P("dp", "tensor"),
            P("dp"),
            P("dp"),
            P("dp"),
        ),
        check_vma=False,
    )
```

```python
import functools

import jax
import jax.numpy as jnp
import numpy as np
from jax import lax
from jax.experimental import pallas as pl
from jax.experimental.pallas import tpu as pltpu
from jax.sharding import PartitionSpec as P

D = 1152
FF = 6912
HEADS = 4
HEAD_DIM = 256
STEP = 10


eps_norm = 1e-06
query_scale = 0.0625
rope_base = 1000000.0
beta_first = 0.9
beta_second = 0.95
adam_eps = 1e-08
decay_rate = 0.01
masked_fill = -1e30
MESH = pl.DeviceIdType.MESH
low = jnp.bfloat16
full = jnp.float32
CHUNK = 512


def dot_nn(left, right):
    return lax.dot_general(left, right, (((1,), (0,)), ((), ())), preferred_element_type=full)


def dot_nt(left, right):
    return lax.dot_general(left, right, (((1,), (1,)), ((), ())), preferred_element_type=full)


def dot_tn(left, right):
    return lax.dot_general(left, right, (((0,), (0,)), ((), ())), preferred_element_type=full)


def chunks_of(units):
    out = []
    first = 0
    while first < units:
        width = min(CHUNK, units - first)
        out.append((first, width, -(-width // 128) * 128))
        first += width
    return out


def small_columns(head_dim):
    return 2 * head_dim, 3 * head_dim, 4 * head_dim


def packed_columns(units, head_dim):
    at = small_columns(head_dim)[2]
    places = []
    for first, width, _ in chunks_of(units):
        places.append((at, at + width, at + 2 * width))
        at += -(-3 * width // 128) * 128
    return places, at


class Place:
    def __init__(self):
        self.dp = lax.axis_index("dp")
        self.tensor = lax.axis_index("tensor")
        self.z = self.dp // 2
        self.x = self.dp % 2
        self.y = self.tensor // 2
        self.core = self.tensor % 2
        self.homes = (self.z, self.z + 1 - 2 * (self.z % 2), (self.z + 2) % 4, 3 - self.z)
        self.end = ((self.z + 1) // 2 + 1) % 2
        self.middle = self.end == 0
        self.mate = (self.dp, self.y * 2 + (1 - self.core))
        self.across = (self.dp, (1 - self.y) * 2 + self.core)
        self.side = (self.z * 2 + (1 - self.x), self.tensor)
        self.inner = ((1 + self.z % 2) * 2 + self.x, self.tensor)

    def line(self, step):
        return (self.homes[step] * 2 + self.x, self.tensor)

    def peers(self):
        return [self.mate, self.across, self.side] + [self.line(s) for s in (1, 2, 3)]


def greet(place):
    for peer in place.peers():
        pl.semaphore_signal(pltpu.get_barrier_semaphore(), inc=1, device_id=peer, device_id_type=MESH)


def meet(place):
    pl.semaphore_wait(pltpu.get_barrier_semaphore(), len(place.peers()))


def remote(source, target, send_sem, recv_sem, device):
    return pltpu.make_async_remote_copy(
        src_ref=source,
        dst_ref=target,
        send_sem=send_sem,
        recv_sem=recv_sem,
        device_id=device,
        device_id_type=MESH,
    )


class LineGather:
    def __init__(self, place, region, wide, send, recv, relay_send, side_send, side_recv):
        self.place, self.region, self.wide = place, region, wide
        self.send, self.recv, self.relay_send = send, recv, relay_send
        self.side_send, self.side_recv = side_send, side_recv

    def columns(self, group):
        return (0, 1) if self.wide[group] else (0,)

    def origin(self, column, step):
        place = self.place
        return place.homes[step] * 2 + (place.x if column == 0 else 1 - place.x)

    def along(self, group, column, step):
        block = self.region(group, self.origin(column, 0))
        return remote(
            block, block, self.send.at[group, column, step], self.recv.at[group, column, step], self.place.line(step)
        )

    def arrive(self, group, column, step):
        block = self.region(group, self.origin(column, step))
        remote(
            block, block, self.send.at[group, column, step], self.recv.at[group, column, step], self.place.line(step)
        ).wait_recv()

    def relay(self, group, column):
        block = self.region(group, self.origin(column, 2))
        return remote(
            block, block, self.relay_send.at[group, column], self.recv.at[group, column, 3], self.place.line(1)
        )

    def sideways(self, group, step):
        block = self.region(group, self.origin(0, step))
        return remote(
            block, block, self.side_send.at[group, step], self.side_recv.at[group, step], self.place.side
        )

    def arrive_side(self, group, step):
        block = self.region(group, self.origin(1, step))
        remote(
            block, block, self.side_send.at[group, step], self.side_recv.at[group, step], self.place.side
        ).wait_recv()

    def start_line(self, group, column):
        self.along(group, column, 2).start()
        self.along(group, column, 1).start()

        @pl.when(self.place.middle)
        def _():
            self.along(group, column, 3).start()

    def start_side(self, group):
        self.sideways(group, 0).start()

    def start(self, group):
        self.start_side(group)
        self.start_line(group, 0)

    def widen(self, group):
        self.arrive_side(group, 0)
        self.start_line(group, 1)

    def pass_on(self, group, *columns):
        for column in columns or self.columns(group):
            self.arrive(group, column, 2)

            @pl.when(self.place.middle)
            def _():
                self.relay(group, column).start()

            if not self.wide[group]:
                self.sideways(group, 2).start()

    def collect(self, group):
        for column in self.columns(group):
            for step in (1, 3):
                self.arrive(group, column, step)
                if not self.wide[group]:
                    self.sideways(group, step).start()

    def ready(self, group):
        if not self.wide[group]:
            for step in (0, 2, 1, 3):
                self.arrive_side(group, step)

    def finish(self):
        for group in range(len(self.wide)):
            for column in self.columns(group):
                self.along(group, column, 1).wait_send()
                self.along(group, column, 2).wait_send()

                @pl.when(self.place.middle)
                def _():
                    self.along(group, column, 3).wait_send()
                    self.relay(group, column).wait_send()

            for step in (0,) if self.wide[group] else (0, 1, 2, 3):
                self.sideways(group, step).wait_send()


def row_slabs(buffer, rows, first=0, count=None):
    return lambda y, core: buffer.at[pl.ds((y * 2 + core) * rows + first, count or rows)]


def column_slabs(buffer, wide):
    return lambda y, core: buffer.at[:, pl.ds(pl.multiple_of((y * 2 + core) * wide, wide), wide)]


class RowGather:
    def __init__(self, place, source, slab, send, recv):
        self.place, self.source, self.slab = place, source, slab
        self.send, self.recv = send, recv

    def copy(self, index):
        place = self.place
        slab = self.slab(1 - place.y if index == 2 else place.y, place.core)
        source = slab if index == 2 else self.source
        device = place.across if index == 1 else place.mate
        return remote(source, slab, self.send.at[index], self.recv.at[index], device)

    def arrival(self, index, y, core):
        slab = self.slab(y, core)
        remote(slab, slab, self.send.at[index], self.recv.at[index], self.place.mate).wait_recv()

    def start(self):
        self.copy(1).start()
        self.copy(0).start()

    def wait_mate(self):
        self.arrival(0, self.place.y, 1 - self.place.core)

    def wait_across(self):
        self.arrival(1, 1 - self.place.y, self.place.core)
        self.copy(2).start()

    def wait_corner(self):
        self.arrival(2, 1 - self.place.y, 1 - self.place.core)

    def finish(self):
        for index in range(3):
            self.copy(index).wait_send()


class RowScatter:
    def __init__(self, place, slab, first, second, mixed, send, recv):
        self.place, self.slab = place, slab
        self.first, self.second, self.mixed = first, second, mixed
        self.send, self.recv = send, recv

    def copy(self, index):
        place = self.place
        if index == 2:
            return remote(self.mixed, self.second, self.send.at[2], self.recv.at[2], place.across)
        source = self.slab(1 - place.y if index == 0 else place.y, 1 - place.core)
        return remote(source, self.first.at[index], self.send.at[index], self.recv.at[index], place.mate)

    def order(self):
        place = self.place
        return (
            (1 - place.y) * 2 + (1 - place.core),
            (1 - place.y) * 2 + place.core,
            place.y * 2 + (1 - place.core),
            place.y * 2 + place.core,
        )

    def after(self, step):
        if step == 0:
            self.copy(0).start()
        if step == 1:
            self.copy(0).wait_recv()
            mixed = self.slab(1 - self.place.y, self.place.core)[...].astype(full) + self.first[0].astype(full)
            self.mixed[...] = mixed.astype(low)
            self.copy(2).start()
        if step == 2:
            self.copy(1).start()

    def total(self):
        self.copy(1).wait_recv()
        here = self.slab(self.place.y, self.place.core)[...].astype(full) + self.first[1].astype(full)
        self.copy(2).wait_recv()
        return here + self.second[...].astype(full)

    def finish(self):
        for index in range(3):
            self.copy(index).wait_send()


def inverse_rms(rows):
    return lax.rsqrt(jnp.mean(rows * rows, axis=-1, keepdims=True) + eps_norm)


def rotate_rows(rows, cosine, sine):
    half = rows.shape[-1] // 2
    front, back = rows[:, :half], rows[:, half:]
    return jnp.concatenate([front * cosine - back * sine, back * cosine + front * sine], axis=-1)


def rotate_back(rows, cosine, sine):
    half = rows.shape[-1] // 2
    front, back = rows[:, :half], rows[:, half:]
    return jnp.concatenate([front * cosine + back * sine, back * cosine - front * sine], axis=-1)


def gelu_parts(gate):
    scale = 0.7978845608028654
    square = gate * gate
    bent = jnp.tanh(scale * gate * (1.0 + 0.044715 * square))
    return square, bent


def forward_kernel(
    sizes,
    prefix_ref,
    tokens_in,
    cot_in,
    gains_in,
    keyval_in,
    query_in,
    output_in,
    gateup_in,
    down_in,
    cos_in,
    sin_in,
    wall_out,
    normed_out,
    normed_two_out,
    query_out,
    key_out,
    key_rot_out,
    value_out,
    attended_out,
    probs_out,
    gate_out,
    up_out,
    act_out,
    gvec_out,
    proj_out,
    hidden_out,
    grad_down_out,
    dgain_ffn_out,
    block_out_out,
    cot_ref,
    gains_ref,
    keyval_ref,
    query_ref,
    output_ref,
    gateup_ref,
    down_ref,
    cos_ref,
    sin_ref,
    gvec,
    proj_keep,
    hidden_keep,
    dgain_ffn,
    block_out,
    wall,
    normed,
    normed_two,
    query_raw,
    key_raw,
    attended,
    probs,
    gate_keep,
    up_keep,
    act,
    tok_full,
    gains_full,
    key_rot,
    value_low,
    part_one,
    first_one,
    second_one,
    mixed_one,
    down_acc,
    line_send,
    line_recv,
    relay_send,
    side_send,
    side_recv,
    row_send,
    row_recv,
    keep_sem,
    load_sem,
):
    lines, rows, width, head_dim, units = sizes
    place = Place()
    greet(place)
    own_rows = pl.ds(place.tensor * rows, rows)
    loads = {}
    for name, source, target in (
        ("gains", gains_in, gains_ref),
        ("keyval", keyval_in, keyval_ref),
        ("query", query_in, query_ref),
        ("output", output_in, output_ref),
        ("gateup", gateup_in, gateup_ref),
        ("down", down_in, down_ref),
        ("tokens", tokens_in, tok_full.at[own_rows]),
        ("cos", cos_in, cos_ref),
        ("sin", sin_in, sin_ref),
        ("cot", cot_in, cot_ref),
    ):
        loads[name] = pltpu.make_async_copy(source, target, load_sem.at[len(loads)])
        loads[name].start()
    length = 4 * rows
    shard = keyval_ref.shape[0]
    places, columns = packed_columns(units, head_dim)
    chunks = chunks_of(units)
    last = len(chunks) - 1
    kv_end, query_end, output_end = small_columns(head_dim)
    split, split_last = places[last - 1][2] + 128, places[last][2] // 128 * 128
    quarter = kv_end // 4
    own_quarter = pl.ds(pl.multiple_of(place.tensor * quarter, quarter), quarter)
    spans = [(0, kv_end), (kv_end, output_end)]
    spans += [(places[c][0], places[c + 1][0]) for c in range(last - 2)]
    spans += [(places[last - 2][0], places[last - 2][2]), (places[last - 1][0], split)]
    spans += [(places[last - 2][2], places[last - 1][0]), (split, split_last), (split_last, columns)]
    tail = len(spans)

    def region(group, origin):
        if group == 0:
            return gains_full.at[pl.ds(origin * 8, 8)]
        if group == 1:
            return wall.at[pl.ds(origin * shard, shard), own_quarter]
        lo, hi = spans[group - 1]
        return wall.at[pl.ds(origin * shard, shard), lo:hi]

    wide_groups = [False] * (tail - 1) + [True] * 2
    gather = LineGather(place, region, wide_groups, line_send, line_recv, relay_send, side_send, side_recv)
    tokens_all = RowGather(place, tokens_in, row_slabs(tok_full, rows), row_send.at[0], row_recv.at[0])
    kept = []

    def keep(source, target):
        copy = pltpu.make_async_copy(source, target, keep_sem.at[len(kept)])
        copy.start()
        kept.append(copy)

    def keep_span(group):
        lo, hi = spans[group - 1]
        keep(wall.at[:, lo:hi], wall_out.at[:, lo:hi])

    for name in ("gains", "keyval", "query", "output"):
        loads[name].wait()
    own_gains = gains_ref[...].astype(low).astype(full).reshape(1, -1)
    gains_full[pl.ds(place.dp * 8, 8)] = jnp.broadcast_to(own_gains, (8, own_gains.shape[1]))
    own = pl.ds(place.dp * shard, shard)
    wall[own, own_quarter] = keyval_ref[:, own_quarter].astype(low)
    wall[own, kv_end:query_end] = query_ref[...].astype(low)
    wall[own, query_end:output_end] = output_ref[...].astype(low)
    meet(place)
    tokens_all.start()
    for group in range(3):
        gather.start(group)
    loads["gateup"].wait()
    loads["down"].wait()
    for (first, wide, _), at in zip(chunks, places):
        for kind, lo in enumerate(at):
            units_here = slice(first, first + wide)
            piece = down_ref[:, units_here] if kind == 2 else gateup_ref[:, kind, units_here]
            wall[own, lo : lo + wide] = piece.astype(low)
        if first == 0:
            gather.start(3)
    filled = places[last][2] + chunks[last][1]
    if filled < columns:
        wall[own, filled:columns] = jnp.zeros((shard, columns - filled), low)
    gather.start_side(4)
    for name in ("tokens", "cos", "sin", "cot"):
        loads[name].wait()
    tokens_all.wait_mate()
    tokens_all.wait_across()
    gather.pass_on(0)
    gather.pass_on(1)
    gather.collect(0)
    gather.collect(1)
    tokens_all.wait_corner()
    gather.pass_on(2)
    gather.ready(1)
    quarters = column_slabs(wall, quarter)
    keyval_all = RowGather(
        place, quarters(place.y, place.core), quarters, row_send.at[7], row_recv.at[7]
    )
    keyval_all.start()
    gather.collect(2)
    for group in range(5, tail + 1):
        gather.start_side(group)
    gather.start_line(4, 0)
    gather.ready(0)
    step = gains_ref.shape[0]
    for origin in range(2 * lines):
        gvec[:, origin * step : (origin + 1) * step] = gains_full[origin * 8 : origin * 8 + 8]
    keep(gvec, gvec_out)
    gain_in = 1.0 + gvec[0:1, 0:width]
    gain_attn = 1.0 + gvec[0:1, width : 2 * width]
    gain_pre = 1.0 + gvec[0:1, 2 * width : 3 * width]
    gain_ffn = 1.0 + gvec[0:1, 3 * width : 4 * width]
    gain_query = 1.0 + gvec[0:1, 4 * width : 4 * width + head_dim]
    gain_key = 1.0 + gvec[0:1, 4 * width + head_dim : 4 * width + 2 * head_dim]

    def norm_slab(index, carry):
        at = pl.ds(pl.multiple_of(index * rows, rows), rows)
        x = tok_full[at].astype(full)
        normed[at] = (x * inverse_rms(x) * gain_in).astype(low)
        return carry

    lax.fori_loop(0, 4, norm_slab, 0)
    keep(normed, normed_out)
    keyval_all.wait_mate()
    keyval_all.wait_across()
    gather.ready(2)
    keyval_all.wait_corner()

    def project_slab(index, carry):
        at = pl.ds(pl.multiple_of(index * rows, rows), rows)
        n1 = normed[at]
        query_raw[at] = dot_nn(n1, wall[:, kv_end:query_end])
        kv = dot_nn(n1, wall[:, 0:kv_end])
        k = kv[:, :head_dim]
        key_raw[at] = k
        key_rot[at] = rotate_rows(k * inverse_rms(k) * gain_key, cos_ref[at], sin_ref[at]).astype(low)
        value_low[at] = kv[:, head_dim:].astype(low)
        return carry

    lax.fori_loop(0, 4, project_slab, 0)
    gather.pass_on(3)
    gather.start_line(5, 0)
    keep(query_raw, query_out)
    keep(key_raw, key_out)
    keep(key_rot, key_rot_out)
    keep(value_low, value_out)
    keep_span(1)
    keep_span(2)

    out_scatter = RowScatter(
        place, row_slabs(part_one, rows), first_one, second_one, mixed_one, row_send.at[1], row_recv.at[1]
    )

    def attend_slab(index):
        at = pl.ds(pl.multiple_of(index * rows, rows), rows)
        q = query_raw[at]
        qr = rotate_rows(q * inverse_rms(q) * gain_query, cos_ref[at], sin_ref[at]).astype(low)
        scores = dot_nt(qr, key_rot[...]) * query_scale
        row_ids = lax.broadcasted_iota(jnp.int32, (rows, length), 0) + index * rows
        columns = lax.broadcasted_iota(jnp.int32, (rows, length), 1)
        allowed = (columns <= row_ids) | (columns < prefix_ref[0])
        scores = jnp.where(allowed, scores, masked_fill)
        shifted = jnp.exp(scores - jnp.max(scores, axis=-1, keepdims=True))
        soft = (shifted / jnp.sum(shifted, axis=-1, keepdims=True)).astype(low)
        probs[at] = soft
        mixed = dot_nn(soft, value_low[...]).astype(low)
        attended[at] = mixed
        part_one[at] = dot_nt(mixed, wall[:, query_end:output_end]).astype(low)

    for step, index in enumerate(out_scatter.order()):
        attend_slab(index)
        out_scatter.after(step)
    keep(probs, probs_out)
    keep(attended, attended_out)
    gather.collect(3)
    gather.pass_on(4)
    for group in range(6, tail + 1):
        gather.start_line(group, 0)
    projected = out_scatter.total()
    out_scatter.finish()
    proj_keep[...] = projected
    hidden = tok_full[own_rows].astype(full) + projected * inverse_rms(projected) * gain_attn
    hidden_keep[...] = hidden
    keep(proj_keep, proj_out)
    keep(hidden_keep, hidden_out)
    normed_two[own_rows] = (hidden * inverse_rms(hidden) * gain_pre).astype(low)
    two_all = RowGather(place, normed_two.at[own_rows], row_slabs(normed_two, rows), row_send.at[2], row_recv.at[2])
    two_all.start()
    gather.collect(4)
    gather.pass_on(5)
    two_all.wait_mate()
    gather.widen(tail - 1)
    gather.widen(tail)
    two_all.wait_across()
    gather.pass_on(6)
    gather.collect(5)
    two_all.wait_corner()
    keep(normed_two, normed_two_out)

    half = rows // 2
    down_scatters, down_gathers = [], []
    for index in range(2):
        piece = slice(index * half, (index + 1) * half)
        down_scatters.append(
            RowScatter(
                place,
                row_slabs(part_one, rows, index * half, half),
                first_one.at[:, piece],
                second_one.at[piece],
                mixed_one.at[piece],
                row_send.at[3 + index],
                row_recv.at[3 + index],
            )
        )
        slabs = row_slabs(tok_full, rows, index * half, half)
        down_gathers.append(
            RowGather(place, slabs(place.y, place.core), slabs, row_send.at[5 + index], row_recv.at[5 + index])
        )
    block = 2 * rows

    def feed(c):
        first, wide, padded = chunks[c]
        at_gate, at_up, _ = places[c]

        def feed_rows(index, carry):
            at = pl.ds(pl.multiple_of(index * block, block), block)
            n2 = normed_two[at]
            gate = dot_nn(n2, wall[:, at_gate : at_gate + wide])
            up = dot_nn(n2, wall[:, at_up : at_up + wide])
            gate_keep[at, first : first + wide] = gate.astype(low)
            up_keep[at, first : first + wide] = up.astype(low)
            _, bent = gelu_parts(gate)
            act[at, first : first + wide] = (0.5 * gate * (1.0 + bent) * up).astype(low)
            return carry

        lax.fori_loop(0, 2, feed_rows, 0)
        span = slice(first, first + padded)
        keep(gate_keep.at[:, span], gate_out.at[:, span])
        keep(up_keep.at[:, span], up_out.at[:, span])
        keep(act.at[:, span], act_out.at[:, span])

    def lower(c):
        first, wide, _ = chunks[c]
        at_down = places[c][2]

        def lower_rows(index, carry):
            at = pl.ds(pl.multiple_of(index * block, block), block)
            more = dot_nt(act[at, first : first + wide], wall[:, at_down : at_down + wide])
            down_acc[at] = more if c == 0 else down_acc[at] + more
            return carry

        lax.fori_loop(0, 2, lower_rows, 0)

    gather.ready(3)
    keep_span(3)
    feed(0)
    gather.pass_on(7, 0)
    gather.pass_on(8, 0)
    gather.collect(6)
    lower(0)
    gather.ready(4)
    keep_span(4)
    feed(1)
    gather.pass_on(7, 1)
    gather.ready(5)
    keep_span(5)
    feed(2)
    gather.pass_on(8, 1)
    gather.collect(7)
    keep_span(7)
    feed(3)
    lower(2)
    gather.ready(6)
    keep_span(6)
    lower(1)
    gather.collect(8)
    keep_span(8)
    first, wide, _ = chunks[last]
    at_down = places[last][2]
    tokens_all.finish()
    for step, index in enumerate(down_scatters[0].order()):
        at = pl.ds(pl.multiple_of(index * rows, rows), rows)
        part_one[at] = (
            down_acc[at] + dot_nt(act[at, first : first + wide], wall[:, at_down : at_down + wide])
        ).astype(low)
        for scatter in down_scatters:
            scatter.after(step)
    for index, (scatter, spread) in enumerate(zip(down_scatters, down_gathers)):
        piece = slice(index * half, (index + 1) * half)
        f = scatter.total()
        inv = inverse_rms(f)
        cot = cot_ref[piece].astype(full)
        scaled = cot * gain_ffn
        back = inv * (scaled - f * (inv * inv) * jnp.mean(f * scaled, axis=-1, keepdims=True))
        tok_full[pl.ds(place.tensor * rows + index * half, half)] = back.astype(low)
        spread.start()
        block_out[piece] = (hidden_keep[piece] + f * inv * gain_ffn).astype(low)
        grad = jnp.broadcast_to(jnp.sum(cot * f * inv, axis=0, keepdims=True), dgain_ffn.shape)
        dgain_ffn[...] = grad if index == 0 else dgain_ffn[...] + grad

    def keep_slab(y, core):
        at = pl.ds((y * 2 + core) * rows, rows)
        keep(tok_full.at[at], grad_down_out.at[at])

    keep(block_out, block_out_out)
    keep(dgain_ffn, dgain_ffn_out)
    keep_slab(place.y, place.core)
    for spread in down_gathers:
        spread.wait_mate()
    keep_slab(place.y, 1 - place.core)
    for spread in down_gathers:
        spread.wait_across()
    keep_slab(1 - place.y, place.core)
    for spread in down_gathers:
        spread.wait_corner()
    keep_slab(1 - place.y, 1 - place.core)
    gather.finish()
    keyval_all.finish()
    two_all.finish()
    for item in down_scatters + down_gathers:
        item.finish()
    for copy in kept:
        copy.wait()


def forward_call(sizes, prefix, tokens, cotangent, gains, weights, cosine, sine):
    lines, rows, width, head_dim, units = sizes
    length = 4 * rows
    shard = weights[0].shape[0]
    columns = packed_columns(units, head_dim)[1]
    chunks = chunks_of(units)
    padded = sum(c[2] for c in chunks)
    groups = 5 + len(chunks)
    inputs = (tokens, cotangent, gains, *weights, cosine, sine)
    hbm = pl.BlockSpec(memory_space=pl.ANY)
    large = [
        ((2 * lines * shard, columns), low),
        ((length, width), low),
        ((length, width), low),
        ((length, head_dim), full),
        ((length, head_dim), full),
        ((length, head_dim), low),
        ((length, head_dim), low),
        ((length, head_dim), low),
        ((length, length), low),
        ((length, padded), low),
        ((length, padded), low),
        ((length, padded), low),
    ]
    small = [
        ((8, gains.shape[0] * 2 * lines), full),
        ((rows, width), full),
        ((rows, width), full),
        ((length, width), low),
        ((8, width), full),
        ((rows, width), low),
    ]
    inside = [large[i] for i in (0, 1, 2, 3, 4, 7, 8, 9, 10, 11)]
    scatter_set = [
        pltpu.VMEM((2, rows, width), low),
        pltpu.VMEM((rows, width), low),
        pltpu.VMEM((rows, width), low),
    ]
    return pl.pallas_call(
        functools.partial(forward_kernel, sizes),
        out_shape=[jax.ShapeDtypeStruct(*item) for item in large + small],
        in_specs=[pl.BlockSpec(memory_space=pltpu.SMEM)] + [hbm] * len(inputs),
        out_specs=[hbm] * (len(large) + len(small)),
        scratch_shapes=[pltpu.VMEM(a.shape, a.dtype) for a in inputs[1:]]
        + [pltpu.VMEM(*item) for item in small[:3] + small[4:] + inside]
        + [
            pltpu.VMEM((length, width), low),
            pltpu.VMEM((2 * lines * 8, gains.shape[0]), full),
            pltpu.VMEM((length, head_dim), low),
            pltpu.VMEM((length, head_dim), low),
            pltpu.VMEM((length, width), low),
        ]
        + scatter_set
        + [
            pltpu.VMEM((length, width), full),
            pltpu.SemaphoreType.DMA((groups, 2, lines)),
            pltpu.SemaphoreType.DMA((groups, 2, lines)),
            pltpu.SemaphoreType.DMA((groups, 2)),
            pltpu.SemaphoreType.DMA((groups, lines)),
            pltpu.SemaphoreType.DMA((groups, lines)),
            pltpu.SemaphoreType.DMA((8, 3)),
            pltpu.SemaphoreType.DMA((8, 3)),
            pltpu.SemaphoreType.DMA((22 + 4 * len(chunks),)),
            pltpu.SemaphoreType.DMA((len(inputs),)),
        ],
        compiler_params=pltpu.CompilerParams(
            collective_id=0, has_side_effects=True, vmem_limit_bytes=63 * 1024 * 1024
        ),
        name="forward",
    )(prefix, *inputs)


class LineScatter:
    def __init__(self, place, block, side_block, line_block, wide, side_send, side_recv, line_send, line_recv, kind):
        self.place, self.block, self.side_block, self.line_block = place, block, side_block, line_block
        self.wide, self.kind = wide, kind
        self.side_send, self.side_recv, self.line_send, self.line_recv = side_send, side_recv, line_send, line_recv

    def columns(self, group):
        return (0, 1) if self.wide[group] else (0,)

    def own(self, group, column, step):
        place = self.place
        return self.block(group, place.homes[step] * 2 + (place.x if column == 0 else 1 - place.x))

    def sideways(self, group, step):
        home = 0 if self.wide[group] else self.place.homes[step]
        return remote(
            self.own(group, 1, step),
            self.side_block(group, home),
            self.side_send.at[group, step],
            self.side_recv.at[group, step],
            self.place.side,
        )

    def along(self, group, column, step):
        slot = step - 1 if step < 3 else 2 + self.place.end
        return remote(
            self.own(group, column, step),
            self.line_block(group, column, slot),
            self.line_send.at[group, column, step],
            self.line_recv.at[group, column, slot],
            self.place.line(step) if step < 3 else self.place.inner,
        )

    def arrive(self, group, column, slot):
        here = self.line_block(group, column, slot)
        remote(
            here, here, self.line_send.at[group, column, 1], self.line_recv.at[group, column, slot], self.place.line(1)
        ).wait_recv()
        return here[...].astype(full)

    def start(self, group):
        if not self.wide[group]:
            for step in (3, 1, 2, 0):
                self.sideways(group, step).start()
            return
        for step in (3, 1):
            for column in (0, 1):
                self.along(group, column, step).start()

        @pl.when(self.place.end == 1)
        def _():
            for column in (0, 1):
                self.along(group, column, 2).start()

    def with_side(self, group, step):
        self.sideways(group, step).wait_recv()
        return self.own(group, 0, step)[...].astype(full) + self.side_block(group, self.place.homes[step])[...].astype(
            full
        )

    def pump(self, group, *steps):
        for step in steps or (3, 1, 2):
            self.own(group, 0, step)[...] = self.with_side(group, step).astype(self.kind)
            if step != 2:
                self.along(group, 0, step).start()
                continue

            @pl.when(self.place.end == 1)
            def _():
                self.along(group, 0, 2).start()

    def relay(self, group):
        for column in self.columns(group):

            @pl.when(self.place.middle)
            def _():
                block = self.own(group, column, 2)
                block[...] = (block[...].astype(full) + self.arrive(group, column, 3)).astype(self.kind)
                self.along(group, column, 2).start()

    def hand_over(self, group):
        block = self.own(group, 1, 0)
        both = block[...].astype(full) + self.arrive(group, 1, 0) + self.arrive(group, 1, 1)

        @pl.when(self.place.middle)
        def _():
            block[...] = (both + self.arrive(group, 1, 2)).astype(self.kind)

        @pl.when(self.place.end == 1)
        def _():
            block[...] = both.astype(self.kind)

        self.sideways(group, 0).start()

    def settle(self, group):
        self.sideways(group, 0).wait_recv()
        self.arrive(group, 0, 0)
        self.arrive(group, 0, 1)

        @pl.when(self.place.middle)
        def _():
            self.arrive(group, 0, 2)

    def total(self, group, lo, hi, held):
        parts = [
            self.own(group, 0, 0),
            self.side_block(group, 0 if self.wide[group] else self.place.z),
            self.line_block(group, 0, 0),
            self.line_block(group, 0, 1),
        ]
        first, *others = [part[:, lo:hi].astype(full) for part in parts]
        for other in others:
            first = first + other
        held[...] = first

        @pl.when(self.place.middle)
        def _():
            held[...] = first + self.line_block(group, 0, 2)[:, lo:hi].astype(full)

    def finish(self):
        for group in range(len(self.wide)):
            for step in (0,) if self.wide[group] else (0, 1, 2, 3):
                self.sideways(group, step).wait_send()
            for column in self.columns(group):
                for step in (1, 2, 3):
                    self.along(group, column, step).wait_send()


def norm_back(rows, inv, gain, grad):
    scaled = grad * gain
    back = inv * (scaled - rows * (inv * inv) * jnp.mean(rows * scaled, axis=-1, keepdims=True))
    return back, jnp.sum(grad * rows * inv, axis=0, keepdims=True)


def backward_kernel(
    sizes,
    grad_down_in,
    cot_in,
    tokens_in,
    gvec_in,
    dgain_ffn_in,
    proj_in,
    hidden_in,
    cos_in,
    sin_in,
    wall_in,
    normed_in,
    normed_two_in,
    query_in,
    key_in,
    key_rot_in,
    value_in,
    attended_in,
    probs_in,
    gate_in,
    up_in,
    act_in,
    gate_grad,
    up_grad,
    down_grad,
    small_grad,
    tokens_grad_out,
    keyval_grad,
    gains_grad,
    tokens_grad,
    cot_ref,
    tokens_ref,
    gvec,
    dgain_ffn,
    proj_ref,
    hidden_ref,
    cos_ref,
    sin_ref,
    wall,
    side_buf,
    side_wide,
    line_buf,
    line_wide,
    big,
    normed_two,
    row_buf,
    acc,
    first_buf,
    second_buf,
    mixed_buf,
    key_rot,
    value_low,
    dquery,
    dkeyval,
    dhidden,
    dproj,
    kv_first,
    kv_second,
    kv_mixed,
    kv_own,
    dgains,
    gain_part,
    gain_first,
    gain_second,
    gain_side,
    gain_line,
    row_send,
    row_recv,
    side_send,
    side_recv,
    line_send,
    line_recv,
    gain_side_send,
    gain_side_recv,
    gain_line_send,
    gain_line_recv,
    last_send,
    last_recv,
    load_sem,
    store_sem,
):
    lines, rows, width, head_dim, units = sizes
    place = Place()
    length = 4 * rows
    shard = wall.shape[0] // (2 * lines)
    kv_end, query_end, output_end = small_columns(head_dim)
    quarter = head_dim // 2
    places, columns = packed_columns(units, head_dim)
    chunks = chunks_of(units)
    last = len(chunks) - 1
    order = [0, last] + list(range(1, last))
    base_column = kv_end - quarter
    spans = []
    for c in range(last):
        spans += [(places[c][2], places[c + 1][0]), (places[c][0], places[c][2])]
    group_gate, group_up, group_last, group_small = range(len(spans) - 1, len(spans) + 3)
    spans[-1:] = [(places[last - 1][0], places[last - 1][1]), (places[last - 1][1], places[last - 1][2])]
    spans += [(places[last][0], columns), (base_column, output_end)]
    part_wide = 3 * quarter
    group_extra = len(spans)
    spans[0:1] = [(places[0][2], places[0][2] + part_wide)]
    spans.append((places[0][2] + part_wide, places[1][0]))
    loads = {}

    def load(name, source, target):
        copy = pltpu.make_async_copy(source, target, load_sem.at[len(loads)])
        copy.start()
        loads[name] = copy

    def load_chunk(c):
        first, _, padded = chunks[c]
        lo, hi = places[c][0], columns if c == last else places[c + 1][0]
        base = (order.index(c) % 2) * 3 * CHUNK
        cut = places[c][2] // 128 * 128
        load(("down", c), wall_in.at[:, cut:hi], wall.at[:, cut:hi])
        for k, source in enumerate((gate_in, up_in, act_in)):
            at = base + k * CHUNK
            load((k, c), source.at[:, first : first + padded], big.at[:, at : at + padded])
        load(("gateup", c), wall_in.at[:, lo:cut], wall.at[:, lo:cut])

    greet(place)
    own_rows = pl.ds(place.tensor * rows, rows)
    load("down", grad_down_in, row_buf)
    load_chunk(order[0])
    load("two", normed_two_in, normed_two)
    load("gvec", gvec_in, gvec)
    load("dgain", dgain_ffn_in, dgain_ffn)
    load_chunk(order[1])
    load("hidden", hidden_in, hidden_ref)
    load("cot", cot_in, cot_ref)
    load("proj", proj_in, proj_ref)
    load("tokens", tokens_in, tokens_ref)
    load("cos", cos_in, cos_ref)
    load("sin", sin_in, sin_ref)
    load("kv", wall_in.at[:, 0:kv_end], wall.at[:, 0:kv_end])
    load("qo", wall_in.at[:, kv_end:output_end], wall.at[:, kv_end:output_end])
    load("key_rot", key_rot_in, key_rot)
    load("value", value_in, value_low)
    loads["gvec"].wait()
    loads["dgain"].wait()
    gain_in = 1.0 + gvec[0:1, 0:width]
    gain_attn = 1.0 + gvec[0:1, width : 2 * width]
    gain_pre = 1.0 + gvec[0:1, 2 * width : 3 * width]
    gain_query = 1.0 + gvec[0:1, 4 * width : 4 * width + head_dim]
    gain_key = 1.0 + gvec[0:1, 4 * width + head_dim : 4 * width + 2 * head_dim]
    dgains[...] = jnp.zeros_like(dgains)
    dgains[0:1, 3 * width : 4 * width] = dgain_ffn[0:1]
    loads["down"].wait()

    def block(group, origin):
        lo, hi = spans[group]
        return wall.at[pl.ds(origin * shard, shard), lo:hi]

    def side_block(group, home):
        if wide_groups[group]:
            return side_wide.at[:, wide_at[group] : wide_at[group] + spans[group][1] - spans[group][0]]
        lo, hi = spans[group]
        return side_buf.at[pl.ds(home * shard, shard), lo - base_column : hi - base_column]

    def line_block(group, column, slot):
        lo, hi = spans[group]
        if wide_groups[group]:
            at = slice(wide_at[group], wide_at[group] + hi - lo)
            return line_wide.at[pl.ds((column * 4 + slot) * shard, shard), at]
        return line_buf.at[pl.ds(slot * shard, shard), lo - base_column : hi - base_column]

    wide_groups = [group in (group_last, group_extra) for group in range(len(spans))]
    wide_at = {group_last: 0, group_extra: spans[group_last][1] - spans[group_last][0]}
    scatter = LineScatter(
        place, block, side_block, line_block, wide_groups, side_send, side_recv, line_send, line_recv, low
    )
    part = big.at[:, 0:width]
    pre_scatter = RowScatter(
        place, row_slabs(part, rows), first_buf, second_buf, mixed_buf, row_send.at[1], row_recv.at[1]
    )
    half = 2 * rows
    third = width // 3

    def weight_gradient(lo, wide, left, right):
        for m in range(0, width, third):
            wall[m : m + third, lo : lo + wide] = dot_tn(left[:, m : m + third], right).astype(low)

    for position, c in enumerate(order):
        first, wide, padded = chunks[c]
        at_gate, at_up, at_down = places[c]
        base = (position % 2) * 3 * CHUNK
        for name in ("down", 0, 1):
            loads[name, c].wait()
        if 1 <= position < last:
            load_chunk(order[position + 1])
        of_gate = slice(base, base + wide)
        of_up = slice(base + CHUNK, base + CHUNK + wide)
        of_act = slice(base + 2 * CHUNK, base + 2 * CHUNK + wide)

        def unit_rows(index, carry):
            at = pl.ds(pl.multiple_of(index * half, half), half)
            dz = dot_nn(row_buf[at], wall[:, at_down : at_down + wide])
            gate = big[at, of_gate].astype(full)
            up = big[at, of_up].astype(full)
            square, bent = gelu_parts(gate)
            middle = 0.5 * (1.0 + bent)
            slope = middle + 0.5 * gate * (1.0 - bent * bent) * (0.7978845608028654 * (1.0 + 0.134145 * square))
            big[at, of_gate] = (dz * up * slope).astype(low)
            big[at, of_up] = (dz * gate * middle).astype(low)
            return carry

        lax.fori_loop(0, 2, unit_rows, 0)
        loads[2, c].wait()
        weight_gradient(at_down, wide, row_buf, big[:, of_act])
        loads["gateup", c].wait()
        if position == 0:
            meet(place)
        if c < last:
            scatter.start(2 * c)
        if position == 0:
            scatter.start(group_extra)

        def back_rows(at):
            more = dot_nt(big[at, of_gate], wall[:, at_gate : at_gate + wide])
            more = more + dot_nt(big[at, of_up], wall[:, at_up : at_up + wide])
            return more if position == 0 else acc[at] + more

        if position < last:

            def collect_rows(index, carry):
                at = pl.ds(pl.multiple_of(index * half, half), half)
                acc[at] = back_rows(at)
                return carry

            lax.fori_loop(0, 2, collect_rows, 0)
        else:
            for step, index in enumerate(pre_scatter.order()):
                at = pl.ds(pl.multiple_of(index * rows, rows), rows)
                part[at] = back_rows(at).astype(low)
                pre_scatter.after(step)
        if position == 0:
            loads["two"].wait()
        weight_gradient(at_gate, wide, normed_two, big[:, of_gate])
        weight_gradient(at_up, wide, normed_two, big[:, of_up])
        if c < last:
            scatter.start(2 * c + 1)
            if position == 0:
                scatter.relay(group_extra)
        else:
            scatter.pump(0)
            scatter.start(group_last)
        if position == 2:
            scatter.relay(0)
            scatter.hand_over(group_extra)
        if position == 3:
            scatter.relay(group_last)
            scatter.pump(1, 3, 1)

    at_normed = width
    at_att = at_normed + width
    load("normed", normed_in, big.at[:, at_normed : at_normed + width])
    load("attended", attended_in, big.at[:, at_att : at_att + head_dim])
    load("query", query_in, acc.at[:, 2 * head_dim : 3 * head_dim])
    load("key", key_in, acc.at[:, 3 * head_dim : 4 * head_dim])

    scatter.pump(1, 2)
    dn2 = pre_scatter.total()
    for name in ("hidden", "cot", "proj", "tokens", "cos", "sin"):
        loads[name].wait()
    hidden = hidden_ref[...]
    back, grad = norm_back(hidden, inverse_rms(hidden), gain_pre, dn2)
    dgains[0:1, 2 * width : 3 * width] = grad
    dh = cot_ref[...].astype(full) + back
    dhidden[...] = dh
    proj = proj_ref[...]
    back, grad = norm_back(proj, inverse_rms(proj), gain_attn, dh)
    dgains[0:1, width : 2 * width] = grad
    dproj[...] = back.astype(low)
    row_buf[own_rows] = dproj[...]
    proj_all = RowGather(place, dproj, row_slabs(row_buf, rows), row_send.at[2], row_recv.at[2])
    proj_all.start()
    pre_scatter.finish()
    load("probs", probs_in, big.at[:, 0:length])
    acc[:, 0 : 2 * head_dim] = jnp.zeros((length, 2 * head_dim), full)
    proj_all.wait_mate()
    scatter.pump(2)
    proj_all.wait_across()
    scatter.relay(1)
    proj_all.wait_corner()
    for name in ("kv", "qo", "key_rot", "value", "normed", "attended", "query", "key", "probs"):
        loads[name].wait()

    def attend_back(index, carry):
        at = pl.ds(pl.multiple_of(index * rows, rows), rows)
        da = dot_nn(row_buf[at], wall[:, query_end:output_end]).astype(low)
        soft = big[at, 0:length]
        wide_soft = soft.astype(full)
        dp = dot_nt(da, value_low[...])
        ds = (wide_soft * (dp - jnp.sum(wide_soft * dp, axis=-1, keepdims=True))).astype(low)
        q = acc[at, 2 * head_dim : 3 * head_dim]
        inv = inverse_rms(q)
        cosine, sine = cos_ref[at], sin_ref[at]
        qr = rotate_rows(q * inv * gain_query, cosine, sine).astype(low)
        dqr = dot_nn(ds, key_rot[...]) * query_scale
        acc[:, 0:head_dim] += dot_tn(ds, qr)
        acc[:, head_dim : 2 * head_dim] += dot_tn(soft, da)
        dq, grad = norm_back(q, inv, gain_query, rotate_back(dqr, cosine, sine))
        dquery[at] = dq.astype(low)
        dgains[0:1, 4 * width : 4 * width + head_dim] += grad
        return carry

    scatter.hand_over(group_last)
    scatter.pump(3, 3)
    lax.fori_loop(0, 4, attend_back, 0)

    def key_back(index, carry):
        at = pl.ds(pl.multiple_of(index * rows, rows), rows)
        k = acc[at, 3 * head_dim : 4 * head_dim]
        dkr = rotate_back(acc[at, 0:head_dim] * query_scale, cos_ref[at], sin_ref[at])
        dk, grad = norm_back(k, inverse_rms(k), gain_key, dkr)
        dkeyval[at, 0:head_dim] = dk.astype(low)
        dkeyval[at, head_dim : 2 * head_dim] = acc[at, head_dim : 2 * head_dim].astype(low)
        dgains[0:1, 4 * width + head_dim : 4 * width + 2 * head_dim] += grad
        return carry

    lax.fori_loop(0, 4, key_back, 0)
    scatter.pump(3, 1)
    in_scatter = RowScatter(
        place, row_slabs(part, rows), first_buf, second_buf, mixed_buf, row_send.at[3], row_recv.at[3]
    )
    for step, index in enumerate(in_scatter.order()):
        at = pl.ds(pl.multiple_of(index * rows, rows), rows)
        more = dot_nt(dquery[at], wall[:, kv_end:query_end]) + dot_nt(dkeyval[at], wall[:, 0:kv_end])
        part[at] = more.astype(low)
        in_scatter.after(step)
    scatter.pump(3, 2)
    scatter.relay(2)

    normed = big.at[:, at_normed : at_normed + width]
    for m in range(0, width, third):
        wall[m : m + third, 0:kv_end] = dot_tn(normed[:, m : m + third], dkeyval[...]).astype(low)

    def kv_block(y, core):
        return wall.at[:, pl.ds(pl.multiple_of((y * 2 + core) * quarter, quarter), quarter)]

    def kv_copy(index):
        send, recv = last_send.at[index], last_recv.at[index]
        if index == 2:
            return remote(kv_mixed, kv_second, send, recv, place.across)
        return remote(
            kv_block(1 - place.y if index == 0 else place.y, 1 - place.core), kv_first.at[index], send, recv, place.mate
        )

    kv_copy(0).start()
    kv_copy(1).start()
    weight_gradient(kv_end, head_dim, normed, dquery[...])
    weight_gradient(query_end, head_dim, row_buf, big[:, at_att : at_att + head_dim])
    kv_copy(0).wait_recv()
    kv_mixed[...] = (kv_block(1 - place.y, place.core)[...].astype(full) + kv_first[0].astype(full)).astype(low)
    kv_copy(2).start()
    scatter.pump(4, 3, 1)
    scatter.relay(3)

    dn1 = in_scatter.total()
    x = tokens_ref[...].astype(full)
    back, grad = norm_back(x, inverse_rms(x), gain_in, dn1)
    dgains[0:1, 0:width] = grad
    tokens_grad[...] = (dhidden[...] + back).astype(low)
    tokens_copy = pltpu.make_async_copy(tokens_grad, tokens_grad_out, store_sem.at[2 + 3 * len(chunks)])
    tokens_copy.start()
    step = gains_grad.shape[1]
    for origin in range(2 * lines):
        gain_part[origin * 8 : origin * 8 + 8] = dgains[:, origin * step : (origin + 1) * step]

    def gain_copy(index):
        source, target, device = (
            (gain_part, gain_first, place.mate) if index == 0 else (gain_part, gain_second, place.across)
        )
        return remote(source, target, last_send.at[3 + index], last_recv.at[3 + index], device)

    gain_copy(0).start()
    scatter.pump(4, 2)
    kv_copy(1).wait_recv()
    kv_copy(2).wait_recv()
    kv_copy(0).wait_send()
    kv_copy(1).wait_send()
    wall[:, base_column:kv_end] = (
        kv_block(place.y, place.core)[...].astype(full) + kv_first[1].astype(full) + kv_second[...].astype(full)
    ).astype(low)
    scatter.relay(4)
    gain_copy(0).wait_recv()
    gain_copy(0).wait_send()
    gain_part[...] = gain_part[...] + gain_first[...]
    gain_copy(1).start()
    scatter.pump(group_gate, 3)
    gain_copy(1).wait_recv()
    gain_copy(1).wait_send()
    gain_part[...] = gain_part[...] + gain_second[...]

    gain_scatter = LineScatter(
        place,
        lambda group, origin: gain_part.at[pl.ds(origin * 8, 8)],
        lambda group, home: gain_side.at[pl.ds(home * 8, 8)],
        lambda group, column, slot: gain_line.at[pl.ds(slot * 8, 8)],
        [False],
        gain_side_send,
        gain_side_recv,
        gain_line_send,
        gain_line_recv,
        full,
    )
    gain_scatter.start(0)
    scatter.start(group_small)
    scatter.start(group_up)
    scatter.pump(group_gate, 1, 2)

    stores = []

    def store(group, targets, first, wide, padded):
        scatter.settle(group)
        for k, target in enumerate(targets):
            slot = 3 * len(chunks) if target is small_grad else len([done for done in stores if done[1]])
            down, right = slot // 2 * shard, slot % 2 * CHUNK
            if group == group_extra:
                down, right = 6 * shard, output_end - base_column
            held = acc.at[down : down + shard, right : right + padded]
            scatter.total(group, k * wide, (k + 1) * wide, held.at[:, 0:wide])
            copy = pltpu.make_async_copy(held, target.at[:, first : first + padded], store_sem.at[len(stores)])
            copy.start()
            stores.append((copy, target is not small_grad and group != group_extra))
            if target is small_grad:
                kv_own[...] = held[:, 0:quarter].astype(low)

    for c in range(last - 1):
        store(2 * c, (down_grad,), chunks[c][0], *[part_wide if c == 0 else CHUNK] * 2)
        store(2 * c + 1, (gate_grad, up_grad), *chunks[c])
    store(group_extra, (down_grad,), part_wide, CHUNK - part_wide, CHUNK - part_wide)
    scatter.relay(group_gate)
    store(group_last, (gate_grad, up_grad, down_grad), *chunks[last])
    gain_scatter.pump(0)
    store(2 * last - 2, (down_grad,), *chunks[last - 1])
    scatter.pump(group_small)
    gain_scatter.relay(0)
    scatter.relay(group_small)
    store(group_gate, (gate_grad,), *chunks[last - 1])
    scatter.pump(group_up, 3, 1)
    store(group_small, (small_grad,), 0, output_end - base_column, output_end - base_column)

    def own_block(y, core):
        return keyval_grad.at[:, pl.ds(pl.multiple_of((y * 2 + core) * quarter, quarter), quarter)]

    own_block(place.y, place.core)[...] = kv_own[...]
    targets = (place.mate, place.across, (place.dp, (1 - place.y) * 2 + (1 - place.core)))
    sends = [
        remote(kv_own, own_block(place.y, place.core), last_send.at[5 + i], last_recv.at[5 + i], target)
        for i, target in enumerate(targets)
    ]
    for copy in sends:
        copy.start()
    scatter.pump(group_up, 2)
    scatter.relay(group_up)
    gain_scatter.settle(0)
    gain_scatter.total(0, 0, gains_grad.shape[1], gains_grad)
    store(group_up, (up_grad,), *chunks[last - 1])
    for i, (y, core) in enumerate(
        ((place.y, 1 - place.core), (1 - place.y, place.core), (1 - place.y, 1 - place.core))
    ):
        remote(kv_own, own_block(y, core), last_send.at[5 + i], last_recv.at[5 + i], targets[i]).wait_recv()
    for copy in sends:
        copy.wait_send()
    kv_copy(2).wait_send()
    scatter.finish()
    gain_scatter.finish()
    proj_all.finish()
    in_scatter.finish()
    for copy, _ in stores:
        copy.wait()
    tokens_copy.wait()


def backward_call(sizes, small_args, hbm_args):
    lines, rows, width, head_dim, units = sizes
    length = 4 * rows
    columns = hbm_args[0].shape[1]
    shard = hbm_args[0].shape[0] // (2 * lines)
    gains = small_args[3].shape[1]
    quarter = head_dim // 2
    base_column = 2 * head_dim - quarter
    chunks = chunks_of(units)
    groups = 2 * len(chunks) + 2
    last_wide = columns - packed_columns(units, head_dim)[0][-1][0]
    vm = pl.BlockSpec(memory_space=pltpu.VMEM)
    hbm = pl.BlockSpec(memory_space=pl.ANY)
    padded = sum(c[2] for c in chunks)
    large = [((shard, padded), full)] * 3 + [((shard, 5 * quarter), full), ((rows, width), low)]
    outs = [
        ((shard, 2 * head_dim), low),
        ((8, gains // (2 * lines)), full),
    ]
    scratch = [((rows, width), low)] + [(a.shape, a.dtype) for a in small_args[1:]]
    scratch += [
        (hbm_args[0].shape, low),
        ((lines * shard, packed_columns(units, head_dim)[0][-1][0] - base_column), low),
        ((shard, last_wide + 2 * quarter), low),
        ((lines * shard, packed_columns(units, head_dim)[0][-1][0] - base_column), low),
        ((2 * lines * shard, last_wide + 2 * quarter), low),
        ((length, 6 * CHUNK), low),
        ((length, width), low),
        ((length, width), low),
        ((length, width), full),
        ((2, rows, width), low),
        ((rows, width), low),
        ((rows, width), low),
        ((length, head_dim), low),
        ((length, head_dim), low),
        ((length, head_dim), low),
        ((length, 2 * head_dim), low),
        ((rows, width), full),
        ((rows, width), low),
        ((2, width, quarter), low),
        ((width, quarter), low),
        ((width, quarter), low),
        ((shard, quarter), low),
        ((8, gains), full),
        ((2 * lines * 8, gains // (2 * lines)), full),
        ((2 * lines * 8, gains // (2 * lines)), full),
        ((2 * lines * 8, gains // (2 * lines)), full),
        ((lines * 8, gains // (2 * lines)), full),
        ((lines * 8, gains // (2 * lines)), full),
    ]
    sems = [(4, 3), (4, 3), (groups, 4), (groups, 4), (groups, 2, 4), (groups, 2, 4)]
    sems += [(1, 4), (1, 4), (1, 1, 4), (1, 1, 4), (8,), (8,)]
    sems += [(19 + 5 * len(chunks),), (3 + 3 * len(chunks),)]
    return pl.pallas_call(
        functools.partial(backward_kernel, sizes),
        out_shape=[jax.ShapeDtypeStruct(*item) for item in large + outs],
        in_specs=[hbm] * (len(small_args) + len(hbm_args)),
        out_specs=[hbm] * len(large) + [vm] * len(outs),
        scratch_shapes=[pltpu.VMEM(*item) for item in scratch] + [pltpu.SemaphoreType.DMA(dims) for dims in sems],
        compiler_params=pltpu.CompilerParams(
            collective_id=1, has_side_effects=True, vmem_limit_bytes=63 * 1024 * 1024
        ),
        name="backward",
    )(*small_args, *hbm_args)


def adam_values(weight, gradient, first, second, step_rate):
    moment = beta_first * first + (1.0 - beta_first) * gradient
    square = beta_second * second + (1.0 - beta_second) * gradient * gradient
    scaled = moment / (1.0 - beta_first**STEP) / (jnp.sqrt(square / (1.0 - beta_second**STEP)) + adam_eps)
    return moment, square, weight - step_rate * (scaled + decay_rate * weight)


def update_kernel(units, head_dim, cut, *refs):
    passed, grads, old = refs[:2], refs[2:8], refs[8:26]
    passed_out, new = refs[26:28], refs[28:46]
    held_passed, held_grads, held, load_sem, store_sem = refs[46:48], refs[48:54], refs[54:72], refs[72], refs[73]
    gate_grad, up_grad, down_grad, small_grad, keyval_grad, gains_grad = held_grads
    quarter = head_dim // 2
    shard = old[0].shape[0]
    rows = shard // cut
    wide = D ** (-0.5)
    count = [0, 0]

    def load(source, target, part):
        at = slice(None) if part is None else pl.ds(part * rows, rows)
        copy = pltpu.make_async_copy(source.at[at], target.at[at], load_sem.at[count[0]])
        count[0] += 1
        copy.start()
        return copy

    def store(source, target, part):
        at = slice(None) if part is None else pl.ds(part * rows, rows)
        copy = pltpu.make_async_copy(source.at[at], target.at[at], store_sem.at[count[1]])
        count[1] += 1
        copy.start()
        return copy

    jobs = [(3, part, (0, 1)) for part in range(cut)] + [(4, part, (2,)) for part in range(cut)]
    jobs += [(1, None, (4,)), (0, None, (3,)), (2, None, ()), (5, None, (5,))]
    waits = []
    for index, part, needs in jobs:
        own = range(3 * index, 3 * index + 3)
        waits.append(
            [load(old[i], held[i], part) for i in own] + [load(grads[i], held_grads[i], part) for i in needs]
        )
    through = [load(source, target, None) for source, target in zip(passed, held_passed)]
    waiting = []

    def work(index, part):
        weight, first, second = held[3 * index : 3 * index + 3]
        if index == 5:
            values = adam_values(weight[...], gains_grad[0], first[...], second[...], 0.3)
            for target, value in zip((first, second, weight), values):
                target[...] = value
            return
        step = rows if part is not None else shard // 3

        def some_rows(at):
            if index == 3:
                for kind, grad in enumerate((gate_grad, up_grad)):
                    values = adam_values(
                        weight[at, kind, :], grad[at, 0:units], first[at, kind, :], second[at, kind, :], wide
                    )
                    for target, value in zip((first, second, weight), values):
                        target[at, kind, :] = value
                return
            if index == 4:
                gradient, rate = down_grad[at, 0:units], FF ** (-0.5)
            elif index == 1:
                gradient, rate = keyval_grad[at].astype(full), wide
            elif index == 0:
                gradient, rate = small_grad[at, quarter : quarter + head_dim], wide
            else:
                gradient = small_grad[at, quarter + head_dim : quarter + 2 * head_dim]
                rate = (HEADS * HEAD_DIM) ** (-0.5)
            values = adam_values(weight[at], gradient, first[at], second[at], rate)
            for target, value in zip((first, second, weight), values):
                target[at] = value

        if part is not None:
            some_rows(pl.ds(part * rows, rows))
        else:

            def body(i, carry):
                some_rows(pl.ds(pl.multiple_of(i * step, step), step))
                return carry

            lax.fori_loop(0, 3, body, 0)

    for (index, part, _), copies in zip(jobs, waits):
        if index == 1:
            for copy, source, target in zip(through, held_passed, passed_out):
                copy.wait()
                waiting.append(store(source, target, None))
        for copy in copies:
            copy.wait()
        work(index, part)
        for kind, place in ((1, 0), (2, 1), (0, 2)):
            waiting.append(store(held[3 * index + kind], new[3 * index + place], part))
    for copy in waiting:
        copy.wait()


def update_call(units, head_dim, passed, grads, old, cut):
    hbm = pl.BlockSpec(memory_space=pl.ANY)
    outs = list(passed)
    for index in range(6):
        outs += [old[3 * index + kind] for kind in (1, 2, 0)]
    loads = 9 * cut + 18
    return pl.pallas_call(
        functools.partial(update_kernel, units, head_dim, cut),
        out_shape=[jax.ShapeDtypeStruct(a.shape, a.dtype) for a in outs],
        in_specs=[hbm] * (len(passed) + len(grads) + len(old)),
        out_specs=[hbm] * len(outs),
        scratch_shapes=[pltpu.VMEM(a.shape, a.dtype) for a in (*passed, *grads, *old)]
        + [pltpu.SemaphoreType.DMA((loads,)), pltpu.SemaphoreType.DMA((2 + 6 * cut + 12,))],
        compiler_params=pltpu.CompilerParams(vmem_limit_bytes=60 * 1024 * 1024),
        name="update",
    )(*passed, *grads, *old)


def mixed_dot(left, right):
    return jnp.dot(left, right, preferred_element_type=jnp.float32)


def rms_scale(vector, gain_vec):
    return (
        vector
        * lax.rsqrt(jnp.mean(vector * vector, axis=-1, keepdims=True) + eps_norm)
        * (1.0 + gain_vec)
    )


def rotate(vector, positions):
    half_dim = vector.shape[-1] // 2
    inv_freq = rope_base ** (-2.0 * jnp.arange(half_dim).astype(jnp.float32) / vector.shape[-1])
    angles = positions[:, None] * inv_freq[None, :]
    cosine = jnp.cos(angles)[:, None, :]
    sine_v = jnp.sin(angles)[:, None, :]
    front_half = vector[..., :half_dim]
    back_half = vector[..., half_dim:]
    return jnp.concatenate(
        [front_half * cosine - back_half * sine_v, back_half * cosine + front_half * sine_v],
        axis=-1,
    )


def adam_step(weight, gradient, moment, second, step_rate):
    moment = beta_first * moment + (1.0 - beta_first) * gradient
    second = beta_second * second + (1.0 - beta_second) * gradient * gradient
    scaled = (
        moment
        / (1.0 - beta_first**STEP)
        / (jnp.sqrt(second / (1.0 - beta_second**STEP)) + adam_eps)
    )
    return (moment, second, weight - step_rate * (scaled + decay_rate * weight))


def plain_device(
    tokens,
    cotangent,
    prefix,
    query_weight,
    keyval_weight,
    output_weight,
    gateup_weight,
    down_weight,
    norm_gains,
    query_first,
    keyval_first,
    output_first,
    gateup_first,
    down_first,
    gains_first,
    query_second,
    keyval_second,
    output_second,
    gateup_second,
    down_second,
    gains_second,
):
    rows_dev, width = tokens.shape
    length = rows_dev * lax.axis_size("tensor")
    query_full, keyval_full, output_full, gateup_full, down_full, gains_full = (
        lax.all_gather(query_weight.astype(jnp.bfloat16), "dp", axis=0, tiled=True),
        lax.all_gather(keyval_weight.astype(jnp.bfloat16), "dp", axis=0, tiled=True),
        lax.all_gather(output_weight.astype(jnp.bfloat16), "dp", axis=0, tiled=True),
        lax.all_gather(gateup_weight.astype(jnp.bfloat16), "dp", axis=0, tiled=True),
        lax.all_gather(down_weight.astype(jnp.bfloat16), "dp", axis=0, tiled=True),
        lax.all_gather(norm_gains.astype(jnp.bfloat16), "dp", axis=0, tiled=True),
    )
    head_dim = keyval_full.shape[1] // 2
    heads_dev = query_full.shape[1] // head_dim
    units = down_full.shape[1]
    gain_values = gains_full.astype(jnp.float32)
    gain_input = gain_values[0:width]
    gain_attn = gain_values[width : 2 * width]
    gain_pre = gain_values[2 * width : 3 * width]
    gain_ffn = gain_values[3 * width : 4 * width]
    gain_query = gain_values[4 * width : 4 * width + head_dim]
    gain_key = gain_values[4 * width + head_dim : 4 * width + 2 * head_dim]
    positions = jnp.arange(length).astype(jnp.float32)
    span_rows = min(512, length)
    count_blocks = length // span_rows
    starts = jnp.arange(0, length, span_rows, dtype=jnp.int32)
    columns = jnp.arange(length, dtype=jnp.int32)
    prefix_len = prefix[0]
    gateup_flat = gateup_full.reshape(width, 2 * units)

    def shape_query(raw_rows, gain_vec):
        return rotate(rms_scale(raw_rows, gain_vec), positions)

    def shape_key(raw_rows, gain_vec):
        return rotate(rms_scale(raw_rows[:, None, :], gain_vec), positions)[:, 0]

    token_rows = tokens.astype(jnp.float32)
    normed_local = rms_scale(token_rows, gain_input).astype(jnp.bfloat16)
    normed = lax.all_gather(normed_local, "tensor", axis=0, tiled=True)
    query_raw = mixed_dot(normed, query_full).reshape(length, heads_dev, head_dim)
    keyval_raw = mixed_dot(normed, keyval_full)
    query_rot = shape_query(query_raw, gain_query).astype(jnp.bfloat16)
    key_rot = shape_key(keyval_raw[:, :head_dim], gain_key).astype(jnp.bfloat16)
    value_low = keyval_raw[:, head_dim:].astype(jnp.bfloat16)

    def scores_of(row_start):
        row_ids = row_start + jnp.arange(span_rows, dtype=jnp.int32)
        q_blk = lax.dynamic_slice_in_dim(query_rot, row_start, span_rows, 0)
        raw_scores = (
            jnp.einsum("rhd,kd->hrk", q_blk, key_rot, preferred_element_type=jnp.float32)
            * query_scale
        )
        allowed = (columns[None, :] <= row_ids[:, None]) | (columns[None, :] < prefix_len)
        return (jnp.where(allowed[None], raw_scores, masked_fill), q_blk)

    def forward_block(row_start):
        scores, q_blk = scores_of(row_start)
        row_peak = jnp.max(scores, axis=-1, keepdims=True)
        shifted = jnp.exp(scores - row_peak)
        denom_sum = jnp.sum(shifted, axis=-1, keepdims=True)
        soft_probs = (shifted / denom_sum).astype(jnp.bfloat16)
        mixed_rows = jnp.einsum(
            "hrk,kd->rhd", soft_probs, value_low, preferred_element_type=jnp.float32
        )
        return (mixed_rows, (row_peak + jnp.log(denom_sum))[..., 0])

    attended_blocks, log_sums = lax.map(forward_block, starts)
    attended = attended_blocks.reshape(length, heads_dev * head_dim).astype(jnp.bfloat16)
    attn_part = jnp.einsum("rk,dk->rd", attended, output_full, preferred_element_type=jnp.float32)
    projected = lax.psum_scatter(
        attn_part.astype(jnp.bfloat16), "tensor", scatter_dimension=0, tiled=True
    ).astype(jnp.float32)
    hidden_state = token_rows + rms_scale(projected, gain_attn)
    normed_two = lax.all_gather(
        rms_scale(hidden_state, gain_pre).astype(jnp.bfloat16), "tensor", axis=0, tiled=True
    )
    gateup = mixed_dot(normed_two, gateup_flat)
    gate_part = gateup[:, :units]
    up_part = gateup[:, units:]
    activation = (jax.nn.gelu(gate_part, approximate=True) * up_part).astype(jnp.bfloat16)
    down_part = jnp.einsum("ru,du->rd", activation, down_full, preferred_element_type=jnp.float32)
    down_sum = lax.psum_scatter(
        down_part.astype(jnp.bfloat16), "tensor", scatter_dimension=0, tiled=True
    ).astype(jnp.float32)
    block_out = hidden_state + rms_scale(down_sum, gain_ffn)
    grad_out = cotangent.astype(jnp.float32)
    pull_ffn = jax.vjp(rms_scale, down_sum, gain_ffn)[1]
    grad_down, grad_gain_ffn = pull_ffn(grad_out)
    down_back = lax.all_gather(grad_down.astype(jnp.bfloat16), "tensor", axis=0, tiled=True)
    grad_activation = mixed_dot(down_back, down_full)
    grad_down_w = jnp.einsum("rd,ru->du", down_back, activation, preferred_element_type=jnp.float32)

    def geglu(gate_in, up_in):
        return jax.nn.gelu(gate_in, approximate=True) * up_in

    pull_act = jax.vjp(geglu, gate_part, up_part)[1]
    grad_gate, grad_up = pull_act(grad_activation)
    grad_gateup = jnp.concatenate([grad_gate, grad_up], axis=1).astype(jnp.bfloat16)
    grad_gateup_w = jnp.einsum(
        "rd,ru->du", normed_two, grad_gateup, preferred_element_type=jnp.float32
    ).reshape(width, 2, units)
    grad_normed_two = jnp.einsum(
        "ru,du->rd", grad_gateup, gateup_flat, preferred_element_type=jnp.float32
    )
    grad_pre_rows = lax.psum_scatter(
        grad_normed_two.astype(jnp.bfloat16), "tensor", scatter_dimension=0, tiled=True
    ).astype(jnp.float32)
    pull_pre = jax.vjp(rms_scale, hidden_state, gain_pre)[1]
    grad_hidden_norm, grad_gain_pre = pull_pre(grad_pre_rows)
    grad_hidden = grad_out + grad_hidden_norm
    pull_attn = jax.vjp(rms_scale, projected, gain_attn)[1]
    grad_proj, grad_gain_attn = pull_attn(grad_hidden)
    proj_back = lax.all_gather(grad_proj.astype(jnp.bfloat16), "tensor", axis=0, tiled=True)
    grad_output_w = jnp.einsum("rd,rk->dk", proj_back, attended, preferred_element_type=jnp.float32)
    grad_attended = (
        mixed_dot(proj_back, output_full)
        .astype(jnp.bfloat16)
        .reshape(count_blocks, span_rows, heads_dev, head_dim)
    )

    def backward_block(carry, batch_item):
        key_acc, value_acc = carry
        row_start, grad_att, lse_blk = batch_item
        scores, q_blk = scores_of(row_start)
        soft_full = jnp.exp(scores - lse_blk[..., None])
        grad_probs = jnp.einsum(
            "rhd,kd->hrk", grad_att, value_low, preferred_element_type=jnp.float32
        )
        delta_rows = jnp.sum(soft_full * grad_probs, axis=-1, keepdims=True)
        grad_scores = (soft_full * (grad_probs - delta_rows)).astype(jnp.bfloat16)
        grad_query = (
            jnp.einsum("hrk,kd->rhd", grad_scores, key_rot, preferred_element_type=jnp.float32)
            * query_scale
        )
        key_acc = (
            key_acc
            + jnp.einsum("hrk,rhd->kd", grad_scores, q_blk, preferred_element_type=jnp.float32)
            * query_scale
        )
        value_acc = value_acc + jnp.einsum(
            "hrk,rhd->kd",
            soft_full.astype(jnp.bfloat16),
            grad_att,
            preferred_element_type=jnp.float32,
        )
        return ((key_acc, value_acc), grad_query)

    zero_rows = jnp.zeros((length, head_dim), jnp.float32)
    (grad_key_rot, grad_value), grad_query_blocks = lax.scan(
        backward_block, (zero_rows, zero_rows), (starts, grad_attended, log_sums)
    )
    grad_query_rot = grad_query_blocks.reshape(length, heads_dev, head_dim)
    pull_query = jax.vjp(shape_query, query_raw, gain_query)[1]
    grad_query_raw, grad_gain_query = pull_query(grad_query_rot)
    pull_key = jax.vjp(shape_key, keyval_raw[:, :head_dim], gain_key)[1]
    grad_key_raw, grad_gain_key = pull_key(grad_key_rot)
    grad_query_low = grad_query_raw.reshape(length, heads_dev * head_dim).astype(jnp.bfloat16)
    grad_keyval = jnp.concatenate([grad_key_raw, grad_value], axis=1)
    grad_query_w = jnp.einsum(
        "rd,rk->dk", normed, grad_query_low, preferred_element_type=jnp.float32
    )
    grad_normed_query = jnp.einsum(
        "rk,dk->rd", grad_query_low, query_full, preferred_element_type=jnp.float32
    )
    grad_normed_part, grad_keyval_own = (
        lax.psum_scatter(
            grad_normed_query.astype(jnp.bfloat16), "tensor", scatter_dimension=0, tiled=True
        ).astype(jnp.float32),
        lax.psum_scatter(
            grad_keyval.astype(jnp.bfloat16), "tensor", scatter_dimension=0, tiled=True
        ).astype(jnp.float32),
    )
    grad_keyval_low = grad_keyval_own.astype(jnp.bfloat16)
    grad_keyval_w = jnp.einsum(
        "rd,rk->dk", normed_local, grad_keyval_low, preferred_element_type=jnp.float32
    )
    grad_normed = grad_normed_part + jnp.einsum(
        "rk,dk->rd", grad_keyval_low, keyval_full, preferred_element_type=jnp.float32
    )
    pull_input = jax.vjp(rms_scale, token_rows, gain_input)[1]
    grad_token_norm, grad_gain_input = pull_input(grad_normed)
    tokens_grad = (grad_hidden + grad_token_norm).astype(jnp.bfloat16)
    grad_gains = jnp.concatenate(
        [
            grad_gain_input,
            grad_gain_attn,
            grad_gain_pre,
            grad_gain_ffn,
            grad_gain_query,
            grad_gain_key,
        ]
    )
    keyval_total, gains_total = (
        lax.psum(grad_keyval_w.astype(jnp.bfloat16), "tensor").astype(jnp.float32),
        lax.psum(grad_gains.astype(jnp.bfloat16), "tensor").astype(jnp.float32),
    )
    query_sum, keyval_sum, output_sum, gateup_sum, down_grad_sum, gains_sum = (
        lax.psum_scatter(grad_query_w, "dp", scatter_dimension=0, tiled=True),
        lax.psum_scatter(keyval_total, "dp", scatter_dimension=0, tiled=True),
        lax.psum_scatter(grad_output_w, "dp", scatter_dimension=0, tiled=True),
        lax.psum_scatter(grad_gateup_w, "dp", scatter_dimension=0, tiled=True),
        lax.psum_scatter(grad_down_w, "dp", scatter_dimension=0, tiled=True),
        lax.psum_scatter(gains_total, "dp", scatter_dimension=0, tiled=True),
    )
    query_moment, query_square, query_master = adam_step(
        query_weight, query_sum, query_first, query_second, D ** (-0.5)
    )
    keyval_moment, keyval_square, keyval_master = adam_step(
        keyval_weight, keyval_sum, keyval_first, keyval_second, D ** (-0.5)
    )
    output_moment, output_square, output_master = adam_step(
        output_weight, output_sum, output_first, output_second, (HEADS * HEAD_DIM) ** (-0.5)
    )
    gateup_moment, gateup_square, gateup_master = adam_step(
        gateup_weight, gateup_sum, gateup_first, gateup_second, D ** (-0.5)
    )
    down_moment, down_square, down_master = adam_step(
        down_weight, down_grad_sum, down_first, down_second, FF ** (-0.5)
    )
    gains_moment, gains_square, gains_master = adam_step(
        norm_gains, gains_sum, gains_first, gains_second, 0.3
    )
    return (
        block_out.astype(jnp.bfloat16),
        tokens_grad,
        query_moment,
        query_square,
        query_master,
        keyval_moment,
        keyval_square,
        keyval_master,
        output_moment,
        output_square,
        output_master,
        gateup_moment,
        gateup_square,
        gateup_master,
        down_moment,
        down_square,
        down_master,
        gains_moment,
        gains_square,
        gains_master,
    )


def per_device(
    tokens,
    cotangent,
    prefix,
    query_weight,
    keyval_weight,
    output_weight,
    gateup_weight,
    down_weight,
    norm_gains,
    query_first,
    keyval_first,
    output_first,
    gateup_first,
    down_first,
    gains_first,
    query_second,
    keyval_second,
    output_second,
    gateup_second,
    down_second,
    gains_second,
):
    rows, width = tokens.shape
    lines = lax.axis_size("dp") // 2
    shard = query_weight.shape[0]
    head_dim = keyval_weight.shape[1] // 2
    units = down_weight.shape[1]
    fits = (
        lax.axis_size("tensor") == 4
        and lax.axis_size("dp") == 8
        and len(chunks_of(units)) == 4
        and query_weight.shape[1] == head_dim
        and shard % 16 == 0
        and norm_gains.shape[0] % 128 == 0
        and (3 * len(chunks_of(units)) + 2) // 2 * shard <= 4 * rows
    )
    if not fits:
        return plain_device(
            tokens,
            cotangent,
            prefix,
            query_weight,
            keyval_weight,
            output_weight,
            gateup_weight,
            down_weight,
            norm_gains,
            query_first,
            keyval_first,
            output_first,
            gateup_first,
            down_first,
            gains_first,
            query_second,
            keyval_second,
            output_second,
            gateup_second,
            down_second,
            gains_second,
        )
    length = 4 * rows
    sizes = (lines, rows, width, head_dim, units)
    weights = (keyval_weight, query_weight, output_weight, gateup_weight, down_weight)
    angles = np.arange(length)[:, None] * (rope_base ** (-2.0 * np.arange(head_dim // 2) / head_dim))[None, :]
    cosine = jnp.asarray(np.cos(angles), full)
    sine = jnp.asarray(np.sin(angles), full)
    *saved, gvec, proj, hidden, grad_down, dgain_ffn, block_out = forward_call(
        sizes, prefix, tokens, cotangent, norm_gains, weights, cosine, sine
    )
    *grads, tokens_grad, keyval_sum, gains_sum = backward_call(
        sizes, (grad_down, cotangent, tokens, gvec, dgain_ffn, proj, hidden, cosine, sine), saved
    )
    old = (
        query_weight,
        query_first,
        query_second,
        keyval_weight,
        keyval_first,
        keyval_second,
        output_weight,
        output_first,
        output_second,
        gateup_weight,
        gateup_first,
        gateup_second,
        down_weight,
        down_first,
        down_second,
        norm_gains,
        gains_first,
        gains_second,
    )
    return tuple(update_call(units, head_dim, (block_out, tokens_grad), (*grads, keyval_sum, gains_sum), old, 3))


def solution(mesh):
    placed = (
        P(("dp", "tensor"), None),
        P(("dp", "tensor"), None),
        P("dp"),
        P("dp", "tensor"),
        P("dp", None),
        P("dp", "tensor"),
        P("dp", None, "tensor"),
        P("dp", "tensor"),
        P("dp"),
        P("dp", "tensor"),
        P("dp", None),
        P("dp", "tensor"),
        P("dp", None, "tensor"),
        P("dp", "tensor"),
        P("dp"),
        P("dp", "tensor"),
        P("dp", None),
        P("dp", "tensor"),
        P("dp", None, "tensor"),
        P("dp", "tensor"),
        P("dp"),
    )
    return jax.shard_map(
        per_device,
        mesh=mesh,
        in_specs=placed,
        out_specs=(
            P(("dp", "tensor"), None),
            P(("dp", "tensor"), None),
            P("dp", "tensor"),
            P("dp", "tensor"),
            P("dp", "tensor"),
            P("dp", None),
            P("dp", None),
            P("dp", None),
            P("dp", "tensor"),
            P("dp", "tensor"),
            P("dp", "tensor"),
            P("dp", None, "tensor"),
            P("dp", None, "tensor"),
            P("dp", None, "tensor"),
            P("dp", "tensor"),
            P("dp", "tensor"),
            P("dp", "tensor"),
            P("dp"),
            P("dp"),
            P("dp"),
        ),
        check_vma=False,
    )
```
